32 devices in a mesh: groups: 2 (over y), store: 16 (over z, x, core).
Axes of the slice: x: 2, y: 2, z: 4, core: 2. Of those that a mesh axis runs over, the one named last changes fastest.
Arguments:
- store: bfloat16 [4096, 16, 1024], P(('groups', 'store')), parts along dimension 0, may hold values from -6 to 6
- page_table: int32 [32, 128], P(('groups', 'store')), parts along dimension 0, may hold values from 0 to 2047, as said below
- sel_pos: int32 [32, 160], P(('groups', 'store')), parts along dimension 0, may hold values from 0 to 2047, as said below
- fresh_kv: bfloat16 [32, 160, 1024], P(('groups', 'store')), parts along dimension 0, may hold values from -6 to 6
- queries: bfloat16 [32, 160, 6144], P(('groups', 'store')), parts along dimension 0, may hold values from -256 to 256
Outputs:
- attended: bfloat16 [32, 160, 6144], P(('groups', 'store')), parts along dimension 0
- store_out: bfloat16 [4096, 16, 1024], P(('groups', 'store')), parts along dimension 0
The draws below stay inside these ranges and needn't reach their ends.
There are 2 independent parts, one for each index of `groups`. The reference program is written for one: setup_inputs(seed, part) draws one part's arguments, and reference() takes and returns one part's arrays. A program takes and returns all parts, laid end to end along the dimension named above; each array names one. Nothing has to cross between parts.
Inputs may be any that keep to these rules, and one draw needn't show every extreme that they name: `page_table`: every page slot appears exactly once in the whole table. Slot s lies on device s // 128 of store. One request has at most 8 pages on any one device, and exactly 8 on some. `sel_pos`: each row rises strictly. At most 2 positions of one row fall in one page of 16 tokens, and exactly 2 in some page of every row.
All inputs are finite; a program needn't handle non-finite values.
Results may differ from the reference program's by a relative error of at most 0.0039.
Values may be sent and summed in bfloat16 or wider, within the bound.
No kernel may reach another device: no remote copies, remote signals or barrier semaphores. Data moves between devices by JAX's collectives and lax.ppermute only.
A program may use at most 192 MiB of HBM per device.

```python
import jax
import jax.numpy as jnp
from jax import lax

HEAD_WIDTH = 128
KEY_VALUE_HEADS = 4
QUERY_GROUP = 12
PAGE_TOKENS = 16
SELP = 2
HQ = 48
TOKEN_FEATURES = 1024
PAGES_REQ = 128
CONTEXT_TOKENS = 2048
HOLD = 128
REDONE_TOKENS = 160
REQUEST_COUNT = 16
STORE_SLOTS = 2048


def base_keys(key):
    sampled_values = jax.random.normal(jax.random.fold_in(key, 11), (REQUEST_COUNT, REDONE_TOKENS, KEY_VALUE_HEADS * HEAD_WIDTH), jnp.float32)
    return jnp.clip(sampled_values, -6.0, 6.0)


def draw_page_table(key, part):
    key = jax.random.fold_in(key, 3)
    first, second, third = jax.random.split(key, 3)
    offsets = jax.random.permutation(first, REQUEST_COUNT)
    spread = jax.random.permutation(second, PAGES_REQ)
    local_rows = jax.random.permutation(third, PAGES_REQ)
    holders = (offsets[:, None] + spread[None, :]) % REQUEST_COUNT
    return (holders * HOLD + local_rows[None, :]).astype(jnp.int32)


def draw_sel_pos(key, part):
    key = jax.random.fold_in(key, 5)
    first, second = jax.random.split(key, 2)
    pattern = jnp.array([SELP, 1, 3 * SELP // 4, SELP // 2], jnp.int32)
    page_order = jax.vmap(lambda sub: jax.random.permutation(sub, PAGES_REQ))(jax.random.split(first, REQUEST_COUNT))
    counts = pattern[page_order % 4]
    inside = jax.vmap(lambda sub: jax.random.permutation(sub, PAGE_TOKENS))(jax.random.split(second, REQUEST_COUNT * PAGES_REQ))
    inside = inside.reshape(REQUEST_COUNT, PAGES_REQ, PAGE_TOKENS)
    picked_rows = (inside < counts[:, :, None]).reshape(REQUEST_COUNT, CONTEXT_TOKENS)
    picked = jax.vmap(lambda marks: jnp.nonzero(marks, size=REDONE_TOKENS)[0])(picked_rows)
    return picked.astype(jnp.int32)


def draw_fresh_kv(key, part):
    key_rows = base_keys(key)
    key = jax.random.fold_in(key, 7)
    value_rows = jnp.clip(jax.random.normal(key, (REQUEST_COUNT, REDONE_TOKENS, KEY_VALUE_HEADS * HEAD_WIDTH), jnp.float32), -6.0, 6.0)
    return jnp.concatenate([key_rows, value_rows], axis=-1).astype(jnp.bfloat16)


def draw_queries(key, part):
    key = jax.random.fold_in(key, 9)
    sampled_values = jnp.clip(jax.random.normal(key, (REQUEST_COUNT, REDONE_TOKENS, KEY_VALUE_HEADS, QUERY_GROUP, HEAD_WIDTH), jnp.float32), -6.0, 6.0)
    return sampled_values.reshape(REQUEST_COUNT, REDONE_TOKENS, KEY_VALUE_HEADS * QUERY_GROUP * HEAD_WIDTH).astype(jnp.bfloat16)


def steps_of(own_key, shape, shards, low, top_value):
    loudness, own = 1.0, jax.random.fold_in(own_key, 6)
    for axis_at, blocks in shards:
        draws = jnp.exp(jax.random.uniform(jax.random.fold_in(own, axis_at), (blocks,), jnp.float32, low / len(shards), top_value / len(shards)))
        loudness = loudness * jnp.repeat(draws, shape[axis_at] // blocks).reshape([-1 if axis == axis_at else 1 for axis in range(len(shape))])
    return loudness


def gaussian(rng, dims, deviation, reach, shards=(), kind=jnp.bfloat16):
    values = jax.random.normal(rng, dims, jnp.float32) * deviation
    if len(shards) > 0:
        values = steps_of(rng, dims, shards, -0.22, 0.18) * values
    return jnp.clip(values, min=-reach, max=reach).astype(kind)


def setup_inputs(seed: int = 0, part: int = 0) -> dict:
    seeds = jax.random.split(jax.random.key(seed), 6)
    own_keys = jax.random.split(jax.random.fold_in(seeds[5], part), 6)
    return {
        "store": gaussian(own_keys[0], (STORE_SLOTS, PAGE_TOKENS, TOKEN_FEATURES), 1.0, 6.0, ((0, 16),)),
        "page_table": draw_page_table(jax.random.fold_in(jax.random.fold_in(seeds[5], part), 71), part),
        "sel_pos": draw_sel_pos(jax.random.fold_in(jax.random.fold_in(seeds[5], part), 71), part),
        "fresh_kv": draw_fresh_kv(jax.random.fold_in(jax.random.fold_in(seeds[5], part), 71), part),
        "queries": draw_queries(jax.random.fold_in(jax.random.fold_in(seeds[5], part), 71), part),
    }


def attend(query_matrix, mixed_output, positions):
    query_head_rows = query_matrix.reshape(REDONE_TOKENS, KEY_VALUE_HEADS, QUERY_GROUP, HEAD_WIDTH).astype(jnp.float32)
    key_portion = mixed_output[:, :KEY_VALUE_HEADS * HEAD_WIDTH].reshape(CONTEXT_TOKENS, KEY_VALUE_HEADS, HEAD_WIDTH).astype(jnp.float32)
    value_portion = mixed_output[:, KEY_VALUE_HEADS * HEAD_WIDTH:].reshape(CONTEXT_TOKENS, KEY_VALUE_HEADS, HEAD_WIDTH).astype(jnp.float32)
    scores = jnp.einsum('sgih,cgh->sgic', query_head_rows, key_portion) / jnp.sqrt(jnp.float32(HEAD_WIDTH))
    visible = jnp.arange(CONTEXT_TOKENS)[None, :] <= positions[:, None]
    scores = jnp.where(visible[:, None, None, :], scores, jnp.float32(-1e+30))
    peak = lax.optimization_barrier(jnp.max(scores, axis=-1, keepdims=True))
    raised = jnp.exp(scores - peak)
    total = lax.optimization_barrier(jnp.sum(raised, axis=-1, keepdims=True))
    weights = raised.astype(jnp.bfloat16).astype(jnp.float32)
    mixed = jnp.einsum('sgic,cgh->sgih', weights, value_portion) / total
    return mixed.astype(jnp.bfloat16).reshape(REDONE_TOKENS, HQ * HEAD_WIDTH)

def reference(store, page_table, sel_pos, fresh_kv, queries):

    def one_request(request):
        request_context = jnp.take(store, page_table[request], axis=0).reshape(CONTEXT_TOKENS, TOKEN_FEATURES)
        request_context = request_context.at[sel_pos[request]].set(fresh_kv[request])
        return attend(queries[request], request_context, sel_pos[request])
    attended = lax.map(one_request, jnp.arange(REQUEST_COUNT, dtype=jnp.int32))
    page_index = (sel_pos // PAGE_TOKENS).astype(jnp.int32)
    slot_ids = jnp.take_along_axis(page_table, page_index, axis=1)
    targets = (slot_ids * PAGE_TOKENS + sel_pos % PAGE_TOKENS).astype(jnp.int32)
    flattened_store = store.reshape(STORE_SLOTS * PAGE_TOKENS, TOKEN_FEATURES)
    flattened_store = flattened_store.at[targets.reshape(-1)].set(fresh_kv.reshape(REQUEST_COUNT * REDONE_TOKENS, TOKEN_FEATURES))
    return (attended, flattened_store.reshape(STORE_SLOTS, PAGE_TOKENS, TOKEN_FEATURES))
```

```python
import functools

import jax
import jax.numpy as jnp
from jax import lax
from jax.experimental import pallas as pl
from jax.experimental.pallas import tpu as pltpu
from jax.sharding import PartitionSpec as P

HEAD_WIDTH = 128
KEY_VALUE_HEADS = 4
QUERY_GROUP = 12
SELP = 2
LANES = 128
OFFSET_LANE = 64
QUERY_BLOCK = 32
TILE_PAGES = 16
HIDDEN = -1e30


def nt_dot(a, b):
    return lax.dot_general(a, b, (((1,), (1,)), ((), ())), preferred_element_type=jnp.float32)


def plan_kernel(hold, holders, row_slots, page_len, table_ref, sel_ref, fresh_ref, out_ref, wide):
    pages = table_ref.shape[1]
    picked = sel_ref.shape[1]
    wide_lanes = wide.shape[1]
    chunks = fresh_ref.shape[1] // LANES
    f32 = jnp.float32
    slot_row = jnp.broadcast_to(table_ref[...], (pages, pages))
    owner_row = slot_row // hold
    local_row = (slot_row - owner_row * hold).astype(f32)
    owner_row = owner_row.astype(f32)
    owner_col = owner_row.T
    sub = lax.broadcasted_iota(jnp.int32, (pages, pages), 0)
    lane = lax.broadcasted_iota(jnp.int32, (pages, pages), 1)
    earlier = jnp.where((owner_row == owner_col) & (lane < sub), 1.0, 0.0)
    rank_col = jnp.sum(earlier, axis=1, keepdims=True)
    owner_col = owner_col[:, 0:1]

    holder = lax.broadcasted_iota(jnp.int32, (holders, pages), 0).astype(f32)
    owned = jnp.where(holder == owner_row[0:1, :], local_row[0:1, :], 0.0)
    at_rank = jnp.where(lane.astype(f32) == rank_col, 1.0, 0.0)
    numbers = jnp.dot(
        owned.astype(jnp.bfloat16), at_rank.astype(jnp.bfloat16), preferred_element_type=f32
    )

    wide[...] = jnp.full(wide.shape, -1, jnp.int32)
    wide[0:1, 0:picked] = sel_ref[...]
    position = wide[...]
    page = lax.shift_right_arithmetic(position, page_len.bit_length() - 1)
    offset = (position & (page_len - 1)).astype(f32)
    lane8 = lax.broadcasted_iota(jnp.int32, wide.shape, 1)
    second = jnp.where((page == pltpu.roll(page, 1, axis=1)) & (lane8 > 0), 1.0, 0.0)
    page, offset, second = page[0:1], offset[0:1], second[0:1]
    valid = lane8[0:1] < picked
    sub_wide = lax.broadcasted_iota(jnp.int32, (pages, wide_lanes), 0)
    in_page = jnp.where(sub_wide == page, 1.0, 0.0)
    owner = jnp.sum(in_page * owner_col, axis=0, keepdims=True)
    place = SELP * jnp.sum(in_page * rank_col, axis=0, keepdims=True) + second
    spot = jnp.where(valid, owner * row_slots + place, -1.0)

    holder_wide = lax.broadcasted_iota(jnp.int32, (holders, wide_lanes), 0).astype(f32)
    marked = jnp.where((holder_wide == owner) & valid, offset + 1.0, 0.0)
    place_lane = lax.broadcasted_iota(jnp.int32, (LANES, wide_lanes), 0).astype(f32)
    at_place = jnp.where(place_lane == place + OFFSET_LANE, 1.0, 0.0)
    offsets = nt_dot(marked.astype(jnp.bfloat16), at_place.astype(jnp.bfloat16))
    index_rows = numbers + offsets

    spot_row = spot[:, 0:picked]
    spots = holders * row_slots
    step = min(spots, 256)
    for start in range(0, spots, step):
        spot_id = lax.broadcasted_iota(jnp.int32, (step, picked), 0).astype(f32) + float(start)
        choose = jnp.where(spot_id == spot_row, 1.0, 0.0).astype(jnp.bfloat16)
        rows = jnp.dot(choose, fresh_ref[...], preferred_element_type=f32).astype(jnp.bfloat16)
        for h in range(step // row_slots):
            for c in range(chunks):
                out_ref[start // row_slots + h, c * row_slots : (c + 1) * row_slots, :] = rows[
                    h * row_slots : (h + 1) * row_slots, c * LANES : (c + 1) * LANES
                ]
    for h in range(holders):
        out_ref[h, chunks * row_slots :, :] = jnp.broadcast_to(
            index_rows[h : h + 1, :], (16, LANES)
        ).astype(jnp.bfloat16)


def apply_kernel(splits, row_slots, entries_ref, store_ref, store_out, *rest):
    sends = rest[: len(splits)]
    blended, index_vmem, index_smem, load_sem, index_sem, store_sem, send_sem = rest[len(splits) :]
    holders, capacity = blended.shape[0], blended.shape[1]
    page_len, width = store_ref.shape[1], store_ref.shape[2]
    chunks = width // LANES

    def index_row(r, carry):
        block = entries_ref[r, chunks * row_slots :, :].astype(jnp.float32).astype(jnp.int32)
        index_vmem[pl.ds(r, 1), :] = block[0:1, :]
        return carry

    lax.fori_loop(0, holders, index_row, 0)
    index_copy = pltpu.make_async_copy(index_vmem, index_smem, index_sem)
    index_copy.start()
    index_copy.wait()

    row_id = lax.broadcasted_iota(jnp.int32, (page_len, LANES), 0)

    def one_request(r, carry):
        for k in range(capacity):
            number = index_smem[r, k]
            first = index_smem[r, OFFSET_LANE + SELP * k] - 1
            second = index_smem[r, OFFSET_LANE + SELP * k + 1] - 1
            is_first = row_id == first
            is_second = row_id == second
            for c in range(chunks):
                rows = entries_ref[r, c * row_slots : (c + 1) * row_slots, :].astype(jnp.float32)
                old = store_ref[number, :, c * LANES : (c + 1) * LANES].astype(jnp.float32)
                new = jnp.where(is_first, rows[SELP * k : SELP * k + 1, :], old)
                new = jnp.where(is_second, rows[SELP * k + 1 : SELP * k + 2, :], new)
                blended[r, k, :, c * LANES : (c + 1) * LANES] = new.astype(jnp.bfloat16)
        for (low, high), send in zip(splits, sends):
            pltpu.make_async_copy(blended.at[r, pl.ds(low, high - low)], send.at[r], send_sem).start()
        for k in range(capacity):
            number = index_smem[r, k]
            pltpu.make_async_copy(blended.at[r, k], store_out.at[number], store_sem).start()
        return carry

    lax.fori_loop(0, holders, one_request, 0)
    for (low, high), send in zip(splits, sends):
        pltpu.make_async_copy(send, send, send_sem).wait()
    pltpu.make_async_copy(store_out, store_out, store_sem).wait()


def attend_kernel(first, last, source_ref, tiles_ref, sel_ref, position_ref, query_ref, *rest):
    rest = list(rest)
    state_in = [] if first else [rest.pop(0) for _ in range(3)]
    context = rest.pop(0)
    outs = [rest.pop(0) for _ in range(1 if last else 3)]
    kv, mixed, peak, total, sem = rest
    pages, page_len = context.shape[0], context.shape[1]
    block = query_ref.shape[0]
    tile = TILE_PAGES * page_len
    rows = QUERY_GROUP * block
    scale = 1.4426950408889634 / HEAD_WIDTH**0.5
    f32 = jnp.float32
    step = pl.program_id(0)

    @pl.when(step == 0)
    def _():
        def fetch(i, carry):
            pltpu.make_async_copy(context.at[source_ref[i]], kv.at[i], sem).start()
            return carry

        lax.fori_loop(0, pages, fetch, 0)
        pltpu.make_async_copy(context, kv, sem).wait()

    lane = lax.broadcasted_iota(jnp.int32, (block, LANES), 1)
    for g in range(KEY_VALUE_HEADS):
        for i in range(QUERY_GROUP):
            head = g * QUERY_GROUP + i
            part = slice(i * block, (i + 1) * block)
            if first:
                mixed[g, part, :] = jnp.zeros((block, LANES), f32)
                peak[g, part, :] = jnp.full((block, LANES), HIDDEN, f32)
                total[g, part, :] = jnp.zeros((block, LANES), f32)
            else:
                mixed[g, part, :] = state_in[0][:, head * LANES : (head + 1) * LANES]
                peak[g, part, :] = jnp.broadcast_to(
                    state_in[1][:, head : head + 1], (block, LANES)
                )
                total[g, part, :] = jnp.where(lane == 0, state_in[2][:, head : head + 1], 0.0)

    sel = sel_ref[...]

    def one_tile(t, carry):
        start = pl.multiple_of(t * tile, tile)
        where_page = pl.ds(pl.multiple_of(t * TILE_PAGES, TILE_PAGES), TILE_PAGES)
        position = position_ref[:, pl.ds(start, tile)]
        bias = jnp.where(position <= sel, 0.0, HIDDEN).astype(f32)
        bias = jnp.concatenate([bias] * QUERY_GROUP, axis=0)
        for g in range(KEY_VALUE_HEADS):
            q = jnp.concatenate(
                [
                    query_ref[:, (g * QUERY_GROUP + i) * LANES : (g * QUERY_GROUP + i + 1) * LANES]
                    for i in range(QUERY_GROUP)
                ],
                axis=0,
            )
            key = kv[where_page, :, g * LANES : (g + 1) * LANES].reshape(tile, LANES)
            at = (KEY_VALUE_HEADS + g) * LANES
            value = kv[where_page, :, at : at + LANES].reshape(tile, LANES)
            scores = nt_dot(q, key) + bias
            old = peak[g, :, 0:1]
            new = jnp.maximum(old, jnp.max(scores, axis=1, keepdims=True))
            raised = jnp.exp2((scores - new) * scale)
            shrink = jnp.exp2((old - new) * scale)
            partial = raised[:, 0:LANES]
            for c in range(1, tile // LANES):
                partial = partial + raised[:, c * LANES : (c + 1) * LANES]
            total[g] = total[g] * shrink + partial
            mixed[g] = mixed[g] * shrink + jnp.dot(
                raised.astype(jnp.bfloat16), value, preferred_element_type=f32
            )
            peak[g] = jnp.broadcast_to(new, (rows, LANES))
        return carry

    lax.fori_loop(0, tiles_ref[step], one_tile, 0)

    for g in range(KEY_VALUE_HEADS):
        whole = jnp.sum(total[g], axis=1, keepdims=True)
        if last:
            done = (mixed[g] / whole).astype(jnp.bfloat16)
        for i in range(QUERY_GROUP):
            head = g * QUERY_GROUP + i
            part = slice(i * block, (i + 1) * block)
            if last:
                outs[0][:, head * LANES : (head + 1) * LANES] = done[part, :]
            else:
                outs[0][:, head * LANES : (head + 1) * LANES] = mixed[g, part, :]
                outs[1][:, head : head + 1] = peak[g, part, 0:1]
                outs[2][:, head : head + 1] = whole[part, :]


def attend(first, last, source, tiles, sel_column, position, queries, state, context):
    picked, features = queries.shape
    pages, page_len, width = context.shape
    steps = picked // QUERY_BLOCK
    rows = QUERY_GROUP * QUERY_BLOCK
    wide = pl.BlockSpec((QUERY_BLOCK, features), lambda b, *_: (b, 0))
    narrow = pl.BlockSpec((QUERY_BLOCK, LANES), lambda b, *_: (b, 0))
    state_specs = [wide, narrow, narrow]
    state_shapes = [
        jax.ShapeDtypeStruct((picked, features), jnp.float32),
        jax.ShapeDtypeStruct((picked, LANES), jnp.float32),
        jax.ShapeDtypeStruct((picked, LANES), jnp.float32),
    ]
    share = 0.6
    return pl.pallas_call(
        functools.partial(attend_kernel, first, last),
        grid_spec=pltpu.PrefetchScalarGridSpec(
            num_scalar_prefetch=2,
            grid=(steps,),
            in_specs=[
                pl.BlockSpec((QUERY_BLOCK, 1), lambda b, *_: (b, 0)),
                pl.BlockSpec((1, pages * page_len), lambda b, *_: (0, 0)),
                wide,
                *([] if first else state_specs),
                pl.BlockSpec(memory_space=pl.ANY),
            ],
            out_specs=[wide] if last else state_specs,
            scratch_shapes=[
                pltpu.VMEM((pages, page_len, width), jnp.bfloat16),
                pltpu.VMEM((KEY_VALUE_HEADS, rows, LANES), jnp.float32),
                pltpu.VMEM((KEY_VALUE_HEADS, rows, LANES), jnp.float32),
                pltpu.VMEM((KEY_VALUE_HEADS, rows, LANES), jnp.float32),
                pltpu.SemaphoreType.DMA,
            ],
        ),
        out_shape=[jax.ShapeDtypeStruct((picked, features), jnp.bfloat16)] if last else state_shapes,
        compiler_params=pltpu.CompilerParams(
            dimension_semantics=("arbitrary",), vmem_limit_bytes=40 * 1024 * 1024
        ),
        cost_estimate=pl.CostEstimate(
            flops=int(share * 8 * picked * features * pages * page_len),
            bytes_accessed=2 * pages * page_len * width + 6 * picked * features,
            transcendentals=int(share * picked * features // LANES * pages * page_len),
        ),
    )(source, tiles, sel_column, position, queries, *state, context)


def page_order(slots, positions, hold, splits, page_len):
    pages = slots.shape[0]
    number = jnp.arange(pages)
    before = number[None, :] < number[:, None]
    owners = slots // hold
    ranks = jnp.sum(((owners[None, :] == owners[:, None]) & before).astype(jnp.int32), axis=1)
    last_page = positions.reshape(-1, QUERY_BLOCK)[:, -1] // page_len
    orders = []
    for low, high in splits:
        member = (ranks >= low) & (ranks < high)
        count = pages * (high - low) // splits[-1][1]
        place = jnp.sum((member[None, :] & before).astype(jnp.int32), axis=1)
        hit = (member[None, :] & (place[None, :] == jnp.arange(count)[:, None])).astype(jnp.int32)
        source = jnp.sum(hit * (owners * (high - low) + ranks - low)[None, :], axis=1)
        page = jnp.sum(hit * number[None, :], axis=1)
        position = (page[:, None] * page_len + jnp.arange(page_len)[None, :]).reshape(1, -1)
        seen = jnp.sum((page[None, :] <= last_page[:, None]).astype(jnp.int32), axis=1)
        orders.append((source, (seen + TILE_PAGES - 1) // TILE_PAGES, position))
    return orders


def per_device(store, page_table, sel_pos, fresh_kv, queries):
    holders = lax.axis_size("store")
    hold, page_len, width = store.shape
    pages = page_table.shape[1]
    picked = sel_pos.shape[1]
    capacity = max(1, pages // holders)
    row_slots = -(-SELP * capacity // 16) * 16
    chunks = width // LANES
    packed_rows = chunks * row_slots + 16
    late = capacity // 4
    splits = ((0, capacity - late), (capacity - late, capacity)) if late else ((0, capacity),)

    packed = pl.pallas_call(
        functools.partial(plan_kernel, hold, holders, row_slots, page_len),
        out_shape=jax.ShapeDtypeStruct((holders, packed_rows, LANES), jnp.bfloat16),
        scratch_shapes=[pltpu.VMEM((8, -(-picked // LANES) * LANES), jnp.int32)],
        compiler_params=pltpu.CompilerParams(vmem_limit_bytes=32 * 1024 * 1024),
    )(page_table, sel_pos, fresh_kv[0])
    entries = lax.all_to_all(packed, "store", split_axis=0, concat_axis=0, tiled=True)

    any_space = pl.BlockSpec(memory_space=pl.ANY)
    vmem = pl.BlockSpec(memory_space=pltpu.VMEM)
    store_out, *parts = pl.pallas_call(
        functools.partial(apply_kernel, splits, row_slots),
        out_shape=[
            jax.ShapeDtypeStruct(store.shape, store.dtype),
            *[
                jax.ShapeDtypeStruct((holders, high - low, page_len, width), store.dtype)
                for low, high in splits
            ],
        ],
        in_specs=[vmem, vmem],
        out_specs=[any_space] * (1 + len(splits)),
        scratch_shapes=[
            pltpu.VMEM((holders, capacity, page_len, width), store.dtype),
            pltpu.VMEM((holders, LANES), jnp.int32),
            pltpu.SMEM((holders, LANES), jnp.int32),
            pltpu.SemaphoreType.DMA,
            pltpu.SemaphoreType.DMA,
            pltpu.SemaphoreType.DMA,
            pltpu.SemaphoreType.DMA,
        ],
        compiler_params=pltpu.CompilerParams(vmem_limit_bytes=32 * 1024 * 1024),
    )(entries, store)

    orders = page_order(page_table[0], sel_pos[0], hold, splits, page_len)
    sel_column = sel_pos.reshape(picked, 1)
    arrived = [
        lax.all_to_all(part, "store", split_axis=0, concat_axis=0, tiled=True).reshape(
            -1, page_len, width
        )
        for part in parts
    ]
    state = ()
    for at, (context, (source, tiles, position)) in enumerate(zip(arrived, orders)):
        state = attend(
            at == 0,
            at == len(splits) - 1,
            source,
            tiles,
            sel_column,
            position,
            queries[0],
            state,
            context,
        )
    return (state[0][None], store_out)


def solution(mesh):
    return jax.shard_map(
        per_device,
        mesh=mesh,
        in_specs=(
            P(("groups", "store"), None, None),
            P(("groups", "store"), None),
            P(("groups", "store"), None),
            P(("groups", "store"), None, None),
            P(("groups", "store"), None, None),
        ),
        out_specs=(P(("groups", "store"), None, None), P(("groups", "store"), None, None)),
        check_vma=False,
    )
```

```python
import functools

import jax
import jax.numpy as jnp
from jax import lax
from jax.experimental import pallas as pl
from jax.experimental.pallas import tpu as pltpu
from jax.sharding import PartitionSpec as P

HEAD_WIDTH = 128
KEY_VALUE_HEADS = 4
QUERY_GROUP = 12
SELP = 2
LANES = 128
VMEM_LIMIT = 60 * 1024 * 1024
QUERY_BLOCK = 32
TILE_PAGES = 16
HIDDEN = -1e30


def nt_dot(a, b):
    return lax.dot_general(a, b, (((1,), (1,)), ((), ())), preferred_element_type=jnp.float32)


def plan_kernel(hold, holders, row_slots, page_len, table_ref, sel_ref, fresh_ref, out_ref, wide):
    pages = table_ref.shape[1]
    picked = sel_ref.shape[1]
    wide_lanes = wide.shape[1]
    chunks = fresh_ref.shape[1] // LANES
    f32 = jnp.float32
    slot_row = jnp.broadcast_to(table_ref[...], (pages, pages))
    owner_row = slot_row // hold
    local_row = (slot_row - owner_row * hold).astype(f32)
    owner_row = owner_row.astype(f32)
    owner_col = owner_row.T
    sub = lax.broadcasted_iota(jnp.int32, (pages, pages), 0)
    lane = lax.broadcasted_iota(jnp.int32, (pages, pages), 1)
    earlier = jnp.where((owner_row == owner_col) & (lane < sub), 1.0, 0.0)
    rank_col = jnp.sum(earlier, axis=1, keepdims=True)
    owner_col = owner_col[:, 0:1]

    holder = lax.broadcasted_iota(jnp.int32, (holders, pages), 0).astype(f32)
    owned = jnp.where(holder == owner_row[0:1, :], local_row[0:1, :], 0.0)
    at_rank = jnp.where(lane.astype(f32) == rank_col, 1.0, 0.0)
    numbers = jnp.dot(
        owned.astype(jnp.bfloat16), at_rank.astype(jnp.bfloat16), preferred_element_type=f32
    )

    wide[...] = jnp.full(wide.shape, -1, jnp.int32)
    wide[0:1, 0:picked] = sel_ref[...]
    position = wide[...]
    page = lax.shift_right_arithmetic(position, page_len.bit_length() - 1)
    offset = (position & (page_len - 1)).astype(f32)
    lane8 = lax.broadcasted_iota(jnp.int32, wide.shape, 1)
    second = jnp.where((page == pltpu.roll(page, 1, axis=1)) & (lane8 > 0), 1.0, 0.0)
    page, offset, second = page[0:1], offset[0:1], second[0:1]
    valid = lane8[0:1] < picked
    sub_wide = lax.broadcasted_iota(jnp.int32, (pages, wide_lanes), 0)
    in_page = jnp.where(sub_wide == page, 1.0, 0.0)
    owner = jnp.sum(in_page * owner_col, axis=0, keepdims=True)
    rank = jnp.sum(in_page * rank_col, axis=0, keepdims=True)
    place = SELP * rank + second
    spot = jnp.where(valid, owner * row_slots + place, -1.0)

    holder_wide = lax.broadcasted_iota(jnp.int32, (holders, wide_lanes), 0).astype(f32)
    marked = jnp.where((holder_wide == owner) & valid, rank * page_len + offset + 1.0, 0.0)
    place_lane = lax.broadcasted_iota(jnp.int32, (LANES, wide_lanes), 0).astype(f32)
    at_place = jnp.where(place_lane == place, 1.0, 0.0)
    targets = nt_dot(marked.astype(jnp.bfloat16), at_place.astype(jnp.bfloat16))

    spot_row = spot[:, 0:picked]
    spots = holders * row_slots
    step = min(spots, 256)
    for start in range(0, spots, step):
        spot_id = lax.broadcasted_iota(jnp.int32, (step, picked), 0).astype(f32) + float(start)
        choose = jnp.where(spot_id == spot_row, 1.0, 0.0).astype(jnp.bfloat16)
        rows = jnp.dot(choose, fresh_ref[...], preferred_element_type=f32).astype(jnp.bfloat16)
        for h in range(step // row_slots):
            for c in range(chunks):
                out_ref[start // row_slots + h, c * row_slots : (c + 1) * row_slots, :] = rows[
                    h * row_slots : (h + 1) * row_slots, c * LANES : (c + 1) * LANES
                ]
    sub16 = lax.broadcasted_iota(jnp.int32, (16, LANES), 0)
    for h in range(holders):
        block = jnp.where(sub16 == 0, numbers[h : h + 1, :], 0.0)
        block = jnp.where(sub16 == 1, targets[h : h + 1, :], block)
        out_ref[h, chunks * row_slots :, :] = block.astype(jnp.bfloat16)


def blend_kernel(splits, row_slots, entries_hbm, store_hbm, *rest):
    sends, numbers_out = rest[: len(splits)], rest[len(splits)]
    store, blended, entries, numbers, load_sem, index_sem, entries_sem, send_sem = rest[len(splits) + 1 :]
    holders, capacity, page_len, width = blended.shape
    chunks = width // LANES
    rows_here = capacity * page_len
    f32 = jnp.float32
    load = pltpu.make_async_copy(store_hbm, store, load_sem)
    arrive = pltpu.make_async_copy(entries_hbm, entries, entries_sem)
    arrive.start()
    load.start()
    arrive.wait()

    def index_row(r, carry):
        block = entries[r, chunks * row_slots :, :].astype(f32).astype(jnp.int32)
        numbers_out[pl.ds(r, 1), :] = block[0:1, :]
        return carry

    lax.fori_loop(0, holders, index_row, 0)
    index_copy = pltpu.make_async_copy(numbers_out, numbers, index_sem)
    index_copy.start()
    index_copy.wait()
    load.wait()

    row_id = lax.broadcasted_iota(jnp.int32, (rows_here, row_slots), 0).astype(f32)

    def one_request(r, carry):
        targets = entries[r, chunks * row_slots :, :].astype(f32)[1:2, 0:row_slots] - 1.0
        hit = jnp.where(row_id == targets, 1.0, 0.0)
        keep = 1.0 - jnp.sum(hit, axis=1, keepdims=True)
        keep = jnp.broadcast_to(keep, (rows_here, LANES)).astype(jnp.bfloat16)
        hit = hit.astype(jnp.bfloat16)
        for c in range(chunks):
            lanes = slice(c * LANES, (c + 1) * LANES)
            rows = entries[r, c * row_slots : (c + 1) * row_slots, :]
            fresh = jnp.dot(hit, rows, preferred_element_type=f32).astype(jnp.bfloat16)
            for k in range(capacity):
                part = slice(k * page_len, (k + 1) * page_len)
                blended[r, k, :, lanes] = store[numbers[r, k], :, lanes] * keep[part] + fresh[part]
        for (low, high), send in zip(splits, sends):
            pltpu.make_async_copy(blended.at[r, pl.ds(low, high - low)], send.at[r], send_sem).start()
        return carry

    lax.fori_loop(0, holders, one_request, 0)
    for send in sends:
        pltpu.make_async_copy(send, send, send_sem).wait()


def write_back_kernel(splits, numbers, *rest):
    sends, store_out, sem = rest[: len(splits)], rest[len(splits)], rest[len(splits) + 1]
    holders = numbers.shape[0]

    def one_request(r, carry):
        for (low, high), send in zip(splits, sends):
            for k in range(low, high):
                pltpu.make_async_copy(send.at[r, k - low], store_out.at[numbers[r, k]], sem).start()
        return carry

    lax.fori_loop(0, holders, one_request, 0)
    pltpu.make_async_copy(store_out, store_out, sem).wait()


def attend_kernel(first, last, source, page_number, tiles, sel_ref, query_ref, *rest):
    rest = list(rest)
    state_in = [] if first else [rest.pop(0) for _ in range(2)]
    context = rest.pop(0)
    outs = [rest.pop(0) for _ in range(1 if last else 2)]
    kv, values, query, mixed, stats, sem = rest
    pages, page_len = context.shape[0], context.shape[1]
    block = query_ref.shape[0]
    tile = TILE_PAGES * page_len
    lanes = QUERY_GROUP * block
    scale = 1.4426950408889634 / HEAD_WIDTH**0.5
    f32 = jnp.float32
    step = pl.program_id(0)
    eye = jnp.where(
        lax.broadcasted_iota(jnp.int32, (LANES, LANES), 0)
        == lax.broadcasted_iota(jnp.int32, (LANES, LANES), 1),
        1.0,
        0.0,
    ).astype(jnp.bfloat16)

    @pl.when(step == 0)
    def _():
        def fetch(i, carry):
            pltpu.make_async_copy(context.at[source[i]], kv.at[i], sem).start()
            return carry

        lax.fori_loop(0, pages, fetch, 0)
        pltpu.make_async_copy(context, kv, sem).wait()

        def turn(t, carry):
            here = pl.ds(t * TILE_PAGES, TILE_PAGES)
            for g in range(KEY_VALUE_HEADS):
                at = (KEY_VALUE_HEADS + g) * LANES
                value = kv[here, :, at : at + LANES].reshape(tile, LANES)
                values[t, g] = nt_dot(eye, value).astype(jnp.bfloat16)
            return carry

        lax.fori_loop(0, pages // TILE_PAGES, turn, 0)

    for g in range(KEY_VALUE_HEADS):
        for i in range(QUERY_GROUP):
            head = g * QUERY_GROUP + i
            query[g, i * block : (i + 1) * block, :] = query_ref[:, head * LANES : (head + 1) * LANES]
    if first:
        mixed[...] = jnp.zeros(mixed.shape, f32)
        stats[0:KEY_VALUE_HEADS, :] = jnp.full((KEY_VALUE_HEADS, lanes), HIDDEN, f32)
        stats[KEY_VALUE_HEADS:, :] = jnp.zeros((KEY_VALUE_HEADS, lanes), f32)
    else:
        mixed[...] = state_in[0][0]
        stats[...] = state_in[1][0]

    sel = sel_ref[0]
    in_page = lax.broadcasted_iota(jnp.int32, (page_len, LANES), 0)

    def one_tile(t, carry):
        here = pl.ds(t * TILE_PAGES, TILE_PAGES)
        bias = jnp.concatenate(
            [
                jnp.where(in_page + page_number[t * TILE_PAGES + k] * page_len <= sel, 0.0, HIDDEN)
                for k in range(TILE_PAGES)
            ],
            axis=0,
        ).astype(f32)
        scores = []
        for g in range(KEY_VALUE_HEADS):
            key = kv[here, :, g * LANES : (g + 1) * LANES].reshape(tile, LANES)
            scores.append(nt_dot(key, query[g]))
        for g in range(KEY_VALUE_HEADS):
            raised, shrinks = [], []
            for n in range(lanes // LANES):
                part = slice(n * LANES, (n + 1) * LANES)
                s = scores[g][:, part] + bias
                old = stats[g : g + 1, part]
                new = jnp.maximum(old, jnp.max(s, axis=0, keepdims=True))
                p = jnp.exp2((s - new) * scale)
                shrink = jnp.exp2((old - new) * scale)
                at = KEY_VALUE_HEADS + g
                stats[at : at + 1, part] = stats[at : at + 1, part] * shrink + jnp.sum(
                    p, axis=0, keepdims=True
                )
                stats[g : g + 1, part] = new
                raised.append(p.astype(jnp.bfloat16))
                shrinks.append(shrink)
            raised = jnp.concatenate(raised, axis=1)
            shrink = jnp.concatenate(shrinks, axis=1)
            mixed[g] = mixed[g] * shrink + jnp.dot(
                values[t, g], raised, preferred_element_type=f32
            )
        return carry

    lax.fori_loop(0, tiles[step], one_tile, 0)

    if last:
        for g in range(KEY_VALUE_HEADS):
            at = KEY_VALUE_HEADS + g
            done = (mixed[g] * (1.0 / stats[at : at + 1, :])).astype(jnp.bfloat16)
            for n in range(lanes // LANES):
                turned = nt_dot(eye, done[:, n * LANES : (n + 1) * LANES]).astype(jnp.bfloat16)
                for i in range(LANES // block):
                    head = g * QUERY_GROUP + n * (LANES // block) + i
                    outs[0][:, head * LANES : (head + 1) * LANES] = turned[
                        i * block : (i + 1) * block, :
                    ]
    else:
        outs[0][0] = mixed[...]
        outs[1][0] = stats[...]


def attend(first, last, order, sel_lanes, queries, state, context):
    picked, features = queries.shape
    pages, page_len, width = context.shape
    steps = picked // QUERY_BLOCK
    lanes = QUERY_GROUP * QUERY_BLOCK
    wide = pl.BlockSpec((QUERY_BLOCK, features), lambda b, *_: (b, 0))
    state_specs = [
        pl.BlockSpec((1, KEY_VALUE_HEADS, LANES, lanes), lambda b, *_: (b, 0, 0, 0)),
        pl.BlockSpec((1, 2 * KEY_VALUE_HEADS, lanes), lambda b, *_: (b, 0, 0)),
    ]
    state_shapes = [
        jax.ShapeDtypeStruct((steps, KEY_VALUE_HEADS, LANES, lanes), jnp.float32),
        jax.ShapeDtypeStruct((steps, 2 * KEY_VALUE_HEADS, lanes), jnp.float32),
    ]
    share = 0.6
    return pl.pallas_call(
        functools.partial(attend_kernel, first, last),
        grid_spec=pltpu.PrefetchScalarGridSpec(
            num_scalar_prefetch=3,
            grid=(steps,),
            in_specs=[
                pl.BlockSpec((1, 1, LANES), lambda b, *_: (b, 0, 0)),
                wide,
                *([] if first else state_specs),
                pl.BlockSpec(memory_space=pltpu.HBM),
            ],
            out_specs=[wide] if last else state_specs,
            scratch_shapes=[
                pltpu.VMEM((pages, page_len, width), jnp.bfloat16),
                pltpu.VMEM(
                    (pages // TILE_PAGES, KEY_VALUE_HEADS, LANES, TILE_PAGES * page_len), jnp.bfloat16
                ),
                pltpu.VMEM((KEY_VALUE_HEADS, lanes, LANES), jnp.bfloat16),
                pltpu.VMEM((KEY_VALUE_HEADS, LANES, lanes), jnp.float32),
                pltpu.VMEM((2 * KEY_VALUE_HEADS, lanes), jnp.float32),
                pltpu.SemaphoreType.DMA,
            ],
        ),
        out_shape=[jax.ShapeDtypeStruct((picked, features), jnp.bfloat16)] if last else state_shapes,
        compiler_params=pltpu.CompilerParams(
            dimension_semantics=("arbitrary",), vmem_limit_bytes=VMEM_LIMIT
        ),
        cost_estimate=pl.CostEstimate(
            flops=int(share * 8 * picked * features * pages * page_len),
            bytes_accessed=2 * pages * page_len * width + 6 * picked * features,
            transcendentals=int(share * picked * features // LANES * pages * page_len),
        ),
    )(*order, sel_lanes, queries, *state, context)


def page_order(slots, positions, hold, splits, page_len):
    pages = slots.shape[0]
    number = jnp.arange(pages)
    before = number[None, :] < number[:, None]
    owners = slots // hold
    ranks = jnp.sum(((owners[None, :] == owners[:, None]) & before).astype(jnp.int32), axis=1)
    last_page = positions.reshape(-1, QUERY_BLOCK)[:, -1] // page_len
    orders = []
    for low, high in splits:
        member = (ranks >= low) & (ranks < high)
        count = pages * (high - low) // splits[-1][1]
        place = jnp.sum((member[None, :] & before).astype(jnp.int32), axis=1)
        hit = (member[None, :] & (place[None, :] == jnp.arange(count)[:, None])).astype(jnp.int32)
        source = jnp.sum(hit * (owners * (high - low) + ranks - low)[None, :], axis=1)
        page = jnp.sum(hit * number[None, :], axis=1)
        seen = jnp.sum((page[None, :] <= last_page[:, None]).astype(jnp.int32), axis=1)
        orders.append((source, page, (seen + TILE_PAGES - 1) // TILE_PAGES))
    return orders


def per_device(store, page_table, sel_pos, fresh_kv, queries):
    holders = lax.axis_size("store")
    hold, page_len, width = store.shape
    pages = page_table.shape[1]
    picked = sel_pos.shape[1]
    capacity = max(1, pages // holders)
    row_slots = -(-SELP * capacity // 16) * 16
    chunks = width // LANES
    packed_rows = chunks * row_slots + 16
    late = capacity // 4
    splits = ((0, capacity - late), (capacity - late, capacity)) if late else ((0, capacity),)
    hbm = pl.BlockSpec(memory_space=pltpu.HBM)
    vmem = pl.BlockSpec(memory_space=pltpu.VMEM)
    params = pltpu.CompilerParams(vmem_limit_bytes=VMEM_LIMIT)

    packed = pl.pallas_call(
        functools.partial(plan_kernel, hold, holders, row_slots, page_len),
        out_shape=jax.ShapeDtypeStruct((holders, packed_rows, LANES), jnp.bfloat16),
        scratch_shapes=[pltpu.VMEM((8, -(-picked // LANES) * LANES), jnp.int32)],
        compiler_params=params,
    )(page_table, sel_pos, fresh_kv[0])
    entries = lax.all_to_all(packed, "store", split_axis=0, concat_axis=0, tiled=True)

    *parts, numbers = pl.pallas_call(
        functools.partial(blend_kernel, splits, row_slots),
        out_shape=[
            *[
                jax.ShapeDtypeStruct((holders, high - low, page_len, width), store.dtype)
                for low, high in splits
            ],
            jax.ShapeDtypeStruct((holders, LANES), jnp.int32),
        ],
        in_specs=[hbm, hbm],
        out_specs=[hbm] * len(splits) + [vmem],
        scratch_shapes=[
            pltpu.VMEM(store.shape, store.dtype),
            pltpu.VMEM((holders, capacity, page_len, width), store.dtype),
            pltpu.VMEM((holders, packed_rows, LANES), store.dtype),
            pltpu.SMEM((holders, LANES), jnp.int32),
            pltpu.SemaphoreType.DMA,
            pltpu.SemaphoreType.DMA,
            pltpu.SemaphoreType.DMA,
            pltpu.SemaphoreType.DMA,
        ],
        compiler_params=params,
    )(entries, store)

    store_out = pl.pallas_call(
        functools.partial(write_back_kernel, splits),
        grid_spec=pltpu.PrefetchScalarGridSpec(
            num_scalar_prefetch=1,
            grid=(1,),
            in_specs=[hbm] * len(splits),
            out_specs=hbm,
            scratch_shapes=[pltpu.SemaphoreType.DMA],
        ),
        out_shape=jax.ShapeDtypeStruct(store.shape, store.dtype),
        compiler_params=params,
        cost_estimate=pl.CostEstimate(flops=0, bytes_accessed=4 * store.size, transcendentals=0),
    )(numbers, *parts)

    orders = page_order(page_table[0], sel_pos[0], hold, splits, page_len)
    sel_lanes = jnp.tile(sel_pos.reshape(-1, 1, QUERY_BLOCK), (1, 1, LANES // QUERY_BLOCK))
    arrived = [
        lax.all_to_all(part, "store", split_axis=0, concat_axis=0, tiled=True).reshape(
            -1, page_len, width
        )
        for part in parts
    ]
    state = ()
    for at, (context, order) in enumerate(zip(arrived, orders)):
        state = attend(
            at == 0, at == len(splits) - 1, order, sel_lanes, queries[0], state, context
        )
    return (state[0][None], store_out)


def solution(mesh):
    return jax.shard_map(
        per_device,
        mesh=mesh,
        in_specs=(
            P(("groups", "store"), None, None),
            P(("groups", "store"), None),
            P(("groups", "store"), None),
            P(("groups", "store"), None, None),
            P(("groups", "store"), None, None),
        ),
        out_specs=(P(("groups", "store"), None, None), P(("groups", "store"), None, None)),
        check_vma=False,
    )
```

```python
import functools

import jax
import jax.numpy as jnp
from jax import lax
from jax.experimental import pallas as pl
from jax.experimental.pallas import tpu as pltpu
from jax.sharding import PartitionSpec as P

HEAD_WIDTH = 128
KEY_VALUE_HEADS = 4
QUERY_GROUP = 12
SELP = 2
LANES = 128
VMEM_LIMIT = 60 * 1024 * 1024
QUERY_BLOCK = 32
TILE_PAGES = 16
LATE_TILE_PAGES = 8
HIDDEN = -1e30


def nt_dot(a, b):
    return lax.dot_general(a, b, (((1,), (1,)), ((), ())), preferred_element_type=jnp.float32)


def plan_kernel(hold, holders, row_slots, page_len, table_ref, sel_ref, fresh_ref, out_ref, wide):
    pages = table_ref.shape[1]
    picked = sel_ref.shape[1]
    wide_lanes = wide.shape[1]
    chunks = fresh_ref.shape[1] // LANES
    f32 = jnp.float32
    slot_row = jnp.broadcast_to(table_ref[...], (pages, pages))
    owner_row = slot_row // hold
    local_row = (slot_row - owner_row * hold).astype(f32)
    owner_row = owner_row.astype(f32)
    owner_col = owner_row.T
    sub = lax.broadcasted_iota(jnp.int32, (pages, pages), 0)
    lane = lax.broadcasted_iota(jnp.int32, (pages, pages), 1)
    earlier = jnp.where((owner_row == owner_col) & (lane < sub), 1.0, 0.0)
    rank_col = jnp.sum(earlier, axis=1, keepdims=True)
    owner_col = owner_col[:, 0:1]

    holder = lax.broadcasted_iota(jnp.int32, (holders, pages), 0).astype(f32)
    owned = jnp.where(holder == owner_row[0:1, :], local_row[0:1, :], 0.0)
    at_rank = jnp.where(lane.astype(f32) == rank_col, 1.0, 0.0)
    numbers = jnp.dot(
        owned.astype(jnp.bfloat16), at_rank.astype(jnp.bfloat16), preferred_element_type=f32
    )

    wide[...] = jnp.full(wide.shape, -1, jnp.int32)
    wide[0:1, 0:picked] = sel_ref[...]
    position = wide[...]
    page = lax.shift_right_arithmetic(position, page_len.bit_length() - 1)
    offset = (position & (page_len - 1)).astype(f32)
    lane8 = lax.broadcasted_iota(jnp.int32, wide.shape, 1)
    second = jnp.where((page == pltpu.roll(page, 1, axis=1)) & (lane8 > 0), 1.0, 0.0)
    page, offset, second = page[0:1], offset[0:1], second[0:1]
    valid = lane8[0:1] < picked
    sub_wide = lax.broadcasted_iota(jnp.int32, (pages, wide_lanes), 0)
    in_page = jnp.where(sub_wide == page, 1.0, 0.0)
    owner = jnp.sum(in_page * owner_col, axis=0, keepdims=True)
    rank = jnp.sum(in_page * rank_col, axis=0, keepdims=True)
    place = SELP * rank + second
    spot = jnp.where(valid, owner * row_slots + place, -1.0)

    holder_wide = lax.broadcasted_iota(jnp.int32, (holders, wide_lanes), 0).astype(f32)
    marked = jnp.where((holder_wide == owner) & valid, rank * page_len + offset + 1.0, 0.0)
    place_lane = lax.broadcasted_iota(jnp.int32, (LANES, wide_lanes), 0).astype(f32)
    at_place = jnp.where(place_lane == place, 1.0, 0.0)
    targets = nt_dot(marked.astype(jnp.bfloat16), at_place.astype(jnp.bfloat16))

    spot_row = spot[:, 0:picked]
    spots = holders * row_slots
    step = min(spots, 256)
    for start in range(0, spots, step):
        spot_id = lax.broadcasted_iota(jnp.int32, (step, picked), 0).astype(f32) + float(start)
        choose = jnp.where(spot_id == spot_row, 1.0, 0.0).astype(jnp.bfloat16)
        rows = jnp.dot(choose, fresh_ref[...], preferred_element_type=f32).astype(jnp.bfloat16)
        for h in range(step // row_slots):
            for c in range(chunks):
                out_ref[start // row_slots + h, c * row_slots : (c + 1) * row_slots, :] = rows[
                    h * row_slots : (h + 1) * row_slots, c * LANES : (c + 1) * LANES
                ]
    sub16 = lax.broadcasted_iota(jnp.int32, (16, LANES), 0)
    for h in range(holders):
        block = jnp.where(sub16 == 0, numbers[h : h + 1, :], 0.0)
        block = jnp.where(sub16 == 1, targets[h : h + 1, :], block)
        out_ref[h, chunks * row_slots :, :] = block.astype(jnp.bfloat16)


def blend_kernel(splits, row_slots, entries_hbm, store_hbm, *rest):
    sends, numbers_out = rest[: len(splits)], rest[len(splits)]
    store, blended, entries, numbers, load_sem, index_sem, entries_sem, send_sem = rest[len(splits) + 1 :]
    holders, capacity, page_len, width = blended.shape
    chunks = width // LANES
    rows_here = capacity * page_len
    f32 = jnp.float32
    load = pltpu.make_async_copy(store_hbm, store, load_sem)
    arrive = pltpu.make_async_copy(entries_hbm, entries, entries_sem)
    arrive.start()
    load.start()
    arrive.wait()

    def index_row(r, carry):
        block = entries[r, chunks * row_slots :, :].astype(f32).astype(jnp.int32)
        numbers_out[pl.ds(r, 1), :] = block[0:1, :]
        return carry

    lax.fori_loop(0, holders, index_row, 0)
    index_copy = pltpu.make_async_copy(numbers_out, numbers, index_sem)
    index_copy.start()
    index_copy.wait()
    load.wait()

    row_id = lax.broadcasted_iota(jnp.int32, (rows_here, row_slots), 0).astype(f32)

    def one_request(r, carry):
        targets = entries[r, chunks * row_slots :, :].astype(f32)[1:2, 0:row_slots] - 1.0
        hit = jnp.where(row_id == targets, 1.0, 0.0)
        keep = 1.0 - jnp.sum(hit, axis=1, keepdims=True)
        keep = jnp.broadcast_to(keep, (rows_here, LANES)).astype(jnp.bfloat16)
        hit = hit.astype(jnp.bfloat16)
        for c in range(chunks):
            lanes = slice(c * LANES, (c + 1) * LANES)
            rows = entries[r, c * row_slots : (c + 1) * row_slots, :]
            fresh = jnp.dot(hit, rows, preferred_element_type=f32).astype(jnp.bfloat16)
            for k in range(capacity):
                part = slice(k * page_len, (k + 1) * page_len)
                blended[r, k, :, lanes] = store[numbers[r, k], :, lanes] * keep[part] + fresh[part]
        for (low, high), send in zip(splits, sends):
            pltpu.make_async_copy(blended.at[r, pl.ds(low, high - low)], send.at[r], send_sem).start()
        return carry

    lax.fori_loop(0, holders, one_request, 0)
    for send in sends:
        pltpu.make_async_copy(send, send, send_sem).wait()


def write_back_kernel(splits, numbers, *rest):
    sends, store_out = rest[: len(splits)], rest[len(splits)]
    held, load_sem, sem = rest[len(splits) + 1 : -2], rest[-2], rest[-1]
    holders = numbers.shape[0]
    loads = [pltpu.make_async_copy(send, part, load_sem) for send, part in zip(sends, held)]
    for load in loads:
        load.start()
    for load in loads:
        load.wait()

    def one_request(r, carry):
        for (low, high), part in zip(splits, held):
            for k in range(low, high):
                pltpu.make_async_copy(part.at[r, k - low], store_out.at[numbers[r, k]], sem).start()
        return carry

    lax.fori_loop(0, holders, one_request, 0)
    pltpu.make_async_copy(store_out, store_out, sem).wait()


def attend_kernel(first, last, tile_pages, source, page_number, tiles, sel_ref, query_ref, *rest):
    rest = list(rest)
    state_in = [] if first else [rest.pop(0) for _ in range(2)]
    context = rest.pop(0)
    outs = [rest.pop(0) for _ in range(1 if last else 2)]
    kv, values, query, mixed, stats, sem = rest
    pages, page_len = context.shape[0], context.shape[1]
    block = query_ref.shape[0]
    tile = tile_pages * page_len
    lanes = QUERY_GROUP * block
    scale = 1.4426950408889634 / HEAD_WIDTH**0.5
    f32 = jnp.float32
    step = pl.program_id(0)
    eye = jnp.where(
        lax.broadcasted_iota(jnp.int32, (LANES, LANES), 0)
        == lax.broadcasted_iota(jnp.int32, (LANES, LANES), 1),
        1.0,
        0.0,
    ).astype(jnp.bfloat16)

    @pl.when(step == 0)
    def _():
        def fetch(i, carry):
            pltpu.make_async_copy(context.at[source[i]], kv.at[i], sem).start()
            return carry

        lax.fori_loop(0, pages, fetch, 0)
        pltpu.make_async_copy(context, kv, sem).wait()

        def turn(t, carry):
            here = pl.ds(t * tile_pages, tile_pages)
            for g in range(KEY_VALUE_HEADS):
                at = (KEY_VALUE_HEADS + g) * LANES
                value = kv[here, :, at : at + LANES].reshape(tile, LANES)
                values[t, g] = nt_dot(eye, value).astype(jnp.bfloat16)
            return carry

        lax.fori_loop(0, pages // tile_pages, turn, 0)

    for g in range(KEY_VALUE_HEADS):
        for i in range(QUERY_GROUP):
            head = g * QUERY_GROUP + i
            query[g, i * block : (i + 1) * block, :] = query_ref[:, head * LANES : (head + 1) * LANES]
    if first:
        mixed[...] = jnp.zeros(mixed.shape, f32)
        stats[0:KEY_VALUE_HEADS, :] = jnp.full((KEY_VALUE_HEADS, lanes), HIDDEN, f32)
        stats[KEY_VALUE_HEADS:, :] = jnp.zeros((KEY_VALUE_HEADS, lanes), f32)
    else:
        mixed[...] = state_in[0][0]
        stats[...] = state_in[1][0]

    sel = sel_ref[0]
    in_page = lax.broadcasted_iota(jnp.int32, (page_len, LANES), 0)

    def one_tile(t, carry):
        here = pl.ds(t * tile_pages, tile_pages)
        bias = jnp.concatenate(
            [
                jnp.where(in_page + page_number[t * tile_pages + k] * page_len <= sel, 0.0, HIDDEN)
                for k in range(tile_pages)
            ],
            axis=0,
        ).astype(f32)
        scores = []
        for g in range(KEY_VALUE_HEADS):
            key = kv[here, :, g * LANES : (g + 1) * LANES].reshape(tile, LANES)
            scores.append(nt_dot(key, query[g]))
        for g in range(KEY_VALUE_HEADS):
            raised, shrinks = [], []
            for n in range(lanes // LANES):
                part = slice(n * LANES, (n + 1) * LANES)
                s = scores[g][:, part] + bias
                old = stats[g : g + 1, part]
                new = jnp.maximum(old, jnp.max(s, axis=0, keepdims=True))
                p = jnp.exp2((s - new) * scale)
                shrink = jnp.exp2((old - new) * scale)
                at = KEY_VALUE_HEADS + g
                stats[at : at + 1, part] = stats[at : at + 1, part] * shrink + jnp.sum(
                    p, axis=0, keepdims=True
                )
                stats[g : g + 1, part] = new
                raised.append(p.astype(jnp.bfloat16))
                shrinks.append(shrink)
            raised = jnp.concatenate(raised, axis=1)
            shrink = jnp.concatenate(shrinks, axis=1)
            mixed[g] = mixed[g] * shrink + jnp.dot(
                values[t, g], raised, preferred_element_type=f32
            )
        return carry

    lax.fori_loop(0, tiles[step], one_tile, 0)

    if last:
        for g in range(KEY_VALUE_HEADS):
            at = KEY_VALUE_HEADS + g
            done = (mixed[g] * (1.0 / stats[at : at + 1, :])).astype(jnp.bfloat16)
            for n in range(lanes // LANES):
                turned = nt_dot(eye, done[:, n * LANES : (n + 1) * LANES]).astype(jnp.bfloat16)
                for i in range(LANES // block):
                    head = g * QUERY_GROUP + n * (LANES // block) + i
                    outs[0][:, head * LANES : (head + 1) * LANES] = turned[
                        i * block : (i + 1) * block, :
                    ]
    else:
        outs[0][0] = mixed[...]
        outs[1][0] = stats[...]


def attend(first, last, tile_pages, order, sel_lanes, queries, state, context):
    picked, features = queries.shape
    pages, page_len, width = context.shape
    steps = picked // QUERY_BLOCK
    lanes = QUERY_GROUP * QUERY_BLOCK
    wide = pl.BlockSpec((QUERY_BLOCK, features), lambda b, *_: (b, 0))
    state_specs = [
        pl.BlockSpec((1, KEY_VALUE_HEADS, LANES, lanes), lambda b, *_: (b, 0, 0, 0)),
        pl.BlockSpec((1, 2 * KEY_VALUE_HEADS, lanes), lambda b, *_: (b, 0, 0)),
    ]
    state_shapes = [
        jax.ShapeDtypeStruct((steps, KEY_VALUE_HEADS, LANES, lanes), jnp.float32),
        jax.ShapeDtypeStruct((steps, 2 * KEY_VALUE_HEADS, lanes), jnp.float32),
    ]
    share = 0.6
    return pl.pallas_call(
        functools.partial(attend_kernel, first, last, tile_pages),
        grid_spec=pltpu.PrefetchScalarGridSpec(
            num_scalar_prefetch=3,
            grid=(steps,),
            in_specs=[
                pl.BlockSpec((1, 1, LANES), lambda b, *_: (b, 0, 0)),
                wide,
                *([] if first else state_specs),
                pl.BlockSpec(memory_space=pltpu.HBM),
            ],
            out_specs=[wide] if last else state_specs,
            scratch_shapes=[
                pltpu.VMEM((pages, page_len, width), jnp.bfloat16),
                pltpu.VMEM(
                    (pages // tile_pages, KEY_VALUE_HEADS, LANES, tile_pages * page_len), jnp.bfloat16
                ),
                pltpu.VMEM((KEY_VALUE_HEADS, lanes, LANES), jnp.bfloat16),
                pltpu.VMEM((KEY_VALUE_HEADS, LANES, lanes), jnp.float32),
                pltpu.VMEM((2 * KEY_VALUE_HEADS, lanes), jnp.float32),
                pltpu.SemaphoreType.DMA,
            ],
        ),
        out_shape=[jax.ShapeDtypeStruct((picked, features), jnp.bfloat16)] if last else state_shapes,
        compiler_params=pltpu.CompilerParams(
            dimension_semantics=("arbitrary",), vmem_limit_bytes=VMEM_LIMIT
        ),
        cost_estimate=pl.CostEstimate(
            flops=int(share * 8 * picked * features * pages * page_len),
            bytes_accessed=2 * pages * page_len * width + 6 * picked * features,
            transcendentals=int(share * picked * features // LANES * pages * page_len),
        ),
    )(*order, sel_lanes, queries, *state, context)


def page_order(slots, positions, hold, splits, page_len):
    pages = slots.shape[0]
    number = jnp.arange(pages)
    before = number[None, :] < number[:, None]
    owners = slots // hold
    ranks = jnp.sum(((owners[None, :] == owners[:, None]) & before).astype(jnp.int32), axis=1)
    last_page = positions.reshape(-1, QUERY_BLOCK)[:, -1] // page_len
    orders = []
    for (low, high), tile_pages in splits:
        member = (ranks >= low) & (ranks < high)
        count = pages * (high - low) // splits[-1][0][1]
        place = jnp.sum((member[None, :] & before).astype(jnp.int32), axis=1)
        hit = (member[None, :] & (place[None, :] == jnp.arange(count)[:, None])).astype(jnp.int32)
        source = jnp.sum(hit * (owners * (high - low) + ranks - low)[None, :], axis=1)
        page = jnp.sum(hit * number[None, :], axis=1)
        seen = jnp.sum((page[None, :] <= last_page[:, None]).astype(jnp.int32), axis=1)
        orders.append((source, page, (seen + tile_pages - 1) // tile_pages))
    return orders


def per_device(store, page_table, sel_pos, fresh_kv, queries):
    holders = lax.axis_size("store")
    hold, page_len, width = store.shape
    pages = page_table.shape[1]
    picked = sel_pos.shape[1]
    capacity = max(1, pages // holders)
    row_slots = -(-SELP * capacity // 16) * 16
    chunks = width // LANES
    packed_rows = chunks * row_slots + 16
    late = capacity // 4
    splits = ((0, capacity - late), (capacity - late, capacity)) if late else ((0, capacity),)
    hbm = pl.BlockSpec(memory_space=pltpu.HBM)
    vmem = pl.BlockSpec(memory_space=pltpu.VMEM)
    params = pltpu.CompilerParams(vmem_limit_bytes=VMEM_LIMIT)

    packed = pl.pallas_call(
        functools.partial(plan_kernel, hold, holders, row_slots, page_len),
        out_shape=jax.ShapeDtypeStruct((holders, packed_rows, LANES), jnp.bfloat16),
        scratch_shapes=[pltpu.VMEM((8, -(-picked // LANES) * LANES), jnp.int32)],
        compiler_params=params,
    )(page_table, sel_pos, fresh_kv[0])
    entries = lax.all_to_all(packed, "store", split_axis=0, concat_axis=0, tiled=True)

    *parts, numbers = pl.pallas_call(
        functools.partial(blend_kernel, splits, row_slots),
        out_shape=[
            *[
                jax.ShapeDtypeStruct((holders, high - low, page_len, width), store.dtype)
                for low, high in splits
            ],
            jax.ShapeDtypeStruct((holders, LANES), jnp.int32),
        ],
        in_specs=[hbm, hbm],
        out_specs=[hbm] * len(splits) + [vmem],
        scratch_shapes=[
            pltpu.VMEM(store.shape, store.dtype),
            pltpu.VMEM((holders, capacity, page_len, width), store.dtype),
            pltpu.VMEM((holders, packed_rows, LANES), store.dtype),
            pltpu.SMEM((holders, LANES), jnp.int32),
            pltpu.SemaphoreType.DMA,
            pltpu.SemaphoreType.DMA,
            pltpu.SemaphoreType.DMA,
            pltpu.SemaphoreType.DMA,
        ],
        compiler_params=params,
    )(entries, store)

    store_out = pl.pallas_call(
        functools.partial(write_back_kernel, splits),
        grid_spec=pltpu.PrefetchScalarGridSpec(
            num_scalar_prefetch=1,
            grid=(1,),
            in_specs=[hbm] * len(splits),
            out_specs=hbm,
            scratch_shapes=[
                *[pltpu.VMEM(part.shape, part.dtype) for part in parts],
                pltpu.SemaphoreType.DMA,
                pltpu.SemaphoreType.DMA,
            ],
        ),
        out_shape=jax.ShapeDtypeStruct(store.shape, store.dtype),
        compiler_params=params,
        cost_estimate=pl.CostEstimate(flops=0, bytes_accessed=4 * store.size, transcendentals=0),
    )(numbers, *parts)

    tiles = [LATE_TILE_PAGES if low else TILE_PAGES for low, _ in splits]
    orders = page_order(page_table[0], sel_pos[0], hold, list(zip(splits, tiles)), page_len)
    sel_lanes = jnp.tile(sel_pos.reshape(-1, 1, QUERY_BLOCK), (1, 1, LANES // QUERY_BLOCK))
    if len(parts) > 1:
        parts[1:], store_out, orders, sel_lanes = lax.optimization_barrier(
            (parts[1:], store_out, orders, sel_lanes)
        )
    arrived = [
        lax.all_to_all(part, "store", split_axis=0, concat_axis=0, tiled=True).reshape(
            -1, page_len, width
        )
        for part in parts
    ]
    state = ()
    for at, (context, order) in enumerate(zip(arrived, orders)):
        state = attend(
            at == 0, at == len(splits) - 1, tiles[at], order, sel_lanes, queries[0], state, context
        )
    return (state[0][None], store_out)


def solution(mesh):
    return jax.shard_map(
        per_device,
        mesh=mesh,
        in_specs=(
            P(("groups", "store"), None, None),
            P(("groups", "store"), None),
            P(("groups", "store"), None),
            P(("groups", "store"), None, None),
            P(("groups", "store"), None, None),
        ),
        out_specs=(P(("groups", "store"), None, None), P(("groups", "store"), None, None)),
        check_vma=False,
    )
```

```python
import functools

import jax
import jax.numpy as jnp
from jax import lax
from jax.experimental import pallas as pl
from jax.experimental.pallas import tpu as pltpu
from jax.sharding import PartitionSpec as P

HEAD_WIDTH = 128
KEY_VALUE_HEADS = 4
QUERY_GROUP = 12
SELP = 2
LANES = 128
VMEM_LIMIT = 60 * 1024 * 1024
QUERY_BLOCK = 32
TILE_PAGES = 16
LATE_TILE_PAGES = 8
HIDDEN = -1e30


def nt_dot(a, b):
    return lax.dot_general(a, b, (((1,), (1,)), ((), ())), preferred_element_type=jnp.float32)


def plan_kernel(hold, holders, row_slots, page_len, table_ref, sel_ref, fresh_ref, out_ref, wide):
    pages = table_ref.shape[1]
    picked = sel_ref.shape[1]
    wide_lanes = wide.shape[1]
    chunks = fresh_ref.shape[1] // LANES
    f32 = jnp.float32
    slot_row = jnp.broadcast_to(table_ref[...], (pages, pages))
    owner_row = slot_row // hold
    local_row = (slot_row - owner_row * hold).astype(f32)
    owner_row = owner_row.astype(f32)
    owner_col = owner_row.T
    sub = lax.broadcasted_iota(jnp.int32, (pages, pages), 0)
    lane = lax.broadcasted_iota(jnp.int32, (pages, pages), 1)
    earlier = jnp.where((owner_row == owner_col) & (lane < sub), 1.0, 0.0)
    rank_col = jnp.sum(earlier, axis=1, keepdims=True)
    owner_col = owner_col[:, 0:1]

    holder = lax.broadcasted_iota(jnp.int32, (holders, pages), 0).astype(f32)
    owned = jnp.where(holder == owner_row[0:1, :], local_row[0:1, :], 0.0)
    at_rank = jnp.where(lane.astype(f32) == rank_col, 1.0, 0.0)
    numbers = jnp.dot(
        owned.astype(jnp.bfloat16), at_rank.astype(jnp.bfloat16), preferred_element_type=f32
    )

    wide[...] = jnp.full(wide.shape, -1, jnp.int32)
    wide[0:1, 0:picked] = sel_ref[...]
    position = wide[...]
    page = lax.shift_right_arithmetic(position, page_len.bit_length() - 1)
    offset = (position & (page_len - 1)).astype(f32)
    lane8 = lax.broadcasted_iota(jnp.int32, wide.shape, 1)
    second = jnp.where((page == pltpu.roll(page, 1, axis=1)) & (lane8 > 0), 1.0, 0.0)
    page, offset, second = page[0:1], offset[0:1], second[0:1]
    valid = lane8[0:1] < picked
    sub_wide = lax.broadcasted_iota(jnp.int32, (pages, wide_lanes), 0)
    in_page = jnp.where(sub_wide == page, 1.0, 0.0)
    owner = jnp.sum(in_page * owner_col, axis=0, keepdims=True)
    rank = jnp.sum(in_page * rank_col, axis=0, keepdims=True)
    place = SELP * rank + second
    spot = jnp.where(valid, owner * row_slots + place, -1.0)

    holder_wide = lax.broadcasted_iota(jnp.int32, (holders, wide_lanes), 0).astype(f32)
    marked = jnp.where((holder_wide == owner) & valid, rank * page_len + offset + 1.0, 0.0)
    place_lane = lax.broadcasted_iota(jnp.int32, (LANES, wide_lanes), 0).astype(f32)
    at_place = jnp.where(place_lane == place, 1.0, 0.0)
    targets = nt_dot(marked.astype(jnp.bfloat16), at_place.astype(jnp.bfloat16))

    spot_row = spot[:, 0:picked]
    spots = holders * row_slots
    step = min(spots, 256)
    for start in range(0, spots, step):
        spot_id = lax.broadcasted_iota(jnp.int32, (step, picked), 0).astype(f32) + float(start)
        choose = jnp.where(spot_id == spot_row, 1.0, 0.0).astype(jnp.bfloat16)
        rows = jnp.dot(choose, fresh_ref[...], preferred_element_type=f32).astype(jnp.bfloat16)
        for h in range(step // row_slots):
            for c in range(chunks):
                out_ref[start // row_slots + h, c * row_slots : (c + 1) * row_slots, :] = rows[
                    h * row_slots : (h + 1) * row_slots, c * LANES : (c + 1) * LANES
                ]
    sub16 = lax.broadcasted_iota(jnp.int32, (16, LANES), 0)
    for h in range(holders):
        block = jnp.where(sub16 == 0, numbers[h : h + 1, :], 0.0)
        block = jnp.where(sub16 == 1, targets[h : h + 1, :], block)
        out_ref[h, chunks * row_slots :, :] = block.astype(jnp.bfloat16)


def blend_kernel(row_slots, own, entries_hbm, store_hbm, *rest):
    holders = entries_hbm.shape[0]
    sends, numbers_out = rest[:holders], rest[holders]
    store, blended, entries, numbers, load_sem, index_sem, entries_sem, send_sem = rest[holders + 1 :]
    _, capacity, page_len, width = blended.shape
    chunks = width // LANES
    rows_here = capacity * page_len
    f32 = jnp.float32
    load = pltpu.make_async_copy(store_hbm, store, load_sem)
    arrive = pltpu.make_async_copy(entries_hbm, entries, entries_sem)
    arrive.start()
    load.start()
    arrive.wait()

    def index_row(r, carry):
        block = entries[r, chunks * row_slots :, :].astype(f32).astype(jnp.int32)
        numbers_out[pl.ds(r, 1), :] = block[0:1, :]
        return carry

    lax.fori_loop(0, holders, index_row, 0)
    index_copy = pltpu.make_async_copy(numbers_out, numbers, index_sem)
    index_copy.start()
    index_copy.wait()
    load.wait()

    row_id = lax.broadcasted_iota(jnp.int32, (rows_here, row_slots), 0).astype(f32)
    for d in range(holders):
        r = own[0] ^ d
        targets = entries[r, chunks * row_slots :, :].astype(f32)[1:2, 0:row_slots] - 1.0
        hit = jnp.where(row_id == targets, 1.0, 0.0)
        keep = 1.0 - jnp.sum(hit, axis=1, keepdims=True)
        keep = jnp.broadcast_to(keep, (rows_here, LANES)).astype(jnp.bfloat16)
        hit = hit.astype(jnp.bfloat16)
        for c in range(chunks):
            lanes = slice(c * LANES, (c + 1) * LANES)
            rows = entries[r, c * row_slots : (c + 1) * row_slots, :]
            fresh = jnp.dot(hit, rows, preferred_element_type=f32).astype(jnp.bfloat16)
            for k in range(capacity):
                part = slice(k * page_len, (k + 1) * page_len)
                blended[d, k, :, lanes] = store[numbers[r, k], :, lanes] * keep[part] + fresh[part]
        pltpu.make_async_copy(blended.at[d], sends[d], send_sem).start()
    pltpu.make_async_copy(blended, blended, send_sem).wait()


def write_back_kernel(own, numbers, *rest):
    holders = numbers.shape[0]
    sends, store_out = rest[:holders], rest[holders]
    held, load_sem, sem = rest[holders + 1 :]
    capacity = held.shape[1]
    for d in range(holders):
        pltpu.make_async_copy(sends[d], held.at[d], load_sem).start()
    pltpu.make_async_copy(held, held, load_sem).wait()

    def one_request(d, carry):
        r = own[0] ^ d
        for k in range(capacity):
            pltpu.make_async_copy(held.at[d, k], store_out.at[numbers[r, k]], sem).start()
        return carry

    lax.fori_loop(0, holders, one_request, 0)
    pltpu.make_async_copy(store_out, store_out, sem).wait()


def attend_kernel(first, last, tile_pages, sources, place, page_number, tiles, sel_ref, query_ref, *rest):
    rest = list(rest)
    state_in = [] if first else [rest.pop(0) for _ in range(2)]
    contexts = [rest.pop(0) for _ in range(sources)]
    outs = [rest.pop(0) for _ in range(1 if last else 2)]
    kv, values, query, mixed, stats, sem = rest
    pages, page_len = kv.shape[0], kv.shape[1]
    capacity = pages // sources
    block = query_ref.shape[0]
    tile = tile_pages * page_len
    lanes = QUERY_GROUP * block
    scale = 1.4426950408889634 / HEAD_WIDTH**0.5
    f32 = jnp.float32
    step = pl.program_id(0)
    eye = jnp.where(
        lax.broadcasted_iota(jnp.int32, (LANES, LANES), 0)
        == lax.broadcasted_iota(jnp.int32, (LANES, LANES), 1),
        1.0,
        0.0,
    ).astype(jnp.bfloat16)

    @pl.when(step == 0)
    def _():
        for i, context in enumerate(contexts):
            for k in range(capacity):
                pltpu.make_async_copy(context.at[k], kv.at[place[i * capacity + k]], sem).start()
        pltpu.make_async_copy(kv, kv, sem).wait()

        def turn(t, carry):
            here = pl.ds(t * tile_pages, tile_pages)
            for g in range(KEY_VALUE_HEADS):
                at = (KEY_VALUE_HEADS + g) * LANES
                value = kv[here, :, at : at + LANES].reshape(tile, LANES)
                values[t, g] = nt_dot(eye, value).astype(jnp.bfloat16)
            return carry

        lax.fori_loop(0, pages // tile_pages, turn, 0)

    for g in range(KEY_VALUE_HEADS):
        for i in range(QUERY_GROUP):
            head = g * QUERY_GROUP + i
            query[g, i * block : (i + 1) * block, :] = query_ref[:, head * LANES : (head + 1) * LANES]
    if first:
        mixed[...] = jnp.zeros(mixed.shape, f32)
        stats[0:KEY_VALUE_HEADS, :] = jnp.full((KEY_VALUE_HEADS, lanes), HIDDEN, f32)
        stats[KEY_VALUE_HEADS:, :] = jnp.zeros((KEY_VALUE_HEADS, lanes), f32)
    else:
        mixed[...] = state_in[0][0]
        stats[...] = state_in[1][0]

    sel = sel_ref[0]
    in_page = lax.broadcasted_iota(jnp.int32, (page_len, LANES), 0)

    def one_tile(t, carry):
        here = pl.ds(t * tile_pages, tile_pages)
        bias = jnp.concatenate(
            [
                jnp.where(in_page + page_number[t * tile_pages + k] * page_len <= sel, 0.0, HIDDEN)
                for k in range(tile_pages)
            ],
            axis=0,
        ).astype(f32)
        scores = []
        for g in range(KEY_VALUE_HEADS):
            key = kv[here, :, g * LANES : (g + 1) * LANES].reshape(tile, LANES)
            scores.append(nt_dot(key, query[g]))
        for g in range(KEY_VALUE_HEADS):
            raised, shrinks = [], []
            for n in range(lanes // LANES):
                part = slice(n * LANES, (n + 1) * LANES)
                s = scores[g][:, part] + bias
                old = stats[g : g + 1, part]
                new = jnp.maximum(old, jnp.max(s, axis=0, keepdims=True))
                p = jnp.exp2((s - new) * scale)
                shrink = jnp.exp2((old - new) * scale)
                at = KEY_VALUE_HEADS + g
                stats[at : at + 1, part] = stats[at : at + 1, part] * shrink + jnp.sum(
                    p, axis=0, keepdims=True
                )
                stats[g : g + 1, part] = new
                raised.append(p.astype(jnp.bfloat16))
                shrinks.append(shrink)
            raised = jnp.concatenate(raised, axis=1)
            shrink = jnp.concatenate(shrinks, axis=1)
            mixed[g] = mixed[g] * shrink + jnp.dot(
                values[t, g], raised, preferred_element_type=f32
            )
        return carry

    lax.fori_loop(0, tiles[step], one_tile, 0)

    if last:
        for g in range(KEY_VALUE_HEADS):
            at = KEY_VALUE_HEADS + g
            done = (mixed[g] * (1.0 / stats[at : at + 1, :])).astype(jnp.bfloat16)
            for n in range(lanes // LANES):
                turned = nt_dot(eye, done[:, n * LANES : (n + 1) * LANES]).astype(jnp.bfloat16)
                for i in range(LANES // block):
                    head = g * QUERY_GROUP + n * (LANES // block) + i
                    outs[0][:, head * LANES : (head + 1) * LANES] = turned[
                        i * block : (i + 1) * block, :
                    ]
    else:
        outs[0][0] = mixed[...]
        outs[1][0] = stats[...]


def attend(first, last, tile_pages, order, sel_lanes, queries, state, contexts):
    picked, features = queries.shape
    capacity, page_len, width = contexts[0].shape
    pages = capacity * len(contexts)
    steps = picked // QUERY_BLOCK
    lanes = QUERY_GROUP * QUERY_BLOCK
    wide = pl.BlockSpec((QUERY_BLOCK, features), lambda b, *_: (b, 0))
    state_specs = [
        pl.BlockSpec((1, KEY_VALUE_HEADS, LANES, lanes), lambda b, *_: (b, 0, 0, 0)),
        pl.BlockSpec((1, 2 * KEY_VALUE_HEADS, lanes), lambda b, *_: (b, 0, 0)),
    ]
    state_shapes = [
        jax.ShapeDtypeStruct((steps, KEY_VALUE_HEADS, LANES, lanes), jnp.float32),
        jax.ShapeDtypeStruct((steps, 2 * KEY_VALUE_HEADS, lanes), jnp.float32),
    ]
    share = 0.6
    return pl.pallas_call(
        functools.partial(attend_kernel, first, last, tile_pages, len(contexts)),
        grid_spec=pltpu.PrefetchScalarGridSpec(
            num_scalar_prefetch=3,
            grid=(steps,),
            in_specs=[
                pl.BlockSpec((1, 1, LANES), lambda b, *_: (b, 0, 0)),
                wide,
                *([] if first else state_specs),
                *[pl.BlockSpec(memory_space=pltpu.HBM)] * len(contexts),
            ],
            out_specs=[wide] if last else state_specs,
            scratch_shapes=[
                pltpu.VMEM((pages, page_len, width), jnp.bfloat16),
                pltpu.VMEM(
                    (pages // tile_pages, KEY_VALUE_HEADS, LANES, tile_pages * page_len), jnp.bfloat16
                ),
                pltpu.VMEM((KEY_VALUE_HEADS, lanes, LANES), jnp.bfloat16),
                pltpu.VMEM((KEY_VALUE_HEADS, LANES, lanes), jnp.float32),
                pltpu.VMEM((2 * KEY_VALUE_HEADS, lanes), jnp.float32),
                pltpu.SemaphoreType.DMA,
            ],
        ),
        out_shape=[jax.ShapeDtypeStruct((picked, features), jnp.bfloat16)] if last else state_shapes,
        compiler_params=pltpu.CompilerParams(
            dimension_semantics=("arbitrary",), vmem_limit_bytes=VMEM_LIMIT
        ),
        cost_estimate=pl.CostEstimate(
            flops=int(share * 8 * picked * features * pages * page_len),
            bytes_accessed=2 * pages * page_len * width + 6 * picked * features,
            transcendentals=int(share * picked * features // LANES * pages * page_len),
        ),
    )(*order, sel_lanes, queries, *state, *contexts)


def page_order(slots, positions, own, hold, capacity, groups, page_len):
    pages = slots.shape[0]
    number = jnp.arange(pages)
    before = number[None, :] < number[:, None]
    owners = slots // hold
    ranks = jnp.sum(((owners[None, :] == owners[:, None]) & before).astype(jnp.int32), axis=1)
    distance = owners ^ own
    last_page = positions.reshape(-1, QUERY_BLOCK)[:, -1] // page_len
    orders = []
    for group, tile_pages in groups:
        count = len(group) * capacity
        arrival = jnp.full((pages,), -1, jnp.int32)
        for i, d in enumerate(group):
            arrival = jnp.where(distance == d, i * capacity + ranks, arrival)
        member = arrival >= 0
        place = jnp.sum((member[None, :] & before).astype(jnp.int32), axis=1)
        index = jnp.arange(count)[:, None]
        places = jnp.sum(jnp.where(arrival[None, :] == index, place[None, :], 0), axis=1)
        page = jnp.sum(
            jnp.where(member[None, :] & (place[None, :] == index), number[None, :], 0), axis=1
        )
        seen = jnp.sum((page[None, :] <= last_page[:, None]).astype(jnp.int32), axis=1)
        orders.append((places, page, (seen + tile_pages - 1) // tile_pages))
    return orders


def per_device(store, page_table, sel_pos, fresh_kv, queries):
    holders = lax.axis_size("store")
    hold, page_len, width = store.shape
    pages = page_table.shape[1]
    picked = sel_pos.shape[1]
    capacity = max(1, pages // holders)
    row_slots = -(-SELP * capacity // 16) * 16
    chunks = width // LANES
    packed_rows = chunks * row_slots + 16
    hbm = pl.BlockSpec(memory_space=pltpu.HBM)
    vmem = pl.BlockSpec(memory_space=pltpu.VMEM)
    params = pltpu.CompilerParams(vmem_limit_bytes=VMEM_LIMIT)
    own = lax.axis_index("store")
    own_word = own.reshape(1).astype(jnp.int32)
    if holders == 16:
        groups = [((0, 8, 12, 4, 9, 13, 5, 1, 6, 2, 7, 3), TILE_PAGES), ((10, 14, 11, 15), LATE_TILE_PAGES)]
    else:
        groups = [(tuple(range(holders)), TILE_PAGES)]

    packed = pl.pallas_call(
        functools.partial(plan_kernel, hold, holders, row_slots, page_len),
        out_shape=jax.ShapeDtypeStruct((holders, packed_rows, LANES), jnp.bfloat16),
        scratch_shapes=[pltpu.VMEM((8, -(-picked // LANES) * LANES), jnp.int32)],
        compiler_params=params,
    )(page_table, sel_pos, fresh_kv[0])
    entries = lax.all_to_all(packed, "store", split_axis=0, concat_axis=0, tiled=True)

    *parts, numbers = pl.pallas_call(
        functools.partial(blend_kernel, row_slots),
        grid_spec=pltpu.PrefetchScalarGridSpec(
            num_scalar_prefetch=1,
            grid=(1,),
            in_specs=[hbm, hbm],
            out_specs=[hbm] * holders + [vmem],
            scratch_shapes=[
                pltpu.VMEM(store.shape, store.dtype),
                pltpu.VMEM((holders, capacity, page_len, width), store.dtype),
                pltpu.VMEM((holders, packed_rows, LANES), store.dtype),
                pltpu.SMEM((holders, LANES), jnp.int32),
                pltpu.SemaphoreType.DMA,
                pltpu.SemaphoreType.DMA,
                pltpu.SemaphoreType.DMA,
                pltpu.SemaphoreType.DMA,
            ],
        ),
        out_shape=[
            *[jax.ShapeDtypeStruct((capacity, page_len, width), store.dtype)] * holders,
            jax.ShapeDtypeStruct((holders, LANES), jnp.int32),
        ],
        compiler_params=params,
    )(own_word, entries, store)

    store_out = pl.pallas_call(
        write_back_kernel,
        grid_spec=pltpu.PrefetchScalarGridSpec(
            num_scalar_prefetch=2,
            grid=(1,),
            in_specs=[hbm] * holders,
            out_specs=hbm,
            scratch_shapes=[
                pltpu.VMEM((holders, capacity, page_len, width), store.dtype),
                pltpu.SemaphoreType.DMA,
                pltpu.SemaphoreType.DMA,
            ],
        ),
        out_shape=jax.ShapeDtypeStruct(store.shape, store.dtype),
        compiler_params=params,
        cost_estimate=pl.CostEstimate(flops=0, bytes_accessed=4 * store.size, transcendentals=0),
    )(own_word, numbers, *parts)

    orders = page_order(page_table[0], sel_pos[0], own, hold, capacity, groups, page_len)
    sel_lanes = jnp.tile(sel_pos.reshape(-1, 1, QUERY_BLOCK), (1, 1, LANES // QUERY_BLOCK))
    arrived = {0: parts[0]}
    for group, _ in groups:
        for d in group:
            if d:
                pairs = [(h, h ^ d) for h in range(holders)]
                arrived[d] = lax.ppermute(parts[d], "store", pairs)
    state = ()
    for at, ((group, tile_pages), order) in enumerate(zip(groups, orders)):
        contexts = [arrived[d] for d in group]
        state = attend(
            at == 0, at == len(groups) - 1, tile_pages, order, sel_lanes, queries[0], state, contexts
        )
    return (state[0][None], store_out)


def solution(mesh):
    return jax.shard_map(
        per_device,
        mesh=mesh,
        in_specs=(
            P(("groups", "store"), None, None),
            P(("groups", "store"), None),
            P(("groups", "store"), None),
            P(("groups", "store"), None, None),
            P(("groups", "store"), None, None),
        ),
        out_specs=(P(("groups", "store"), None, None), P(("groups", "store"), None, None)),
        check_vma=False,
    )
```

```python
import functools

import jax
import jax.numpy as jnp
from jax import lax
from jax.experimental import pallas as pl
from jax.experimental.pallas import tpu as pltpu
from jax.sharding import PartitionSpec as P

HEAD_WIDTH = 128
KEY_VALUE_HEADS = 4
QUERY_GROUP = 12
SELP = 2
LANES = 128
ROW_SLOTS = 16
VMEM_LIMIT = 60 * 1024 * 1024
QUERY_BLOCK = 32
TILE_PAGES = 16
LATE_TILE_PAGES = 8
HIDDEN = -1e30
FAR_PAGE = 1 << 20


def nt_dot(a, b):
    return lax.dot_general(a, b, (((1,), (1,)), ((), ())), preferred_element_type=jnp.float32)


def one_hot(condition):
    return jnp.where(condition, 1.0, 0.0)


def pair_places(hold, page_len, table_ref, sel_ref, wide):
    pages = table_ref.shape[1]
    picked = sel_ref.shape[1]
    f32 = jnp.float32
    slots = jnp.broadcast_to(table_ref[...], (pages, pages))
    owners = slots // hold
    local_row = (slots - owners * hold).astype(f32)[0:1]
    owner_row = owners.astype(f32)
    owner_col = owner_row.T
    sub = lax.broadcasted_iota(jnp.int32, (pages, pages), 0)
    lane = lax.broadcasted_iota(jnp.int32, (pages, pages), 1)
    earlier = one_hot((owner_row == owner_col) & (lane < sub))
    rank_col = jnp.sum(earlier, axis=1, keepdims=True)

    wide[...] = jnp.full(wide.shape, -1, jnp.int32)
    wide[0:1, 0:picked] = sel_ref[...]
    position = wide[...]
    page = lax.shift_right_arithmetic(position, page_len.bit_length() - 1)
    offset = (position & (page_len - 1)).astype(f32)[0:1]
    lane_wide = lax.broadcasted_iota(jnp.int32, wide.shape, 1)
    second = one_hot((page == pltpu.roll(page, 1, axis=1)) & (lane_wide > 0))[0:1]
    valid = lane_wide[0:1] < picked
    sub_wide = lax.broadcasted_iota(jnp.int32, (pages, wide.shape[1]), 0)
    in_page = one_hot(sub_wide == page[0:1])
    owner = jnp.sum(in_page * owner_col[:, 0:1], axis=0, keepdims=True)
    rank = jnp.sum(in_page * rank_col, axis=0, keepdims=True)
    return owner_row[0:1], local_row, rank_col, owner, rank, second, offset, valid


def index_kernel(hold, page_len, table_ref, sel_ref, out_ref, wide):
    holders = out_ref.shape[0]
    pages = table_ref.shape[1]
    f32 = jnp.float32
    bf16 = jnp.bfloat16
    owner_row, local_row, rank_col, owner, rank, second, offset, valid = pair_places(
        hold, page_len, table_ref, sel_ref, wide
    )
    holder = lax.broadcasted_iota(jnp.int32, (holders, pages), 0).astype(f32)
    owned = jnp.where(holder == owner_row, local_row, 0.0)
    lane = lax.broadcasted_iota(jnp.int32, (pages, LANES), 1).astype(f32)
    numbers = jnp.dot(
        owned.astype(bf16), one_hot(lane == rank_col).astype(bf16), preferred_element_type=f32
    )
    holder_wide = lax.broadcasted_iota(jnp.int32, (holders, wide.shape[1]), 0).astype(f32)
    marked = jnp.where((holder_wide == owner) & valid, rank * page_len + offset + 1.0, 0.0)
    place_lane = lax.broadcasted_iota(jnp.int32, (LANES, wide.shape[1]), 0).astype(f32)
    at_place = one_hot(place_lane == SELP * rank + second)
    targets = nt_dot(marked.astype(bf16), at_place.astype(bf16))
    for h in range(holders):
        out_ref[h, 0:1, :] = numbers[h : h + 1, :].astype(jnp.int32)
        out_ref[h, 1:2, :] = targets[h : h + 1, :].astype(jnp.int32)


def rows_kernel(hold, page_len, early, own, table_ref, sel_ref, fresh_ref, packed_out, *rest):
    outs, wide, packed, sem = rest[:-3], rest[-3], rest[-2], rest[-1]
    holders = packed.shape[0]
    picked = sel_ref.shape[1]
    f32 = jnp.float32
    _, _, _, owner, rank, second, _, valid = pair_places(hold, page_len, table_ref, sel_ref, wide)
    spot = jnp.where(valid, owner * ROW_SLOTS + SELP * rank + second, -1.0)[:, 0:picked]
    step = min(holders, 16)
    for start in range(0, holders, step):
        spot_id = lax.broadcasted_iota(jnp.int32, (step * ROW_SLOTS, picked), 0).astype(f32)
        choose = one_hot(spot_id + float(start * ROW_SLOTS) == spot).astype(jnp.bfloat16)
        rows = jnp.dot(choose, fresh_ref[...], preferred_element_type=f32).astype(jnp.bfloat16)
        packed[start : start + step] = rows.reshape(step, ROW_SLOTS, fresh_ref.shape[1])
    copies = [pltpu.make_async_copy(packed, packed_out, sem)]
    for d, out in zip(early, outs):
        copies.append(pltpu.make_async_copy(packed.at[pl.ds(own[0] ^ d, 1)], out, sem))
    for copy in copies:
        copy.start()
    for copy in copies:
        copy.wait()


def gather_kernel(capacity, own, index, store_hbm, rows_hbm, *rest):
    sends, (store, rows, load_sem, rows_sem, send_sem) = rest[:-5], rest[-5:]
    load = pltpu.make_async_copy(store_hbm, store, load_sem)
    load_rows = pltpu.make_async_copy(rows_hbm, rows, rows_sem)
    load.start()
    load_rows.start()
    load_rows.wait()
    load.wait()
    for d, send in enumerate(sends):
        r = own[0] ^ d
        for k in range(capacity):
            pltpu.make_async_copy(store.at[index[r, 0, k]], send.at[k], send_sem).start()
        if send.shape[0] > capacity:
            pltpu.make_async_copy(rows.at[r], send.at[capacity], send_sem).start()
    for send in sends:
        pltpu.make_async_copy(send, send, send_sem).wait()


def write_back_kernel(own, index, targets_ref, store_hbm, *rest):
    holders = index.shape[0]
    arrived, store_out = rest[:holders], rest[holders]
    store, rows, blended, load_sem, rows_sem, out_sem = rest[holders + 1 :]
    _, capacity, page_len, width = blended.shape
    rows_here = capacity * page_len
    f32 = jnp.float32
    load = pltpu.make_async_copy(store_hbm, store, load_sem)
    load.start()
    for d in range(holders):
        last = arrived[d].shape[0] - 1
        pltpu.make_async_copy(arrived[d].at[last], rows.at[d], rows_sem).start()
    pltpu.make_async_copy(rows, rows, rows_sem).wait()
    load.wait()
    row_id = lax.broadcasted_iota(jnp.int32, (rows_here, ROW_SLOTS), 0)

    def one_request(d, carry):
        r = own[0] ^ d
        hit = one_hot(row_id == targets_ref[r][1:2, 0:ROW_SLOTS] - 1)
        keep = 1.0 - jnp.sum(hit, axis=1, keepdims=True)
        keep = jnp.broadcast_to(keep, (rows_here, LANES)).astype(jnp.bfloat16)
        hit = hit.astype(jnp.bfloat16)
        for c in range(width // LANES):
            lanes = slice(c * LANES, (c + 1) * LANES)
            fresh = jnp.dot(hit, rows[d, :, lanes], preferred_element_type=f32).astype(jnp.bfloat16)
            for k in range(capacity):
                part = slice(k * page_len, (k + 1) * page_len)
                blended[d, k, :, lanes] = store[index[r, 0, k], :, lanes] * keep[part] + fresh[part]
        for k in range(capacity):
            pltpu.make_async_copy(blended.at[d, k], store_out.at[index[r, 0, k]], out_sem).start()
        return carry

    lax.fori_loop(0, holders, one_request, 0)
    pltpu.make_async_copy(store_out, store_out, out_sem).wait()


def attend_kernel(first, last, tile_pages, sources, capacity, place, page_number, tiles, *rest):
    sel_ref, positions_ref, fresh_ref, query_ref, *rest = rest
    state_in = [] if first else [rest.pop(0) for _ in range(2)]
    contexts = [rest.pop(0) for _ in range(sources)]
    outs = [rest.pop(0) for _ in range(1 if last else 2)]
    kv, values, query, mixed, stats, sem = rest
    pages, page_len, width = kv.shape
    used = sources * capacity
    block = query_ref.shape[0]
    tile = tile_pages * page_len
    lanes = QUERY_GROUP * block
    scale = 1.4426950408889634 / HEAD_WIDTH**0.5
    f32 = jnp.float32
    bf16 = jnp.bfloat16
    step = pl.program_id(0)
    eye = one_hot(
        lax.broadcasted_iota(jnp.int32, (LANES, LANES), 0)
        == lax.broadcasted_iota(jnp.int32, (LANES, LANES), 1)
    ).astype(bf16)

    @pl.when(step == 0)
    def _():
        for i, context in enumerate(contexts):
            for k in range(capacity):
                pltpu.make_async_copy(context.at[k], kv.at[place[i * capacity + k]], sem).start()
        if pages > used:
            kv[used:] = jnp.zeros((pages - used, page_len, width), bf16)
        pltpu.make_async_copy(kv.at[0:used], kv.at[0:used], sem).wait()
        positions = positions_ref[...]
        row = lax.broadcasted_iota(jnp.int32, (page_len, positions.shape[1]), 0)
        ones = jnp.ones((positions.shape[1], LANES), bf16)

        def blend_and_turn(t, carry):
            here = pl.ds(t * tile_pages, tile_pages)
            hit = jnp.concatenate(
                [
                    one_hot(row + page_number[t * tile_pages + k] * page_len == positions)
                    for k in range(tile_pages)
                ],
                axis=0,
            ).astype(bf16)
            keep = (1.0 - jnp.dot(hit, ones, preferred_element_type=f32)).astype(bf16)
            for c in range(width // LANES):
                part = slice(c * LANES, (c + 1) * LANES)
                fresh = jnp.dot(hit, fresh_ref[:, part], preferred_element_type=f32).astype(bf16)
                old = kv[here, :, part].reshape(tile, LANES)
                new = old * keep + fresh
                kv[here, :, part] = new.reshape(tile_pages, page_len, LANES)
                if c >= KEY_VALUE_HEADS:
                    values[t, c - KEY_VALUE_HEADS] = nt_dot(eye, new).astype(bf16)
            return carry

        lax.fori_loop(0, pages // tile_pages, blend_and_turn, 0)

    for g in range(KEY_VALUE_HEADS):
        for i in range(QUERY_GROUP):
            head = g * QUERY_GROUP + i
            query[g, i * block : (i + 1) * block, :] = query_ref[:, head * LANES : (head + 1) * LANES]
    if first:
        mixed[...] = jnp.zeros(mixed.shape, f32)
        stats[0:KEY_VALUE_HEADS, :] = jnp.full((KEY_VALUE_HEADS, lanes), HIDDEN, f32)
        stats[KEY_VALUE_HEADS:, :] = jnp.zeros((KEY_VALUE_HEADS, lanes), f32)
    else:
        mixed[...] = state_in[0][0]
        stats[...] = state_in[1][0]

    sel = sel_ref[0]
    in_page = lax.broadcasted_iota(jnp.int32, (page_len, LANES), 0)

    def one_tile(t, carry):
        here = pl.ds(t * tile_pages, tile_pages)
        bias = jnp.concatenate(
            [
                jnp.where(in_page + page_number[t * tile_pages + k] * page_len <= sel, 0.0, HIDDEN)
                for k in range(tile_pages)
            ],
            axis=0,
        ).astype(f32)

        def score(g):
            key = kv[here, :, g * LANES : (g + 1) * LANES].reshape(tile, LANES)
            return nt_dot(key, query[g])

        upcoming = score(0)
        for g in range(KEY_VALUE_HEADS):
            scores = upcoming
            if g + 1 < KEY_VALUE_HEADS:
                upcoming = score(g + 1)
            raised, shrinks = [], []
            at = KEY_VALUE_HEADS + g
            for n in range(lanes // LANES):
                part = slice(n * LANES, (n + 1) * LANES)
                s = scores[:, part] + bias
                old = stats[g : g + 1, part]
                new = jnp.maximum(old, jnp.max(s, axis=0, keepdims=True))
                p = jnp.exp2((s - new) * scale)
                shrink = jnp.exp2((old - new) * scale)
                stats[at : at + 1, part] = stats[at : at + 1, part] * shrink + jnp.sum(
                    p, axis=0, keepdims=True
                )
                stats[g : g + 1, part] = new
                raised.append(p.astype(bf16))
                shrinks.append(shrink)
            raised = jnp.concatenate(raised, axis=1)
            shrink = jnp.concatenate(shrinks, axis=1)
            mixed[g] = mixed[g] * shrink + jnp.dot(
                values[t, g], raised, preferred_element_type=f32
            )
        return carry

    lax.fori_loop(0, tiles[step], one_tile, 0)

    if last:
        done = []
        for g in range(KEY_VALUE_HEADS):
            at = KEY_VALUE_HEADS + g
            part = (mixed[g] * (1.0 / stats[at : at + 1, :])).astype(bf16)
            done += [part[:, n * LANES : (n + 1) * LANES] for n in range(lanes // LANES)]
        turned = nt_dot(eye, jnp.concatenate(done, axis=0)).astype(bf16)
        for n in range(len(done)):
            for i in range(LANES // block):
                head = n * (LANES // block) + i
                outs[0][:, head * LANES : (head + 1) * LANES] = turned[
                    i * block : (i + 1) * block, n * LANES : (n + 1) * LANES
                ]
    else:
        outs[0][0] = mixed[...]
        outs[1][0] = stats[...]


def attend(first, last, tile_pages, capacity, order, sel_lanes, positions, fresh, queries, state, contexts):
    picked, features = queries.shape
    _, page_len, width = contexts[0].shape
    pages = order[1].shape[0]
    steps = picked // QUERY_BLOCK
    lanes = QUERY_GROUP * QUERY_BLOCK
    wide = pl.BlockSpec((QUERY_BLOCK, features), lambda b, *_: (b, 0))
    state_specs = [
        pl.BlockSpec((1, KEY_VALUE_HEADS, LANES, lanes), lambda b, *_: (b, 0, 0, 0)),
        pl.BlockSpec((1, 2 * KEY_VALUE_HEADS, lanes), lambda b, *_: (b, 0, 0)),
    ]
    state_shapes = [
        jax.ShapeDtypeStruct((steps, KEY_VALUE_HEADS, LANES, lanes), jnp.float32),
        jax.ShapeDtypeStruct((steps, 2 * KEY_VALUE_HEADS, lanes), jnp.float32),
    ]
    share = 0.6
    return pl.pallas_call(
        functools.partial(attend_kernel, first, last, tile_pages, len(contexts), capacity),
        grid_spec=pltpu.PrefetchScalarGridSpec(
            num_scalar_prefetch=3,
            grid=(steps,),
            in_specs=[
                pl.BlockSpec((1, 1, LANES), lambda b, *_: (b, 0, 0)),
                pl.BlockSpec(positions.shape, lambda b, *_: (0, 0)),
                pl.BlockSpec(fresh.shape, lambda b, *_: (0, 0)),
                wide,
                *([] if first else state_specs),
                *[pl.BlockSpec(memory_space=pltpu.HBM)] * len(contexts),
            ],
            out_specs=[wide] if last else state_specs,
            scratch_shapes=[
                pltpu.VMEM((pages, page_len, width), jnp.bfloat16),
                pltpu.VMEM(
                    (pages // tile_pages, KEY_VALUE_HEADS, LANES, tile_pages * page_len), jnp.bfloat16
                ),
                pltpu.VMEM((KEY_VALUE_HEADS, lanes, LANES), jnp.bfloat16),
                pltpu.VMEM((KEY_VALUE_HEADS, LANES, lanes), jnp.float32),
                pltpu.VMEM((2 * KEY_VALUE_HEADS, lanes), jnp.float32),
                pltpu.SemaphoreType.DMA,
            ],
        ),
        out_shape=[jax.ShapeDtypeStruct((picked, features), jnp.bfloat16)] if last else state_shapes,
        compiler_params=pltpu.CompilerParams(
            dimension_semantics=("arbitrary",), vmem_limit_bytes=VMEM_LIMIT
        ),
        cost_estimate=pl.CostEstimate(
            flops=int(share * 8 * picked * features * pages * page_len),
            bytes_accessed=2 * pages * page_len * width + 6 * picked * features,
            transcendentals=int(share * picked * features // LANES * pages * page_len),
        ),
    )(*order, sel_lanes, positions, fresh, queries, *state, *contexts)


def page_order(slots, positions, own, hold, capacity, groups, page_len):
    pages = slots.shape[0]
    number = jnp.arange(pages)
    before = number[None, :] < number[:, None]
    owners = slots // hold
    ranks = jnp.sum(((owners[None, :] == owners[:, None]) & before).astype(jnp.int32), axis=1)
    distance = owners ^ own
    last_page = positions.reshape(-1, QUERY_BLOCK)[:, -1] // page_len
    orders = []
    for group, tile_pages in groups:
        count = len(group) * capacity
        arrival = jnp.full((pages,), -1, jnp.int32)
        for i, d in enumerate(group):
            arrival = jnp.where(distance == d, i * capacity + ranks, arrival)
        member = arrival >= 0
        place = jnp.sum((member[None, :] & before).astype(jnp.int32), axis=1)
        index = jnp.arange(count)[:, None]
        places = jnp.sum(jnp.where(arrival[None, :] == index, place[None, :], 0), axis=1)
        index = jnp.arange(-(-count // tile_pages) * tile_pages)[:, None]
        page = jnp.sum(
            jnp.where(member[None, :] & (place[None, :] == index), number[None, :], 0), axis=1
        )
        page = jnp.where(index[:, 0] < count, page, FAR_PAGE)
        seen = jnp.sum((page[None, :] <= last_page[:, None]).astype(jnp.int32), axis=1)
        orders.append((places, page, (seen + tile_pages - 1) // tile_pages))
    return orders


def per_device(store, page_table, sel_pos, fresh_kv, queries):
    holders = lax.axis_size("store")
    hold, page_len, width = store.shape
    pages = page_table.shape[1]
    picked = sel_pos.shape[1]
    capacity = max(1, pages // holders)
    hbm = pl.BlockSpec(memory_space=pltpu.HBM)
    vmem = pl.BlockSpec(memory_space=pltpu.VMEM)
    dma = pltpu.SemaphoreType.DMA
    params = pltpu.CompilerParams(vmem_limit_bytes=VMEM_LIMIT)
    own = lax.axis_index("store")
    own_word = own.reshape(1).astype(jnp.int32)
    fresh = fresh_kv[0]
    wide = pltpu.VMEM((8, -(-picked // LANES) * LANES), jnp.int32)
    if holders == 16:
        order = (8, 4, 12, 5, 9, 6, 13, 7, 10, 1, 14, 2, 11, 3, 15)
        late = (14, 11, 15)
        early_rows = late
    else:
        order = tuple(range(1, holders))
        late = ()
        early_rows = ()
    groups = [((0, *[d for d in order if d not in late]), TILE_PAGES)]
    if late:
        groups.append((late, LATE_TILE_PAGES))

    def swap(x, d):
        return lax.ppermute(x, "store", [(h, h ^ d) for h in range(holders)])

    index = pl.pallas_call(
        functools.partial(index_kernel, hold, page_len),
        out_shape=jax.ShapeDtypeStruct((holders, 2, LANES), jnp.int32),
        scratch_shapes=[wide],
        compiler_params=params,
    )(page_table, sel_pos)
    index, table, positions = lax.optimization_barrier((index, page_table, sel_pos))
    index_in = lax.all_to_all(index, "store", split_axis=0, concat_axis=0, tiled=True)

    packed, *early_parts = pl.pallas_call(
        functools.partial(rows_kernel, hold, page_len, early_rows),
        grid_spec=pltpu.PrefetchScalarGridSpec(
            num_scalar_prefetch=1,
            grid=(1,),
            in_specs=[vmem, vmem, vmem],
            out_specs=[hbm] * (1 + len(early_rows)),
            scratch_shapes=[wide, pltpu.VMEM((holders, ROW_SLOTS, width), store.dtype), dma],
        ),
        out_shape=[
            jax.ShapeDtypeStruct((holders, ROW_SLOTS, width), store.dtype),
            *[jax.ShapeDtypeStruct((1, ROW_SLOTS, width), store.dtype)] * len(early_rows),
        ],
        compiler_params=params,
    )(own_word, table, positions, fresh)
    rows_in = {d: swap(part, d) for d, part in zip(early_rows, early_parts)}

    parts = pl.pallas_call(
        functools.partial(gather_kernel, capacity),
        grid_spec=pltpu.PrefetchScalarGridSpec(
            num_scalar_prefetch=2,
            grid=(1,),
            in_specs=[hbm, hbm],
            out_specs=[hbm] * holders,
            scratch_shapes=[
                pltpu.VMEM(store.shape, store.dtype),
                pltpu.VMEM((holders, ROW_SLOTS, width), store.dtype),
                dma,
                dma,
                dma,
            ],
        ),
        out_shape=[
            jax.ShapeDtypeStruct((capacity + (d not in early_rows), page_len, width), store.dtype)
            for d in range(holders)
        ],
        compiler_params=params,
    )(own_word, index_in, store, packed)
    arrived = {0: parts[0]}
    for d in order:
        arrived[d] = swap(parts[d], d)

    store_out = pl.pallas_call(
        write_back_kernel,
        grid_spec=pltpu.PrefetchScalarGridSpec(
            num_scalar_prefetch=2,
            grid=(1,),
            in_specs=[vmem, hbm] + [hbm] * holders,
            out_specs=hbm,
            scratch_shapes=[
                pltpu.VMEM(store.shape, store.dtype),
                pltpu.VMEM((holders, ROW_SLOTS, width), store.dtype),
                pltpu.VMEM((holders, capacity, page_len, width), store.dtype),
                dma,
                dma,
                dma,
            ],
        ),
        out_shape=jax.ShapeDtypeStruct(store.shape, store.dtype),
        compiler_params=params,
        cost_estimate=pl.CostEstimate(flops=0, bytes_accessed=4 * store.size, transcendentals=0),
    )(own_word, index_in, index_in, store, *[rows_in.get(d, arrived[d]) for d in range(holders)])

    orders = page_order(table[0], positions[0], own, hold, capacity, groups, page_len)
    sel_lanes = jnp.tile(positions.reshape(-1, 1, QUERY_BLOCK), (1, 1, LANES // QUERY_BLOCK))
    store_out, sel_lanes = lax.optimization_barrier((store_out, sel_lanes))
    state = ()
    for at, ((group, tile_pages), order) in enumerate(zip(groups, orders)):
        state = attend(
            at == 0,
            at == len(groups) - 1,
            tile_pages,
            capacity,
            order,
            sel_lanes,
            sel_pos,
            fresh,
            queries[0],
            state,
            [arrived[d] for d in group],
        )
    return (state[0][None], store_out)


def solution(mesh):
    return jax.shard_map(
        per_device,
        mesh=mesh,
        in_specs=(
            P(("groups", "store"), None, None),
            P(("groups", "store"), None),
            P(("groups", "store"), None),
            P(("groups", "store"), None, None),
            P(("groups", "store"), None, None),
        ),
        out_specs=(P(("groups", "store"), None, None), P(("groups", "store"), None, None)),
        check_vma=False,
    )
```

```python
import functools

import jax
import jax.numpy as jnp
from jax import lax
from jax.experimental import pallas as pl
from jax.experimental.pallas import tpu as pltpu
from jax.sharding import PartitionSpec as P

HEAD_WIDTH = 128
KEY_VALUE_HEADS = 4
QUERY_GROUP = 12
SELP = 2
LANES = 128
ROW_SLOTS = 16
VMEM_LIMIT = 60 * 1024 * 1024
QUERY_BLOCK = 32
TILE_PAGES = 16
HIDDEN = -1e30
FAR_POSITION = 1 << 24


def nt_dot(a, b):
    return lax.dot_general(a, b, (((1,), (1,)), ((), ())), preferred_element_type=jnp.float32)


def one_hot(condition):
    return jnp.where(condition, 1.0, 0.0)


def pair_places(hold, page_len, table_ref, sel_ref, wide):
    pages = table_ref.shape[1]
    picked = sel_ref.shape[1]
    f32 = jnp.float32
    slots = jnp.broadcast_to(table_ref[...], (pages, pages))
    owners = slots // hold
    local_row = (slots - owners * hold).astype(f32)[0:1]
    owner_row = owners.astype(f32)
    owner_col = owner_row.T
    sub = lax.broadcasted_iota(jnp.int32, (pages, pages), 0)
    lane = lax.broadcasted_iota(jnp.int32, (pages, pages), 1)
    earlier = one_hot((owner_row == owner_col) & (lane < sub))
    rank_col = jnp.sum(earlier, axis=1, keepdims=True)

    wide[...] = jnp.full(wide.shape, -1, jnp.int32)
    wide[0:1, 0:picked] = sel_ref[...]
    position = wide[...]
    page = lax.shift_right_arithmetic(position, page_len.bit_length() - 1)
    offset = (position & (page_len - 1)).astype(f32)[0:1]
    lane_wide = lax.broadcasted_iota(jnp.int32, wide.shape, 1)
    second = one_hot((page == pltpu.roll(page, 1, axis=1)) & (lane_wide > 0))[0:1]
    valid = lane_wide[0:1] < picked
    sub_wide = lax.broadcasted_iota(jnp.int32, (pages, wide.shape[1]), 0)
    in_page = one_hot(sub_wide == page[0:1])
    owner = jnp.sum(in_page * owner_col[:, 0:1], axis=0, keepdims=True)
    rank = jnp.sum(in_page * rank_col, axis=0, keepdims=True)
    return owner_row[0:1], local_row, rank_col, owner, rank, second, offset, valid


def index_kernel(hold, page_len, first, own, table_ref, sel_ref, out_ref, *rest):
    first_refs, wide = rest[:-1], rest[-1]
    holders = out_ref.shape[0]
    pages = table_ref.shape[1]
    f32 = jnp.float32
    bf16 = jnp.bfloat16
    owner_row, local_row, rank_col, owner, rank, second, offset, valid = pair_places(
        hold, page_len, table_ref, sel_ref, wide
    )
    holder = lax.broadcasted_iota(jnp.int32, (holders, pages), 0).astype(f32)
    owned = jnp.where(holder == owner_row, local_row, 0.0)
    lane = lax.broadcasted_iota(jnp.int32, (pages, LANES), 1).astype(f32)
    numbers = jnp.dot(
        owned.astype(bf16), one_hot(lane == rank_col).astype(bf16), preferred_element_type=f32
    )
    holder_wide = lax.broadcasted_iota(jnp.int32, (holders, wide.shape[1]), 0).astype(f32)
    marked = jnp.where((holder_wide == owner) & valid, rank * page_len + offset + 1.0, 0.0)
    place_lane = lax.broadcasted_iota(jnp.int32, (LANES, wide.shape[1]), 0).astype(f32)
    at_place = one_hot(place_lane == SELP * rank + second)
    targets = nt_dot(marked.astype(bf16), at_place.astype(bf16))
    for h in range(holders):
        out_ref[h, 0:1, :] = numbers[h : h + 1, :].astype(jnp.int32)
        out_ref[h, 1:2, :] = targets[h : h + 1, :].astype(jnp.int32)
    for d, ref in zip(first, first_refs):
        ref[0] = out_ref[own[0] ^ d]


def rows_kernel(hold, page_len, table_ref, sel_ref, fresh_ref, packed, wide):
    holders = packed.shape[0]
    picked = sel_ref.shape[1]
    f32 = jnp.float32
    _, _, _, owner, rank, second, _, valid = pair_places(hold, page_len, table_ref, sel_ref, wide)
    spot = jnp.where(valid, owner * ROW_SLOTS + SELP * rank + second, -1.0)[:, 0:picked]
    step = min(holders, 16)
    for start in range(0, holders, step):
        spot_id = lax.broadcasted_iota(jnp.int32, (step * ROW_SLOTS, picked), 0).astype(f32)
        choose = one_hot(spot_id + float(start * ROW_SLOTS) == spot).astype(jnp.bfloat16)
        rows = jnp.dot(choose, fresh_ref[...], preferred_element_type=f32).astype(jnp.bfloat16)
        packed[start : start + step] = rows.reshape(step, ROW_SLOTS, fresh_ref.shape[1])


def first_gather_kernel(count, *refs):
    lists, store_hbm, sends = refs[:count], refs[count], refs[count + 1 : 2 * count + 1]
    held, load_sem, send_sem = refs[2 * count + 1 :]
    capacity = held.shape[1]
    for i, numbers in enumerate(lists):
        for k in range(capacity):
            pltpu.make_async_copy(store_hbm.at[numbers[0, 0, k]], held.at[i, k], load_sem).start()
    pltpu.make_async_copy(held, held, load_sem).wait()
    for i, send in enumerate(sends):
        pltpu.make_async_copy(held.at[i], send, send_sem).start()
    pltpu.make_async_copy(held, held, send_sem).wait()


def gather_kernel(capacity, distances, own, index, store_hbm, *rest):
    sends, (store, load_sem, send_sem) = rest[:-3], rest[-3:]
    load = pltpu.make_async_copy(store_hbm, store, load_sem)
    load.start()
    load.wait()
    for i in range(len(distances) if distances else index.shape[0]):
        r = own[0] ^ distances[i] if distances else i
        send = sends[i] if distances else sends[0].at[i]
        for k in range(capacity):
            pltpu.make_async_copy(store.at[index[r, 0, k]], send.at[k], send_sem).start()
    for send in sends:
        pltpu.make_async_copy(send, send, send_sem).wait()


def write_back_kernel(index, targets_ref, store_hbm, rows_hbm, store_out, *scratch):
    store, rows, blended, load_sem, rows_sem, out_sem = scratch
    holders, capacity, page_len, width = blended.shape
    rows_here = capacity * page_len
    f32 = jnp.float32
    load = pltpu.make_async_copy(store_hbm, store, load_sem)
    load_rows = pltpu.make_async_copy(rows_hbm, rows, rows_sem)
    load.start()
    load_rows.start()
    load_rows.wait()
    load.wait()
    row_id = lax.broadcasted_iota(jnp.int32, (rows_here, ROW_SLOTS), 0)

    def one_request(r, carry):
        hit = one_hot(row_id == targets_ref[r][1:2, 0:ROW_SLOTS] - 1)
        keep = 1.0 - jnp.sum(hit, axis=1, keepdims=True)
        keep = jnp.broadcast_to(keep, (rows_here, LANES)).astype(jnp.bfloat16)
        hit = hit.astype(jnp.bfloat16)
        for c in range(width // LANES):
            lanes = slice(c * LANES, (c + 1) * LANES)
            fresh = jnp.dot(hit, rows[r, :, lanes], preferred_element_type=f32).astype(jnp.bfloat16)
            for k in range(capacity):
                part = slice(k * page_len, (k + 1) * page_len)
                blended[r, k, :, lanes] = store[index[r, 0, k], :, lanes] * keep[part] + fresh[part]
        for k in range(capacity):
            pltpu.make_async_copy(blended.at[r, k], store_out.at[index[r, 0, k]], out_sem).start()
        return carry

    lax.fori_loop(0, holders, one_request, 0)
    pltpu.make_async_copy(store_out, store_out, out_sem).wait()


def attend_kernel(first, last, sources, place, page_number, tiles, *rest):
    sel_ref, positions_ref, query_ref, *rest = rest
    if first:
        fresh_ref, fresh_positions, *rest = rest
    state_in = () if first else rest[:2]
    rest = rest if first else rest[2:]
    contexts, rest = rest[:sources], rest[sources:]
    outs, rest = (rest[:1], rest[1:]) if last else (rest[:2], rest[2:])
    kv, values, position, query, mixed, stats, sem = rest
    pages, page_len, width = kv.shape
    each = contexts[0].shape[0]
    ahead = TILE_PAGES if first else 0
    block = query_ref.shape[0]
    tile = TILE_PAGES * page_len
    lanes = QUERY_GROUP * block
    scale = 1.4426950408889634 / HEAD_WIDTH**0.5
    f32 = jnp.float32
    bf16 = jnp.bfloat16
    step = pl.program_id(0)
    eye = one_hot(
        lax.broadcasted_iota(jnp.int32, (LANES, LANES), 0)
        == lax.broadcasted_iota(jnp.int32, (LANES, LANES), 1)
    ).astype(bf16)

    @pl.when(step == 0)
    def _():
        for i, context in enumerate(contexts):
            for k in range(each):
                pltpu.make_async_copy(context.at[k], kv.at[ahead + place[i * each + k]], sem).start()
        if first:
            picked = fresh_ref.shape[0]
            count = picked // page_len
            kv[0:count] = fresh_ref[...].reshape(count, page_len, width)
            kv[count:ahead] = jnp.zeros((ahead - count, page_len, width), bf16)
            position[0:picked, :] = fresh_positions[...]
            position[picked:tile, :] = jnp.full((tile - picked, LANES), FAR_POSITION, jnp.int32)
        positions = positions_ref[...]
        row = lax.broadcasted_iota(jnp.int32, (page_len, positions.shape[1]), 0)
        ones = jnp.ones((positions.shape[1], LANES), bf16)
        row_lanes = lax.broadcasted_iota(jnp.int32, (page_len, LANES), 0)

        def place_rows(t, carry):
            starts = [page_number[t * TILE_PAGES + k] * page_len for k in range(TILE_PAGES)]
            hit = jnp.concatenate([one_hot(row + start == positions) for start in starts], axis=0)
            hidden = jnp.dot(hit.astype(bf16), ones, preferred_element_type=f32)
            plain = jnp.concatenate([row_lanes + start for start in starts], axis=0)
            here = pl.ds(pl.multiple_of(ahead * page_len + t * tile, tile), tile)
            position[here, :] = jnp.where(hidden > 0.0, FAR_POSITION, plain)
            return carry

        lax.fori_loop(0, (pages - ahead) // TILE_PAGES, place_rows, 0)
        used = kv.at[ahead:]
        pltpu.make_async_copy(used, used, sem).wait()

        def turn(t, carry):
            here = pl.ds(t * TILE_PAGES, TILE_PAGES)
            for g in range(KEY_VALUE_HEADS):
                at = (KEY_VALUE_HEADS + g) * LANES
                value = kv[here, :, at : at + LANES].reshape(tile, LANES)
                values[t, g] = nt_dot(eye, value).astype(bf16)
            return carry

        lax.fori_loop(0, pages // TILE_PAGES, turn, 0)

    for g in range(KEY_VALUE_HEADS):
        for i in range(QUERY_GROUP):
            head = g * QUERY_GROUP + i
            query[g, i * block : (i + 1) * block, :] = query_ref[:, head * LANES : (head + 1) * LANES]
    if first:
        mixed[...] = jnp.zeros(mixed.shape, f32)
        stats[0:KEY_VALUE_HEADS, :] = jnp.full((KEY_VALUE_HEADS, lanes), HIDDEN, f32)
        stats[KEY_VALUE_HEADS:, :] = jnp.zeros((KEY_VALUE_HEADS, lanes), f32)
    else:
        mixed[...] = state_in[0][0]
        stats[...] = state_in[1][0]

    sel = sel_ref[0]

    def one_tile(t, carry):
        here = pl.ds(t * TILE_PAGES, TILE_PAGES)
        bias = jnp.where(
            position[pl.ds(pl.multiple_of(t * tile, tile), tile), :] <= sel, 0.0, HIDDEN
        ).astype(f32)

        def score(g):
            key = kv[here, :, g * LANES : (g + 1) * LANES].reshape(tile, LANES)
            return nt_dot(key, query[g])

        upcoming = score(0)
        for g in range(KEY_VALUE_HEADS):
            scores = upcoming
            if g + 1 < KEY_VALUE_HEADS:
                upcoming = score(g + 1)
            raised, shrinks = [], []
            at = KEY_VALUE_HEADS + g
            for n in range(lanes // LANES):
                part = slice(n * LANES, (n + 1) * LANES)
                s = scores[:, part] + bias
                old = stats[g : g + 1, part]
                new = jnp.maximum(old, jnp.max(s, axis=0, keepdims=True))
                p = jnp.exp2((s - new) * scale)
                shrink = jnp.exp2((old - new) * scale)
                stats[at : at + 1, part] = stats[at : at + 1, part] * shrink + jnp.sum(
                    p, axis=0, keepdims=True
                )
                stats[g : g + 1, part] = new
                raised.append(p.astype(bf16))
                shrinks.append(shrink)
            raised = jnp.concatenate(raised, axis=1)
            shrink = jnp.concatenate(shrinks, axis=1)
            mixed[g] = mixed[g] * shrink + jnp.dot(
                values[t, g], raised, preferred_element_type=f32
            )
        return carry

    lax.fori_loop(0, tiles[step], one_tile, 0)

    if last:
        done = []
        for g in range(KEY_VALUE_HEADS):
            at = KEY_VALUE_HEADS + g
            part = (mixed[g] * (1.0 / stats[at : at + 1, :])).astype(bf16)
            done += [part[:, n * LANES : (n + 1) * LANES] for n in range(lanes // LANES)]
        turned = nt_dot(eye, jnp.concatenate(done, axis=0)).astype(bf16)
        for n in range(len(done)):
            for i in range(LANES // block):
                head = n * (LANES // block) + i
                outs[0][:, head * LANES : (head + 1) * LANES] = turned[
                    i * block : (i + 1) * block, n * LANES : (n + 1) * LANES
                ]
    else:
        outs[0][0] = mixed[...]
        outs[1][0] = stats[...]


def attend(first, last, order, sel_lanes, positions, queries, fresh, state, contexts):
    picked, features = queries.shape
    each, page_len, width = contexts[0].shape
    pages = each * len(contexts) + (TILE_PAGES if first else 0)
    steps = picked // QUERY_BLOCK
    lanes = QUERY_GROUP * QUERY_BLOCK
    wide = pl.BlockSpec((QUERY_BLOCK, features), lambda b, *_: (b, 0))
    state_specs = [
        pl.BlockSpec((1, KEY_VALUE_HEADS, LANES, lanes), lambda b, *_: (b, 0, 0, 0)),
        pl.BlockSpec((1, 2 * KEY_VALUE_HEADS, lanes), lambda b, *_: (b, 0, 0)),
    ]
    state_shapes = [
        jax.ShapeDtypeStruct((steps, KEY_VALUE_HEADS, LANES, lanes), jnp.float32),
        jax.ShapeDtypeStruct((steps, 2 * KEY_VALUE_HEADS, lanes), jnp.float32),
    ]
    share = 0.6
    return pl.pallas_call(
        functools.partial(attend_kernel, first, last, len(contexts)),
        grid_spec=pltpu.PrefetchScalarGridSpec(
            num_scalar_prefetch=3,
            grid=(steps,),
            in_specs=[
                pl.BlockSpec((1, 1, LANES), lambda b, *_: (b, 0, 0)),
                pl.BlockSpec(positions.shape, lambda b, *_: (0, 0)),
                wide,
                *[pl.BlockSpec(x.shape, lambda b, *_: (0, 0)) for x in fresh if first],
                *([] if first else state_specs),
                *[pl.BlockSpec(memory_space=pltpu.HBM)] * len(contexts),
            ],
            out_specs=[wide] if last else state_specs,
            scratch_shapes=[
                pltpu.VMEM((pages, page_len, width), jnp.bfloat16),
                pltpu.VMEM(
                    (pages // TILE_PAGES, KEY_VALUE_HEADS, LANES, TILE_PAGES * page_len), jnp.bfloat16
                ),
                pltpu.VMEM((pages * page_len, LANES), jnp.int32),
                pltpu.VMEM((KEY_VALUE_HEADS, lanes, LANES), jnp.bfloat16),
                pltpu.VMEM((KEY_VALUE_HEADS, LANES, lanes), jnp.float32),
                pltpu.VMEM((2 * KEY_VALUE_HEADS, lanes), jnp.float32),
                pltpu.SemaphoreType.DMA,
            ],
        ),
        out_shape=[jax.ShapeDtypeStruct((picked, features), jnp.bfloat16)] if last else state_shapes,
        compiler_params=pltpu.CompilerParams(
            dimension_semantics=("arbitrary",), vmem_limit_bytes=VMEM_LIMIT
        ),
        cost_estimate=pl.CostEstimate(
            flops=int(share * 8 * picked * features * pages * page_len),
            bytes_accessed=2 * pages * page_len * width + 6 * picked * features,
            transcendentals=int(share * picked * features // LANES * pages * page_len),
        ),
    )(*order, sel_lanes, positions, queries, *[x for x in fresh if first], *state, *contexts)


def page_order(slots, positions, own, hold, capacity, groups, page_len):
    pages = slots.shape[0]
    number = jnp.arange(pages)
    before = number[None, :] < number[:, None]
    owners = slots // hold
    ranks = jnp.sum(((owners[None, :] == owners[:, None]) & before).astype(jnp.int32), axis=1)
    distance = owners ^ own
    last_page = positions.reshape(-1, QUERY_BLOCK)[:, -1] // page_len
    orders = []
    for at, group in enumerate(groups):
        if group is None:
            arrival = owners * capacity + ranks
            count = pages
        else:
            arrival = jnp.full((pages,), -1, jnp.int32)
            for i, d in enumerate(group):
                arrival = jnp.where(distance == d, i * capacity + ranks, arrival)
            count = len(group) * capacity
        member = arrival >= 0
        place = jnp.sum((member[None, :] & before).astype(jnp.int32), axis=1)
        index = jnp.arange(count)[:, None]
        places = jnp.sum(jnp.where(arrival[None, :] == index, place[None, :], 0), axis=1)
        page = jnp.sum(
            jnp.where(member[None, :] & (place[None, :] == index), number[None, :], 0), axis=1
        )
        seen = jnp.sum((page[None, :] <= last_page[:, None]).astype(jnp.int32), axis=1)
        orders.append((places, page, (seen + TILE_PAGES - 1) // TILE_PAGES + (at == 0)))
    return orders


def per_device(store, page_table, sel_pos, fresh_kv, queries):
    holders = lax.axis_size("store")
    hold, page_len, width = store.shape
    pages = page_table.shape[1]
    picked = sel_pos.shape[1]
    capacity = max(1, pages // holders)
    hbm = pl.BlockSpec(memory_space=pltpu.HBM)
    vmem = pl.BlockSpec(memory_space=pltpu.VMEM)
    dma = pltpu.SemaphoreType.DMA
    params = pltpu.CompilerParams(vmem_limit_bytes=VMEM_LIMIT)
    own = lax.axis_index("store")
    own_word = own.reshape(1).astype(jnp.int32)
    fresh = fresh_kv[0]
    wide = pltpu.VMEM((8, -(-picked // LANES) * LANES), jnp.int32)
    if holders == 16:
        first = (8, 12)
        groups = [(0, 8, 12, 4, 5, 1), (9, 6, 13, 7, 10, 2, 14, 3), (11, 15)]
        others = [d for group in groups for d in group if d not in first]
    else:
        first = ()
        groups = [None]
        others = None

    def swap(x, d):
        return lax.ppermute(x, "store", [(h, h ^ d) for h in range(holders)])

    def exchange(x):
        return lax.all_to_all(x, "store", split_axis=0, concat_axis=0, tiled=True)

    index, *lists = pl.pallas_call(
        functools.partial(index_kernel, hold, page_len, first),
        grid_spec=pltpu.PrefetchScalarGridSpec(
            num_scalar_prefetch=1,
            grid=(1,),
            in_specs=[vmem, vmem],
            out_specs=[vmem] * (1 + len(first)),
            scratch_shapes=[wide],
        ),
        out_shape=[
            jax.ShapeDtypeStruct((holders, 2, LANES), jnp.int32),
            *[jax.ShapeDtypeStruct((1, 2, LANES), jnp.int32)] * len(first),
        ],
        compiler_params=params,
    )(own_word, page_table, sel_pos)
    arrived = {}
    if first:
        lists = [swap(x, d) for x, d in zip(lists, first)]
        parts = pl.pallas_call(
            functools.partial(first_gather_kernel, len(first)),
            grid_spec=pltpu.PrefetchScalarGridSpec(
                num_scalar_prefetch=len(first),
                grid=(1,),
                in_specs=[hbm],
                out_specs=[hbm] * len(first),
                scratch_shapes=[
                    pltpu.VMEM((len(first), capacity, page_len, width), store.dtype),
                    dma,
                    dma,
                ],
            ),
            out_shape=[jax.ShapeDtypeStruct((capacity, page_len, width), store.dtype)] * len(first),
            compiler_params=params,
        )(*lists, store)
        parts, index, table, positions = lax.optimization_barrier(
            (parts, index, page_table, sel_pos)
        )
        arrived = {d: swap(part, d) for d, part in zip(first, parts)}
    else:
        table, positions = page_table, sel_pos
    index_in = exchange(index)

    packed = pl.pallas_call(
        functools.partial(rows_kernel, hold, page_len),
        out_shape=jax.ShapeDtypeStruct((holders, ROW_SLOTS, width), store.dtype),
        scratch_shapes=[wide],
        compiler_params=params,
    )(table, positions, fresh)

    each = jax.ShapeDtypeStruct((capacity, page_len, width), store.dtype)
    whole = jax.ShapeDtypeStruct((holders, capacity, page_len, width), store.dtype)
    parts = pl.pallas_call(
        functools.partial(gather_kernel, capacity, others),
        grid_spec=pltpu.PrefetchScalarGridSpec(
            num_scalar_prefetch=2,
            grid=(1,),
            in_specs=[hbm],
            out_specs=[hbm] * (len(others) if others else 1),
            scratch_shapes=[pltpu.VMEM(store.shape, store.dtype), dma, dma],
        ),
        out_shape=[each] * len(others) if others else [whole],
        compiler_params=params,
    )(own_word, index_in, store)
    parts, packed, table, positions = lax.optimization_barrier((parts, packed, table, positions))
    if others:
        for d, part in zip(others, parts):
            arrived[d] = swap(part, d) if d else part
        contexts = [[arrived[d] for d in group] for group in groups]
    else:
        contexts = [[exchange(parts[0]).reshape(pages, page_len, width)]]
    rows_in = exchange(packed)

    store_out = pl.pallas_call(
        write_back_kernel,
        grid_spec=pltpu.PrefetchScalarGridSpec(
            num_scalar_prefetch=1,
            grid=(1,),
            in_specs=[vmem, hbm, hbm],
            out_specs=hbm,
            scratch_shapes=[
                pltpu.VMEM(store.shape, store.dtype),
                pltpu.VMEM((holders, ROW_SLOTS, width), store.dtype),
                pltpu.VMEM((holders, capacity, page_len, width), store.dtype),
                dma,
                dma,
                dma,
            ],
        ),
        out_shape=jax.ShapeDtypeStruct(store.shape, store.dtype),
        compiler_params=params,
        cost_estimate=pl.CostEstimate(flops=0, bytes_accessed=4 * store.size, transcendentals=0),
    )(index_in, index_in, store, rows_in)

    orders = page_order(table[0], positions[0], own, hold, capacity, groups, page_len)
    sel_lanes = jnp.tile(positions.reshape(-1, 1, QUERY_BLOCK), (1, 1, LANES // QUERY_BLOCK))
    sel_rows = jnp.broadcast_to(positions.reshape(picked, 1), (picked, LANES))
    store_out, sel_lanes = lax.optimization_barrier((store_out, sel_lanes))
    state = ()
    for at, (arrays, order) in enumerate(zip(contexts, orders)):
        state = attend(
            at == 0,
            at == len(groups) - 1,
            order,
            sel_lanes,
            positions,
            queries[0],
            (fresh, sel_rows),
            state,
            arrays,
        )
    return (state[0][None], store_out)


def solution(mesh):
    return jax.shard_map(
        per_device,
        mesh=mesh,
        in_specs=(
            P(("groups", "store"), None, None),
            P(("groups", "store"), None),
            P(("groups", "store"), None),
            P(("groups", "store"), None, None),
            P(("groups", "store"), None, None),
        ),
        out_specs=(P(("groups", "store"), None, None), P(("groups", "store"), None, None)),
        check_vma=False,
    )
```

```python
import functools

import jax
import jax.numpy as jnp
from jax import lax
from jax.experimental import pallas as pl
from jax.experimental.pallas import tpu as pltpu
from jax.sharding import PartitionSpec as P

HEAD_WIDTH = 128
KEY_VALUE_HEADS = 4
QUERY_GROUP = 12
SELP = 2
LANES = 128
ROW_SLOTS = 16
VMEM_LIMIT = 60 * 1024 * 1024
QUERY_BLOCK = 32
TILE_PAGES = 16
HIDDEN = -1e30
FAR_POSITION = 1 << 24


def nt_dot(a, b):
    return lax.dot_general(a, b, (((1,), (1,)), ((), ())), preferred_element_type=jnp.float32)


def one_hot(condition):
    return jnp.where(condition, 1.0, 0.0)


def pair_places(hold, page_len, table_ref, sel_ref, wide):
    pages = table_ref.shape[1]
    picked = sel_ref.shape[1]
    f32 = jnp.float32
    slots = jnp.broadcast_to(table_ref[...], (pages, pages))
    owners = slots // hold
    local_row = (slots - owners * hold).astype(f32)[0:1]
    owner_row = owners.astype(f32)
    owner_col = owner_row.T
    sub = lax.broadcasted_iota(jnp.int32, (pages, pages), 0)
    lane = lax.broadcasted_iota(jnp.int32, (pages, pages), 1)
    earlier = one_hot((owner_row == owner_col) & (lane < sub))
    rank_col = jnp.sum(earlier, axis=1, keepdims=True)

    wide[...] = jnp.full(wide.shape, -1, jnp.int32)
    wide[0:1, 0:picked] = sel_ref[...]
    position = wide[...]
    page = lax.shift_right_arithmetic(position, page_len.bit_length() - 1)
    offset = (position & (page_len - 1)).astype(f32)[0:1]
    lane_wide = lax.broadcasted_iota(jnp.int32, wide.shape, 1)
    second = one_hot((page == pltpu.roll(page, 1, axis=1)) & (lane_wide > 0))[0:1]
    valid = lane_wide[0:1] < picked
    sub_wide = lax.broadcasted_iota(jnp.int32, (pages, wide.shape[1]), 0)
    in_page = one_hot(sub_wide == page[0:1])
    owner = jnp.sum(in_page * owner_col[:, 0:1], axis=0, keepdims=True)
    rank = jnp.sum(in_page * rank_col, axis=0, keepdims=True)
    return owner_row[0:1], local_row, rank_col, owner, rank, second, offset, valid


def index_kernel(hold, page_len, first, own, table_ref, sel_ref, out_ref, *rest):
    first_refs, wide = rest[:-1], rest[-1]
    holders = out_ref.shape[0]
    pages = table_ref.shape[1]
    f32 = jnp.float32
    bf16 = jnp.bfloat16
    owner_row, local_row, rank_col, owner, rank, second, offset, valid = pair_places(
        hold, page_len, table_ref, sel_ref, wide
    )
    holder = lax.broadcasted_iota(jnp.int32, (holders, pages), 0).astype(f32)
    owned = jnp.where(holder == owner_row, local_row, 0.0)
    lane = lax.broadcasted_iota(jnp.int32, (pages, LANES), 1).astype(f32)
    numbers = jnp.dot(
        owned.astype(bf16), one_hot(lane == rank_col).astype(bf16), preferred_element_type=f32
    )
    holder_wide = lax.broadcasted_iota(jnp.int32, (holders, wide.shape[1]), 0).astype(f32)
    marked = jnp.where((holder_wide == owner) & valid, rank * page_len + offset + 1.0, 0.0)
    place_lane = lax.broadcasted_iota(jnp.int32, (LANES, wide.shape[1]), 0).astype(f32)
    at_place = one_hot(place_lane == SELP * rank + second)
    targets = nt_dot(marked.astype(bf16), at_place.astype(bf16))
    for h in range(holders):
        out_ref[h, 0:1, :] = numbers[h : h + 1, :].astype(jnp.int32)
        out_ref[h, 1:2, :] = targets[h : h + 1, :].astype(jnp.int32)
    for d, ref in zip(first, first_refs):
        ref[0] = out_ref[own[0] ^ d]


def rows_kernel(hold, page_len, table_ref, sel_ref, fresh_ref, packed, wide):
    holders = packed.shape[0]
    picked = sel_ref.shape[1]
    f32 = jnp.float32
    _, _, _, owner, rank, second, _, valid = pair_places(hold, page_len, table_ref, sel_ref, wide)
    spot = jnp.where(valid, owner * ROW_SLOTS + SELP * rank + second, -1.0)[:, 0:picked]
    step = min(holders, 16)
    for start in range(0, holders, step):
        spot_id = lax.broadcasted_iota(jnp.int32, (step * ROW_SLOTS, picked), 0).astype(f32)
        choose = one_hot(spot_id + float(start * ROW_SLOTS) == spot).astype(jnp.bfloat16)
        rows = jnp.dot(choose, fresh_ref[...], preferred_element_type=f32).astype(jnp.bfloat16)
        packed[start : start + step] = rows.reshape(step, ROW_SLOTS, fresh_ref.shape[1])


def first_gather_kernel(count, *refs):
    lists, store_hbm, sends = refs[:count], refs[count], refs[count + 1 : 2 * count + 1]
    held, load_sem, send_sem = refs[2 * count + 1 :]
    capacity = held.shape[1]
    for i, numbers in enumerate(lists):
        for k in range(capacity):
            pltpu.make_async_copy(store_hbm.at[numbers[0, 0, k]], held.at[i, k], load_sem).start()
    pltpu.make_async_copy(held, held, load_sem).wait()
    for i, send in enumerate(sends):
        pltpu.make_async_copy(held.at[i], send, send_sem).start()
    pltpu.make_async_copy(held, held, send_sem).wait()


def gather_kernel(capacity, distances, own, index, store_hbm, *rest):
    sends, (store, load_sem, send_sem) = rest[:-3], rest[-3:]
    load = pltpu.make_async_copy(store_hbm, store, load_sem)
    load.start()
    load.wait()
    for i in range(len(distances) if distances else index.shape[0]):
        r = own[0] ^ distances[i] if distances else i
        send = sends[i] if distances else sends[0].at[i]
        for k in range(capacity):
            pltpu.make_async_copy(store.at[index[r, 0, k]], send.at[k], send_sem).start()
    for send in sends:
        pltpu.make_async_copy(send, send, send_sem).wait()


def write_back_kernel(index, targets_ref, store_hbm, rows_hbm, store_out, *scratch):
    store, rows, blended, load_sem, rows_sem, out_sem = scratch
    holders, capacity, page_len, width = blended.shape
    rows_here = capacity * page_len
    f32 = jnp.float32
    load = pltpu.make_async_copy(store_hbm, store, load_sem)
    load_rows = pltpu.make_async_copy(rows_hbm, rows, rows_sem)
    load.start()
    load_rows.start()
    load_rows.wait()
    load.wait()
    row_id = lax.broadcasted_iota(jnp.int32, (rows_here, ROW_SLOTS), 0)

    def one_request(r, carry):
        hit = one_hot(row_id == targets_ref[r][1:2, 0:ROW_SLOTS] - 1)
        keep = 1.0 - jnp.sum(hit, axis=1, keepdims=True)
        keep = jnp.broadcast_to(keep, (rows_here, LANES)).astype(jnp.bfloat16)
        hit = hit.astype(jnp.bfloat16)
        for c in range(width // LANES):
            lanes = slice(c * LANES, (c + 1) * LANES)
            fresh = jnp.dot(hit, rows[r, :, lanes], preferred_element_type=f32).astype(jnp.bfloat16)
            for k in range(capacity):
                part = slice(k * page_len, (k + 1) * page_len)
                blended[r, k, :, lanes] = store[index[r, 0, k], :, lanes] * keep[part] + fresh[part]
        for k in range(capacity):
            pltpu.make_async_copy(blended.at[r, k], store_out.at[index[r, 0, k]], out_sem).start()
        return carry

    lax.fori_loop(0, holders, one_request, 0)
    pltpu.make_async_copy(store_out, store_out, out_sem).wait()


def attend_kernel(first, last, sources, place, page_number, tiles, *rest):
    sel_ref, positions_ref, query_ref, *rest = rest
    if first:
        fresh_ref, fresh_positions, *rest = rest
    state_in = () if first else rest[:2]
    rest = rest if first else rest[2:]
    contexts, rest = rest[:sources], rest[sources:]
    outs, rest = (rest[:1], rest[1:]) if last else (rest[:2], rest[2:])
    kv, values, position, query, mixed, stats, sem = rest
    pages, page_len, width = kv.shape
    each = contexts[0].shape[0]
    ahead = TILE_PAGES if first else 0
    block = query_ref.shape[0]
    tile = TILE_PAGES * page_len
    lanes = QUERY_GROUP * block
    scale = 1.4426950408889634 / HEAD_WIDTH**0.5
    f32 = jnp.float32
    bf16 = jnp.bfloat16
    step = pl.program_id(0)
    eye = one_hot(
        lax.broadcasted_iota(jnp.int32, (LANES, LANES), 0)
        == lax.broadcasted_iota(jnp.int32, (LANES, LANES), 1)
    ).astype(bf16)

    @pl.when(step == 0)
    def _():
        for i, context in enumerate(contexts):
            for k in range(each):
                pltpu.make_async_copy(context.at[k], kv.at[ahead + place[i * each + k]], sem).start()
        if first:
            picked = fresh_ref.shape[0]
            count = picked // page_len
            kv[0:count] = fresh_ref[...].reshape(count, page_len, width)
            kv[count:ahead] = jnp.zeros((ahead - count, page_len, width), bf16)
            position[0:picked, :] = fresh_positions[...]
            position[picked:tile, :] = jnp.full((tile - picked, LANES), FAR_POSITION, jnp.int32)
        positions = positions_ref[...]
        row = lax.broadcasted_iota(jnp.int32, (page_len, positions.shape[1]), 0)
        ones = jnp.ones((positions.shape[1], LANES), bf16)
        row_lanes = lax.broadcasted_iota(jnp.int32, (page_len, LANES), 0)

        def place_rows(t, carry):
            starts = [page_number[t * TILE_PAGES + k] * page_len for k in range(TILE_PAGES)]
            hit = jnp.concatenate([one_hot(row + start == positions) for start in starts], axis=0)
            hidden = jnp.dot(hit.astype(bf16), ones, preferred_element_type=f32)
            plain = jnp.concatenate([row_lanes + start for start in starts], axis=0)
            here = pl.ds(pl.multiple_of(ahead * page_len + t * tile, tile), tile)
            position[here, :] = jnp.where(hidden > 0.0, FAR_POSITION, plain)
            return carry

        lax.fori_loop(0, (pages - ahead) // TILE_PAGES, place_rows, 0)
        used = kv.at[ahead:]
        pltpu.make_async_copy(used, used, sem).wait()

        def turn(t, carry):
            here = pl.ds(t * TILE_PAGES, TILE_PAGES)
            for g in range(KEY_VALUE_HEADS):
                at = (KEY_VALUE_HEADS + g) * LANES
                value = kv[here, :, at : at + LANES].reshape(tile, LANES)
                values[t, g] = nt_dot(eye, value).astype(bf16)
            return carry

        lax.fori_loop(0, pages // TILE_PAGES, turn, 0)

    for g in range(KEY_VALUE_HEADS):
        for i in range(QUERY_GROUP):
            head = g * QUERY_GROUP + i
            query[g, i * block : (i + 1) * block, :] = query_ref[:, head * LANES : (head + 1) * LANES]
    if first:
        mixed[...] = jnp.zeros(mixed.shape, f32)
        stats[0:KEY_VALUE_HEADS, :] = jnp.full((KEY_VALUE_HEADS, lanes), HIDDEN, f32)
        stats[KEY_VALUE_HEADS:, :] = jnp.zeros((KEY_VALUE_HEADS, lanes), f32)
    else:
        mixed[...] = state_in[0][0]
        stats[...] = state_in[1][0]

    sel = sel_ref[0]

    def one_tile(t, carry):
        here = pl.ds(t * TILE_PAGES, TILE_PAGES)
        bias = jnp.where(
            position[pl.ds(pl.multiple_of(t * tile, tile), tile), :] <= sel, 0.0, HIDDEN
        ).astype(f32)

        def score(g):
            key = kv[here, :, g * LANES : (g + 1) * LANES].reshape(tile, LANES)
            return nt_dot(key, query[g])

        upcoming = score(0)
        for g in range(KEY_VALUE_HEADS):
            scores = upcoming
            if g + 1 < KEY_VALUE_HEADS:
                upcoming = score(g + 1)
            raised, shrinks = [], []
            at = KEY_VALUE_HEADS + g
            for n in range(lanes // LANES):
                part = slice(n * LANES, (n + 1) * LANES)
                s = scores[:, part] + bias
                old = stats[g : g + 1, part]
                new = jnp.maximum(old, jnp.max(s, axis=0, keepdims=True))
                p = jnp.exp2((s - new) * scale)
                shrink = jnp.exp2((old - new) * scale)
                stats[at : at + 1, part] = stats[at : at + 1, part] * shrink + jnp.sum(
                    p, axis=0, keepdims=True
                )
                stats[g : g + 1, part] = new
                raised.append(p.astype(bf16))
                shrinks.append(shrink)
            raised = jnp.concatenate(raised, axis=1)
            shrink = jnp.concatenate(shrinks, axis=1)
            mixed[g] = mixed[g] * shrink + jnp.dot(
                values[t, g], raised, preferred_element_type=f32
            )
        return carry

    lax.fori_loop(0, tiles[step], one_tile, 0)

    if last:
        done = []
        for g in range(KEY_VALUE_HEADS):
            at = KEY_VALUE_HEADS + g
            part = (mixed[g] * (1.0 / stats[at : at + 1, :])).astype(bf16)
            done += [part[:, n * LANES : (n + 1) * LANES] for n in range(lanes // LANES)]
        turned = nt_dot(eye, jnp.concatenate(done, axis=0)).astype(bf16)
        for n in range(len(done)):
            for i in range(LANES // block):
                head = n * (LANES // block) + i
                outs[0][:, head * LANES : (head + 1) * LANES] = turned[
                    i * block : (i + 1) * block, n * LANES : (n + 1) * LANES
                ]
    else:
        outs[0][0] = mixed[...]
        outs[1][0] = stats[...]


def attend(first, last, order, sel_lanes, positions, queries, fresh, state, contexts):
    picked, features = queries.shape
    each, page_len, width = contexts[0].shape
    pages = each * len(contexts) + (TILE_PAGES if first else 0)
    steps = picked // QUERY_BLOCK
    lanes = QUERY_GROUP * QUERY_BLOCK
    wide = pl.BlockSpec((QUERY_BLOCK, features), lambda b, *_: (b, 0))
    state_specs = [
        pl.BlockSpec((1, KEY_VALUE_HEADS, LANES, lanes), lambda b, *_: (b, 0, 0, 0)),
        pl.BlockSpec((1, 2 * KEY_VALUE_HEADS, lanes), lambda b, *_: (b, 0, 0)),
    ]
    state_shapes = [
        jax.ShapeDtypeStruct((steps, KEY_VALUE_HEADS, LANES, lanes), jnp.float32),
        jax.ShapeDtypeStruct((steps, 2 * KEY_VALUE_HEADS, lanes), jnp.float32),
    ]
    share = 0.6
    return pl.pallas_call(
        functools.partial(attend_kernel, first, last, len(contexts)),
        grid_spec=pltpu.PrefetchScalarGridSpec(
            num_scalar_prefetch=3,
            grid=(steps,),
            in_specs=[
                pl.BlockSpec((1, 1, LANES), lambda b, *_: (b, 0, 0)),
                pl.BlockSpec(positions.shape, lambda b, *_: (0, 0)),
                wide,
                *[pl.BlockSpec(x.shape, lambda b, *_: (0, 0)) for x in fresh if first],
                *([] if first else state_specs),
                *[pl.BlockSpec(memory_space=pltpu.HBM)] * len(contexts),
            ],
            out_specs=[wide] if last else state_specs,
            scratch_shapes=[
                pltpu.VMEM((pages, page_len, width), jnp.bfloat16),
                pltpu.VMEM(
                    (pages // TILE_PAGES, KEY_VALUE_HEADS, LANES, TILE_PAGES * page_len), jnp.bfloat16
                ),
                pltpu.VMEM((pages * page_len, LANES), jnp.int32),
                pltpu.VMEM((KEY_VALUE_HEADS, lanes, LANES), jnp.bfloat16),
                pltpu.VMEM((KEY_VALUE_HEADS, LANES, lanes), jnp.float32),
                pltpu.VMEM((2 * KEY_VALUE_HEADS, lanes), jnp.float32),
                pltpu.SemaphoreType.DMA,
            ],
        ),
        out_shape=[jax.ShapeDtypeStruct((picked, features), jnp.bfloat16)] if last else state_shapes,
        compiler_params=pltpu.CompilerParams(
            dimension_semantics=("arbitrary",), vmem_limit_bytes=VMEM_LIMIT
        ),
        cost_estimate=pl.CostEstimate(
            flops=int(share * 8 * picked * features * pages * page_len),
            bytes_accessed=2 * pages * page_len * width + 6 * picked * features,
            transcendentals=int(share * picked * features // LANES * pages * page_len),
        ),
    )(*order, sel_lanes, positions, queries, *[x for x in fresh if first], *state, *contexts)


def page_order(slots, positions, own, hold, capacity, groups, page_len):
    pages = slots.shape[0]
    number = jnp.arange(pages)
    before = number[None, :] < number[:, None]
    owners = slots // hold
    ranks = jnp.sum(((owners[None, :] == owners[:, None]) & before).astype(jnp.int32), axis=1)
    distance = owners ^ own
    last_page = positions.reshape(-1, QUERY_BLOCK)[:, -1] // page_len
    orders = []
    for at, group in enumerate(groups):
        if group is None:
            arrival = owners * capacity + ranks
            count = pages
        else:
            arrival = jnp.full((pages,), -1, jnp.int32)
            for i, d in enumerate(group):
                arrival = jnp.where(distance == d, i * capacity + ranks, arrival)
            count = len(group) * capacity
        member = arrival >= 0
        place = jnp.sum((member[None, :] & before).astype(jnp.int32), axis=1)
        index = jnp.arange(count)[:, None]
        places = jnp.sum(jnp.where(arrival[None, :] == index, place[None, :], 0), axis=1)
        page = jnp.sum(
            jnp.where(member[None, :] & (place[None, :] == index), number[None, :], 0), axis=1
        )
        seen = jnp.sum((page[None, :] <= last_page[:, None]).astype(jnp.int32), axis=1)
        orders.append((places, page, (seen + TILE_PAGES - 1) // TILE_PAGES + (at == 0)))
    return orders


def per_device(store, page_table, sel_pos, fresh_kv, queries):
    holders = lax.axis_size("store")
    hold, page_len, width = store.shape
    pages = page_table.shape[1]
    picked = sel_pos.shape[1]
    capacity = max(1, pages // holders)
    hbm = pl.BlockSpec(memory_space=pltpu.HBM)
    vmem = pl.BlockSpec(memory_space=pltpu.VMEM)
    dma = pltpu.SemaphoreType.DMA
    params = pltpu.CompilerParams(vmem_limit_bytes=VMEM_LIMIT)
    own = lax.axis_index("store")
    own_word = own.reshape(1).astype(jnp.int32)
    fresh = fresh_kv[0]
    wide = pltpu.VMEM((8, -(-picked // LANES) * LANES), jnp.int32)
    if holders == 16:
        first = (8, 12)
        groups = [(0, 8, 12, 4, 5, 1), (9, 13, 6, 7, 10, 2, 14, 3), (11, 15)]
        others = (0, 9, 13, 4, 5, 1, 6, 7, 10, 2, 14, 3, 11, 15)
    else:
        first = ()
        groups = [None]
        others = None

    def swap(x, d):
        return lax.ppermute(x, "store", [(h, h ^ d) for h in range(holders)])

    def exchange(x):
        return lax.all_to_all(x, "store", split_axis=0, concat_axis=0, tiled=True)

    index, *lists = pl.pallas_call(
        functools.partial(index_kernel, hold, page_len, first),
        grid_spec=pltpu.PrefetchScalarGridSpec(
            num_scalar_prefetch=1,
            grid=(1,),
            in_specs=[vmem, vmem],
            out_specs=[vmem] * (1 + len(first)),
            scratch_shapes=[wide],
        ),
        out_shape=[
            jax.ShapeDtypeStruct((holders, 2, LANES), jnp.int32),
            *[jax.ShapeDtypeStruct((1, 2, LANES), jnp.int32)] * len(first),
        ],
        compiler_params=params,
    )(own_word, page_table, sel_pos)
    arrived = {}
    if first:
        lists = [swap(x, d) for x, d in zip(lists, first)]
        parts = pl.pallas_call(
            functools.partial(first_gather_kernel, len(first)),
            grid_spec=pltpu.PrefetchScalarGridSpec(
                num_scalar_prefetch=len(first),
                grid=(1,),
                in_specs=[hbm],
                out_specs=[hbm] * len(first),
                scratch_shapes=[
                    pltpu.VMEM((len(first), capacity, page_len, width), store.dtype),
                    dma,
                    dma,
                ],
            ),
            out_shape=[jax.ShapeDtypeStruct((capacity, page_len, width), store.dtype)] * len(first),
            compiler_params=params,
        )(*lists, store)
        parts, index, table, positions = lax.optimization_barrier(
            (parts, index, page_table, sel_pos)
        )
        arrived = {d: swap(part, d) for d, part in zip(first, parts)}
    else:
        table, positions = page_table, sel_pos
    packed = pl.pallas_call(
        functools.partial(rows_kernel, hold, page_len),
        out_shape=jax.ShapeDtypeStruct((holders, ROW_SLOTS, width), store.dtype),
        scratch_shapes=[wide],
        compiler_params=params,
    )(table, positions, fresh)
    if first:
        index, packed = lax.optimization_barrier((index, packed))
    index_in = exchange(index)

    each = jax.ShapeDtypeStruct((capacity, page_len, width), store.dtype)
    whole = jax.ShapeDtypeStruct((holders, capacity, page_len, width), store.dtype)
    parts = pl.pallas_call(
        functools.partial(gather_kernel, capacity, others),
        grid_spec=pltpu.PrefetchScalarGridSpec(
            num_scalar_prefetch=2,
            grid=(1,),
            in_specs=[hbm],
            out_specs=[hbm] * (len(others) if others else 1),
            scratch_shapes=[pltpu.VMEM(store.shape, store.dtype), dma, dma],
        ),
        out_shape=[each] * len(others) if others else [whole],
        compiler_params=params,
    )(own_word, index_in, store)
    parts, packed, table, positions = lax.optimization_barrier((parts, packed, table, positions))
    if others:
        for d, part in zip(others, parts):
            arrived[d] = swap(part, d) if d else part
        contexts = [[arrived[d] for d in group] for group in groups]
    else:
        contexts = [[exchange(parts[0]).reshape(pages, page_len, width)]]
    rows_in = exchange(packed)

    store_out = pl.pallas_call(
        write_back_kernel,
        grid_spec=pltpu.PrefetchScalarGridSpec(
            num_scalar_prefetch=1,
            grid=(1,),
            in_specs=[vmem, hbm, hbm],
            out_specs=hbm,
            scratch_shapes=[
                pltpu.VMEM(store.shape, store.dtype),
                pltpu.VMEM((holders, ROW_SLOTS, width), store.dtype),
                pltpu.VMEM((holders, capacity, page_len, width), store.dtype),
                dma,
                dma,
                dma,
            ],
        ),
        out_shape=jax.ShapeDtypeStruct(store.shape, store.dtype),
        compiler_params=params,
        cost_estimate=pl.CostEstimate(flops=0, bytes_accessed=4 * store.size, transcendentals=0),
    )(index_in, index_in, store, rows_in)

    orders = page_order(table[0], positions[0], own, hold, capacity, groups, page_len)
    sel_lanes = jnp.tile(positions.reshape(-1, 1, QUERY_BLOCK), (1, 1, LANES // QUERY_BLOCK))
    sel_rows = jnp.broadcast_to(positions.reshape(picked, 1), (picked, LANES))
    store_out, sel_lanes = lax.optimization_barrier((store_out, sel_lanes))
    state = ()
    for at, (arrays, order) in enumerate(zip(contexts, orders)):
        state = attend(
            at == 0,
            at == len(groups) - 1,
            order,
            sel_lanes,
            positions,
            queries[0],
            (fresh, sel_rows),
            state,
            arrays,
        )
    return (state[0][None], store_out)


def solution(mesh):
    return jax.shard_map(
        per_device,
        mesh=mesh,
        in_specs=(
            P(("groups", "store"), None, None),
            P(("groups", "store"), None),
            P(("groups", "store"), None),
            P(("groups", "store"), None, None),
            P(("groups", "store"), None, None),
        ),
        out_specs=(P(("groups", "store"), None, None), P(("groups", "store"), None, None)),
        check_vma=False,
    )
```

```python
import functools

import jax
import jax.numpy as jnp
from jax import lax
from jax.experimental import pallas as pl
from jax.experimental.pallas import tpu as pltpu
from jax.sharding import PartitionSpec as P

HEAD_WIDTH = 128
KEY_VALUE_HEADS = 4
QUERY_GROUP = 12
SELP = 2
LANES = 128
ROW_SLOTS = 16
VMEM_LIMIT = 60 * 1024 * 1024
QUERY_BLOCK = 32
TILE_PAGES = 16
HIDDEN = -1e30
FAR_POSITION = 1 << 24


def nt_dot(a, b):
    return lax.dot_general(a, b, (((1,), (1,)), ((), ())), preferred_element_type=jnp.float32)


def distance(own, step):
    mask, even, odd = step
    bits = own & mask
    bits = bits ^ (bits >> 2)
    bits = (bits ^ (bits >> 1)) & 1
    return even + bits * (odd - even)


def one_hot(condition):
    return jnp.where(condition, 1.0, 0.0)


def pair_places(hold, page_len, table_ref, sel_ref, wide):
    pages = table_ref.shape[1]
    picked = sel_ref.shape[1]
    f32 = jnp.float32
    slots = jnp.broadcast_to(table_ref[...], (pages, pages))
    owners = slots // hold
    local_row = (slots - owners * hold).astype(f32)[0:1]
    owner_row = owners.astype(f32)
    owner_col = owner_row.T
    sub = lax.broadcasted_iota(jnp.int32, (pages, pages), 0)
    lane = lax.broadcasted_iota(jnp.int32, (pages, pages), 1)
    earlier = one_hot((owner_row == owner_col) & (lane < sub))
    rank_col = jnp.sum(earlier, axis=1, keepdims=True)

    wide[...] = jnp.full(wide.shape, -1, jnp.int32)
    wide[0:1, 0:picked] = sel_ref[...]
    position = wide[...]
    page = lax.shift_right_arithmetic(position, page_len.bit_length() - 1)
    offset = (position & (page_len - 1)).astype(f32)[0:1]
    lane_wide = lax.broadcasted_iota(jnp.int32, wide.shape, 1)
    second = one_hot((page == pltpu.roll(page, 1, axis=1)) & (lane_wide > 0))[0:1]
    valid = lane_wide[0:1] < picked
    sub_wide = lax.broadcasted_iota(jnp.int32, (pages, wide.shape[1]), 0)
    in_page = one_hot(sub_wide == page[0:1])
    owner = jnp.sum(in_page * owner_col[:, 0:1], axis=0, keepdims=True)
    rank = jnp.sum(in_page * rank_col, axis=0, keepdims=True)
    return owner_row[0:1], local_row, rank_col, owner, rank, second, offset, valid


def index_kernel(hold, page_len, first, own, table_ref, sel_ref, out_ref, *rest):
    first_refs, wide = rest[:-1], rest[-1]
    holders = out_ref.shape[0]
    pages = table_ref.shape[1]
    f32 = jnp.float32
    bf16 = jnp.bfloat16
    owner_row, local_row, rank_col, owner, rank, second, offset, valid = pair_places(
        hold, page_len, table_ref, sel_ref, wide
    )
    holder = lax.broadcasted_iota(jnp.int32, (holders, pages), 0).astype(f32)
    owned = jnp.where(holder == owner_row, local_row, 0.0)
    lane = lax.broadcasted_iota(jnp.int32, (pages, LANES), 1).astype(f32)
    numbers = jnp.dot(
        owned.astype(bf16), one_hot(lane == rank_col).astype(bf16), preferred_element_type=f32
    )
    holder_wide = lax.broadcasted_iota(jnp.int32, (holders, wide.shape[1]), 0).astype(f32)
    marked = jnp.where((holder_wide == owner) & valid, rank * page_len + offset + 1.0, 0.0)
    place_lane = lax.broadcasted_iota(jnp.int32, (LANES, wide.shape[1]), 0).astype(f32)
    at_place = one_hot(place_lane == SELP * rank + second)
    targets = nt_dot(marked.astype(bf16), at_place.astype(bf16))
    for h in range(holders):
        out_ref[h, 0:1, :] = numbers[h : h + 1, :].astype(jnp.int32)
        out_ref[h, 1:2, :] = targets[h : h + 1, :].astype(jnp.int32)
    for d, ref in zip(first, first_refs):
        ref[0] = out_ref[own[0] ^ distance(own[0], d)]


def rows_kernel(hold, page_len, table_ref, sel_ref, fresh_ref, packed, wide):
    holders = packed.shape[0]
    picked = sel_ref.shape[1]
    f32 = jnp.float32
    _, _, _, owner, rank, second, _, valid = pair_places(hold, page_len, table_ref, sel_ref, wide)
    spot = jnp.where(valid, owner * ROW_SLOTS + SELP * rank + second, -1.0)[:, 0:picked]
    step = min(holders, 16)
    for start in range(0, holders, step):
        spot_id = lax.broadcasted_iota(jnp.int32, (step * ROW_SLOTS, picked), 0).astype(f32)
        choose = one_hot(spot_id + float(start * ROW_SLOTS) == spot).astype(jnp.bfloat16)
        rows = jnp.dot(choose, fresh_ref[...], preferred_element_type=f32).astype(jnp.bfloat16)
        packed[start : start + step] = rows.reshape(step, ROW_SLOTS, fresh_ref.shape[1])


def first_gather_kernel(count, *refs):
    lists, store_hbm, sends = refs[:count], refs[count], refs[count + 1 : 2 * count + 1]
    held, load_sem, send_sem = refs[2 * count + 1 :]
    capacity = held.shape[1]
    for i, numbers in enumerate(lists):
        for k in range(capacity):
            pltpu.make_async_copy(store_hbm.at[numbers[0, 0, k]], held.at[i, k], load_sem).start()
    pltpu.make_async_copy(held, held, load_sem).wait()
    for i, send in enumerate(sends):
        pltpu.make_async_copy(held.at[i], send, send_sem).start()
    pltpu.make_async_copy(held, held, send_sem).wait()


def gather_kernel(capacity, steps, own, index, *rest):
    if steps:
        numbers, *rest = rest
    store_hbm, *sends = rest[:-3]
    store, load_sem, send_sem = rest[-3:]
    load = pltpu.make_async_copy(store_hbm, store, load_sem)
    load.start()
    load.wait()
    for i in range(len(steps) if steps else index.shape[0]):
        r = own[0] ^ distance(own[0], steps[i]) if steps else i
        send = sends[i] if steps else sends[0].at[i]
        for k in range(capacity):
            number = numbers[0, 0, k] if steps and i == 0 else index[r, 0, k]
            pltpu.make_async_copy(store.at[number], send.at[k], send_sem).start()
    for send in sends:
        pltpu.make_async_copy(send, send, send_sem).wait()


def write_back_kernel(index, targets_ref, store_hbm, rows_hbm, store_out, *scratch):
    store, rows, blended, load_sem, rows_sem, out_sem = scratch
    holders, capacity, page_len, width = blended.shape
    rows_here = capacity * page_len
    f32 = jnp.float32
    load = pltpu.make_async_copy(store_hbm, store, load_sem)
    load_rows = pltpu.make_async_copy(rows_hbm, rows, rows_sem)
    load.start()
    load_rows.start()
    load_rows.wait()
    load.wait()
    row_id = lax.broadcasted_iota(jnp.int32, (rows_here, ROW_SLOTS), 0)

    def one_request(r, carry):
        hit = one_hot(row_id == targets_ref[r][1:2, 0:ROW_SLOTS] - 1)
        keep = 1.0 - jnp.sum(hit, axis=1, keepdims=True)
        keep = jnp.broadcast_to(keep, (rows_here, LANES)).astype(jnp.bfloat16)
        hit = hit.astype(jnp.bfloat16)
        for c in range(width // LANES):
            lanes = slice(c * LANES, (c + 1) * LANES)
            fresh = jnp.dot(hit, rows[r, :, lanes], preferred_element_type=f32).astype(jnp.bfloat16)
            for k in range(capacity):
                part = slice(k * page_len, (k + 1) * page_len)
                blended[r, k, :, lanes] = store[index[r, 0, k], :, lanes] * keep[part] + fresh[part]
        for k in range(capacity):
            pltpu.make_async_copy(blended.at[r, k], store_out.at[index[r, 0, k]], out_sem).start()
        return carry

    lax.fori_loop(0, holders, one_request, 0)
    pltpu.make_async_copy(store_out, store_out, out_sem).wait()


def attend_kernel(first, last, sources, place, page_number, tiles, *rest):
    sel_ref, positions_ref, query_ref, *rest = rest
    if first:
        fresh_ref, fresh_positions, *rest = rest
    state_in = () if first else rest[:2]
    rest = rest if first else rest[2:]
    contexts, rest = rest[:sources], rest[sources:]
    outs, rest = (rest[:1], rest[1:]) if last else (rest[:2], rest[2:])
    kv, values, position, query, mixed, stats, sem = rest
    pages, page_len, width = kv.shape
    each = contexts[0].shape[0]
    ahead = TILE_PAGES if first else 0
    block = query_ref.shape[0]
    tile = TILE_PAGES * page_len
    lanes = QUERY_GROUP * block
    scale = 1.4426950408889634 / HEAD_WIDTH**0.5
    f32 = jnp.float32
    bf16 = jnp.bfloat16
    step = pl.program_id(0)
    eye = one_hot(
        lax.broadcasted_iota(jnp.int32, (LANES, LANES), 0)
        == lax.broadcasted_iota(jnp.int32, (LANES, LANES), 1)
    ).astype(bf16)

    @pl.when(step == 0)
    def _():
        for i, context in enumerate(contexts):
            for k in range(each):
                pltpu.make_async_copy(context.at[k], kv.at[ahead + place[i * each + k]], sem).start()
        if first:
            picked = fresh_ref.shape[0]
            count = picked // page_len
            kv[0:count] = fresh_ref[...].reshape(count, page_len, width)
            kv[count:ahead] = jnp.zeros((ahead - count, page_len, width), bf16)
            position[0:picked, :] = fresh_positions[...]
            position[picked:tile, :] = jnp.full((tile - picked, LANES), FAR_POSITION, jnp.int32)
        positions = positions_ref[...]
        row = lax.broadcasted_iota(jnp.int32, (page_len, positions.shape[1]), 0)
        ones = jnp.ones((positions.shape[1], LANES), bf16)
        row_lanes = lax.broadcasted_iota(jnp.int32, (page_len, LANES), 0)

        def place_rows(t, carry):
            starts = [page_number[t * TILE_PAGES + k] * page_len for k in range(TILE_PAGES)]
            hit = jnp.concatenate([one_hot(row + start == positions) for start in starts], axis=0)
            hidden = jnp.dot(hit.astype(bf16), ones, preferred_element_type=f32)
            plain = jnp.concatenate([row_lanes + start for start in starts], axis=0)
            here = pl.ds(pl.multiple_of(ahead * page_len + t * tile, tile), tile)
            position[here, :] = jnp.where(hidden > 0.0, FAR_POSITION, plain)
            return carry

        lax.fori_loop(0, (pages - ahead) // TILE_PAGES, place_rows, 0)
        used = kv.at[ahead:]
        pltpu.make_async_copy(used, used, sem).wait()

        def turn(t, carry):
            here = pl.ds(t * TILE_PAGES, TILE_PAGES)
            for g in range(KEY_VALUE_HEADS):
                at = (KEY_VALUE_HEADS + g) * LANES
                value = kv[here, :, at : at + LANES].reshape(tile, LANES)
                values[t, g] = nt_dot(eye, value).astype(bf16)
            return carry

        lax.fori_loop(0, pages // TILE_PAGES, turn, 0)

    for g in range(KEY_VALUE_HEADS):
        for i in range(QUERY_GROUP):
            head = g * QUERY_GROUP + i
            query[g, i * block : (i + 1) * block, :] = query_ref[:, head * LANES : (head + 1) * LANES]
    if first:
        mixed[...] = jnp.zeros(mixed.shape, f32)
        stats[0:KEY_VALUE_HEADS, :] = jnp.full((KEY_VALUE_HEADS, lanes), HIDDEN, f32)
        stats[KEY_VALUE_HEADS:, :] = jnp.zeros((KEY_VALUE_HEADS, lanes), f32)
    else:
        mixed[...] = state_in[0][0]
        stats[...] = state_in[1][0]

    sel = sel_ref[0]

    def one_tile(t, carry):
        here = pl.ds(t * TILE_PAGES, TILE_PAGES)
        bias = jnp.where(
            position[pl.ds(pl.multiple_of(t * tile, tile), tile), :] <= sel, 0.0, HIDDEN
        ).astype(f32)

        def score(g):
            key = kv[here, :, g * LANES : (g + 1) * LANES].reshape(tile, LANES)
            return nt_dot(key, query[g])

        upcoming = score(0)
        for g in range(KEY_VALUE_HEADS):
            scores = upcoming
            if g + 1 < KEY_VALUE_HEADS:
                upcoming = score(g + 1)
            raised, shrinks = [], []
            at = KEY_VALUE_HEADS + g
            for n in range(lanes // LANES):
                part = slice(n * LANES, (n + 1) * LANES)
                s = scores[:, part] + bias
                old = stats[g : g + 1, part]
                new = jnp.maximum(old, jnp.max(s, axis=0, keepdims=True))
                p = jnp.exp2((s - new) * scale)
                shrink = jnp.exp2((old - new) * scale)
                stats[at : at + 1, part] = stats[at : at + 1, part] * shrink + jnp.sum(
                    p, axis=0, keepdims=True
                )
                stats[g : g + 1, part] = new
                raised.append(p.astype(bf16))
                shrinks.append(shrink)
            raised = jnp.concatenate(raised, axis=1)
            shrink = jnp.concatenate(shrinks, axis=1)
            mixed[g] = mixed[g] * shrink + jnp.dot(
                values[t, g], raised, preferred_element_type=f32
            )
        return carry

    lax.fori_loop(0, tiles[step], one_tile, 0)

    if last:
        done = []
        for g in range(KEY_VALUE_HEADS):
            at = KEY_VALUE_HEADS + g
            part = (mixed[g] * (1.0 / stats[at : at + 1, :])).astype(bf16)
            done += [part[:, n * LANES : (n + 1) * LANES] for n in range(lanes // LANES)]
        turned = nt_dot(eye, jnp.concatenate(done, axis=0)).astype(bf16)
        for n in range(len(done)):
            for i in range(LANES // block):
                head = n * (LANES // block) + i
                outs[0][:, head * LANES : (head + 1) * LANES] = turned[
                    i * block : (i + 1) * block, n * LANES : (n + 1) * LANES
                ]
    else:
        outs[0][0] = mixed[...]
        outs[1][0] = stats[...]


def attend(first, last, order, sel_lanes, positions, queries, fresh, state, contexts):
    picked, features = queries.shape
    each, page_len, width = contexts[0].shape
    pages = each * len(contexts) + (TILE_PAGES if first else 0)
    steps = picked // QUERY_BLOCK
    lanes = QUERY_GROUP * QUERY_BLOCK
    wide = pl.BlockSpec((QUERY_BLOCK, features), lambda b, *_: (b, 0))
    state_specs = [
        pl.BlockSpec((1, KEY_VALUE_HEADS, LANES, lanes), lambda b, *_: (b, 0, 0, 0)),
        pl.BlockSpec((1, 2 * KEY_VALUE_HEADS, lanes), lambda b, *_: (b, 0, 0)),
    ]
    state_shapes = [
        jax.ShapeDtypeStruct((steps, KEY_VALUE_HEADS, LANES, lanes), jnp.float32),
        jax.ShapeDtypeStruct((steps, 2 * KEY_VALUE_HEADS, lanes), jnp.float32),
    ]
    share = 0.6
    return pl.pallas_call(
        functools.partial(attend_kernel, first, last, len(contexts)),
        grid_spec=pltpu.PrefetchScalarGridSpec(
            num_scalar_prefetch=3,
            grid=(steps,),
            in_specs=[
                pl.BlockSpec((1, 1, LANES), lambda b, *_: (b, 0, 0)),
                pl.BlockSpec(positions.shape, lambda b, *_: (0, 0)),
                wide,
                *[pl.BlockSpec(x.shape, lambda b, *_: (0, 0)) for x in fresh if first],
                *([] if first else state_specs),
                *[pl.BlockSpec(memory_space=pltpu.HBM)] * len(contexts),
            ],
            out_specs=[wide] if last else state_specs,
            scratch_shapes=[
                pltpu.VMEM((pages, page_len, width), jnp.bfloat16),
                pltpu.VMEM(
                    (pages // TILE_PAGES, KEY_VALUE_HEADS, LANES, TILE_PAGES * page_len), jnp.bfloat16
                ),
                pltpu.VMEM((pages * page_len, LANES), jnp.int32),
                pltpu.VMEM((KEY_VALUE_HEADS, lanes, LANES), jnp.bfloat16),
                pltpu.VMEM((KEY_VALUE_HEADS, LANES, lanes), jnp.float32),
                pltpu.VMEM((2 * KEY_VALUE_HEADS, lanes), jnp.float32),
                pltpu.SemaphoreType.DMA,
            ],
        ),
        out_shape=[jax.ShapeDtypeStruct((picked, features), jnp.bfloat16)] if last else state_shapes,
        compiler_params=pltpu.CompilerParams(
            dimension_semantics=("arbitrary",), vmem_limit_bytes=VMEM_LIMIT
        ),
        cost_estimate=pl.CostEstimate(
            flops=int(share * 8 * picked * features * pages * page_len),
            bytes_accessed=2 * pages * page_len * width + 6 * picked * features,
            transcendentals=int(share * picked * features // LANES * pages * page_len),
        ),
    )(*order, sel_lanes, positions, queries, *[x for x in fresh if first], *state, *contexts)


def page_order(slots, positions, own, hold, capacity, groups, page_len):
    pages = slots.shape[0]
    number = jnp.arange(pages)
    before = number[None, :] < number[:, None]
    owners = slots // hold
    ranks = jnp.sum(((owners[None, :] == owners[:, None]) & before).astype(jnp.int32), axis=1)
    last_page = positions.reshape(-1, QUERY_BLOCK)[:, -1] // page_len
    orders = []
    for at, group in enumerate(groups):
        if group is None:
            arrival = owners * capacity + ranks
            count = pages
        else:
            arrival = jnp.full((pages,), -1, jnp.int32)
            for i, step in enumerate(group):
                arrival = jnp.where(owners ^ own == distance(own, step), i * capacity + ranks, arrival)
            count = len(group) * capacity
        member = arrival >= 0
        place = jnp.sum((member[None, :] & before).astype(jnp.int32), axis=1)
        index = jnp.arange(count)[:, None]
        places = jnp.sum(jnp.where(arrival[None, :] == index, place[None, :], 0), axis=1)
        page = jnp.sum(
            jnp.where(member[None, :] & (place[None, :] == index), number[None, :], 0), axis=1
        )
        seen = jnp.sum((page[None, :] <= last_page[:, None]).astype(jnp.int32), axis=1)
        orders.append((places, page, (seen + TILE_PAGES - 1) // TILE_PAGES + (at == 0)))
    return orders


def per_device(store, page_table, sel_pos, fresh_kv, queries):
    holders = lax.axis_size("store")
    hold, page_len, width = store.shape
    pages = page_table.shape[1]
    picked = sel_pos.shape[1]
    capacity = max(1, pages // holders)
    hbm = pl.BlockSpec(memory_space=pltpu.HBM)
    vmem = pl.BlockSpec(memory_space=pltpu.VMEM)
    dma = pltpu.SemaphoreType.DMA
    params = pltpu.CompilerParams(vmem_limit_bytes=VMEM_LIMIT)
    own = lax.axis_index("store")
    own_word = own.reshape(1).astype(jnp.int32)
    fresh = fresh_kv[0]
    wide = pltpu.VMEM((8, -(-picked // LANES) * LANES), jnp.int32)
    if holders == 16:
        local, near, first = (0, 0, 0), (0, 1, 1), [(0, 8, 8), (0, 12, 12)]
        mixed = [(5, 13, 5), (9, 9, 4), (1, 10, 2), (1, 14, 6), (3, 11, 3), (3, 15, 7)]
        mixed = [step for m, a, b in mixed for step in ((m, a, b), (m, b, a))]
        groups = [[local, *first, near, *mixed[0:2]], mixed[2:6], mixed[6:10], mixed[10:12]]
        others = [near, local, *mixed]
    else:
        first = []
        groups = [None]
        others = None

    def swap(x, step):
        return lax.ppermute(x, "store", [(h, h ^ distance(h, step)) for h in range(holders)])

    def exchange(x):
        return lax.all_to_all(x, "store", split_axis=0, concat_axis=0, tiled=True)

    ahead = [*first, near] if first else []
    index, *lists = pl.pallas_call(
        functools.partial(index_kernel, hold, page_len, ahead),
        grid_spec=pltpu.PrefetchScalarGridSpec(
            num_scalar_prefetch=1,
            grid=(1,),
            in_specs=[vmem, vmem],
            out_specs=[vmem] * (1 + len(ahead)),
            scratch_shapes=[wide],
        ),
        out_shape=[
            jax.ShapeDtypeStruct((holders, 2, LANES), jnp.int32),
            *[jax.ShapeDtypeStruct((1, 2, LANES), jnp.int32)] * len(ahead),
        ],
        compiler_params=params,
    )(own_word, page_table, sel_pos)
    arrived = {}
    near_list = []
    if first:
        early = [swap(x, step) for x, step in zip(lists, first)]
        parts = pl.pallas_call(
            functools.partial(first_gather_kernel, len(first)),
            grid_spec=pltpu.PrefetchScalarGridSpec(
                num_scalar_prefetch=len(first),
                grid=(1,),
                in_specs=[hbm],
                out_specs=[hbm] * len(first),
                scratch_shapes=[
                    pltpu.VMEM((len(first), capacity, page_len, width), store.dtype),
                    dma,
                    dma,
                ],
            ),
            out_shape=[jax.ShapeDtypeStruct((capacity, page_len, width), store.dtype)] * len(first),
            compiler_params=params,
        )(*early, store)
        parts, near_list = lax.optimization_barrier((parts, lists[len(first)]))
        arrived = {step: swap(part, step) for step, part in zip(first, parts)}
        near_list, index, table, positions = lax.optimization_barrier(
            (swap(near_list, near), index, page_table, sel_pos)
        )
        near_list = [near_list]
    else:
        table, positions = page_table, sel_pos
    packed = pl.pallas_call(
        functools.partial(rows_kernel, hold, page_len),
        out_shape=jax.ShapeDtypeStruct((holders, ROW_SLOTS, width), store.dtype),
        scratch_shapes=[wide],
        compiler_params=params,
    )(table, positions, fresh)
    index_in = exchange(index)

    each = jax.ShapeDtypeStruct((capacity, page_len, width), store.dtype)
    whole = jax.ShapeDtypeStruct((holders, capacity, page_len, width), store.dtype)
    parts = pl.pallas_call(
        functools.partial(gather_kernel, capacity, others),
        grid_spec=pltpu.PrefetchScalarGridSpec(
            num_scalar_prefetch=2 + len(near_list),
            grid=(1,),
            in_specs=[hbm],
            out_specs=[hbm] * (len(others) if others else 1),
            scratch_shapes=[pltpu.VMEM(store.shape, store.dtype), dma, dma],
        ),
        out_shape=[each] * len(others) if others else [whole],
        compiler_params=params,
    )(own_word, index_in, *near_list, store)
    parts, packed, table, positions = lax.optimization_barrier((parts, packed, table, positions))
    if others:
        for step, part in zip(others, parts):
            arrived[step] = part if step == local else swap(part, step)
        contexts = [[arrived[step] for step in group] for group in groups]
    else:
        contexts = [[exchange(parts[0]).reshape(pages, page_len, width)]]
    rows_in = exchange(packed)

    store_out = pl.pallas_call(
        write_back_kernel,
        grid_spec=pltpu.PrefetchScalarGridSpec(
            num_scalar_prefetch=1,
            grid=(1,),
            in_specs=[vmem, hbm, hbm],
            out_specs=hbm,
            scratch_shapes=[
                pltpu.VMEM(store.shape, store.dtype),
                pltpu.VMEM((holders, ROW_SLOTS, width), store.dtype),
                pltpu.VMEM((holders, capacity, page_len, width), store.dtype),
                dma,
                dma,
                dma,
            ],
        ),
        out_shape=jax.ShapeDtypeStruct(store.shape, store.dtype),
        compiler_params=params,
        cost_estimate=pl.CostEstimate(flops=0, bytes_accessed=4 * store.size, transcendentals=0),
    )(index_in, index_in, store, rows_in)

    orders = page_order(table[0], positions[0], own, hold, capacity, groups, page_len)
    sel_lanes = jnp.tile(positions.reshape(-1, 1, QUERY_BLOCK), (1, 1, LANES // QUERY_BLOCK))
    sel_rows = jnp.broadcast_to(positions.reshape(picked, 1), (picked, LANES))
    store_out, sel_lanes = lax.optimization_barrier((store_out, sel_lanes))
    state = ()
    for at, (arrays, order) in enumerate(zip(contexts, orders)):
        state = attend(
            at == 0,
            at == len(groups) - 1,
            order,
            sel_lanes,
            positions,
            queries[0],
            (fresh, sel_rows),
            state,
            arrays,
        )
    return (state[0][None], store_out)


def solution(mesh):
    return jax.shard_map(
        per_device,
        mesh=mesh,
        in_specs=(
            P(("groups", "store"), None, None),
            P(("groups", "store"), None),
            P(("groups", "store"), None),
            P(("groups", "store"), None, None),
            P(("groups", "store"), None, None),
        ),
        out_specs=(P(("groups", "store"), None, None), P(("groups", "store"), None, None)),
        check_vma=False,
    )
```

```python
import functools

import jax
import jax.numpy as jnp
from jax import lax
from jax.experimental import pallas as pl
from jax.experimental.pallas import tpu as pltpu
from jax.sharding import PartitionSpec as P

HEAD_WIDTH = 128
KEY_VALUE_HEADS = 4
QUERY_GROUP = 12
SELP = 2
LANES = 128
ROW_SLOTS = 16
VMEM_LIMIT = 60 * 1024 * 1024
QUERY_BLOCK = 32
TILE_PAGES = 16
HIDDEN = -1e30
FAR_POSITION = 1 << 24


def nt_dot(a, b):
    return lax.dot_general(a, b, (((1,), (1,)), ((), ())), preferred_element_type=jnp.float32)


def one_hot(condition):
    return jnp.where(condition, 1.0, 0.0)


def pair_places(hold, page_len, table_ref, sel_ref, wide):
    pages = table_ref.shape[1]
    picked = sel_ref.shape[1]
    f32 = jnp.float32
    slots = jnp.broadcast_to(table_ref[...], (pages, pages))
    owners = slots // hold
    local_row = (slots - owners * hold).astype(f32)[0:1]
    owner_row = owners.astype(f32)
    owner_col = owner_row.T
    sub = lax.broadcasted_iota(jnp.int32, (pages, pages), 0)
    lane = lax.broadcasted_iota(jnp.int32, (pages, pages), 1)
    earlier = one_hot((owner_row == owner_col) & (lane < sub))
    rank_col = jnp.sum(earlier, axis=1, keepdims=True)

    wide[...] = jnp.full(wide.shape, -1, jnp.int32)
    wide[0:1, 0:picked] = sel_ref[...]
    position = wide[...]
    page = lax.shift_right_arithmetic(position, page_len.bit_length() - 1)
    offset = (position & (page_len - 1)).astype(f32)[0:1]
    lane_wide = lax.broadcasted_iota(jnp.int32, wide.shape, 1)
    second = one_hot((page == pltpu.roll(page, 1, axis=1)) & (lane_wide > 0))[0:1]
    valid = lane_wide[0:1] < picked
    sub_wide = lax.broadcasted_iota(jnp.int32, (pages, wide.shape[1]), 0)
    in_page = one_hot(sub_wide == page[0:1])
    owner = jnp.sum(in_page * owner_col[:, 0:1], axis=0, keepdims=True)
    rank = jnp.sum(in_page * rank_col, axis=0, keepdims=True)
    return owner_row[0:1], local_row, rank_col, owner, rank, second, offset, valid


def index_kernel(hold, page_len, first, own, table_ref, sel_ref, out_ref, *rest):
    first_refs, wide = rest[:-1], rest[-1]
    holders = out_ref.shape[0]
    pages = table_ref.shape[1]
    f32 = jnp.float32
    bf16 = jnp.bfloat16
    owner_row, local_row, rank_col, owner, rank, second, offset, valid = pair_places(
        hold, page_len, table_ref, sel_ref, wide
    )
    holder = lax.broadcasted_iota(jnp.int32, (holders, pages), 0).astype(f32)
    owned = jnp.where(holder == owner_row, local_row, 0.0)
    lane = lax.broadcasted_iota(jnp.int32, (pages, LANES), 1).astype(f32)
    numbers = jnp.dot(
        owned.astype(bf16), one_hot(lane == rank_col).astype(bf16), preferred_element_type=f32
    )
    holder_wide = lax.broadcasted_iota(jnp.int32, (holders, wide.shape[1]), 0).astype(f32)
    marked = jnp.where((holder_wide == owner) & valid, rank * page_len + offset + 1.0, 0.0)
    place_lane = lax.broadcasted_iota(jnp.int32, (LANES, wide.shape[1]), 0).astype(f32)
    at_place = one_hot(place_lane == SELP * rank + second)
    targets = nt_dot(marked.astype(bf16), at_place.astype(bf16))
    for h in range(holders):
        out_ref[h, 0:1, :] = numbers[h : h + 1, :].astype(jnp.int32)
        out_ref[h, 1:2, :] = targets[h : h + 1, :].astype(jnp.int32)
    for d, ref in zip(first, first_refs):
        ref[0] = out_ref[own[0] ^ d]


def rows_kernel(hold, page_len, table_ref, sel_ref, fresh_ref, packed, wide):
    holders = packed.shape[0]
    picked = sel_ref.shape[1]
    f32 = jnp.float32
    _, _, _, owner, rank, second, _, valid = pair_places(hold, page_len, table_ref, sel_ref, wide)
    spot = jnp.where(valid, owner * ROW_SLOTS + SELP * rank + second, -1.0)[:, 0:picked]
    step = min(holders, 16)
    for start in range(0, holders, step):
        spot_id = lax.broadcasted_iota(jnp.int32, (step * ROW_SLOTS, picked), 0).astype(f32)
        choose = one_hot(spot_id + float(start * ROW_SLOTS) == spot).astype(jnp.bfloat16)
        rows = jnp.dot(choose, fresh_ref[...], preferred_element_type=f32).astype(jnp.bfloat16)
        packed[start : start + step] = rows.reshape(step, ROW_SLOTS, fresh_ref.shape[1])


def first_gather_kernel(count, *refs):
    lists, store_hbm, sends = refs[:count], refs[count], refs[count + 1 : 2 * count + 1]
    held, load_sem, send_sem = refs[2 * count + 1 :]
    capacity = held.shape[1]
    for i, numbers in enumerate(lists):
        for k in range(capacity):
            pltpu.make_async_copy(store_hbm.at[numbers[0, 0, k]], held.at[i, k], load_sem).start()
    pltpu.make_async_copy(held, held, load_sem).wait()
    for i, send in enumerate(sends):
        pltpu.make_async_copy(held.at[i], send, send_sem).start()
    pltpu.make_async_copy(held, held, send_sem).wait()


def gather_kernel(capacity, distances, own, index, store_hbm, *rest):
    sends, (store, load_sem, send_sem) = rest[:-3], rest[-3:]
    load = pltpu.make_async_copy(store_hbm, store, load_sem)
    load.start()
    load.wait()
    for i in range(len(distances) if distances else index.shape[0]):
        r = own[0] ^ distances[i] if distances else i
        send = sends[i] if distances else sends[0].at[i]
        for k in range(capacity):
            pltpu.make_async_copy(store.at[index[r, 0, k]], send.at[k], send_sem).start()
    for send in sends:
        pltpu.make_async_copy(send, send, send_sem).wait()


def write_back_kernel(index, targets_ref, store_hbm, rows_hbm, store_out, *scratch):
    store, rows, blended, load_sem, rows_sem, out_sem = scratch
    holders, capacity, page_len, width = blended.shape
    rows_here = capacity * page_len
    f32 = jnp.float32
    load = pltpu.make_async_copy(store_hbm, store, load_sem)
    load_rows = pltpu.make_async_copy(rows_hbm, rows, rows_sem)
    load.start()
    load_rows.start()
    load_rows.wait()
    load.wait()
    row_id = lax.broadcasted_iota(jnp.int32, (rows_here, ROW_SLOTS), 0)

    def one_request(r, carry):
        hit = one_hot(row_id == targets_ref[r][1:2, 0:ROW_SLOTS] - 1)
        keep = 1.0 - jnp.sum(hit, axis=1, keepdims=True)
        keep = jnp.broadcast_to(keep, (rows_here, LANES)).astype(jnp.bfloat16)
        hit = hit.astype(jnp.bfloat16)
        for c in range(width // LANES):
            lanes = slice(c * LANES, (c + 1) * LANES)
            fresh = jnp.dot(hit, rows[r, :, lanes], preferred_element_type=f32).astype(jnp.bfloat16)
            for k in range(capacity):
                part = slice(k * page_len, (k + 1) * page_len)
                blended[r, k, :, lanes] = store[index[r, 0, k], :, lanes] * keep[part] + fresh[part]
        for k in range(capacity):
            pltpu.make_async_copy(blended.at[r, k], store_out.at[index[r, 0, k]], out_sem).start()
        return carry

    lax.fori_loop(0, holders, one_request, 0)
    pltpu.make_async_copy(store_out, store_out, out_sem).wait()


def attend_kernel(first, last, sources, place, page_number, tiles, *rest):
    sel_ref, positions_ref, query_ref, *rest = rest
    if first:
        fresh_ref, fresh_positions, *rest = rest
    state_in = () if first else rest[:2]
    rest = rest if first else rest[2:]
    contexts, rest = rest[:sources], rest[sources:]
    outs, rest = (rest[:1], rest[1:]) if last else (rest[:2], rest[2:])
    kv, values, position, query, mixed, stats, sem = rest
    pages, page_len, width = kv.shape
    each = contexts[0].shape[0]
    ahead = TILE_PAGES if first else 0
    block = query_ref.shape[0]
    tile = TILE_PAGES * page_len
    lanes = QUERY_GROUP * block
    scale = 1.4426950408889634 / HEAD_WIDTH**0.5
    f32 = jnp.float32
    bf16 = jnp.bfloat16
    step = pl.program_id(0)
    eye = one_hot(
        lax.broadcasted_iota(jnp.int32, (LANES, LANES), 0)
        == lax.broadcasted_iota(jnp.int32, (LANES, LANES), 1)
    ).astype(bf16)

    @pl.when(step == 0)
    def _():
        for i, context in enumerate(contexts):
            for k in range(each):
                pltpu.make_async_copy(context.at[k], kv.at[ahead + place[i * each + k]], sem).start()
        if first:
            picked = fresh_ref.shape[0]
            count = picked // page_len
            kv[0:count] = fresh_ref[...].reshape(count, page_len, width)
            kv[count:ahead] = jnp.zeros((ahead - count, page_len, width), bf16)
            position[0:picked, :] = fresh_positions[...]
            position[picked:tile, :] = jnp.full((tile - picked, LANES), FAR_POSITION, jnp.int32)
        positions = positions_ref[...]
        row = lax.broadcasted_iota(jnp.int32, (page_len, positions.shape[1]), 0)
        ones = jnp.ones((positions.shape[1], LANES), bf16)
        row_lanes = lax.broadcasted_iota(jnp.int32, (page_len, LANES), 0)

        def place_rows(t, carry):
            starts = [page_number[t * TILE_PAGES + k] * page_len for k in range(TILE_PAGES)]
            hit = jnp.concatenate([one_hot(row + start == positions) for start in starts], axis=0)
            hidden = jnp.dot(hit.astype(bf16), ones, preferred_element_type=f32)
            plain = jnp.concatenate([row_lanes + start for start in starts], axis=0)
            here = pl.ds(pl.multiple_of(ahead * page_len + t * tile, tile), tile)
            position[here, :] = jnp.where(hidden > 0.0, FAR_POSITION, plain)
            return carry

        lax.fori_loop(0, (pages - ahead) // TILE_PAGES, place_rows, 0)
        used = kv.at[ahead:]
        pltpu.make_async_copy(used, used, sem).wait()

        def turn(t, carry):
            here = pl.ds(t * TILE_PAGES, TILE_PAGES)
            for g in range(KEY_VALUE_HEADS):
                at = (KEY_VALUE_HEADS + g) * LANES
                value = kv[here, :, at : at + LANES].reshape(tile, LANES)
                values[t, g] = nt_dot(eye, value).astype(bf16)
            return carry

        lax.fori_loop(0, pages // TILE_PAGES, turn, 0)

    for g in range(KEY_VALUE_HEADS):
        heads = [
            query_ref[:, (g * QUERY_GROUP + i) * LANES : (g * QUERY_GROUP + i + 1) * LANES]
            for i in range(QUERY_GROUP)
        ]
        query[g] = nt_dot(eye, jnp.concatenate(heads, axis=0)).astype(bf16)
    if first:
        mixed[...] = jnp.zeros(mixed.shape, f32)
        stats[0:KEY_VALUE_HEADS, :] = jnp.full((KEY_VALUE_HEADS, lanes), HIDDEN, f32)
        stats[KEY_VALUE_HEADS:, :] = jnp.zeros((KEY_VALUE_HEADS, lanes), f32)
    else:
        mixed[...] = state_in[0][0]
        stats[...] = state_in[1][0]

    sel = sel_ref[0]

    def one_tile(t, carry):
        here = pl.ds(t * TILE_PAGES, TILE_PAGES)
        bias = jnp.where(
            position[pl.ds(pl.multiple_of(t * tile, tile), tile), :] <= sel, 0.0, HIDDEN
        ).astype(f32)

        def score(g):
            key = kv[here, :, g * LANES : (g + 1) * LANES].reshape(tile, LANES)
            return jnp.dot(key, query[g], preferred_element_type=f32)

        upcoming = score(0)
        for g in range(KEY_VALUE_HEADS):
            scores = upcoming
            if g + 1 < KEY_VALUE_HEADS:
                upcoming = score(g + 1)
            raised, shrinks = [], []
            at = KEY_VALUE_HEADS + g
            for n in range(lanes // LANES):
                part = slice(n * LANES, (n + 1) * LANES)
                s = scores[:, part] + bias
                old = stats[g : g + 1, part]
                new = jnp.maximum(old, jnp.max(s, axis=0, keepdims=True))
                p = jnp.exp2((s - new) * scale)
                shrink = jnp.exp2((old - new) * scale)
                stats[at : at + 1, part] = stats[at : at + 1, part] * shrink + jnp.sum(
                    p, axis=0, keepdims=True
                )
                stats[g : g + 1, part] = new
                raised.append(p.astype(bf16))
                shrinks.append(shrink)
            raised = jnp.concatenate(raised, axis=1)
            shrink = jnp.concatenate(shrinks, axis=1)
            mixed[g] = mixed[g] * shrink + jnp.dot(
                values[t, g], raised, preferred_element_type=f32
            )
        return carry

    lax.fori_loop(0, tiles[step], one_tile, 0)

    if last:
        done = []
        for g in range(KEY_VALUE_HEADS):
            at = KEY_VALUE_HEADS + g
            part = (mixed[g] * (1.0 / stats[at : at + 1, :])).astype(bf16)
            done += [part[:, n * LANES : (n + 1) * LANES] for n in range(lanes // LANES)]
        turned = nt_dot(eye, jnp.concatenate(done, axis=0)).astype(bf16)
        for n in range(len(done)):
            for i in range(LANES // block):
                head = n * (LANES // block) + i
                outs[0][:, head * LANES : (head + 1) * LANES] = turned[
                    i * block : (i + 1) * block, n * LANES : (n + 1) * LANES
                ]
    else:
        outs[0][0] = mixed[...]
        outs[1][0] = stats[...]


def attend(first, last, order, sel_lanes, positions, queries, fresh, state, contexts):
    picked, features = queries.shape
    each, page_len, width = contexts[0].shape
    pages = each * len(contexts) + (TILE_PAGES if first else 0)
    steps = picked // QUERY_BLOCK
    lanes = QUERY_GROUP * QUERY_BLOCK
    wide = pl.BlockSpec((QUERY_BLOCK, features), lambda b, *_: (b, 0))
    state_specs = [
        pl.BlockSpec((1, KEY_VALUE_HEADS, LANES, lanes), lambda b, *_: (b, 0, 0, 0)),
        pl.BlockSpec((1, 2 * KEY_VALUE_HEADS, lanes), lambda b, *_: (b, 0, 0)),
    ]
    state_shapes = [
        jax.ShapeDtypeStruct((steps, KEY_VALUE_HEADS, LANES, lanes), jnp.float32),
        jax.ShapeDtypeStruct((steps, 2 * KEY_VALUE_HEADS, lanes), jnp.float32),
    ]
    share = 0.6
    return pl.pallas_call(
        functools.partial(attend_kernel, first, last, len(contexts)),
        grid_spec=pltpu.PrefetchScalarGridSpec(
            num_scalar_prefetch=3,
            grid=(steps,),
            in_specs=[
                pl.BlockSpec((1, 1, LANES), lambda b, *_: (b, 0, 0)),
                pl.BlockSpec(positions.shape, lambda b, *_: (0, 0)),
                wide,
                *[pl.BlockSpec(x.shape, lambda b, *_: (0, 0)) for x in fresh if first],
                *([] if first else state_specs),
                *[pl.BlockSpec(memory_space=pltpu.HBM)] * len(contexts),
            ],
            out_specs=[wide] if last else state_specs,
            scratch_shapes=[
                pltpu.VMEM((pages, page_len, width), jnp.bfloat16),
                pltpu.VMEM(
                    (pages // TILE_PAGES, KEY_VALUE_HEADS, LANES, TILE_PAGES * page_len), jnp.bfloat16
                ),
                pltpu.VMEM((pages * page_len, LANES), jnp.int32),
                pltpu.VMEM((KEY_VALUE_HEADS, LANES, lanes), jnp.bfloat16),
                pltpu.VMEM((KEY_VALUE_HEADS, LANES, lanes), jnp.float32),
                pltpu.VMEM((2 * KEY_VALUE_HEADS, lanes), jnp.float32),
                pltpu.SemaphoreType.DMA,
            ],
        ),
        out_shape=[jax.ShapeDtypeStruct((picked, features), jnp.bfloat16)] if last else state_shapes,
        compiler_params=pltpu.CompilerParams(
            dimension_semantics=("arbitrary",), vmem_limit_bytes=VMEM_LIMIT
        ),
        cost_estimate=pl.CostEstimate(
            flops=int(share * 8 * picked * features * pages * page_len),
            bytes_accessed=2 * pages * page_len * width + 6 * picked * features,
            transcendentals=int(share * picked * features // LANES * pages * page_len),
        ),
    )(*order, sel_lanes, positions, queries, *[x for x in fresh if first], *state, *contexts)


def page_order(slots, positions, own, hold, capacity, groups, page_len):
    pages = slots.shape[0]
    number = jnp.arange(pages)
    before = number[None, :] < number[:, None]
    owners = slots // hold
    ranks = jnp.sum(((owners[None, :] == owners[:, None]) & before).astype(jnp.int32), axis=1)
    distance = owners ^ own
    last_page = positions.reshape(-1, QUERY_BLOCK)[:, -1] // page_len
    orders = []
    for at, group in enumerate(groups):
        if group is None:
            arrival = owners * capacity + ranks
            count = pages
        else:
            arrival = jnp.full((pages,), -1, jnp.int32)
            for i, d in enumerate(group):
                arrival = jnp.where(distance == d, i * capacity + ranks, arrival)
            count = len(group) * capacity
        member = arrival >= 0
        place = jnp.sum((member[None, :] & before).astype(jnp.int32), axis=1)
        index = jnp.arange(count)[:, None]
        places = jnp.sum(jnp.where(arrival[None, :] == index, place[None, :], 0), axis=1)
        page = jnp.sum(
            jnp.where(member[None, :] & (place[None, :] == index), number[None, :], 0), axis=1
        )
        seen = jnp.sum((page[None, :] <= last_page[:, None]).astype(jnp.int32), axis=1)
        orders.append((places, page, (seen + TILE_PAGES - 1) // TILE_PAGES + (at == 0)))
    return orders


def per_device(store, page_table, sel_pos, fresh_kv, queries):
    holders = lax.axis_size("store")
    hold, page_len, width = store.shape
    pages = page_table.shape[1]
    picked = sel_pos.shape[1]
    capacity = max(1, pages // holders)
    hbm = pl.BlockSpec(memory_space=pltpu.HBM)
    vmem = pl.BlockSpec(memory_space=pltpu.VMEM)
    dma = pltpu.SemaphoreType.DMA
    params = pltpu.CompilerParams(vmem_limit_bytes=VMEM_LIMIT)
    own = lax.axis_index("store")
    own_word = own.reshape(1).astype(jnp.int32)
    fresh = fresh_kv[0]
    wide = pltpu.VMEM((8, -(-picked // LANES) * LANES), jnp.int32)
    if holders == 16:
        first = (8, 12)
        groups = [(0, 8, 12, 4, 5, 1), (9, 13, 6, 10, 7, 2, 14, 3), (11, 15)]
        others = (0, 9, 4, 13, 5, 1, 6, 10, 7, 2, 14, 3, 11, 15)
    else:
        first = ()
        groups = [None]
        others = None

    def swap(x, d):
        return lax.ppermute(x, "store", [(h, h ^ d) for h in range(holders)])

    def exchange(x):
        return lax.all_to_all(x, "store", split_axis=0, concat_axis=0, tiled=True)

    index, *lists = pl.pallas_call(
        functools.partial(index_kernel, hold, page_len, first),
        grid_spec=pltpu.PrefetchScalarGridSpec(
            num_scalar_prefetch=1,
            grid=(1,),
            in_specs=[vmem, vmem],
            out_specs=[vmem] * (1 + len(first)),
            scratch_shapes=[wide],
        ),
        out_shape=[
            jax.ShapeDtypeStruct((holders, 2, LANES), jnp.int32),
            *[jax.ShapeDtypeStruct((1, 2, LANES), jnp.int32)] * len(first),
        ],
        compiler_params=params,
    )(own_word, page_table, sel_pos)
    arrived = {}
    if first:
        lists = [swap(x, d) for x, d in zip(lists, first)]
        parts = pl.pallas_call(
            functools.partial(first_gather_kernel, len(first)),
            grid_spec=pltpu.PrefetchScalarGridSpec(
                num_scalar_prefetch=len(first),
                grid=(1,),
                in_specs=[hbm],
                out_specs=[hbm] * len(first),
                scratch_shapes=[
                    pltpu.VMEM((len(first), capacity, page_len, width), store.dtype),
                    dma,
                    dma,
                ],
            ),
            out_shape=[jax.ShapeDtypeStruct((capacity, page_len, width), store.dtype)] * len(first),
            compiler_params=params,
        )(*lists, store)
        parts, table, positions = lax.optimization_barrier((parts, page_table, sel_pos))
        arrived = {d: swap(part, d) for d, part in zip(first, parts)}
        lists = lax.all_gather(index, "store", axis=0)
        index_in = lax.dynamic_index_in_dim(lists, own, axis=1, keepdims=False)
        index_in, _ = lax.optimization_barrier((index_in, arrived[first[0]]))
    else:
        table, positions = page_table, sel_pos
        index_in = exchange(index)

    packed = pl.pallas_call(
        functools.partial(rows_kernel, hold, page_len),
        out_shape=jax.ShapeDtypeStruct((holders, ROW_SLOTS, width), store.dtype),
        scratch_shapes=[wide],
        compiler_params=params,
    )(table, positions, fresh)
    rows_in = exchange(packed)

    each = jax.ShapeDtypeStruct((capacity, page_len, width), store.dtype)
    whole = jax.ShapeDtypeStruct((holders, capacity, page_len, width), store.dtype)
    parts = pl.pallas_call(
        functools.partial(gather_kernel, capacity, others),
        grid_spec=pltpu.PrefetchScalarGridSpec(
            num_scalar_prefetch=2,
            grid=(1,),
            in_specs=[hbm],
            out_specs=[hbm] * (len(others) if others else 1),
            scratch_shapes=[pltpu.VMEM(store.shape, store.dtype), dma, dma],
        ),
        out_shape=[each] * len(others) if others else [whole],
        compiler_params=params,
    )(own_word, index_in, store)
    parts, table, positions = lax.optimization_barrier((parts, table, positions))
    if others:
        for d, part in zip(others, parts):
            arrived[d] = swap(part, d) if d else part
        contexts = [[arrived[d] for d in group] for group in groups]
    else:
        contexts = [[exchange(parts[0]).reshape(pages, page_len, width)]]

    store_out = pl.pallas_call(
        write_back_kernel,
        grid_spec=pltpu.PrefetchScalarGridSpec(
            num_scalar_prefetch=1,
            grid=(1,),
            in_specs=[vmem, hbm, hbm],
            out_specs=hbm,
            scratch_shapes=[
                pltpu.VMEM(store.shape, store.dtype),
                pltpu.VMEM((holders, ROW_SLOTS, width), store.dtype),
                pltpu.VMEM((holders, capacity, page_len, width), store.dtype),
                dma,
                dma,
                dma,
            ],
        ),
        out_shape=jax.ShapeDtypeStruct(store.shape, store.dtype),
        compiler_params=params,
        cost_estimate=pl.CostEstimate(flops=0, bytes_accessed=4 * store.size, transcendentals=0),
    )(index_in, index_in, store, rows_in)

    orders = page_order(table[0], positions[0], own, hold, capacity, groups, page_len)
    sel_lanes = jnp.tile(positions.reshape(-1, 1, QUERY_BLOCK), (1, 1, LANES // QUERY_BLOCK))
    sel_rows = jnp.broadcast_to(positions.reshape(picked, 1), (picked, LANES))
    store_out, sel_lanes = lax.optimization_barrier((store_out, sel_lanes))
    state = ()
    for at, (arrays, order) in enumerate(zip(contexts, orders)):
        state = attend(
            at == 0,
            at == len(groups) - 1,
            order,
            sel_lanes,
            positions,
            queries[0],
            (fresh, sel_rows),
            state,
            arrays,
        )
    return (state[0][None], store_out)


def solution(mesh):
    return jax.shard_map(
        per_device,
        mesh=mesh,
        in_specs=(
            P(("groups", "store"), None, None),
            P(("groups", "store"), None),
            P(("groups", "store"), None),
            P(("groups", "store"), None, None),
            P(("groups", "store"), None, None),
        ),
        out_specs=(P(("groups", "store"), None, None), P(("groups", "store"), None, None)),
        check_vma=False,
    )
```

```python
import functools

import jax
import jax.numpy as jnp
from jax import lax
from jax.experimental import pallas as pl
from jax.experimental.pallas import tpu as pltpu
from jax.sharding import PartitionSpec as P

HEAD_WIDTH = 128
KEY_VALUE_HEADS = 4
QUERY_GROUP = 12
SELP = 2
LANES = 128
ROW_SLOTS = 16
VMEM_LIMIT = 60 * 1024 * 1024
QUERY_BLOCK = 32
TILE_PAGES = 16
HIDDEN = -1e30
FAR_POSITION = 1 << 24


def nt_dot(a, b):
    return lax.dot_general(a, b, (((1,), (1,)), ((), ())), preferred_element_type=jnp.float32)


def one_hot(condition):
    return jnp.where(condition, 1.0, 0.0)


def over_rows(reduce, x):
    blocks = reduce(x.reshape(x.shape[0] // 8, 8, x.shape[1]), axis=0)
    return reduce(blocks, axis=0, keepdims=True)


def pair_places(hold, page_len, table_ref, sel_ref, wide):
    pages = table_ref.shape[1]
    picked = sel_ref.shape[1]
    f32 = jnp.float32
    slots = jnp.broadcast_to(table_ref[...], (pages, pages))
    owners = slots // hold
    local_row = (slots - owners * hold).astype(f32)[0:1]
    owner_row = owners.astype(f32)
    owner_col = owner_row.T
    sub = lax.broadcasted_iota(jnp.int32, (pages, pages), 0)
    lane = lax.broadcasted_iota(jnp.int32, (pages, pages), 1)
    earlier = one_hot((owner_row == owner_col) & (lane < sub))
    rank_col = jnp.sum(earlier, axis=1, keepdims=True)

    wide[...] = jnp.full(wide.shape, -1, jnp.int32)
    wide[0:1, 0:picked] = sel_ref[...]
    position = wide[...]
    page = lax.shift_right_arithmetic(position, page_len.bit_length() - 1)
    offset = (position & (page_len - 1)).astype(f32)[0:1]
    lane_wide = lax.broadcasted_iota(jnp.int32, wide.shape, 1)
    second = one_hot((page == pltpu.roll(page, 1, axis=1)) & (lane_wide > 0))[0:1]
    valid = lane_wide[0:1] < picked
    sub_wide = lax.broadcasted_iota(jnp.int32, (pages, wide.shape[1]), 0)
    in_page = one_hot(sub_wide == page[0:1])
    owner = jnp.sum(in_page * owner_col[:, 0:1], axis=0, keepdims=True)
    rank = jnp.sum(in_page * rank_col, axis=0, keepdims=True)
    return owner_row[0:1], local_row, rank_col, owner, rank, second, offset, valid


def index_kernel(hold, page_len, first, own, table_ref, sel_ref, out_ref, *rest):
    first_refs, wide = rest[:-1], rest[-1]
    holders = out_ref.shape[0]
    pages = table_ref.shape[1]
    f32 = jnp.float32
    bf16 = jnp.bfloat16
    owner_row, local_row, rank_col, owner, rank, second, offset, valid = pair_places(
        hold, page_len, table_ref, sel_ref, wide
    )
    holder = lax.broadcasted_iota(jnp.int32, (holders, pages), 0).astype(f32)
    owned = jnp.where(holder == owner_row, local_row, 0.0)
    lane = lax.broadcasted_iota(jnp.int32, (pages, LANES), 1).astype(f32)
    numbers = jnp.dot(
        owned.astype(bf16), one_hot(lane == rank_col).astype(bf16), preferred_element_type=f32
    )
    holder_wide = lax.broadcasted_iota(jnp.int32, (holders, wide.shape[1]), 0).astype(f32)
    marked = jnp.where((holder_wide == owner) & valid, rank * page_len + offset + 1.0, 0.0)
    place_lane = lax.broadcasted_iota(jnp.int32, (LANES, wide.shape[1]), 0).astype(f32)
    at_place = one_hot(place_lane == SELP * rank + second)
    targets = nt_dot(marked.astype(bf16), at_place.astype(bf16))
    for h in range(holders):
        out_ref[h, 0:1, :] = numbers[h : h + 1, :].astype(jnp.int32)
        out_ref[h, 1:2, :] = targets[h : h + 1, :].astype(jnp.int32)
    for d, ref in zip(first, first_refs):
        ref[0] = out_ref[own[0] ^ d]


def rows_kernel(hold, page_len, table_ref, sel_ref, fresh_ref, packed, wide):
    holders = packed.shape[0]
    picked = sel_ref.shape[1]
    f32 = jnp.float32
    _, _, _, owner, rank, second, _, valid = pair_places(hold, page_len, table_ref, sel_ref, wide)
    spot = jnp.where(valid, owner * ROW_SLOTS + SELP * rank + second, -1.0)[:, 0:picked]
    step = min(holders, 16)
    for start in range(0, holders, step):
        spot_id = lax.broadcasted_iota(jnp.int32, (step * ROW_SLOTS, picked), 0).astype(f32)
        choose = one_hot(spot_id + float(start * ROW_SLOTS) == spot).astype(jnp.bfloat16)
        rows = jnp.dot(choose, fresh_ref[...], preferred_element_type=f32).astype(jnp.bfloat16)
        packed[start : start + step] = rows.reshape(step, ROW_SLOTS, fresh_ref.shape[1])


def first_gather_kernel(count, *refs):
    lists, store_hbm, sends = refs[:count], refs[count], refs[count + 1 : 2 * count + 1]
    held, load_sem, send_sem = refs[2 * count + 1 :]
    capacity = held.shape[1]
    for i, numbers in enumerate(lists):
        for k in range(capacity):
            pltpu.make_async_copy(store_hbm.at[numbers[0, 0, k]], held.at[i, k], load_sem).start()
    pltpu.make_async_copy(held, held, load_sem).wait()
    for i, send in enumerate(sends):
        pltpu.make_async_copy(held.at[i], send, send_sem).start()
    pltpu.make_async_copy(held, held, send_sem).wait()


def gather_kernel(capacity, distances, own, index, store_hbm, *rest):
    sends, (store, load_sem, send_sem) = rest[:-3], rest[-3:]
    load = pltpu.make_async_copy(store_hbm, store, load_sem)
    load.start()
    load.wait()
    for i in range(len(distances) if distances else index.shape[0]):
        r = own[0] ^ distances[i] if distances else i
        send = sends[i] if distances else sends[0].at[i]
        for k in range(capacity):
            pltpu.make_async_copy(store.at[index[r, 0, k]], send.at[k], send_sem).start()
    for send in sends:
        pltpu.make_async_copy(send, send, send_sem).wait()


def write_back_kernel(index, targets_ref, store_hbm, rows_hbm, store_out, *scratch):
    store, rows, blended, load_sem, rows_sem, out_sem = scratch
    holders, capacity, page_len, width = blended.shape
    rows_here = capacity * page_len
    f32 = jnp.float32
    load = pltpu.make_async_copy(store_hbm, store, load_sem)
    load_rows = pltpu.make_async_copy(rows_hbm, rows, rows_sem)
    load.start()
    load_rows.start()
    load_rows.wait()
    load.wait()
    row_id = lax.broadcasted_iota(jnp.int32, (rows_here, ROW_SLOTS), 0)

    def one_request(r, carry):
        hit = one_hot(row_id == targets_ref[r][1:2, 0:ROW_SLOTS] - 1)
        keep = 1.0 - jnp.sum(hit, axis=1, keepdims=True)
        keep = jnp.broadcast_to(keep, (rows_here, LANES)).astype(jnp.bfloat16)
        hit = hit.astype(jnp.bfloat16)
        for c in range(width // LANES):
            lanes = slice(c * LANES, (c + 1) * LANES)
            fresh = jnp.dot(hit, rows[r, :, lanes], preferred_element_type=f32).astype(jnp.bfloat16)
            for k in range(capacity):
                part = slice(k * page_len, (k + 1) * page_len)
                blended[r, k, :, lanes] = store[index[r, 0, k], :, lanes] * keep[part] + fresh[part]
        for k in range(capacity):
            pltpu.make_async_copy(blended.at[r, k], store_out.at[index[r, 0, k]], out_sem).start()
        return carry

    lax.fori_loop(0, holders, one_request, 0)
    pltpu.make_async_copy(store_out, store_out, out_sem).wait()


def attend_kernel(first, last, sources, place, page_number, tiles, *rest):
    sel_ref, positions_ref, query_ref, *rest = rest
    if first:
        fresh_ref, fresh_positions, *rest = rest
    state_in = () if first else rest[:2]
    rest = rest if first else rest[2:]
    contexts, rest = rest[:sources], rest[sources:]
    outs, rest = (rest[:1], rest[1:]) if last else (rest[:2], rest[2:])
    kv, values, position, query, mixed, stats, sem = rest
    pages, page_len, width = kv.shape
    each = contexts[0].shape[0]
    ahead = TILE_PAGES if first else 0
    block = query_ref.shape[0]
    tile = TILE_PAGES * page_len
    lanes = QUERY_GROUP * block
    scale = 1.4426950408889634 / HEAD_WIDTH**0.5
    f32 = jnp.float32
    bf16 = jnp.bfloat16
    step = pl.program_id(0)
    eye = one_hot(
        lax.broadcasted_iota(jnp.int32, (LANES, LANES), 0)
        == lax.broadcasted_iota(jnp.int32, (LANES, LANES), 1)
    ).astype(bf16)

    @pl.when(step == 0)
    def _():
        for i, context in enumerate(contexts):
            for k in range(each):
                pltpu.make_async_copy(context.at[k], kv.at[ahead + place[i * each + k]], sem).start()
        if first:
            picked = fresh_ref.shape[0]
            count = picked // page_len
            kv[0:count] = fresh_ref[...].reshape(count, page_len, width)
            kv[count:ahead] = jnp.zeros((ahead - count, page_len, width), bf16)
            position[0:picked, :] = fresh_positions[...]
            position[picked:tile, :] = jnp.full((tile - picked, LANES), FAR_POSITION, jnp.int32)
        positions = positions_ref[...]
        row = lax.broadcasted_iota(jnp.int32, (page_len, positions.shape[1]), 0)
        ones = jnp.ones((positions.shape[1], LANES), bf16)
        row_lanes = lax.broadcasted_iota(jnp.int32, (page_len, LANES), 0)

        def place_rows(t, carry):
            starts = [page_number[t * TILE_PAGES + k] * page_len for k in range(TILE_PAGES)]
            hit = jnp.concatenate([one_hot(row + start == positions) for start in starts], axis=0)
            hidden = jnp.dot(hit.astype(bf16), ones, preferred_element_type=f32)
            plain = jnp.concatenate([row_lanes + start for start in starts], axis=0)
            here = pl.ds(pl.multiple_of(ahead * page_len + t * tile, tile), tile)
            position[here, :] = jnp.where(hidden > 0.0, FAR_POSITION, plain)
            return carry

        lax.fori_loop(0, (pages - ahead) // TILE_PAGES, place_rows, 0)
        used = kv.at[ahead:]
        pltpu.make_async_copy(used, used, sem).wait()

        def turn(t, carry):
            here = pl.ds(t * TILE_PAGES, TILE_PAGES)
            for g in range(KEY_VALUE_HEADS):
                at = (KEY_VALUE_HEADS + g) * LANES
                value = kv[here, :, at : at + LANES].reshape(tile, LANES)
                values[t, g] = nt_dot(eye, value).astype(bf16)
            return carry

        lax.fori_loop(0, pages // TILE_PAGES, turn, 0)

    for g in range(KEY_VALUE_HEADS):
        for i in range(QUERY_GROUP):
            head = g * QUERY_GROUP + i
            query[g, i * block : (i + 1) * block, :] = query_ref[:, head * LANES : (head + 1) * LANES]
    if first:
        mixed[...] = jnp.zeros(mixed.shape, f32)
        stats[0:KEY_VALUE_HEADS, :] = jnp.full((KEY_VALUE_HEADS, lanes), HIDDEN, f32)
        stats[KEY_VALUE_HEADS:, :] = jnp.zeros((KEY_VALUE_HEADS, lanes), f32)
    else:
        mixed[...] = state_in[0][0]
        stats[...] = state_in[1][0]

    sel = sel_ref[0]

    def one_tile(t, carry):
        here = pl.ds(t * TILE_PAGES, TILE_PAGES)
        bias = jnp.where(
            position[pl.ds(pl.multiple_of(t * tile, tile), tile), :] <= sel, 0.0, HIDDEN
        ).astype(f32)

        def score(g):
            key = kv[here, :, g * LANES : (g + 1) * LANES].reshape(tile, LANES)
            return nt_dot(key, query[g])

        upcoming = score(0)
        for g in range(KEY_VALUE_HEADS):
            scores = upcoming
            if g + 1 < KEY_VALUE_HEADS:
                upcoming = score(g + 1)
            raised, shrinks = [], []
            at = KEY_VALUE_HEADS + g
            for n in range(lanes // LANES):
                part = slice(n * LANES, (n + 1) * LANES)
                s = scores[:, part] + bias
                old = stats[g : g + 1, part]
                new = jnp.maximum(old, over_rows(jnp.max, s))
                p = jnp.exp2((s - new) * scale)
                shrink = jnp.exp2((old - new) * scale)
                stats[at : at + 1, part] = stats[at : at + 1, part] * shrink + over_rows(jnp.sum, p)
                stats[g : g + 1, part] = new
                raised.append(p.astype(bf16))
                shrinks.append(shrink)
            raised = jnp.concatenate(raised, axis=1)
            shrink = jnp.concatenate(shrinks, axis=1)
            mixed[g] = mixed[g] * shrink + jnp.dot(
                values[t, g], raised, preferred_element_type=f32
            )
        return carry

    lax.fori_loop(0, tiles[step], one_tile, 0)

    if last:
        done = []
        for g in range(KEY_VALUE_HEADS):
            at = KEY_VALUE_HEADS + g
            part = (mixed[g] * (1.0 / stats[at : at + 1, :])).astype(bf16)
            done += [part[:, n * LANES : (n + 1) * LANES] for n in range(lanes // LANES)]
        turned = nt_dot(eye, jnp.concatenate(done, axis=0)).astype(bf16)
        for n in range(len(done)):
            for i in range(LANES // block):
                head = n * (LANES // block) + i
                outs[0][:, head * LANES : (head + 1) * LANES] = turned[
                    i * block : (i + 1) * block, n * LANES : (n + 1) * LANES
                ]
    else:
        outs[0][0] = mixed[...]
        outs[1][0] = stats[...]


def attend(first, last, order, sel_lanes, positions, queries, fresh, state, contexts):
    picked, features = queries.shape
    each, page_len, width = contexts[0].shape
    pages = each * len(contexts) + (TILE_PAGES if first else 0)
    steps = picked // QUERY_BLOCK
    lanes = QUERY_GROUP * QUERY_BLOCK
    wide = pl.BlockSpec((QUERY_BLOCK, features), lambda b, *_: (b, 0))
    state_specs = [
        pl.BlockSpec((1, KEY_VALUE_HEADS, LANES, lanes), lambda b, *_: (b, 0, 0, 0)),
        pl.BlockSpec((1, 2 * KEY_VALUE_HEADS, lanes), lambda b, *_: (b, 0, 0)),
    ]
    state_shapes = [
        jax.ShapeDtypeStruct((steps, KEY_VALUE_HEADS, LANES, lanes), jnp.float32),
        jax.ShapeDtypeStruct((steps, 2 * KEY_VALUE_HEADS, lanes), jnp.float32),
    ]
    share = 0.6
    return pl.pallas_call(
        functools.partial(attend_kernel, first, last, len(contexts)),
        grid_spec=pltpu.PrefetchScalarGridSpec(
            num_scalar_prefetch=3,
            grid=(steps,),
            in_specs=[
                pl.BlockSpec((1, 1, LANES), lambda b, *_: (b, 0, 0)),
                pl.BlockSpec(positions.shape, lambda b, *_: (0, 0)),
                wide,
                *[pl.BlockSpec(x.shape, lambda b, *_: (0, 0)) for x in fresh if first],
                *([] if first else state_specs),
                *[pl.BlockSpec(memory_space=pltpu.HBM)] * len(contexts),
            ],
            out_specs=[wide] if last else state_specs,
            scratch_shapes=[
                pltpu.VMEM((pages, page_len, width), jnp.bfloat16),
                pltpu.VMEM(
                    (pages // TILE_PAGES, KEY_VALUE_HEADS, LANES, TILE_PAGES * page_len), jnp.bfloat16
                ),
                pltpu.VMEM((pages * page_len, LANES), jnp.int32),
                pltpu.VMEM((KEY_VALUE_HEADS, lanes, LANES), jnp.bfloat16),
                pltpu.VMEM((KEY_VALUE_HEADS, LANES, lanes), jnp.float32),
                pltpu.VMEM((2 * KEY_VALUE_HEADS, lanes), jnp.float32),
                pltpu.SemaphoreType.DMA,
            ],
        ),
        out_shape=[jax.ShapeDtypeStruct((picked, features), jnp.bfloat16)] if last else state_shapes,
        compiler_params=pltpu.CompilerParams(
            dimension_semantics=("arbitrary",), vmem_limit_bytes=VMEM_LIMIT
        ),
        cost_estimate=pl.CostEstimate(
            flops=int(share * 8 * picked * features * pages * page_len),
            bytes_accessed=2 * pages * page_len * width + 6 * picked * features,
            transcendentals=int(share * picked * features // LANES * pages * page_len),
        ),
    )(*order, sel_lanes, positions, queries, *[x for x in fresh if first], *state, *contexts)


def page_order(slots, positions, own, hold, capacity, groups, page_len):
    pages = slots.shape[0]
    number = jnp.arange(pages)
    before = number[None, :] < number[:, None]
    owners = slots // hold
    ranks = jnp.sum(((owners[None, :] == owners[:, None]) & before).astype(jnp.int32), axis=1)
    distance = owners ^ own
    last_page = positions.reshape(-1, QUERY_BLOCK)[:, -1] // page_len
    orders = []
    for at, group in enumerate(groups):
        if group is None:
            arrival = owners * capacity + ranks
            count = pages
        else:
            arrival = jnp.full((pages,), -1, jnp.int32)
            for i, d in enumerate(group):
                arrival = jnp.where(distance == d, i * capacity + ranks, arrival)
            count = len(group) * capacity
        member = arrival >= 0
        place = jnp.sum((member[None, :] & before).astype(jnp.int32), axis=1)
        index = jnp.arange(count)[:, None]
        places = jnp.sum(jnp.where(arrival[None, :] == index, place[None, :], 0), axis=1)
        page = jnp.sum(
            jnp.where(member[None, :] & (place[None, :] == index), number[None, :], 0), axis=1
        )
        seen = jnp.sum((page[None, :] <= last_page[:, None]).astype(jnp.int32), axis=1)
        orders.append((places, page, (seen + TILE_PAGES - 1) // TILE_PAGES + (at == 0)))
    return orders


def per_device(store, page_table, sel_pos, fresh_kv, queries):
    holders = lax.axis_size("store")
    hold, page_len, width = store.shape
    pages = page_table.shape[1]
    picked = sel_pos.shape[1]
    capacity = max(1, pages // holders)
    hbm = pl.BlockSpec(memory_space=pltpu.HBM)
    vmem = pl.BlockSpec(memory_space=pltpu.VMEM)
    dma = pltpu.SemaphoreType.DMA
    params = pltpu.CompilerParams(vmem_limit_bytes=VMEM_LIMIT)
    own = lax.axis_index("store")
    own_word = own.reshape(1).astype(jnp.int32)
    fresh = fresh_kv[0]
    wide = pltpu.VMEM((8, -(-picked // LANES) * LANES), jnp.int32)
    if holders == 16:
        first = (8, 12)
        groups = [(0, 8, 12, 4, 5, 1), (9, 6, 13, 7, 10, 2, 14, 3), (11, 15)]
        others = [d for group in groups for d in group if d not in first]
    else:
        first = ()
        groups = [None]
        others = None

    def swap(x, d):
        return lax.ppermute(x, "store", [(h, h ^ d) for h in range(holders)])

    def exchange(x):
        return lax.all_to_all(x, "store", split_axis=0, concat_axis=0, tiled=True)

    index, *lists = pl.pallas_call(
        functools.partial(index_kernel, hold, page_len, first),
        grid_spec=pltpu.PrefetchScalarGridSpec(
            num_scalar_prefetch=1,
            grid=(1,),
            in_specs=[vmem, vmem],
            out_specs=[vmem] * (1 + len(first)),
            scratch_shapes=[wide],
        ),
        out_shape=[
            jax.ShapeDtypeStruct((holders, 2, LANES), jnp.int32),
            *[jax.ShapeDtypeStruct((1, 2, LANES), jnp.int32)] * len(first),
        ],
        compiler_params=params,
    )(own_word, page_table, sel_pos)
    arrived = {}
    if first:
        lists = [swap(x, d) for x, d in zip(lists, first)]
        parts = pl.pallas_call(
            functools.partial(first_gather_kernel, len(first)),
            grid_spec=pltpu.PrefetchScalarGridSpec(
                num_scalar_prefetch=len(first),
                grid=(1,),
                in_specs=[hbm],
                out_specs=[hbm] * len(first),
                scratch_shapes=[
                    pltpu.VMEM((len(first), capacity, page_len, width), store.dtype),
                    dma,
                    dma,
                ],
            ),
            out_shape=[jax.ShapeDtypeStruct((capacity, page_len, width), store.dtype)] * len(first),
            compiler_params=params,
        )(*lists, store)
        parts, table, positions = lax.optimization_barrier((parts, page_table, sel_pos))
        arrived = {d: swap(part, d) for d, part in zip(first, parts)}
    else:
        table, positions = page_table, sel_pos
    packed = pl.pallas_call(
        functools.partial(rows_kernel, hold, page_len),
        out_shape=jax.ShapeDtypeStruct((holders, ROW_SLOTS, width), store.dtype),
        scratch_shapes=[wide],
        compiler_params=params,
    )(table, positions, fresh)
    if first:
        index, packed = lax.optimization_barrier((index, packed))
        index_in = exchange(index)
        index_in, _ = lax.optimization_barrier((index_in, [arrived[d] for d in first]))
    else:
        index_in = exchange(index)
    rows_in = exchange(packed)

    each = jax.ShapeDtypeStruct((capacity, page_len, width), store.dtype)
    whole = jax.ShapeDtypeStruct((holders, capacity, page_len, width), store.dtype)
    parts = pl.pallas_call(
        functools.partial(gather_kernel, capacity, others),
        grid_spec=pltpu.PrefetchScalarGridSpec(
            num_scalar_prefetch=2,
            grid=(1,),
            in_specs=[hbm],
            out_specs=[hbm] * (len(others) if others else 1),
            scratch_shapes=[pltpu.VMEM(store.shape, store.dtype), dma, dma],
        ),
        out_shape=[each] * len(others) if others else [whole],
        compiler_params=params,
    )(own_word, index_in, store)
    parts, table, positions = lax.optimization_barrier((parts, table, positions))
    if others:
        for d, part in zip(others, parts):
            arrived[d] = swap(part, d) if d else part
        contexts = [[arrived[d] for d in group] for group in groups]
    else:
        contexts = [[exchange(parts[0]).reshape(pages, page_len, width)]]

    store_out = pl.pallas_call(
        write_back_kernel,
        grid_spec=pltpu.PrefetchScalarGridSpec(
            num_scalar_prefetch=1,
            grid=(1,),
            in_specs=[vmem, hbm, hbm],
            out_specs=hbm,
            scratch_shapes=[
                pltpu.VMEM(store.shape, store.dtype),
                pltpu.VMEM((holders, ROW_SLOTS, width), store.dtype),
                pltpu.VMEM((holders, capacity, page_len, width), store.dtype),
                dma,
                dma,
                dma,
            ],
        ),
        out_shape=jax.ShapeDtypeStruct(store.shape, store.dtype),
        compiler_params=params,
        cost_estimate=pl.CostEstimate(flops=0, bytes_accessed=4 * store.size, transcendentals=0),
    )(index_in, index_in, store, rows_in)

    orders = page_order(table[0], positions[0], own, hold, capacity, groups, page_len)
    sel_lanes = jnp.tile(positions.reshape(-1, 1, QUERY_BLOCK), (1, 1, LANES // QUERY_BLOCK))
    sel_rows = jnp.broadcast_to(positions.reshape(picked, 1), (picked, LANES))
    store_out, sel_lanes = lax.optimization_barrier((store_out, sel_lanes))
    state = ()
    for at, (arrays, order) in enumerate(zip(contexts, orders)):
        state = attend(
            at == 0,
            at == len(groups) - 1,
            order,
            sel_lanes,
            positions,
            queries[0],
            (fresh, sel_rows),
            state,
            arrays,
        )
    return (state[0][None], store_out)


def solution(mesh):
    return jax.shard_map(
        per_device,
        mesh=mesh,
        in_specs=(
            P(("groups", "store"), None, None),
            P(("groups", "store"), None),
            P(("groups", "store"), None),
            P(("groups", "store"), None, None),
            P(("groups", "store"), None, None),
        ),
        out_specs=(P(("groups", "store"), None, None), P(("groups", "store"), None, None)),
        check_vma=False,
    )
```

```python
import functools

import jax
import jax.numpy as jnp
from jax import lax
from jax.experimental import pallas as pl
from jax.experimental.pallas import tpu as pltpu
from jax.sharding import PartitionSpec as P

HEAD_WIDTH = 128
KEY_VALUE_HEADS = 4
QUERY_GROUP = 12
SELP = 2
LANES = 128
ROW_SLOTS = 16
VMEM_LIMIT = 60 * 1024 * 1024
QUERY_BLOCK = 32
TILE_PAGES = 16
HIDDEN = -1e30
FAR_POSITION = 1 << 24


def nt_dot(a, b):
    return lax.dot_general(a, b, (((1,), (1,)), ((), ())), preferred_element_type=jnp.float32)


def one_hot(condition):
    return jnp.where(condition, 1.0, 0.0)


def pair_places(hold, page_len, table_ref, sel_ref, wide):
    pages = table_ref.shape[1]
    picked = sel_ref.shape[1]
    f32 = jnp.float32
    slots = jnp.broadcast_to(table_ref[...], (pages, pages))
    owners = slots // hold
    local_row = (slots - owners * hold).astype(f32)[0:1]
    owner_row = owners.astype(f32)
    owner_col = owner_row.T
    sub = lax.broadcasted_iota(jnp.int32, (pages, pages), 0)
    lane = lax.broadcasted_iota(jnp.int32, (pages, pages), 1)
    earlier = one_hot((owner_row == owner_col) & (lane < sub))
    rank_col = jnp.sum(earlier, axis=1, keepdims=True)

    wide[...] = jnp.full(wide.shape, -1, jnp.int32)
    wide[0:1, 0:picked] = sel_ref[...]
    position = wide[...]
    page = lax.shift_right_arithmetic(position, page_len.bit_length() - 1)
    offset = (position & (page_len - 1)).astype(f32)[0:1]
    lane_wide = lax.broadcasted_iota(jnp.int32, wide.shape, 1)
    second = one_hot((page == pltpu.roll(page, 1, axis=1)) & (lane_wide > 0))[0:1]
    valid = lane_wide[0:1] < picked
    sub_wide = lax.broadcasted_iota(jnp.int32, (pages, wide.shape[1]), 0)
    in_page = one_hot(sub_wide == page[0:1])
    owner = jnp.sum(in_page * owner_col[:, 0:1], axis=0, keepdims=True)
    rank = jnp.sum(in_page * rank_col, axis=0, keepdims=True)
    return owner_row[0:1], local_row, rank_col, owner, rank, second, offset, valid


def index_kernel(hold, page_len, first, own, table_ref, sel_ref, out_ref, *rest):
    first_refs, wide = rest[:-1], rest[-1]
    holders = out_ref.shape[0]
    pages = table_ref.shape[1]
    f32 = jnp.float32
    bf16 = jnp.bfloat16
    owner_row, local_row, rank_col, owner, rank, second, offset, valid = pair_places(
        hold, page_len, table_ref, sel_ref, wide
    )
    holder = lax.broadcasted_iota(jnp.int32, (holders, pages), 0).astype(f32)
    owned = jnp.where(holder == owner_row, local_row, 0.0)
    lane = lax.broadcasted_iota(jnp.int32, (pages, LANES), 1).astype(f32)
    numbers = jnp.dot(
        owned.astype(bf16), one_hot(lane == rank_col).astype(bf16), preferred_element_type=f32
    )
    holder_wide = lax.broadcasted_iota(jnp.int32, (holders, wide.shape[1]), 0).astype(f32)
    marked = jnp.where((holder_wide == owner) & valid, rank * page_len + offset + 1.0, 0.0)
    place_lane = lax.broadcasted_iota(jnp.int32, (LANES, wide.shape[1]), 0).astype(f32)
    at_place = one_hot(place_lane == SELP * rank + second)
    targets = nt_dot(marked.astype(bf16), at_place.astype(bf16))
    for h in range(holders):
        out_ref[h, 0:1, :] = numbers[h : h + 1, :].astype(jnp.int32)
        out_ref[h, 1:2, :] = targets[h : h + 1, :].astype(jnp.int32)
    for d, ref in zip(first, first_refs):
        ref[0] = out_ref[own[0] ^ d]


def rows_kernel(hold, page_len, table_ref, sel_ref, fresh_ref, packed, wide):
    holders = packed.shape[0]
    picked = sel_ref.shape[1]
    f32 = jnp.float32
    _, _, _, owner, rank, second, _, valid = pair_places(hold, page_len, table_ref, sel_ref, wide)
    spot = jnp.where(valid, owner * ROW_SLOTS + SELP * rank + second, -1.0)[:, 0:picked]
    step = min(holders, 16)
    for start in range(0, holders, step):
        spot_id = lax.broadcasted_iota(jnp.int32, (step * ROW_SLOTS, picked), 0).astype(f32)
        choose = one_hot(spot_id + float(start * ROW_SLOTS) == spot).astype(jnp.bfloat16)
        rows = jnp.dot(choose, fresh_ref[...], preferred_element_type=f32).astype(jnp.bfloat16)
        packed[start : start + step] = rows.reshape(step, ROW_SLOTS, fresh_ref.shape[1])


def first_gather_kernel(count, *refs):
    lists, store_hbm, sends = refs[:count], refs[count], refs[count + 1 : 2 * count + 1]
    held, load_sem, send_sem = refs[2 * count + 1 :]
    capacity = held.shape[1]
    for i, numbers in enumerate(lists):
        for k in range(capacity):
            pltpu.make_async_copy(store_hbm.at[numbers[0, 0, k]], held.at[i, k], load_sem).start()
    pltpu.make_async_copy(held, held, load_sem).wait()
    for i, send in enumerate(sends):
        pltpu.make_async_copy(held.at[i], send, send_sem).start()
    pltpu.make_async_copy(held, held, send_sem).wait()


def gather_kernel(capacity, distances, own, index, store_hbm, *rest):
    sends, (store, load_sem, send_sem) = rest[:-3], rest[-3:]
    load = pltpu.make_async_copy(store_hbm, store, load_sem)
    load.start()
    load.wait()
    for i in range(len(distances) if distances else index.shape[0]):
        r = own[0] ^ distances[i] if distances else i
        send = sends[i] if distances else sends[0].at[i]
        for k in range(capacity):
            pltpu.make_async_copy(store.at[index[r, 0, k]], send.at[k], send_sem).start()
    for send in sends:
        pltpu.make_async_copy(send, send, send_sem).wait()


def write_back_kernel(index, targets_ref, store_hbm, rows_hbm, store_out, *scratch):
    store, rows, blended, load_sem, rows_sem, out_sem = scratch
    holders, capacity, page_len, width = blended.shape
    rows_here = capacity * page_len
    f32 = jnp.float32
    load = pltpu.make_async_copy(store_hbm, store, load_sem)
    load_rows = pltpu.make_async_copy(rows_hbm, rows, rows_sem)
    load.start()
    load_rows.start()
    load_rows.wait()
    load.wait()
    row_id = lax.broadcasted_iota(jnp.int32, (rows_here, ROW_SLOTS), 0)

    def one_request(r, carry):
        hit = one_hot(row_id == targets_ref[r][1:2, 0:ROW_SLOTS] - 1)
        keep = 1.0 - jnp.sum(hit, axis=1, keepdims=True)
        keep = jnp.broadcast_to(keep, (rows_here, LANES)).astype(jnp.bfloat16)
        hit = hit.astype(jnp.bfloat16)
        for c in range(width // LANES):
            lanes = slice(c * LANES, (c + 1) * LANES)
            fresh = jnp.dot(hit, rows[r, :, lanes], preferred_element_type=f32).astype(jnp.bfloat16)
            for k in range(capacity):
                part = slice(k * page_len, (k + 1) * page_len)
                blended[r, k, :, lanes] = store[index[r, 0, k], :, lanes] * keep[part] + fresh[part]
        for k in range(capacity):
            pltpu.make_async_copy(blended.at[r, k], store_out.at[index[r, 0, k]], out_sem).start()
        return carry

    lax.fori_loop(0, holders, one_request, 0)
    pltpu.make_async_copy(store_out, store_out, out_sem).wait()


def attend_kernel(first, last, sources, place, page_number, tiles, *rest):
    sel_ref, positions_ref, query_ref, *rest = rest
    if first:
        fresh_ref, fresh_positions, *rest = rest
    state_in = () if first else rest[:2]
    rest = rest if first else rest[2:]
    contexts, rest = rest[:sources], rest[sources:]
    outs, rest = (rest[:1], rest[1:]) if last else (rest[:2], rest[2:])
    kv, values, position, query, mixed, stats, sem = rest
    pages, page_len, width = kv.shape
    each = contexts[0].shape[0]
    ahead = TILE_PAGES if first else 0
    block = query_ref.shape[0]
    tile = TILE_PAGES * page_len
    lanes = QUERY_GROUP * block
    scale = 1.4426950408889634 / HEAD_WIDTH**0.5
    f32 = jnp.float32
    bf16 = jnp.bfloat16
    step = pl.program_id(0)
    eye = one_hot(
        lax.broadcasted_iota(jnp.int32, (LANES, LANES), 0)
        == lax.broadcasted_iota(jnp.int32, (LANES, LANES), 1)
    ).astype(bf16)

    @pl.when(step == 0)
    def _():
        for i, context in enumerate(contexts):
            for k in range(each):
                pltpu.make_async_copy(context.at[k], kv.at[ahead + place[i * each + k]], sem).start()
        if first:
            picked = fresh_ref.shape[0]
            count = picked // page_len
            kv[0:count] = fresh_ref[...].reshape(count, page_len, width)
            kv[count:ahead] = jnp.zeros((ahead - count, page_len, width), bf16)
            position[0:picked, :] = fresh_positions[...]
            position[picked:tile, :] = jnp.full((tile - picked, LANES), FAR_POSITION, jnp.int32)
        positions = positions_ref[...]
        row = lax.broadcasted_iota(jnp.int32, (page_len, positions.shape[1]), 0)
        ones = jnp.ones((positions.shape[1], LANES), bf16)
        row_lanes = lax.broadcasted_iota(jnp.int32, (page_len, LANES), 0)

        def place_rows(t, carry):
            starts = [page_number[t * TILE_PAGES + k] * page_len for k in range(TILE_PAGES)]
            hit = jnp.concatenate([one_hot(row + start == positions) for start in starts], axis=0)
            hidden = jnp.dot(hit.astype(bf16), ones, preferred_element_type=f32)
            plain = jnp.concatenate([row_lanes + start for start in starts], axis=0)
            here = pl.ds(pl.multiple_of(ahead * page_len + t * tile, tile), tile)
            position[here, :] = jnp.where(hidden > 0.0, FAR_POSITION, plain)
            return carry

        lax.fori_loop(0, (pages - ahead) // TILE_PAGES, place_rows, 0)
        used = kv.at[ahead:]
        pltpu.make_async_copy(used, used, sem).wait()

        def turn(t, carry):
            here = pl.ds(t * TILE_PAGES, TILE_PAGES)
            for g in range(KEY_VALUE_HEADS):
                at = (KEY_VALUE_HEADS + g) * LANES
                value = kv[here, :, at : at + LANES].reshape(tile, LANES)
                values[t, g] = nt_dot(eye, value).astype(bf16)
            return carry

        lax.fori_loop(0, pages // TILE_PAGES, turn, 0)

    for g in range(KEY_VALUE_HEADS):
        for i in range(QUERY_GROUP):
            head = g * QUERY_GROUP + i
            query[g, i * block : (i + 1) * block, :] = query_ref[:, head * LANES : (head + 1) * LANES]
    if first:
        mixed[...] = jnp.zeros(mixed.shape, f32)
        stats[0:KEY_VALUE_HEADS, :] = jnp.full((KEY_VALUE_HEADS, lanes), HIDDEN, f32)
        stats[KEY_VALUE_HEADS:, :] = jnp.zeros((KEY_VALUE_HEADS, lanes), f32)
    else:
        mixed[...] = state_in[0][0]
        stats[...] = state_in[1][0]

    sel = sel_ref[0]

    def one_tile(t, carry):
        here = pl.ds(t * TILE_PAGES, TILE_PAGES)
        bias = jnp.where(
            position[pl.ds(pl.multiple_of(t * tile, tile), tile), :] <= sel, 0.0, HIDDEN
        ).astype(f32)

        parts = [slice(n * LANES, (n + 1) * LANES) for n in range(lanes // LANES)]
        chains = [(g, part) for g in range(KEY_VALUE_HEADS) for part in parts]

        def score(chain):
            g, part = chain
            key = kv[here, :, g * LANES : (g + 1) * LANES].reshape(tile, LANES)
            return nt_dot(key, query[g, part, :])

        upcoming = score(chains[0])
        for following, (g, part) in zip([*chains[1:], None], chains):
            s = upcoming + bias
            if following:
                upcoming = score(following)
            at = KEY_VALUE_HEADS + g
            old = stats[g : g + 1, part]
            new = jnp.maximum(old, jnp.max(s, axis=0, keepdims=True))
            p = jnp.exp2((s - new) * scale)
            shrink = jnp.exp2((old - new) * scale)
            stats[at : at + 1, part] = stats[at : at + 1, part] * shrink + jnp.sum(
                p, axis=0, keepdims=True
            )
            stats[g : g + 1, part] = new
            mixed[g, :, part] = mixed[g, :, part] * shrink + jnp.dot(
                values[t, g], p.astype(bf16), preferred_element_type=f32
            )
        return carry

    lax.fori_loop(0, tiles[step], one_tile, 0)

    if last:
        done = []
        for g in range(KEY_VALUE_HEADS):
            at = KEY_VALUE_HEADS + g
            part = (mixed[g] * (1.0 / stats[at : at + 1, :])).astype(bf16)
            done += [part[:, n * LANES : (n + 1) * LANES] for n in range(lanes // LANES)]
        turned = nt_dot(eye, jnp.concatenate(done, axis=0)).astype(bf16)
        for n in range(len(done)):
            for i in range(LANES // block):
                head = n * (LANES // block) + i
                outs[0][:, head * LANES : (head + 1) * LANES] = turned[
                    i * block : (i + 1) * block, n * LANES : (n + 1) * LANES
                ]
    else:
        outs[0][0] = mixed[...]
        outs[1][0] = stats[...]


def attend(first, last, order, sel_lanes, positions, queries, fresh, state, contexts):
    picked, features = queries.shape
    each, page_len, width = contexts[0].shape
    pages = each * len(contexts) + (TILE_PAGES if first else 0)
    steps = picked // QUERY_BLOCK
    lanes = QUERY_GROUP * QUERY_BLOCK
    wide = pl.BlockSpec((QUERY_BLOCK, features), lambda b, *_: (b, 0))
    state_specs = [
        pl.BlockSpec((1, KEY_VALUE_HEADS, LANES, lanes), lambda b, *_: (b, 0, 0, 0)),
        pl.BlockSpec((1, 2 * KEY_VALUE_HEADS, lanes), lambda b, *_: (b, 0, 0)),
    ]
    state_shapes = [
        jax.ShapeDtypeStruct((steps, KEY_VALUE_HEADS, LANES, lanes), jnp.float32),
        jax.ShapeDtypeStruct((steps, 2 * KEY_VALUE_HEADS, lanes), jnp.float32),
    ]
    share = 0.6
    return pl.pallas_call(
        functools.partial(attend_kernel, first, last, len(contexts)),
        grid_spec=pltpu.PrefetchScalarGridSpec(
            num_scalar_prefetch=3,
            grid=(steps,),
            in_specs=[
                pl.BlockSpec((1, 1, LANES), lambda b, *_: (b, 0, 0)),
                pl.BlockSpec(positions.shape, lambda b, *_: (0, 0)),
                wide,
                *[pl.BlockSpec(x.shape, lambda b, *_: (0, 0)) for x in fresh if first],
                *([] if first else state_specs),
                *[pl.BlockSpec(memory_space=pltpu.HBM)] * len(contexts),
            ],
            out_specs=[wide] if last else state_specs,
            scratch_shapes=[
                pltpu.VMEM((pages, page_len, width), jnp.bfloat16),
                pltpu.VMEM(
                    (pages // TILE_PAGES, KEY_VALUE_HEADS, LANES, TILE_PAGES * page_len), jnp.bfloat16
                ),
                pltpu.VMEM((pages * page_len, LANES), jnp.int32),
                pltpu.VMEM((KEY_VALUE_HEADS, lanes, LANES), jnp.bfloat16),
                pltpu.VMEM((KEY_VALUE_HEADS, LANES, lanes), jnp.float32),
                pltpu.VMEM((2 * KEY_VALUE_HEADS, lanes), jnp.float32),
                pltpu.SemaphoreType.DMA,
            ],
        ),
        out_shape=[jax.ShapeDtypeStruct((picked, features), jnp.bfloat16)] if last else state_shapes,
        compiler_params=pltpu.CompilerParams(
            dimension_semantics=("arbitrary",), vmem_limit_bytes=VMEM_LIMIT
        ),
        cost_estimate=pl.CostEstimate(
            flops=int(share * 8 * picked * features * pages * page_len),
            bytes_accessed=2 * pages * page_len * width + 6 * picked * features,
            transcendentals=int(share * picked * features // LANES * pages * page_len),
        ),
    )(*order, sel_lanes, positions, queries, *[x for x in fresh if first], *state, *contexts)


def page_order(slots, positions, own, hold, capacity, groups, page_len):
    pages = slots.shape[0]
    number = jnp.arange(pages)
    before = number[None, :] < number[:, None]
    owners = slots // hold
    ranks = jnp.sum(((owners[None, :] == owners[:, None]) & before).astype(jnp.int32), axis=1)
    distance = owners ^ own
    last_page = positions.reshape(-1, QUERY_BLOCK)[:, -1] // page_len
    orders = []
    for at, group in enumerate(groups):
        if group is None:
            arrival = owners * capacity + ranks
            count = pages
        else:
            arrival = jnp.full((pages,), -1, jnp.int32)
            for i, d in enumerate(group):
                arrival = jnp.where(distance == d, i * capacity + ranks, arrival)
            count = len(group) * capacity
        member = arrival >= 0
        place = jnp.sum((member[None, :] & before).astype(jnp.int32), axis=1)
        index = jnp.arange(count)[:, None]
        places = jnp.sum(jnp.where(arrival[None, :] == index, place[None, :], 0), axis=1)
        page = jnp.sum(
            jnp.where(member[None, :] & (place[None, :] == index), number[None, :], 0), axis=1
        )
        seen = jnp.sum((page[None, :] <= last_page[:, None]).astype(jnp.int32), axis=1)
        orders.append((places, page, (seen + TILE_PAGES - 1) // TILE_PAGES + (at == 0)))
    return orders


def per_device(store, page_table, sel_pos, fresh_kv, queries):
    holders = lax.axis_size("store")
    hold, page_len, width = store.shape
    pages = page_table.shape[1]
    picked = sel_pos.shape[1]
    capacity = max(1, pages // holders)
    hbm = pl.BlockSpec(memory_space=pltpu.HBM)
    vmem = pl.BlockSpec(memory_space=pltpu.VMEM)
    dma = pltpu.SemaphoreType.DMA
    params = pltpu.CompilerParams(vmem_limit_bytes=VMEM_LIMIT)
    own = lax.axis_index("store")
    own_word = own.reshape(1).astype(jnp.int32)
    fresh = fresh_kv[0]
    wide = pltpu.VMEM((8, -(-picked // LANES) * LANES), jnp.int32)
    if holders == 16:
        first = (8, 12)
        groups = [(0, 8, 12, 4, 5, 1), (9, 6, 13, 7, 10, 2, 14, 3), (11, 15)]
        others = [d for group in groups for d in group if d not in first]
    else:
        first = ()
        groups = [None]
        others = None

    def swap(x, d):
        return lax.ppermute(x, "store", [(h, h ^ d) for h in range(holders)])

    def exchange(x):
        return lax.all_to_all(x, "store", split_axis=0, concat_axis=0, tiled=True)

    index, *lists = pl.pallas_call(
        functools.partial(index_kernel, hold, page_len, first),
        grid_spec=pltpu.PrefetchScalarGridSpec(
            num_scalar_prefetch=1,
            grid=(1,),
            in_specs=[vmem, vmem],
            out_specs=[vmem] * (1 + len(first)),
            scratch_shapes=[wide],
        ),
        out_shape=[
            jax.ShapeDtypeStruct((holders, 2, LANES), jnp.int32),
            *[jax.ShapeDtypeStruct((1, 2, LANES), jnp.int32)] * len(first),
        ],
        compiler_params=params,
    )(own_word, page_table, sel_pos)
    arrived = {}
    if first:
        lists = [swap(x, d) for x, d in zip(lists, first)]
        parts = pl.pallas_call(
            functools.partial(first_gather_kernel, len(first)),
            grid_spec=pltpu.PrefetchScalarGridSpec(
                num_scalar_prefetch=len(first),
                grid=(1,),
                in_specs=[hbm],
                out_specs=[hbm] * len(first),
                scratch_shapes=[
                    pltpu.VMEM((len(first), capacity, page_len, width), store.dtype),
                    dma,
                    dma,
                ],
            ),
            out_shape=[jax.ShapeDtypeStruct((capacity, page_len, width), store.dtype)] * len(first),
            compiler_params=params,
        )(*lists, store)
        parts, index, table, positions = lax.optimization_barrier(
            (parts, index, page_table, sel_pos)
        )
        arrived = {d: swap(part, d) for d, part in zip(first, parts)}
    else:
        table, positions = page_table, sel_pos
    index_in = exchange(index)

    packed = pl.pallas_call(
        functools.partial(rows_kernel, hold, page_len),
        out_shape=jax.ShapeDtypeStruct((holders, ROW_SLOTS, width), store.dtype),
        scratch_shapes=[wide],
        compiler_params=params,
    )(table, positions, fresh)

    each = jax.ShapeDtypeStruct((capacity, page_len, width), store.dtype)
    whole = jax.ShapeDtypeStruct((holders, capacity, page_len, width), store.dtype)
    parts = pl.pallas_call(
        functools.partial(gather_kernel, capacity, others),
        grid_spec=pltpu.PrefetchScalarGridSpec(
            num_scalar_prefetch=2,
            grid=(1,),
            in_specs=[hbm],
            out_specs=[hbm] * (len(others) if others else 1),
            scratch_shapes=[pltpu.VMEM(store.shape, store.dtype), dma, dma],
        ),
        out_shape=[each] * len(others) if others else [whole],
        compiler_params=params,
    )(own_word, index_in, store)
    parts, packed, table, positions = lax.optimization_barrier((parts, packed, table, positions))
    if others:
        for d, part in zip(others, parts):
            arrived[d] = swap(part, d) if d else part
        contexts = [[arrived[d] for d in group] for group in groups]
    else:
        contexts = [[exchange(parts[0]).reshape(pages, page_len, width)]]
    rows_in = exchange(packed)

    store_out = pl.pallas_call(
        write_back_kernel,
        grid_spec=pltpu.PrefetchScalarGridSpec(
            num_scalar_prefetch=1,
            grid=(1,),
            in_specs=[vmem, hbm, hbm],
            out_specs=hbm,
            scratch_shapes=[
                pltpu.VMEM(store.shape, store.dtype),
                pltpu.VMEM((holders, ROW_SLOTS, width), store.dtype),
                pltpu.VMEM((holders, capacity, page_len, width), store.dtype),
                dma,
                dma,
                dma,
            ],
        ),
        out_shape=jax.ShapeDtypeStruct(store.shape, store.dtype),
        compiler_params=params,
        cost_estimate=pl.CostEstimate(flops=0, bytes_accessed=4 * store.size, transcendentals=0),
    )(index_in, index_in, store, rows_in)

    orders = page_order(table[0], positions[0], own, hold, capacity, groups, page_len)
    sel_lanes = jnp.tile(positions.reshape(-1, 1, QUERY_BLOCK), (1, 1, LANES // QUERY_BLOCK))
    sel_rows = jnp.broadcast_to(positions.reshape(picked, 1), (picked, LANES))
    store_out, sel_lanes = lax.optimization_barrier((store_out, sel_lanes))
    state = ()
    for at, (arrays, order) in enumerate(zip(contexts, orders)):
        state = attend(
            at == 0,
            at == len(groups) - 1,
            order,
            sel_lanes,
            positions,
            queries[0],
            (fresh, sel_rows),
            state,
            arrays,
        )
    return (state[0][None], store_out)


def solution(mesh):
    return jax.shard_map(
        per_device,
        mesh=mesh,
        in_specs=(
            P(("groups", "store"), None, None),
            P(("groups", "store"), None),
            P(("groups", "store"), None),
            P(("groups", "store"), None, None),
            P(("groups", "store"), None, None),
        ),
        out_specs=(P(("groups", "store"), None, None), P(("groups", "store"), None, None)),
        check_vma=False,
    )
```

```python
import functools

import jax
import jax.numpy as jnp
from jax import lax
from jax.experimental import pallas as pl
from jax.experimental.pallas import tpu as pltpu
from jax.sharding import PartitionSpec as P

HEAD_WIDTH = 128
KEY_VALUE_HEADS = 4
QUERY_GROUP = 12
SELP = 2
LANES = 128
ROW_SLOTS = 16
VMEM_LIMIT = 60 * 1024 * 1024
QUERY_BLOCK = 32
TILE_PAGES = 16
HIDDEN = -1e30
FAR_POSITION = 1 << 24


def nt_dot(a, b):
    return lax.dot_general(a, b, (((1,), (1,)), ((), ())), preferred_element_type=jnp.float32)


def one_hot(condition):
    return jnp.where(condition, 1.0, 0.0)


def pair_places(hold, page_len, table_ref, sel_ref, wide):
    pages = table_ref.shape[1]
    picked = sel_ref.shape[1]
    f32 = jnp.float32
    slots = jnp.broadcast_to(table_ref[...], (pages, pages))
    owners = slots // hold
    local_row = (slots - owners * hold).astype(f32)[0:1]
    owner_row = owners.astype(f32)
    owner_col = owner_row.T
    sub = lax.broadcasted_iota(jnp.int32, (pages, pages), 0)
    lane = lax.broadcasted_iota(jnp.int32, (pages, pages), 1)
    earlier = one_hot((owner_row == owner_col) & (lane < sub))
    rank_col = jnp.sum(earlier, axis=1, keepdims=True)

    wide[...] = jnp.full(wide.shape, -1, jnp.int32)
    wide[0:1, 0:picked] = sel_ref[...]
    position = wide[...]
    page = lax.shift_right_arithmetic(position, page_len.bit_length() - 1)
    offset = (position & (page_len - 1)).astype(f32)[0:1]
    lane_wide = lax.broadcasted_iota(jnp.int32, wide.shape, 1)
    second = one_hot((page == pltpu.roll(page, 1, axis=1)) & (lane_wide > 0))[0:1]
    valid = lane_wide[0:1] < picked
    sub_wide = lax.broadcasted_iota(jnp.int32, (pages, wide.shape[1]), 0)
    in_page = one_hot(sub_wide == page[0:1])
    owner = jnp.sum(in_page * owner_col[:, 0:1], axis=0, keepdims=True)
    rank = jnp.sum(in_page * rank_col, axis=0, keepdims=True)
    return owner_row[0:1], local_row, rank_col, owner, rank, second, offset, valid


def index_kernel(hold, page_len, first, own, table_ref, sel_ref, out_ref, *rest):
    first_refs, wide = rest[:-1], rest[-1]
    holders = out_ref.shape[0]
    pages = table_ref.shape[1]
    f32 = jnp.float32
    bf16 = jnp.bfloat16
    owner_row, local_row, rank_col, owner, rank, second, offset, valid = pair_places(
        hold, page_len, table_ref, sel_ref, wide
    )
    holder = lax.broadcasted_iota(jnp.int32, (holders, pages), 0).astype(f32)
    owned = jnp.where(holder == owner_row, local_row, 0.0)
    lane = lax.broadcasted_iota(jnp.int32, (pages, LANES), 1).astype(f32)
    numbers = jnp.dot(
        owned.astype(bf16), one_hot(lane == rank_col).astype(bf16), preferred_element_type=f32
    )
    holder_wide = lax.broadcasted_iota(jnp.int32, (holders, wide.shape[1]), 0).astype(f32)
    marked = jnp.where((holder_wide == owner) & valid, rank * page_len + offset + 1.0, 0.0)
    place_lane = lax.broadcasted_iota(jnp.int32, (LANES, wide.shape[1]), 0).astype(f32)
    at_place = one_hot(place_lane == SELP * rank + second)
    targets = nt_dot(marked.astype(bf16), at_place.astype(bf16))
    for h in range(holders):
        out_ref[h, 0:1, :] = numbers[h : h + 1, :].astype(jnp.int32)
        out_ref[h, 1:2, :] = targets[h : h + 1, :].astype(jnp.int32)
    for d, ref in zip(first, first_refs):
        ref[0] = out_ref[own[0] ^ d]


def rows_kernel(hold, page_len, table_ref, sel_ref, fresh_ref, packed, wide):
    holders = packed.shape[0]
    picked = sel_ref.shape[1]
    f32 = jnp.float32
    _, _, _, owner, rank, second, _, valid = pair_places(hold, page_len, table_ref, sel_ref, wide)
    spot = jnp.where(valid, owner * ROW_SLOTS + SELP * rank + second, -1.0)[:, 0:picked]
    step = min(holders, 16)
    for start in range(0, holders, step):
        spot_id = lax.broadcasted_iota(jnp.int32, (step * ROW_SLOTS, picked), 0).astype(f32)
        choose = one_hot(spot_id + float(start * ROW_SLOTS) == spot).astype(jnp.bfloat16)
        rows = jnp.dot(choose, fresh_ref[...], preferred_element_type=f32).astype(jnp.bfloat16)
        packed[start : start + step] = rows.reshape(step, ROW_SLOTS, fresh_ref.shape[1])


def first_gather_kernel(count, *refs):
    lists, store_hbm, sends = refs[:count], refs[count], refs[count + 1 : 2 * count + 1]
    held, load_sem, send_sem = refs[2 * count + 1 :]
    capacity = held.shape[1]
    for i, numbers in enumerate(lists):
        for k in range(capacity):
            pltpu.make_async_copy(store_hbm.at[numbers[0, 0, k]], held.at[i, k], load_sem).start()
    pltpu.make_async_copy(held, held, load_sem).wait()
    for i, send in enumerate(sends):
        pltpu.make_async_copy(held.at[i], send, send_sem).start()
    pltpu.make_async_copy(held, held, send_sem).wait()


def gather_kernel(capacity, distances, own, index, store_hbm, *rest):
    sends, (store, load_sem, send_sem) = rest[:-3], rest[-3:]
    load = pltpu.make_async_copy(store_hbm, store, load_sem)
    load.start()
    load.wait()
    for i in range(len(distances) if distances else index.shape[0]):
        r = own[0] ^ distances[i] if distances else i
        send = sends[i] if distances else sends[0].at[i]
        for k in range(capacity):
            pltpu.make_async_copy(store.at[index[r, 0, k]], send.at[k], send_sem).start()
    for send in sends:
        pltpu.make_async_copy(send, send, send_sem).wait()


def write_back_kernel(index, targets_ref, store_hbm, rows_hbm, store_out, *scratch):
    store, rows, blended, load_sem, rows_sem, out_sem = scratch
    holders, capacity, page_len, width = blended.shape
    rows_here = capacity * page_len
    f32 = jnp.float32
    load = pltpu.make_async_copy(store_hbm, store, load_sem)
    load_rows = pltpu.make_async_copy(rows_hbm, rows, rows_sem)
    load.start()
    load_rows.start()
    load_rows.wait()
    load.wait()
    row_id = lax.broadcasted_iota(jnp.int32, (rows_here, ROW_SLOTS), 0)

    def one_request(r, carry):
        hit = one_hot(row_id == targets_ref[r][1:2, 0:ROW_SLOTS] - 1)
        keep = 1.0 - jnp.sum(hit, axis=1, keepdims=True)
        keep = jnp.broadcast_to(keep, (rows_here, LANES)).astype(jnp.bfloat16)
        hit = hit.astype(jnp.bfloat16)
        for c in range(width // LANES):
            lanes = slice(c * LANES, (c + 1) * LANES)
            fresh = jnp.dot(hit, rows[r, :, lanes], preferred_element_type=f32).astype(jnp.bfloat16)
            for k in range(capacity):
                part = slice(k * page_len, (k + 1) * page_len)
                blended[r, k, :, lanes] = store[index[r, 0, k], :, lanes] * keep[part] + fresh[part]
        for k in range(capacity):
            pltpu.make_async_copy(blended.at[r, k], store_out.at[index[r, 0, k]], out_sem).start()
        return carry

    lax.fori_loop(0, holders, one_request, 0)
    pltpu.make_async_copy(store_out, store_out, out_sem).wait()


def attend_kernel(first, last, sources, place, page_number, tiles, *rest):
    sel_ref, positions_ref, query_ref, *rest = rest
    if first:
        fresh_ref, fresh_positions, *rest = rest
    state_in = () if first else rest[:2]
    rest = rest if first else rest[2:]
    contexts, rest = rest[:sources], rest[sources:]
    outs, rest = (rest[:1], rest[1:]) if last else (rest[:2], rest[2:])
    kv, values, position, query, mixed, stats, sem = rest
    pages, page_len, width = kv.shape
    each = contexts[0].shape[0]
    ahead = TILE_PAGES if first else 0
    block = query_ref.shape[0]
    tile = TILE_PAGES * page_len
    lanes = QUERY_GROUP * block
    scale = 1.0 / HEAD_WIDTH**0.5
    f32 = jnp.float32
    bf16 = jnp.bfloat16
    step = pl.program_id(0)
    eye = one_hot(
        lax.broadcasted_iota(jnp.int32, (LANES, LANES), 0)
        == lax.broadcasted_iota(jnp.int32, (LANES, LANES), 1)
    ).astype(bf16)

    @pl.when(step == 0)
    def _():
        for i, context in enumerate(contexts):
            for k in range(each):
                pltpu.make_async_copy(context.at[k], kv.at[ahead + place[i * each + k]], sem).start()
        if first:
            picked = fresh_ref.shape[0]
            count = picked // page_len
            kv[0:count] = fresh_ref[...].reshape(count, page_len, width)
            kv[count:ahead] = jnp.zeros((ahead - count, page_len, width), bf16)
            position[0:picked, :] = fresh_positions[...]
            position[picked:tile, :] = jnp.full((tile - picked, LANES), FAR_POSITION, jnp.int32)
        positions = positions_ref[...]
        row = lax.broadcasted_iota(jnp.int32, (page_len, positions.shape[1]), 0)
        ones = jnp.ones((positions.shape[1], LANES), bf16)
        row_lanes = lax.broadcasted_iota(jnp.int32, (page_len, LANES), 0)

        def place_rows(t, carry):
            starts = [page_number[t * TILE_PAGES + k] * page_len for k in range(TILE_PAGES)]
            hit = jnp.concatenate([one_hot(row + start == positions) for start in starts], axis=0)
            hidden = jnp.dot(hit.astype(bf16), ones, preferred_element_type=f32)
            plain = jnp.concatenate([row_lanes + start for start in starts], axis=0)
            here = pl.ds(pl.multiple_of(ahead * page_len + t * tile, tile), tile)
            position[here, :] = jnp.where(hidden > 0.0, FAR_POSITION, plain)
            return carry

        lax.fori_loop(0, (pages - ahead) // TILE_PAGES, place_rows, 0)
        used = kv.at[ahead:]
        pltpu.make_async_copy(used, used, sem).wait()

        def turn(t, carry):
            here = pl.ds(t * TILE_PAGES, TILE_PAGES)
            for g in range(KEY_VALUE_HEADS):
                at = (KEY_VALUE_HEADS + g) * LANES
                value = kv[here, :, at : at + LANES].reshape(tile, LANES)
                values[t, g] = nt_dot(eye, value).astype(bf16)
            return carry

        lax.fori_loop(0, pages // TILE_PAGES, turn, 0)

    for g in range(KEY_VALUE_HEADS):
        for i in range(QUERY_GROUP):
            head = g * QUERY_GROUP + i
            query[g, i * block : (i + 1) * block, :] = query_ref[:, head * LANES : (head + 1) * LANES]
    if first:
        mixed[...] = jnp.zeros(mixed.shape, f32)
        stats[0:KEY_VALUE_HEADS, :] = jnp.full((KEY_VALUE_HEADS, lanes), HIDDEN, f32)
        stats[KEY_VALUE_HEADS:, :] = jnp.zeros((KEY_VALUE_HEADS, lanes), f32)
    else:
        mixed[...] = state_in[0][0]
        stats[...] = state_in[1][0]

    sel = sel_ref[0]

    def one_tile(t, carry):
        here = pl.ds(t * TILE_PAGES, TILE_PAGES)
        bias = jnp.where(
            position[pl.ds(pl.multiple_of(t * tile, tile), tile), :] <= sel, 0.0, HIDDEN
        ).astype(f32)

        def score(g):
            key = kv[here, :, g * LANES : (g + 1) * LANES].reshape(tile, LANES)
            return nt_dot(key, query[g])

        upcoming = score(0)
        for g in range(KEY_VALUE_HEADS):
            scores = upcoming
            if g + 1 < KEY_VALUE_HEADS:
                upcoming = score(g + 1)
            raised, shrinks = [], []
            at = KEY_VALUE_HEADS + g
            for n in range(lanes // LANES):
                part = slice(n * LANES, (n + 1) * LANES)
                s = scores[:, part] + bias
                old = stats[g : g + 1, part]
                new = jnp.maximum(old, jnp.max(s, axis=0, keepdims=True))
                p = jnp.exp((s - new) * scale)
                shrink = jnp.exp((old - new) * scale)
                stats[at : at + 1, part] = stats[at : at + 1, part] * shrink + jnp.sum(
                    p, axis=0, keepdims=True
                )
                stats[g : g + 1, part] = new
                raised.append(p.astype(bf16))
                shrinks.append(shrink)
            raised = jnp.concatenate(raised, axis=1)
            shrink = jnp.concatenate(shrinks, axis=1)
            mixed[g] = mixed[g] * shrink + jnp.dot(
                values[t, g], raised, preferred_element_type=f32
            )
        return carry

    lax.fori_loop(0, tiles[step], one_tile, 0)

    if last:
        done = []
        for g in range(KEY_VALUE_HEADS):
            at = KEY_VALUE_HEADS + g
            part = (mixed[g] * (1.0 / stats[at : at + 1, :])).astype(bf16)
            done += [part[:, n * LANES : (n + 1) * LANES] for n in range(lanes // LANES)]
        turned = nt_dot(eye, jnp.concatenate(done, axis=0)).astype(bf16)
        for n in range(len(done)):
            for i in range(LANES // block):
                head = n * (LANES // block) + i
                outs[0][:, head * LANES : (head + 1) * LANES] = turned[
                    i * block : (i + 1) * block, n * LANES : (n + 1) * LANES
                ]
    else:
        outs[0][0] = mixed[...]
        outs[1][0] = stats[...]


def attend(first, last, order, sel_lanes, positions, queries, fresh, state, contexts):
    picked, features = queries.shape
    each, page_len, width = contexts[0].shape
    pages = each * len(contexts) + (TILE_PAGES if first else 0)
    steps = picked // QUERY_BLOCK
    lanes = QUERY_GROUP * QUERY_BLOCK
    wide = pl.BlockSpec((QUERY_BLOCK, features), lambda b, *_: (b, 0))
    state_specs = [
        pl.BlockSpec((1, KEY_VALUE_HEADS, LANES, lanes), lambda b, *_: (b, 0, 0, 0)),
        pl.BlockSpec((1, 2 * KEY_VALUE_HEADS, lanes), lambda b, *_: (b, 0, 0)),
    ]
    state_shapes = [
        jax.ShapeDtypeStruct((steps, KEY_VALUE_HEADS, LANES, lanes), jnp.float32),
        jax.ShapeDtypeStruct((steps, 2 * KEY_VALUE_HEADS, lanes), jnp.float32),
    ]
    share = 0.6
    return pl.pallas_call(
        functools.partial(attend_kernel, first, last, len(contexts)),
        grid_spec=pltpu.PrefetchScalarGridSpec(
            num_scalar_prefetch=3,
            grid=(steps,),
            in_specs=[
                pl.BlockSpec((1, 1, LANES), lambda b, *_: (b, 0, 0)),
                pl.BlockSpec(positions.shape, lambda b, *_: (0, 0)),
                wide,
                *[pl.BlockSpec(x.shape, lambda b, *_: (0, 0)) for x in fresh if first],
                *([] if first else state_specs),
                *[pl.BlockSpec(memory_space=pltpu.HBM)] * len(contexts),
            ],
            out_specs=[wide] if last else state_specs,
            scratch_shapes=[
                pltpu.VMEM((pages, page_len, width), jnp.bfloat16),
                pltpu.VMEM(
                    (pages // TILE_PAGES, KEY_VALUE_HEADS, LANES, TILE_PAGES * page_len), jnp.bfloat16
                ),
                pltpu.VMEM((pages * page_len, LANES), jnp.int32),
                pltpu.VMEM((KEY_VALUE_HEADS, lanes, LANES), jnp.bfloat16),
                pltpu.VMEM((KEY_VALUE_HEADS, LANES, lanes), jnp.float32),
                pltpu.VMEM((2 * KEY_VALUE_HEADS, lanes), jnp.float32),
                pltpu.SemaphoreType.DMA,
            ],
        ),
        out_shape=[jax.ShapeDtypeStruct((picked, features), jnp.bfloat16)] if last else state_shapes,
        compiler_params=pltpu.CompilerParams(
            dimension_semantics=("arbitrary",), vmem_limit_bytes=VMEM_LIMIT
        ),
        cost_estimate=pl.CostEstimate(
            flops=int(share * 8 * picked * features * pages * page_len),
            bytes_accessed=2 * pages * page_len * width + 6 * picked * features,
            transcendentals=int(share * picked * features // LANES * pages * page_len),
        ),
    )(*order, sel_lanes, positions, queries, *[x for x in fresh if first], *state, *contexts)


def page_order(slots, positions, own, hold, capacity, groups, page_len):
    pages = slots.shape[0]
    number = jnp.arange(pages)
    before = number[None, :] < number[:, None]
    owners = slots // hold
    ranks = jnp.sum(((owners[None, :] == owners[:, None]) & before).astype(jnp.int32), axis=1)
    distance = owners ^ own
    last_page = positions.reshape(-1, QUERY_BLOCK)[:, -1] // page_len
    orders = []
    for at, group in enumerate(groups):
        if group is None:
            arrival = owners * capacity + ranks
            count = pages
        else:
            arrival = jnp.full((pages,), -1, jnp.int32)
            for i, d in enumerate(group):
                arrival = jnp.where(distance == d, i * capacity + ranks, arrival)
            count = len(group) * capacity
        member = arrival >= 0
        place = jnp.sum((member[None, :] & before).astype(jnp.int32), axis=1)
        index = jnp.arange(count)[:, None]
        places = jnp.sum(jnp.where(arrival[None, :] == index, place[None, :], 0), axis=1)
        page = jnp.sum(
            jnp.where(member[None, :] & (place[None, :] == index), number[None, :], 0), axis=1
        )
        seen = jnp.sum((page[None, :] <= last_page[:, None]).astype(jnp.int32), axis=1)
        orders.append((places, page, (seen + TILE_PAGES - 1) // TILE_PAGES + (at == 0)))
    return orders


def per_device(store, page_table, sel_pos, fresh_kv, queries):
    holders = lax.axis_size("store")
    hold, page_len, width = store.shape
    pages = page_table.shape[1]
    picked = sel_pos.shape[1]
    capacity = max(1, pages // holders)
    hbm = pl.BlockSpec(memory_space=pltpu.HBM)
    vmem = pl.BlockSpec(memory_space=pltpu.VMEM)
    dma = pltpu.SemaphoreType.DMA
    params = pltpu.CompilerParams(vmem_limit_bytes=VMEM_LIMIT)
    own = lax.axis_index("store")
    own_word = own.reshape(1).astype(jnp.int32)
    fresh = fresh_kv[0]
    wide = pltpu.VMEM((8, -(-picked // LANES) * LANES), jnp.int32)
    if holders == 16:
        first = (8, 12)
        groups = [(0, 8, 12, 4, 5, 1), (9, 6, 7, 13, 2, 10, 3, 14), (11, 15)]
        others = [d for group in groups for d in group if d not in first]
    else:
        first = ()
        groups = [None]
        others = None

    def swap(x, d):
        return lax.ppermute(x, "store", [(h, h ^ d) for h in range(holders)])

    def exchange(x):
        return lax.all_to_all(x, "store", split_axis=0, concat_axis=0, tiled=True)

    index, *lists = pl.pallas_call(
        functools.partial(index_kernel, hold, page_len, first),
        grid_spec=pltpu.PrefetchScalarGridSpec(
            num_scalar_prefetch=1,
            grid=(1,),
            in_specs=[vmem, vmem],
            out_specs=[vmem] * (1 + len(first)),
            scratch_shapes=[wide],
        ),
        out_shape=[
            jax.ShapeDtypeStruct((holders, 2, LANES), jnp.int32),
            *[jax.ShapeDtypeStruct((1, 2, LANES), jnp.int32)] * len(first),
        ],
        compiler_params=params,
    )(own_word, page_table, sel_pos)
    arrived = {}
    if first:
        lists = [swap(x, d) for x, d in zip(lists, first)]
        parts = pl.pallas_call(
            functools.partial(first_gather_kernel, len(first)),
            grid_spec=pltpu.PrefetchScalarGridSpec(
                num_scalar_prefetch=len(first),
                grid=(1,),
                in_specs=[hbm],
                out_specs=[hbm] * len(first),
                scratch_shapes=[
                    pltpu.VMEM((len(first), capacity, page_len, width), store.dtype),
                    dma,
                    dma,
                ],
            ),
            out_shape=[jax.ShapeDtypeStruct((capacity, page_len, width), store.dtype)] * len(first),
            compiler_params=params,
        )(*lists, store)
        parts, index, table, positions = lax.optimization_barrier(
            (parts, index, page_table, sel_pos)
        )
        arrived = {d: swap(part, d) for d, part in zip(first, parts)}
    else:
        table, positions = page_table, sel_pos
    index_in = exchange(index)

    packed = pl.pallas_call(
        functools.partial(rows_kernel, hold, page_len),
        out_shape=jax.ShapeDtypeStruct((holders, ROW_SLOTS, width), store.dtype),
        scratch_shapes=[wide],
        compiler_params=params,
    )(table, positions, fresh)

    each = jax.ShapeDtypeStruct((capacity, page_len, width), store.dtype)
    whole = jax.ShapeDtypeStruct((holders, capacity, page_len, width), store.dtype)
    parts = pl.pallas_call(
        functools.partial(gather_kernel, capacity, others),
        grid_spec=pltpu.PrefetchScalarGridSpec(
            num_scalar_prefetch=2,
            grid=(1,),
            in_specs=[hbm],
            out_specs=[hbm] * (len(others) if others else 1),
            scratch_shapes=[pltpu.VMEM(store.shape, store.dtype), dma, dma],
        ),
        out_shape=[each] * len(others) if others else [whole],
        compiler_params=params,
    )(own_word, index_in, store)
    parts, packed, table, positions = lax.optimization_barrier((parts, packed, table, positions))
    if others:
        for d, part in zip(others, parts):
            arrived[d] = swap(part, d) if d else part
        contexts = [[arrived[d] for d in group] for group in groups]
    else:
        contexts = [[exchange(parts[0]).reshape(pages, page_len, width)]]
    rows_in = exchange(packed)

    store_out = pl.pallas_call(
        write_back_kernel,
        grid_spec=pltpu.PrefetchScalarGridSpec(
            num_scalar_prefetch=1,
            grid=(1,),
            in_specs=[vmem, hbm, hbm],
            out_specs=hbm,
            scratch_shapes=[
                pltpu.VMEM(store.shape, store.dtype),
                pltpu.VMEM((holders, ROW_SLOTS, width), store.dtype),
                pltpu.VMEM((holders, capacity, page_len, width), store.dtype),
                dma,
                dma,
                dma,
            ],
        ),
        out_shape=jax.ShapeDtypeStruct(store.shape, store.dtype),
        compiler_params=params,
        cost_estimate=pl.CostEstimate(flops=0, bytes_accessed=4 * store.size, transcendentals=0),
    )(index_in, index_in, store, rows_in)

    orders = page_order(table[0], positions[0], own, hold, capacity, groups, page_len)
    sel_lanes = jnp.tile(positions.reshape(-1, 1, QUERY_BLOCK), (1, 1, LANES // QUERY_BLOCK))
    sel_rows = jnp.broadcast_to(positions.reshape(picked, 1), (picked, LANES))
    store_out, sel_lanes = lax.optimization_barrier((store_out, sel_lanes))
    state = ()
    for at, (arrays, order) in enumerate(zip(contexts, orders)):
        state = attend(
            at == 0,
            at == len(groups) - 1,
            order,
            sel_lanes,
            positions,
            queries[0],
            (fresh, sel_rows),
            state,
            arrays,
        )
    return (state[0][None], store_out)


def solution(mesh):
    return jax.shard_map(
        per_device,
        mesh=mesh,
        in_specs=(
            P(("groups", "store"), None, None),
            P(("groups", "store"), None),
            P(("groups", "store"), None),
            P(("groups", "store"), None, None),
            P(("groups", "store"), None, None),
        ),
        out_specs=(P(("groups", "store"), None, None), P(("groups", "store"), None, None)),
        check_vma=False,
    )
```

```python
import functools

import jax
import jax.numpy as jnp
from jax import lax
from jax.experimental import pallas as pl
from jax.experimental.pallas import tpu as pltpu
from jax.sharding import PartitionSpec as P

HEAD_WIDTH = 128
KEY_VALUE_HEADS = 4
QUERY_GROUP = 12
SELP = 2
LANES = 128
ROW_SLOTS = 16
VMEM_LIMIT = 60 * 1024 * 1024
QUERY_BLOCK = 32
TILE_PAGES = 16
HIDDEN = -1e30
FAR_POSITION = 1 << 24


def nt_dot(a, b):
    return lax.dot_general(a, b, (((1,), (1,)), ((), ())), preferred_element_type=jnp.float32)


def one_hot(condition):
    return jnp.where(condition, 1.0, 0.0)


def pair_places(hold, page_len, table_ref, sel_ref, wide):
    pages = table_ref.shape[1]
    picked = sel_ref.shape[1]
    f32 = jnp.float32
    slots = jnp.broadcast_to(table_ref[...], (pages, pages))
    owners = slots // hold
    local_row = (slots - owners * hold).astype(f32)[0:1]
    owner_row = owners.astype(f32)
    owner_col = owner_row.T
    sub = lax.broadcasted_iota(jnp.int32, (pages, pages), 0)
    lane = lax.broadcasted_iota(jnp.int32, (pages, pages), 1)
    earlier = one_hot((owner_row == owner_col) & (lane < sub))
    rank_col = jnp.sum(earlier, axis=1, keepdims=True)

    wide[...] = jnp.full(wide.shape, -1, jnp.int32)
    wide[0:1, 0:picked] = sel_ref[...]
    position = wide[...]
    page = lax.shift_right_arithmetic(position, page_len.bit_length() - 1)
    offset = (position & (page_len - 1)).astype(f32)[0:1]
    lane_wide = lax.broadcasted_iota(jnp.int32, wide.shape, 1)
    second = one_hot((page == pltpu.roll(page, 1, axis=1)) & (lane_wide > 0))[0:1]
    valid = lane_wide[0:1] < picked
    sub_wide = lax.broadcasted_iota(jnp.int32, (pages, wide.shape[1]), 0)
    in_page = one_hot(sub_wide == page[0:1])
    owner = jnp.sum(in_page * owner_col[:, 0:1], axis=0, keepdims=True)
    rank = jnp.sum(in_page * rank_col, axis=0, keepdims=True)
    return owner_row[0:1], local_row, rank_col, owner, rank, second, offset, valid


def index_kernel(hold, page_len, first, own, table_ref, sel_ref, out_ref, *rest):
    first_refs, wide = rest[:-1], rest[-1]
    holders = out_ref.shape[0]
    pages = table_ref.shape[1]
    f32 = jnp.float32
    bf16 = jnp.bfloat16
    owner_row, local_row, rank_col, owner, rank, second, offset, valid = pair_places(
        hold, page_len, table_ref, sel_ref, wide
    )
    holder = lax.broadcasted_iota(jnp.int32, (holders, pages), 0).astype(f32)
    owned = jnp.where(holder == owner_row, local_row, 0.0)
    lane = lax.broadcasted_iota(jnp.int32, (pages, LANES), 1).astype(f32)
    numbers = jnp.dot(
        owned.astype(bf16), one_hot(lane == rank_col).astype(bf16), preferred_element_type=f32
    )
    holder_wide = lax.broadcasted_iota(jnp.int32, (holders, wide.shape[1]), 0).astype(f32)
    marked = jnp.where((holder_wide == owner) & valid, rank * page_len + offset + 1.0, 0.0)
    place_lane = lax.broadcasted_iota(jnp.int32, (LANES, wide.shape[1]), 0).astype(f32)
    at_place = one_hot(place_lane == SELP * rank + second)
    targets = nt_dot(marked.astype(bf16), at_place.astype(bf16))
    for h in range(holders):
        out_ref[h, 0:1, :] = numbers[h : h + 1, :].astype(jnp.int32)
        out_ref[h, 1:2, :] = targets[h : h + 1, :].astype(jnp.int32)
    for d, ref in zip(first, first_refs):
        ref[0] = out_ref[own[0] ^ d]


def rows_kernel(hold, page_len, table_ref, sel_ref, fresh_ref, packed, wide):
    holders = packed.shape[0]
    picked = sel_ref.shape[1]
    f32 = jnp.float32
    _, _, _, owner, rank, second, _, valid = pair_places(hold, page_len, table_ref, sel_ref, wide)
    spot = jnp.where(valid, owner * ROW_SLOTS + SELP * rank + second, -1.0)[:, 0:picked]
    step = min(holders, 16)
    for start in range(0, holders, step):
        spot_id = lax.broadcasted_iota(jnp.int32, (step * ROW_SLOTS, picked), 0).astype(f32)
        choose = one_hot(spot_id + float(start * ROW_SLOTS) == spot).astype(jnp.bfloat16)
        rows = jnp.dot(choose, fresh_ref[...], preferred_element_type=f32).astype(jnp.bfloat16)
        packed[start : start + step] = rows.reshape(step, ROW_SLOTS, fresh_ref.shape[1])


def first_gather_kernel(count, *refs):
    lists, store_hbm, sends = refs[:count], refs[count], refs[count + 1 : 2 * count + 1]
    held, load_sem, send_sem = refs[2 * count + 1 :]
    capacity = held.shape[1]
    for i, numbers in enumerate(lists):
        for k in range(capacity):
            pltpu.make_async_copy(store_hbm.at[numbers[0, 0, k]], held.at[i, k], load_sem).start()
    pltpu.make_async_copy(held, held, load_sem).wait()
    for i, send in enumerate(sends):
        pltpu.make_async_copy(held.at[i], send, send_sem).start()
    pltpu.make_async_copy(held, held, send_sem).wait()


def gather_kernel(capacity, distances, own, index, store_hbm, *rest):
    sends, (store, load_sem, send_sem) = rest[:-3], rest[-3:]
    load = pltpu.make_async_copy(store_hbm, store, load_sem)
    load.start()
    load.wait()
    for i in range(len(distances) if distances else index.shape[0]):
        r = own[0] ^ distances[i] if distances else i
        send = sends[i] if distances else sends[0].at[i]
        for k in range(capacity):
            pltpu.make_async_copy(store.at[index[r, 0, k]], send.at[k], send_sem).start()
    for send in sends:
        pltpu.make_async_copy(send, send, send_sem).wait()


def write_back_kernel(index, targets_ref, store_hbm, rows_hbm, store_out, *scratch):
    store, rows, blended, load_sem, rows_sem, out_sem = scratch
    holders, capacity, page_len, width = blended.shape
    rows_here = capacity * page_len
    f32 = jnp.float32
    load = pltpu.make_async_copy(store_hbm, store, load_sem)
    load_rows = pltpu.make_async_copy(rows_hbm, rows, rows_sem)
    load.start()
    load_rows.start()
    load_rows.wait()
    load.wait()
    row_id = lax.broadcasted_iota(jnp.int32, (rows_here, ROW_SLOTS), 0)

    def one_request(r, carry):
        hit = one_hot(row_id == targets_ref[r][1:2, 0:ROW_SLOTS] - 1)
        keep = 1.0 - jnp.sum(hit, axis=1, keepdims=True)
        keep = jnp.broadcast_to(keep, (rows_here, LANES)).astype(jnp.bfloat16)
        hit = hit.astype(jnp.bfloat16)
        for c in range(width // LANES):
            lanes = slice(c * LANES, (c + 1) * LANES)
            fresh = jnp.dot(hit, rows[r, :, lanes], preferred_element_type=f32).astype(jnp.bfloat16)
            for k in range(capacity):
                part = slice(k * page_len, (k + 1) * page_len)
                blended[r, k, :, lanes] = store[index[r, 0, k], :, lanes] * keep[part] + fresh[part]
        for k in range(capacity):
            pltpu.make_async_copy(blended.at[r, k], store_out.at[index[r, 0, k]], out_sem).start()
        return carry

    lax.fori_loop(0, holders, one_request, 0)
    pltpu.make_async_copy(store_out, store_out, out_sem).wait()


def attend_kernel(first, last, sources, place, page_number, tiles, *rest):
    sel_ref, positions_ref, query_ref, *rest = rest
    if first:
        fresh_ref, fresh_positions, *rest = rest
    state_in = () if first else rest[:2]
    rest = rest if first else rest[2:]
    contexts, rest = rest[:sources], rest[sources:]
    outs, rest = (rest[:1], rest[1:]) if last else (rest[:2], rest[2:])
    kv, values, position, query, mixed, stats, sem = rest
    pages, page_len, width = kv.shape
    each = contexts[0].shape[0]
    ahead = TILE_PAGES if first else 0
    block = query_ref.shape[0]
    tile = TILE_PAGES * page_len
    lanes = QUERY_GROUP * block
    scale = 1.4426950408889634 / HEAD_WIDTH**0.5
    f32 = jnp.float32
    bf16 = jnp.bfloat16
    step = pl.program_id(0)
    eye = one_hot(
        lax.broadcasted_iota(jnp.int32, (LANES, LANES), 0)
        == lax.broadcasted_iota(jnp.int32, (LANES, LANES), 1)
    ).astype(bf16)

    @pl.when(step == 0)
    def _():
        for i, context in enumerate(contexts):
            for k in range(each):
                pltpu.make_async_copy(context.at[k], kv.at[ahead + place[i * each + k]], sem).start()
        if first:
            picked = fresh_ref.shape[0]
            count = picked // page_len
            kv[0:count] = fresh_ref[...].reshape(count, page_len, width)
            kv[count:ahead] = jnp.zeros((ahead - count, page_len, width), bf16)
            position[0:picked, :] = fresh_positions[...]
            position[picked:tile, :] = jnp.full((tile - picked, LANES), FAR_POSITION, jnp.int32)
        positions = positions_ref[...]
        row = lax.broadcasted_iota(jnp.int32, (page_len, positions.shape[1]), 0)
        ones = jnp.ones((positions.shape[1], LANES), bf16)
        row_lanes = lax.broadcasted_iota(jnp.int32, (page_len, LANES), 0)

        def place_rows(t, carry):
            starts = [page_number[t * TILE_PAGES + k] * page_len for k in range(TILE_PAGES)]
            hit = jnp.concatenate([one_hot(row + start == positions) for start in starts], axis=0)
            hidden = jnp.dot(hit.astype(bf16), ones, preferred_element_type=f32)
            plain = jnp.concatenate([row_lanes + start for start in starts], axis=0)
            here = pl.ds(pl.multiple_of(ahead * page_len + t * tile, tile), tile)
            position[here, :] = jnp.where(hidden > 0.0, FAR_POSITION, plain)
            return carry

        lax.fori_loop(0, (pages - ahead) // TILE_PAGES, place_rows, 0)
        used = kv.at[ahead:]
        pltpu.make_async_copy(used, used, sem).wait()

        def turn(t, carry):
            here = pl.ds(t * TILE_PAGES, TILE_PAGES)
            for g in range(KEY_VALUE_HEADS):
                at = (KEY_VALUE_HEADS + g) * LANES
                value = kv[here, :, at : at + LANES].reshape(tile, LANES)
                values[t, g] = nt_dot(eye, value).astype(bf16)
            return carry

        lax.fori_loop(0, pages // TILE_PAGES, turn, 0)

    for g in range(KEY_VALUE_HEADS):
        for i in range(QUERY_GROUP):
            head = g * QUERY_GROUP + i
            query[g, i * block : (i + 1) * block, :] = query_ref[:, head * LANES : (head + 1) * LANES]
    if first:
        mixed[...] = jnp.zeros(mixed.shape, f32)
        stats[0:KEY_VALUE_HEADS, :] = jnp.full((KEY_VALUE_HEADS, lanes), HIDDEN, f32)
        stats[KEY_VALUE_HEADS:, :] = jnp.zeros((KEY_VALUE_HEADS, lanes), f32)
    else:
        mixed[...] = state_in[0][0]
        stats[...] = state_in[1][0]

    sel = sel_ref[0]

    def one_tile(t, carry):
        here = pl.ds(t * TILE_PAGES, TILE_PAGES)
        bias = jnp.where(
            position[pl.ds(pl.multiple_of(t * tile, tile), tile), :] <= sel, 0.0, HIDDEN
        ).astype(f32)

        def score(g):
            key = kv[here, :, g * LANES : (g + 1) * LANES].reshape(tile, LANES)
            return nt_dot(key, query[g])

        upcoming = score(0)
        for g in range(KEY_VALUE_HEADS):
            scores = upcoming
            if g + 1 < KEY_VALUE_HEADS:
                upcoming = score(g + 1)
            raised, shrinks = [], []
            at = KEY_VALUE_HEADS + g
            for n in range(lanes // LANES):
                part = slice(n * LANES, (n + 1) * LANES)
                s = scores[:, part] + bias
                old = stats[g : g + 1, part]
                new = jnp.maximum(old, jnp.max(s, axis=0, keepdims=True))
                p = jnp.exp2((s - new) * scale)
                shrink = jnp.exp2((old - new) * scale)
                stats[at : at + 1, part] = stats[at : at + 1, part] * shrink + jnp.sum(
                    p, axis=0, keepdims=True
                )
                stats[g : g + 1, part] = new
                raised.append(p.astype(bf16))
                shrinks.append(shrink)
            raised = jnp.concatenate(raised, axis=1)
            shrink = jnp.concatenate(shrinks, axis=1)
            mixed[g] = mixed[g] * shrink + jnp.dot(
                values[t, g], raised, preferred_element_type=f32
            )
        return carry

    lax.fori_loop(0, tiles[step], one_tile, 0)

    if last:
        done = []
        for g in range(KEY_VALUE_HEADS):
            at = KEY_VALUE_HEADS + g
            part = (mixed[g] * (1.0 / stats[at : at + 1, :])).astype(bf16)
            done += [part[:, n * LANES : (n + 1) * LANES] for n in range(lanes // LANES)]
        turned = nt_dot(eye, jnp.concatenate(done, axis=0)).astype(bf16)
        for n in range(len(done)):
            for i in range(LANES // block):
                head = n * (LANES // block) + i
                outs[0][:, head * LANES : (head + 1) * LANES] = turned[
                    i * block : (i + 1) * block, n * LANES : (n + 1) * LANES
                ]
    else:
        outs[0][0] = mixed[...]
        outs[1][0] = stats[...]


def attend(first, last, order, sel_lanes, positions, queries, fresh, state, contexts):
    picked, features = queries.shape
    each, page_len, width = contexts[0].shape
    pages = each * len(contexts) + (TILE_PAGES if first else 0)
    steps = picked // QUERY_BLOCK
    lanes = QUERY_GROUP * QUERY_BLOCK
    wide = pl.BlockSpec((QUERY_BLOCK, features), lambda b, *_: (b, 0))
    state_specs = [
        pl.BlockSpec((1, KEY_VALUE_HEADS, LANES, lanes), lambda b, *_: (b, 0, 0, 0)),
        pl.BlockSpec((1, 2 * KEY_VALUE_HEADS, lanes), lambda b, *_: (b, 0, 0)),
    ]
    state_shapes = [
        jax.ShapeDtypeStruct((steps, KEY_VALUE_HEADS, LANES, lanes), jnp.float32),
        jax.ShapeDtypeStruct((steps, 2 * KEY_VALUE_HEADS, lanes), jnp.float32),
    ]
    share = 0.6
    return pl.pallas_call(
        functools.partial(attend_kernel, first, last, len(contexts)),
        grid_spec=pltpu.PrefetchScalarGridSpec(
            num_scalar_prefetch=3,
            grid=(steps,),
            in_specs=[
                pl.BlockSpec((1, 1, LANES), lambda b, *_: (b, 0, 0)),
                pl.BlockSpec(positions.shape, lambda b, *_: (0, 0)),
                wide,
                *[pl.BlockSpec(x.shape, lambda b, *_: (0, 0)) for x in fresh if first],
                *([] if first else state_specs),
                *[pl.BlockSpec(memory_space=pltpu.HBM)] * len(contexts),
            ],
            out_specs=[wide] if last else state_specs,
            scratch_shapes=[
                pltpu.VMEM((pages, page_len, width), jnp.bfloat16),
                pltpu.VMEM(
                    (pages // TILE_PAGES, KEY_VALUE_HEADS, LANES, TILE_PAGES * page_len), jnp.bfloat16
                ),
                pltpu.VMEM((pages * page_len, LANES), jnp.int32),
                pltpu.VMEM((KEY_VALUE_HEADS, lanes, LANES), jnp.bfloat16),
                pltpu.VMEM((KEY_VALUE_HEADS, LANES, lanes), jnp.float32),
                pltpu.VMEM((2 * KEY_VALUE_HEADS, lanes), jnp.float32),
                pltpu.SemaphoreType.DMA,
            ],
        ),
        out_shape=[jax.ShapeDtypeStruct((picked, features), jnp.bfloat16)] if last else state_shapes,
        compiler_params=pltpu.CompilerParams(
            dimension_semantics=("arbitrary",), vmem_limit_bytes=VMEM_LIMIT
        ),
        cost_estimate=pl.CostEstimate(
            flops=int(share * 8 * picked * features * pages * page_len),
            bytes_accessed=2 * pages * page_len * width + 6 * picked * features,
            transcendentals=int(share * picked * features // LANES * pages * page_len),
        ),
    )(*order, sel_lanes, positions, queries, *[x for x in fresh if first], *state, *contexts)


def page_order(slots, positions, own, hold, capacity, groups, page_len):
    pages = slots.shape[0]
    number = jnp.arange(pages)
    before = number[None, :] < number[:, None]
    owners = slots // hold
    ranks = jnp.sum(((owners[None, :] == owners[:, None]) & before).astype(jnp.int32), axis=1)
    distance = owners ^ own
    last_page = positions.reshape(-1, QUERY_BLOCK)[:, -1] // page_len
    orders = []
    for at, group in enumerate(groups):
        if group is None:
            arrival = owners * capacity + ranks
            count = pages
        else:
            arrival = jnp.full((pages,), -1, jnp.int32)
            for i, d in enumerate(group):
                arrival = jnp.where(distance == d, i * capacity + ranks, arrival)
            count = len(group) * capacity
        member = arrival >= 0
        place = jnp.sum((member[None, :] & before).astype(jnp.int32), axis=1)
        index = jnp.arange(count)[:, None]
        places = jnp.sum(jnp.where(arrival[None, :] == index, place[None, :], 0), axis=1)
        page = jnp.sum(
            jnp.where(member[None, :] & (place[None, :] == index), number[None, :], 0), axis=1
        )
        seen = jnp.sum((page[None, :] <= last_page[:, None]).astype(jnp.int32), axis=1)
        orders.append((places, page, (seen + TILE_PAGES - 1) // TILE_PAGES + (at == 0)))
    return orders


def per_device(store, page_table, sel_pos, fresh_kv, queries):
    holders = lax.axis_size("store")
    hold, page_len, width = store.shape
    pages = page_table.shape[1]
    picked = sel_pos.shape[1]
    capacity = max(1, pages // holders)
    hbm = pl.BlockSpec(memory_space=pltpu.HBM)
    vmem = pl.BlockSpec(memory_space=pltpu.VMEM)
    dma = pltpu.SemaphoreType.DMA
    params = pltpu.CompilerParams(vmem_limit_bytes=VMEM_LIMIT)
    own = lax.axis_index("store")
    own_word = own.reshape(1).astype(jnp.int32)
    fresh = fresh_kv[0]
    wide = pltpu.VMEM((8, -(-picked // LANES) * LANES), jnp.int32)
    if holders == 16:
        first = (8, 12)
        groups = [(0, 8, 12, 4), (5, 1, 9, 6), (13, 7, 10, 2, 14, 3), (11, 15)]
        others = [d for group in groups for d in group if d not in first]
    else:
        first = ()
        groups = [None]
        others = None

    def swap(x, d):
        return lax.ppermute(x, "store", [(h, h ^ d) for h in range(holders)])

    def exchange(x):
        return lax.all_to_all(x, "store", split_axis=0, concat_axis=0, tiled=True)

    index, *lists = pl.pallas_call(
        functools.partial(index_kernel, hold, page_len, first),
        grid_spec=pltpu.PrefetchScalarGridSpec(
            num_scalar_prefetch=1,
            grid=(1,),
            in_specs=[vmem, vmem],
            out_specs=[vmem] * (1 + len(first)),
            scratch_shapes=[wide],
        ),
        out_shape=[
            jax.ShapeDtypeStruct((holders, 2, LANES), jnp.int32),
            *[jax.ShapeDtypeStruct((1, 2, LANES), jnp.int32)] * len(first),
        ],
        compiler_params=params,
    )(own_word, page_table, sel_pos)
    arrived = {}
    if first:
        lists = [swap(x, d) for x, d in zip(lists, first)]
        parts = pl.pallas_call(
            functools.partial(first_gather_kernel, len(first)),
            grid_spec=pltpu.PrefetchScalarGridSpec(
                num_scalar_prefetch=len(first),
                grid=(1,),
                in_specs=[hbm],
                out_specs=[hbm] * len(first),
                scratch_shapes=[
                    pltpu.VMEM((len(first), capacity, page_len, width), store.dtype),
                    dma,
                    dma,
                ],
            ),
            out_shape=[jax.ShapeDtypeStruct((capacity, page_len, width), store.dtype)] * len(first),
            compiler_params=params,
        )(*lists, store)
        parts, index, table, positions = lax.optimization_barrier(
            (parts, index, page_table, sel_pos)
        )
        arrived = {d: swap(part, d) for d, part in zip(first, parts)}
    else:
        table, positions = page_table, sel_pos
    index_in = exchange(index)
    if first:
        index_in, _ = lax.optimization_barrier((index_in, arrived[first[0]]))

    packed = pl.pallas_call(
        functools.partial(rows_kernel, hold, page_len),
        out_shape=jax.ShapeDtypeStruct((holders, ROW_SLOTS, width), store.dtype),
        scratch_shapes=[wide],
        compiler_params=params,
    )(table, positions, fresh)

    each = jax.ShapeDtypeStruct((capacity, page_len, width), store.dtype)
    whole = jax.ShapeDtypeStruct((holders, capacity, page_len, width), store.dtype)
    parts = pl.pallas_call(
        functools.partial(gather_kernel, capacity, others),
        grid_spec=pltpu.PrefetchScalarGridSpec(
            num_scalar_prefetch=2,
            grid=(1,),
            in_specs=[hbm],
            out_specs=[hbm] * (len(others) if others else 1),
            scratch_shapes=[pltpu.VMEM(store.shape, store.dtype), dma, dma],
        ),
        out_shape=[each] * len(others) if others else [whole],
        compiler_params=params,
    )(own_word, index_in, store)
    parts, packed, table, positions = lax.optimization_barrier((parts, packed, table, positions))
    if others:
        for d, part in zip(others, parts):
            arrived[d] = swap(part, d) if d else part
        contexts = [[arrived[d] for d in group] for group in groups]
    else:
        contexts = [[exchange(parts[0]).reshape(pages, page_len, width)]]
    rows_in = exchange(packed)

    store_out = pl.pallas_call(
        write_back_kernel,
        grid_spec=pltpu.PrefetchScalarGridSpec(
            num_scalar_prefetch=1,
            grid=(1,),
            in_specs=[vmem, hbm, hbm],
            out_specs=hbm,
            scratch_shapes=[
                pltpu.VMEM(store.shape, store.dtype),
                pltpu.VMEM((holders, ROW_SLOTS, width), store.dtype),
                pltpu.VMEM((holders, capacity, page_len, width), store.dtype),
                dma,
                dma,
                dma,
            ],
        ),
        out_shape=jax.ShapeDtypeStruct(store.shape, store.dtype),
        compiler_params=params,
        cost_estimate=pl.CostEstimate(flops=0, bytes_accessed=4 * store.size, transcendentals=0),
    )(index_in, index_in, store, rows_in)

    orders = page_order(table[0], positions[0], own, hold, capacity, groups, page_len)
    sel_lanes = jnp.tile(positions.reshape(-1, 1, QUERY_BLOCK), (1, 1, LANES // QUERY_BLOCK))
    sel_rows = jnp.broadcast_to(positions.reshape(picked, 1), (picked, LANES))
    state = ()
    for at, (arrays, order) in enumerate(zip(contexts, orders)):
        if at == 1:
            store_out, sel_lanes = lax.optimization_barrier((store_out, sel_lanes))
        state = attend(
            at == 0,
            at == len(groups) - 1,
            order,
            sel_lanes,
            positions,
            queries[0],
            (fresh, sel_rows),
            state,
            arrays,
        )
    return (state[0][None], store_out)


def solution(mesh):
    return jax.shard_map(
        per_device,
        mesh=mesh,
        in_specs=(
            P(("groups", "store"), None, None),
            P(("groups", "store"), None),
            P(("groups", "store"), None),
            P(("groups", "store"), None, None),
            P(("groups", "store"), None, None),
        ),
        out_specs=(P(("groups", "store"), None, None), P(("groups", "store"), None, None)),
        check_vma=False,
    )
```

```python
import functools

import jax
import jax.numpy as jnp
from jax import lax
from jax.experimental import pallas as pl
from jax.experimental.pallas import tpu as pltpu
from jax.sharding import PartitionSpec as P

HEAD_WIDTH = 128
KEY_VALUE_HEADS = 4
QUERY_GROUP = 12
SELP = 2
LANES = 128
ROW_SLOTS = 16
VMEM_LIMIT = 60 * 1024 * 1024
QUERY_BLOCK = 32
TILE_PAGES = 32
LATE_TILE_PAGES = 16
FRESH_PAGES = 16
HIDDEN = -1e30
FAR_POSITION = 1 << 24


def nt_dot(a, b):
    return lax.dot_general(a, b, (((1,), (1,)), ((), ())), preferred_element_type=jnp.float32)


def one_hot(condition):
    return jnp.where(condition, 1.0, 0.0)


def pair_places(hold, page_len, table_ref, sel_ref, wide):
    pages = table_ref.shape[1]
    picked = sel_ref.shape[1]
    f32 = jnp.float32
    slots = jnp.broadcast_to(table_ref[...], (pages, pages))
    owners = slots // hold
    local_row = (slots - owners * hold).astype(f32)[0:1]
    owner_row = owners.astype(f32)
    owner_col = owner_row.T
    sub = lax.broadcasted_iota(jnp.int32, (pages, pages), 0)
    lane = lax.broadcasted_iota(jnp.int32, (pages, pages), 1)
    earlier = one_hot((owner_row == owner_col) & (lane < sub))
    rank_col = jnp.sum(earlier, axis=1, keepdims=True)

    wide[...] = jnp.full(wide.shape, -1, jnp.int32)
    wide[0:1, 0:picked] = sel_ref[...]
    position = wide[...]
    page = lax.shift_right_arithmetic(position, page_len.bit_length() - 1)
    offset = (position & (page_len - 1)).astype(f32)[0:1]
    lane_wide = lax.broadcasted_iota(jnp.int32, wide.shape, 1)
    second = one_hot((page == pltpu.roll(page, 1, axis=1)) & (lane_wide > 0))[0:1]
    valid = lane_wide[0:1] < picked
    sub_wide = lax.broadcasted_iota(jnp.int32, (pages, wide.shape[1]), 0)
    in_page = one_hot(sub_wide == page[0:1])
    owner = jnp.sum(in_page * owner_col[:, 0:1], axis=0, keepdims=True)
    rank = jnp.sum(in_page * rank_col, axis=0, keepdims=True)
    return owner_row[0:1], local_row, rank_col, owner, rank, second, offset, valid


def index_kernel(hold, page_len, first, own, table_ref, sel_ref, out_ref, *rest):
    first_refs, wide = rest[:-1], rest[-1]
    holders = out_ref.shape[0]
    pages = table_ref.shape[1]
    f32 = jnp.float32
    bf16 = jnp.bfloat16
    owner_row, local_row, rank_col, owner, rank, second, offset, valid = pair_places(
        hold, page_len, table_ref, sel_ref, wide
    )
    holder = lax.broadcasted_iota(jnp.int32, (holders, pages), 0).astype(f32)
    owned = jnp.where(holder == owner_row, local_row, 0.0)
    lane = lax.broadcasted_iota(jnp.int32, (pages, LANES), 1).astype(f32)
    numbers = jnp.dot(
        owned.astype(bf16), one_hot(lane == rank_col).astype(bf16), preferred_element_type=f32
    )
    holder_wide = lax.broadcasted_iota(jnp.int32, (holders, wide.shape[1]), 0).astype(f32)
    marked = jnp.where((holder_wide == owner) & valid, rank * page_len + offset + 1.0, 0.0)
    place_lane = lax.broadcasted_iota(jnp.int32, (LANES, wide.shape[1]), 0).astype(f32)
    at_place = one_hot(place_lane == SELP * rank + second)
    targets = nt_dot(marked.astype(bf16), at_place.astype(bf16))
    for h in range(holders):
        out_ref[h, 0:1, :] = numbers[h : h + 1, :].astype(jnp.int32)
        out_ref[h, 1:2, :] = targets[h : h + 1, :].astype(jnp.int32)
    for d, ref in zip(first, first_refs):
        ref[0] = out_ref[own[0] ^ d]


def rows_kernel(hold, page_len, table_ref, sel_ref, fresh_ref, packed, wide):
    holders = packed.shape[0]
    picked = sel_ref.shape[1]
    f32 = jnp.float32
    _, _, _, owner, rank, second, _, valid = pair_places(hold, page_len, table_ref, sel_ref, wide)
    spot = jnp.where(valid, owner * ROW_SLOTS + SELP * rank + second, -1.0)[:, 0:picked]
    step = min(holders, 16)
    for start in range(0, holders, step):
        spot_id = lax.broadcasted_iota(jnp.int32, (step * ROW_SLOTS, picked), 0).astype(f32)
        choose = one_hot(spot_id + float(start * ROW_SLOTS) == spot).astype(jnp.bfloat16)
        rows = jnp.dot(choose, fresh_ref[...], preferred_element_type=f32).astype(jnp.bfloat16)
        packed[start : start + step] = rows.reshape(step, ROW_SLOTS, fresh_ref.shape[1])


def first_gather_kernel(count, *refs):
    lists, store_hbm, sends = refs[:count], refs[count], refs[count + 1 : 2 * count + 1]
    held, load_sem, send_sem = refs[2 * count + 1 :]
    capacity = held.shape[1]
    for i, numbers in enumerate(lists):
        for k in range(capacity):
            pltpu.make_async_copy(store_hbm.at[numbers[0, 0, k]], held.at[i, k], load_sem).start()
    pltpu.make_async_copy(held, held, load_sem).wait()
    for i, send in enumerate(sends):
        pltpu.make_async_copy(held.at[i], send, send_sem).start()
    pltpu.make_async_copy(held, held, send_sem).wait()


def gather_kernel(capacity, distances, own, index, store_hbm, *rest):
    sends, (store, load_sem, send_sem) = rest[:-3], rest[-3:]
    load = pltpu.make_async_copy(store_hbm, store, load_sem)
    load.start()
    load.wait()
    for i in range(len(distances) if distances else index.shape[0]):
        r = own[0] ^ distances[i] if distances else i
        send = sends[i] if distances else sends[0].at[i]
        for k in range(capacity):
            pltpu.make_async_copy(store.at[index[r, 0, k]], send.at[k], send_sem).start()
    for send in sends:
        pltpu.make_async_copy(send, send, send_sem).wait()


def write_back_kernel(index, targets_ref, store_hbm, rows_hbm, store_out, *scratch):
    store, rows, blended, load_sem, rows_sem, out_sem = scratch
    holders, capacity, page_len, width = blended.shape
    rows_here = capacity * page_len
    f32 = jnp.float32
    load = pltpu.make_async_copy(store_hbm, store, load_sem)
    load_rows = pltpu.make_async_copy(rows_hbm, rows, rows_sem)
    load.start()
    load_rows.start()
    load_rows.wait()
    load.wait()
    row_id = lax.broadcasted_iota(jnp.int32, (rows_here, ROW_SLOTS), 0)

    def one_request(r, carry):
        hit = one_hot(row_id == targets_ref[r][1:2, 0:ROW_SLOTS] - 1)
        keep = 1.0 - jnp.sum(hit, axis=1, keepdims=True)
        keep = jnp.broadcast_to(keep, (rows_here, LANES)).astype(jnp.bfloat16)
        hit = hit.astype(jnp.bfloat16)
        for c in range(width // LANES):
            lanes = slice(c * LANES, (c + 1) * LANES)
            fresh = jnp.dot(hit, rows[r, :, lanes], preferred_element_type=f32).astype(jnp.bfloat16)
            for k in range(capacity):
                part = slice(k * page_len, (k + 1) * page_len)
                blended[r, k, :, lanes] = store[index[r, 0, k], :, lanes] * keep[part] + fresh[part]
        for k in range(capacity):
            pltpu.make_async_copy(blended.at[r, k], store_out.at[index[r, 0, k]], out_sem).start()
        return carry

    lax.fori_loop(0, holders, one_request, 0)
    pltpu.make_async_copy(store_out, store_out, out_sem).wait()


def attend_kernel(first, last, tile_pages, sources, place, page_number, tiles, *rest):
    sel_ref, positions_ref, query_ref, *rest = rest
    if first:
        fresh_ref, fresh_positions, *rest = rest
    state_in = () if first else rest[:2]
    rest = rest if first else rest[2:]
    contexts, rest = rest[:sources], rest[sources:]
    outs, rest = (rest[:1], rest[1:]) if last else (rest[:2], rest[2:])
    kv, values, position, query, scores, raised, mixed, stats, sem = rest
    pages, page_len, width = kv.shape
    each = contexts[0].shape[0]
    ahead = FRESH_PAGES if first else 0
    block = query_ref.shape[0]
    tile = tile_pages * page_len
    lanes = QUERY_GROUP * block
    scale = 1.4426950408889634 / HEAD_WIDTH**0.5
    f32 = jnp.float32
    bf16 = jnp.bfloat16
    step = pl.program_id(0)
    eye = one_hot(
        lax.broadcasted_iota(jnp.int32, (LANES, LANES), 0)
        == lax.broadcasted_iota(jnp.int32, (LANES, LANES), 1)
    ).astype(bf16)

    @pl.when(step == 0)
    def _():
        for i, context in enumerate(contexts):
            for k in range(each):
                pltpu.make_async_copy(context.at[k], kv.at[ahead + place[i * each + k]], sem).start()
        if first:
            picked = fresh_ref.shape[0]
            count = picked // page_len
            kv[0:count] = fresh_ref[...].reshape(count, page_len, width)
            kv[count:ahead] = jnp.zeros((ahead - count, page_len, width), bf16)
            position[0:picked, :] = fresh_positions[...]
            start = ahead * page_len
            position[picked:start, :] = jnp.full((start - picked, LANES), FAR_POSITION, jnp.int32)
        positions = positions_ref[...]
        row = lax.broadcasted_iota(jnp.int32, (page_len, positions.shape[1]), 0)
        ones = jnp.ones((positions.shape[1], LANES), bf16)
        row_lanes = lax.broadcasted_iota(jnp.int32, (page_len, LANES), 0)

        def place_rows(t, carry):
            starts = [page_number[t * FRESH_PAGES + k] * page_len for k in range(FRESH_PAGES)]
            hit = jnp.concatenate([one_hot(row + start == positions) for start in starts], axis=0)
            hidden = jnp.dot(hit.astype(bf16), ones, preferred_element_type=f32)
            plain = jnp.concatenate([row_lanes + start for start in starts], axis=0)
            some = FRESH_PAGES * page_len
            here = pl.ds(pl.multiple_of(ahead * page_len + t * some, some), some)
            position[here, :] = jnp.where(hidden > 0.0, FAR_POSITION, plain)
            return carry

        lax.fori_loop(0, (pages - ahead) // FRESH_PAGES, place_rows, 0)
        used = kv.at[ahead:]
        pltpu.make_async_copy(used, used, sem).wait()

        def turn(t, carry):
            here = pl.ds(t * tile_pages, tile_pages)
            for g in range(KEY_VALUE_HEADS):
                at = (KEY_VALUE_HEADS + g) * LANES
                value = kv[here, :, at : at + LANES].reshape(tile, LANES)
                values[t, g] = nt_dot(eye, value).astype(bf16)
            return carry

        lax.fori_loop(0, pages // tile_pages, turn, 0)

    for g in range(KEY_VALUE_HEADS):
        for i in range(QUERY_GROUP):
            head = g * QUERY_GROUP + i
            query[g, i * block : (i + 1) * block, :] = query_ref[:, head * LANES : (head + 1) * LANES]
    if first:
        mixed[...] = jnp.zeros(mixed.shape, f32)
        stats[0:KEY_VALUE_HEADS, :] = jnp.full((KEY_VALUE_HEADS, lanes), HIDDEN, f32)
        stats[KEY_VALUE_HEADS:, :] = jnp.zeros((KEY_VALUE_HEADS, lanes), f32)
    else:
        mixed[...] = state_in[0][0]
        stats[...] = state_in[1][0]

    sel = sel_ref[0]

    def one_tile(t, carry):
        here = pl.ds(t * tile_pages, tile_pages)
        bias = jnp.where(
            position[pl.ds(pl.multiple_of(t * tile, tile), tile), :] <= sel, 0.0, HIDDEN
        ).astype(f32)

        parts = [slice(n * LANES, (n + 1) * LANES) for n in range(lanes // LANES)]
        chains = [(g, part) for g in range(KEY_VALUE_HEADS) for part in parts]
        for g in range(KEY_VALUE_HEADS):
            key = kv[here, :, g * LANES : (g + 1) * LANES].reshape(tile, LANES)
            product = nt_dot(key, query[g])
            for part in parts:
                scores[g, :, part] = product[:, part] + bias
        peaks, shrinks = [], []
        for g, part in chains:
            old = stats[g : g + 1, part]
            new = jnp.maximum(old, jnp.max(scores[g, :, part], axis=0, keepdims=True))
            stats[g : g + 1, part] = new
            peaks.append(new)
            shrinks.append(jnp.exp2((old - new) * scale))
        for (g, part), new, shrink in zip(chains, peaks, shrinks):
            at = KEY_VALUE_HEADS + g
            p = jnp.exp2((scores[g, :, part] - new) * scale)
            stats[at : at + 1, part] = stats[at : at + 1, part] * shrink + jnp.sum(
                p, axis=0, keepdims=True
            )
            raised[g, :, part] = p.astype(bf16)
        for g in range(KEY_VALUE_HEADS):
            shrink = jnp.concatenate(shrinks[g * len(parts) : (g + 1) * len(parts)], axis=1)
            mixed[g] = mixed[g] * shrink + jnp.dot(
                values[t, g], raised[g], preferred_element_type=f32
            )
        return carry

    lax.fori_loop(0, tiles[step], one_tile, 0)

    if last:
        done = []
        for g in range(KEY_VALUE_HEADS):
            at = KEY_VALUE_HEADS + g
            part = (mixed[g] * (1.0 / stats[at : at + 1, :])).astype(bf16)
            done += [part[:, n * LANES : (n + 1) * LANES] for n in range(lanes // LANES)]
        turned = nt_dot(eye, jnp.concatenate(done, axis=0)).astype(bf16)
        for n in range(len(done)):
            for i in range(LANES // block):
                head = n * (LANES // block) + i
                outs[0][:, head * LANES : (head + 1) * LANES] = turned[
                    i * block : (i + 1) * block, n * LANES : (n + 1) * LANES
                ]
    else:
        outs[0][0] = mixed[...]
        outs[1][0] = stats[...]


def attend(first, last, tile_pages, order, sel_lanes, positions, queries, fresh, state, contexts):
    picked, features = queries.shape
    each, page_len, width = contexts[0].shape
    pages = each * len(contexts) + (FRESH_PAGES if first else 0)
    steps = picked // QUERY_BLOCK
    lanes = QUERY_GROUP * QUERY_BLOCK
    wide = pl.BlockSpec((QUERY_BLOCK, features), lambda b, *_: (b, 0))
    state_specs = [
        pl.BlockSpec((1, KEY_VALUE_HEADS, LANES, lanes), lambda b, *_: (b, 0, 0, 0)),
        pl.BlockSpec((1, 2 * KEY_VALUE_HEADS, lanes), lambda b, *_: (b, 0, 0)),
    ]
    state_shapes = [
        jax.ShapeDtypeStruct((steps, KEY_VALUE_HEADS, LANES, lanes), jnp.float32),
        jax.ShapeDtypeStruct((steps, 2 * KEY_VALUE_HEADS, lanes), jnp.float32),
    ]
    share = 0.6
    return pl.pallas_call(
        functools.partial(attend_kernel, first, last, tile_pages, len(contexts)),
        grid_spec=pltpu.PrefetchScalarGridSpec(
            num_scalar_prefetch=3,
            grid=(steps,),
            in_specs=[
                pl.BlockSpec((1, 1, LANES), lambda b, *_: (b, 0, 0)),
                pl.BlockSpec(positions.shape, lambda b, *_: (0, 0)),
                wide,
                *[pl.BlockSpec(x.shape, lambda b, *_: (0, 0)) for x in fresh if first],
                *([] if first else state_specs),
                *[pl.BlockSpec(memory_space=pltpu.HBM)] * len(contexts),
            ],
            out_specs=[wide] if last else state_specs,
            scratch_shapes=[
                pltpu.VMEM((pages, page_len, width), jnp.bfloat16),
                pltpu.VMEM(
                    (pages // tile_pages, KEY_VALUE_HEADS, LANES, tile_pages * page_len), jnp.bfloat16
                ),
                pltpu.VMEM((pages * page_len, LANES), jnp.int32),
                pltpu.VMEM((KEY_VALUE_HEADS, lanes, LANES), jnp.bfloat16),
                pltpu.VMEM((KEY_VALUE_HEADS, tile_pages * page_len, lanes), jnp.float32),
                pltpu.VMEM((KEY_VALUE_HEADS, tile_pages * page_len, lanes), jnp.bfloat16),
                pltpu.VMEM((KEY_VALUE_HEADS, LANES, lanes), jnp.float32),
                pltpu.VMEM((2 * KEY_VALUE_HEADS, lanes), jnp.float32),
                pltpu.SemaphoreType.DMA,
            ],
        ),
        out_shape=[jax.ShapeDtypeStruct((picked, features), jnp.bfloat16)] if last else state_shapes,
        compiler_params=pltpu.CompilerParams(
            dimension_semantics=("arbitrary",), vmem_limit_bytes=VMEM_LIMIT
        ),
        cost_estimate=pl.CostEstimate(
            flops=int(share * 8 * picked * features * pages * page_len),
            bytes_accessed=2 * pages * page_len * width + 6 * picked * features,
            transcendentals=int(share * picked * features // LANES * pages * page_len),
        ),
    )(*order, sel_lanes, positions, queries, *[x for x in fresh if first], *state, *contexts)


def page_order(slots, positions, own, hold, capacity, groups, tiles, page_len):
    pages = slots.shape[0]
    number = jnp.arange(pages)
    before = number[None, :] < number[:, None]
    owners = slots // hold
    ranks = jnp.sum(((owners[None, :] == owners[:, None]) & before).astype(jnp.int32), axis=1)
    distance = owners ^ own
    last_page = positions.reshape(-1, QUERY_BLOCK)[:, -1] // page_len
    orders = []
    for at, (group, tile_pages) in enumerate(zip(groups, tiles)):
        if group is None:
            arrival = owners * capacity + ranks
            count = pages
        else:
            arrival = jnp.full((pages,), -1, jnp.int32)
            for i, d in enumerate(group):
                arrival = jnp.where(distance == d, i * capacity + ranks, arrival)
            count = len(group) * capacity
        member = arrival >= 0
        place = jnp.sum((member[None, :] & before).astype(jnp.int32), axis=1)
        index = jnp.arange(count)[:, None]
        places = jnp.sum(jnp.where(arrival[None, :] == index, place[None, :], 0), axis=1)
        page = jnp.sum(
            jnp.where(member[None, :] & (place[None, :] == index), number[None, :], 0), axis=1
        )
        seen = jnp.sum((page[None, :] <= last_page[:, None]).astype(jnp.int32), axis=1)
        seen = seen + (FRESH_PAGES if at == 0 else 0)
        orders.append((places, page, (seen + tile_pages - 1) // tile_pages))
    return orders


def per_device(store, page_table, sel_pos, fresh_kv, queries):
    holders = lax.axis_size("store")
    hold, page_len, width = store.shape
    pages = page_table.shape[1]
    picked = sel_pos.shape[1]
    capacity = max(1, pages // holders)
    hbm = pl.BlockSpec(memory_space=pltpu.HBM)
    vmem = pl.BlockSpec(memory_space=pltpu.VMEM)
    dma = pltpu.SemaphoreType.DMA
    params = pltpu.CompilerParams(vmem_limit_bytes=VMEM_LIMIT)
    own = lax.axis_index("store")
    own_word = own.reshape(1).astype(jnp.int32)
    fresh = fresh_kv[0]
    wide = pltpu.VMEM((8, -(-picked // LANES) * LANES), jnp.int32)
    if holders == 16:
        first = (8, 12)
        groups = [(0, 8, 12, 4, 5, 1), (9, 6, 13, 7, 10, 2, 14, 3), (11, 15)]
        others = [d for group in groups for d in group if d not in first]
    else:
        first = ()
        groups = [None]
        others = None

    def swap(x, d):
        return lax.ppermute(x, "store", [(h, h ^ d) for h in range(holders)])

    def exchange(x):
        return lax.all_to_all(x, "store", split_axis=0, concat_axis=0, tiled=True)

    index, *lists = pl.pallas_call(
        functools.partial(index_kernel, hold, page_len, first),
        grid_spec=pltpu.PrefetchScalarGridSpec(
            num_scalar_prefetch=1,
            grid=(1,),
            in_specs=[vmem, vmem],
            out_specs=[vmem] * (1 + len(first)),
            scratch_shapes=[wide],
        ),
        out_shape=[
            jax.ShapeDtypeStruct((holders, 2, LANES), jnp.int32),
            *[jax.ShapeDtypeStruct((1, 2, LANES), jnp.int32)] * len(first),
        ],
        compiler_params=params,
    )(own_word, page_table, sel_pos)
    arrived = {}
    if first:
        lists = [swap(x, d) for x, d in zip(lists, first)]
        parts = pl.pallas_call(
            functools.partial(first_gather_kernel, len(first)),
            grid_spec=pltpu.PrefetchScalarGridSpec(
                num_scalar_prefetch=len(first),
                grid=(1,),
                in_specs=[hbm],
                out_specs=[hbm] * len(first),
                scratch_shapes=[
                    pltpu.VMEM((len(first), capacity, page_len, width), store.dtype),
                    dma,
                    dma,
                ],
            ),
            out_shape=[jax.ShapeDtypeStruct((capacity, page_len, width), store.dtype)] * len(first),
            compiler_params=params,
        )(*lists, store)
        parts, index, table, positions = lax.optimization_barrier(
            (parts, index, page_table, sel_pos)
        )
        arrived = {d: swap(part, d) for d, part in zip(first, parts)}
    else:
        table, positions = page_table, sel_pos
    index_in = exchange(index)

    packed = pl.pallas_call(
        functools.partial(rows_kernel, hold, page_len),
        out_shape=jax.ShapeDtypeStruct((holders, ROW_SLOTS, width), store.dtype),
        scratch_shapes=[wide],
        compiler_params=params,
    )(table, positions, fresh)

    each = jax.ShapeDtypeStruct((capacity, page_len, width), store.dtype)
    whole = jax.ShapeDtypeStruct((holders, capacity, page_len, width), store.dtype)
    parts = pl.pallas_call(
        functools.partial(gather_kernel, capacity, others),
        grid_spec=pltpu.PrefetchScalarGridSpec(
            num_scalar_prefetch=2,
            grid=(1,),
            in_specs=[hbm],
            out_specs=[hbm] * (len(others) if others else 1),
            scratch_shapes=[pltpu.VMEM(store.shape, store.dtype), dma, dma],
        ),
        out_shape=[each] * len(others) if others else [whole],
        compiler_params=params,
    )(own_word, index_in, store)
    parts, packed, table, positions = lax.optimization_barrier((parts, packed, table, positions))
    if others:
        for d, part in zip(others, parts):
            arrived[d] = swap(part, d) if d else part
        contexts = [[arrived[d] for d in group] for group in groups]
    else:
        contexts = [[exchange(parts[0]).reshape(pages, page_len, width)]]
    rows_in = exchange(packed)

    store_out = pl.pallas_call(
        write_back_kernel,
        grid_spec=pltpu.PrefetchScalarGridSpec(
            num_scalar_prefetch=1,
            grid=(1,),
            in_specs=[vmem, hbm, hbm],
            out_specs=hbm,
            scratch_shapes=[
                pltpu.VMEM(store.shape, store.dtype),
                pltpu.VMEM((holders, ROW_SLOTS, width), store.dtype),
                pltpu.VMEM((holders, capacity, page_len, width), store.dtype),
                dma,
                dma,
                dma,
            ],
        ),
        out_shape=jax.ShapeDtypeStruct(store.shape, store.dtype),
        compiler_params=params,
        cost_estimate=pl.CostEstimate(flops=0, bytes_accessed=4 * store.size, transcendentals=0),
    )(index_in, index_in, store, rows_in)

    tiles = [LATE_TILE_PAGES if at == len(groups) - 1 else TILE_PAGES for at in range(len(groups))]
    orders = page_order(table[0], positions[0], own, hold, capacity, groups, tiles, page_len)
    sel_lanes = jnp.tile(positions.reshape(-1, 1, QUERY_BLOCK), (1, 1, LANES // QUERY_BLOCK))
    sel_rows = jnp.broadcast_to(positions.reshape(picked, 1), (picked, LANES))
    store_out, sel_lanes = lax.optimization_barrier((store_out, sel_lanes))
    state = ()
    for at, (arrays, order) in enumerate(zip(contexts, orders)):
        state = attend(
            at == 0,
            at == len(groups) - 1,
            tiles[at],
            order,
            sel_lanes,
            positions,
            queries[0],
            (fresh, sel_rows),
            state,
            arrays,
        )
    return (state[0][None], store_out)


def solution(mesh):
    return jax.shard_map(
        per_device,
        mesh=mesh,
        in_specs=(
            P(("groups", "store"), None, None),
            P(("groups", "store"), None),
            P(("groups", "store"), None),
            P(("groups", "store"), None, None),
            P(("groups", "store"), None, None),
        ),
        out_specs=(P(("groups", "store"), None, None), P(("groups", "store"), None, None)),
        check_vma=False,
    )
```

```python
import functools

import jax
import jax.numpy as jnp
from jax import lax
from jax.experimental import pallas as pl
from jax.experimental.pallas import tpu as pltpu
from jax.sharding import PartitionSpec as P

HEAD_WIDTH = 128
KEY_VALUE_HEADS = 4
QUERY_GROUP = 12
SELP = 2
LANES = 128
ROW_SLOTS = 16
VMEM_LIMIT = 60 * 1024 * 1024
QUERY_BLOCK = 32
TILE_PAGES = 16
HIDDEN = -1e30
FAR_POSITION = 1 << 24


def nt_dot(a, b):
    return lax.dot_general(a, b, (((1,), (1,)), ((), ())), preferred_element_type=jnp.float32)


def one_hot(condition):
    return jnp.where(condition, 1.0, 0.0)


def pair_places(hold, page_len, table_ref, sel_ref, wide):
    pages = table_ref.shape[1]
    picked = sel_ref.shape[1]
    f32 = jnp.float32
    slots = jnp.broadcast_to(table_ref[...], (pages, pages))
    owners = slots // hold
    local_row = (slots - owners * hold).astype(f32)[0:1]
    owner_row = owners.astype(f32)
    owner_col = owner_row.T
    sub = lax.broadcasted_iota(jnp.int32, (pages, pages), 0)
    lane = lax.broadcasted_iota(jnp.int32, (pages, pages), 1)
    earlier = one_hot((owner_row == owner_col) & (lane < sub))
    rank_col = jnp.sum(earlier, axis=1, keepdims=True)

    wide[...] = jnp.full(wide.shape, -1, jnp.int32)
    wide[0:1, 0:picked] = sel_ref[...]
    position = wide[...]
    page = lax.shift_right_arithmetic(position, page_len.bit_length() - 1)
    offset = (position & (page_len - 1)).astype(f32)[0:1]
    lane_wide = lax.broadcasted_iota(jnp.int32, wide.shape, 1)
    second = one_hot((page == pltpu.roll(page, 1, axis=1)) & (lane_wide > 0))[0:1]
    valid = lane_wide[0:1] < picked
    sub_wide = lax.broadcasted_iota(jnp.int32, (pages, wide.shape[1]), 0)
    in_page = one_hot(sub_wide == page[0:1])
    owner = jnp.sum(in_page * owner_col[:, 0:1], axis=0, keepdims=True)
    rank = jnp.sum(in_page * rank_col, axis=0, keepdims=True)
    return owner_row[0:1], local_row, rank_col, owner, rank, second, offset, valid


def index_kernel(hold, page_len, first, own, table_ref, sel_ref, out_ref, *rest):
    first_refs, wide = rest[:-1], rest[-1]
    holders = out_ref.shape[0]
    pages = table_ref.shape[1]
    f32 = jnp.float32
    bf16 = jnp.bfloat16
    owner_row, local_row, rank_col, owner, rank, second, offset, valid = pair_places(
        hold, page_len, table_ref, sel_ref, wide
    )
    holder = lax.broadcasted_iota(jnp.int32, (holders, pages), 0).astype(f32)
    owned = jnp.where(holder == owner_row, local_row, 0.0)
    lane = lax.broadcasted_iota(jnp.int32, (pages, LANES), 1).astype(f32)
    numbers = jnp.dot(
        owned.astype(bf16), one_hot(lane == rank_col).astype(bf16), preferred_element_type=f32
    )
    holder_wide = lax.broadcasted_iota(jnp.int32, (holders, wide.shape[1]), 0).astype(f32)
    marked = jnp.where((holder_wide == owner) & valid, rank * page_len + offset + 1.0, 0.0)
    place_lane = lax.broadcasted_iota(jnp.int32, (LANES, wide.shape[1]), 0).astype(f32)
    at_place = one_hot(place_lane == SELP * rank + second)
    targets = nt_dot(marked.astype(bf16), at_place.astype(bf16))
    for h in range(holders):
        out_ref[h, 0:1, :] = numbers[h : h + 1, :].astype(jnp.int32)
        out_ref[h, 1:2, :] = targets[h : h + 1, :].astype(jnp.int32)
    for d, ref in zip(first, first_refs):
        ref[0] = out_ref[own[0] ^ d]


def rows_kernel(hold, page_len, table_ref, sel_ref, fresh_ref, packed, wide):
    holders = packed.shape[0]
    picked = sel_ref.shape[1]
    f32 = jnp.float32
    _, _, _, owner, rank, second, _, valid = pair_places(hold, page_len, table_ref, sel_ref, wide)
    spot = jnp.where(valid, owner * ROW_SLOTS + SELP * rank + second, -1.0)[:, 0:picked]
    step = min(holders, 16)
    for start in range(0, holders, step):
        spot_id = lax.broadcasted_iota(jnp.int32, (step * ROW_SLOTS, picked), 0).astype(f32)
        choose = one_hot(spot_id + float(start * ROW_SLOTS) == spot).astype(jnp.bfloat16)
        rows = jnp.dot(choose, fresh_ref[...], preferred_element_type=f32).astype(jnp.bfloat16)
        packed[start : start + step] = rows.reshape(step, ROW_SLOTS, fresh_ref.shape[1])


def first_gather_kernel(count, *refs):
    lists, store_hbm, sends = refs[:count], refs[count], refs[count + 1 : 2 * count + 1]
    held, load_sem, send_sem = refs[2 * count + 1 :]
    capacity = held.shape[1]
    for i, numbers in enumerate(lists):
        for k in range(capacity):
            pltpu.make_async_copy(store_hbm.at[numbers[0, 0, k]], held.at[i, k], load_sem).start()
    pltpu.make_async_copy(held, held, load_sem).wait()
    for i, send in enumerate(sends):
        pltpu.make_async_copy(held.at[i], send, send_sem).start()
    pltpu.make_async_copy(held, held, send_sem).wait()


def gather_kernel(capacity, distances, own, index, store_hbm, *rest):
    sends, (store, load_sem, send_sem) = rest[:-3], rest[-3:]
    load = pltpu.make_async_copy(store_hbm, store, load_sem)
    load.start()
    load.wait()
    for i in range(len(distances) if distances else index.shape[0]):
        r = own[0] ^ distances[i] if distances else i
        send = sends[i] if distances else sends[0].at[i]
        for k in range(capacity):
            pltpu.make_async_copy(store.at[index[r, 0, k]], send.at[k], send_sem).start()
    for send in sends:
        pltpu.make_async_copy(send, send, send_sem).wait()


def write_back_kernel(index, targets_ref, store_hbm, rows_hbm, store_out, *scratch):
    store, rows, blended, load_sem, rows_sem, out_sem = scratch
    holders, capacity, page_len, width = blended.shape
    rows_here = capacity * page_len
    f32 = jnp.float32
    load = pltpu.make_async_copy(store_hbm, store, load_sem)
    load_rows = pltpu.make_async_copy(rows_hbm, rows, rows_sem)
    load.start()
    load_rows.start()
    load_rows.wait()
    load.wait()
    row_id = lax.broadcasted_iota(jnp.int32, (rows_here, ROW_SLOTS), 0)

    def one_request(r, carry):
        hit = one_hot(row_id == targets_ref[r][1:2, 0:ROW_SLOTS] - 1)
        keep = 1.0 - jnp.sum(hit, axis=1, keepdims=True)
        keep = jnp.broadcast_to(keep, (rows_here, LANES)).astype(jnp.bfloat16)
        hit = hit.astype(jnp.bfloat16)
        for c in range(width // LANES):
            lanes = slice(c * LANES, (c + 1) * LANES)
            fresh = jnp.dot(hit, rows[r, :, lanes], preferred_element_type=f32).astype(jnp.bfloat16)
            for k in range(capacity):
                part = slice(k * page_len, (k + 1) * page_len)
                blended[r, k, :, lanes] = store[index[r, 0, k], :, lanes] * keep[part] + fresh[part]
        for k in range(capacity):
            pltpu.make_async_copy(blended.at[r, k], store_out.at[index[r, 0, k]], out_sem).start()
        return carry

    lax.fori_loop(0, holders, one_request, 0)
    pltpu.make_async_copy(store_out, store_out, out_sem).wait()


def attend_kernel(first, last, sources, place, tiles, position_ref, sel_ref, query_ref, *rest):
    fresh_refs, rest = (rest[:1], rest[1:]) if first else ((), rest)
    state_in, rest = ((), rest) if first else (rest[:3], rest[3:])
    contexts, rest = rest[:sources], rest[sources:]
    outs, rest = (rest[:1], rest[1:]) if last else (rest[:3], rest[3:])
    kv, query, scores, raised, top, mixed, peak, total, sem = rest
    pages, page_len, width = kv.shape
    each = contexts[0].shape[0]
    ahead = TILE_PAGES if first else 0
    block = query_ref.shape[0]
    tile = TILE_PAGES * page_len
    scale = 1.4426950408889634 / HEAD_WIDTH**0.5
    f32 = jnp.float32
    bf16 = jnp.bfloat16
    step = pl.program_id(0)
    heads = [(g, slice(i * block, (i + 1) * block)) for g in range(KEY_VALUE_HEADS) for i in range(QUERY_GROUP)]

    @pl.when(step == 0)
    def _():
        for i, context in enumerate(contexts):
            for k in range(each):
                pltpu.make_async_copy(context.at[k], kv.at[ahead + place[i * each + k]], sem).start()
        for fresh_ref in fresh_refs:
            count = fresh_ref.shape[0] // page_len
            kv[0:count] = fresh_ref[...].reshape(count, page_len, width)
            kv[count:ahead] = jnp.zeros((ahead - count, page_len, width), bf16)
        used = kv.at[ahead:]
        pltpu.make_async_copy(used, used, sem).wait()

    for head, (g, rows) in enumerate(heads):
        query[g, rows, :] = query_ref[:, head * LANES : (head + 1) * LANES]
    if first:
        mixed[...] = jnp.zeros(mixed.shape, f32)
        peak[...] = jnp.full(peak.shape, HIDDEN, f32)
        total[...] = jnp.zeros(total.shape, f32)
        top[...] = jnp.full(top.shape, HIDDEN, f32)
    else:
        top[...] = state_in[1][0]

    def score(t, carry):
        here = pl.ds(t * TILE_PAGES, TILE_PAGES)
        lanes = pl.ds(pl.multiple_of(t * tile, tile), tile)
        bias = jnp.where(position_ref[:, lanes] <= sel_ref[...], 0.0, HIDDEN).astype(f32)
        for g in range(KEY_VALUE_HEADS):
            key = kv[here, :, g * LANES : (g + 1) * LANES].reshape(tile, LANES)
            product = nt_dot(query[g], key)
            for i in range(QUERY_GROUP):
                rows = slice(i * block, (i + 1) * block)
                s = product[rows] + bias
                scores[g, rows, lanes] = s
                best = top[g, rows, :]
                for c in range(tile // LANES):
                    best = jnp.maximum(best, s[:, c * LANES : (c + 1) * LANES])
                top[g, rows, :] = best
        return carry

    lax.fori_loop(0, tiles[step], score, 0)

    for g, rows in heads:
        new = jnp.broadcast_to(jnp.max(top[g, rows, :], axis=1, keepdims=True), (block, LANES))
        if not first:
            shrink = jnp.exp2((state_in[1][0, g, rows, :] - new) * scale)
            mixed[g, rows, :] = state_in[0][0, g, rows, :] * shrink
            total[g, rows, :] = state_in[2][0, g, rows, :] * shrink
        peak[g, rows, :] = new

    def mix(t, carry):
        here = pl.ds(t * TILE_PAGES, TILE_PAGES)
        lanes = pl.ds(pl.multiple_of(t * tile, tile), tile)
        for g in range(KEY_VALUE_HEADS):
            for i in range(QUERY_GROUP):
                rows = slice(i * block, (i + 1) * block)
                s = scores[g, rows, lanes]
                new = peak[g, rows, :]
                sums = total[g, rows, :]
                for c in range(tile // LANES):
                    part = slice(c * LANES, (c + 1) * LANES)
                    p = jnp.exp2((s[:, part] - new) * scale)
                    sums = sums + p
                    raised[g, rows, part] = p.astype(bf16)
                total[g, rows, :] = sums
            at = (KEY_VALUE_HEADS + g) * LANES
            value = kv[here, :, at : at + LANES].reshape(tile, LANES)
            mixed[g] = mixed[g] + jnp.dot(raised[g], value, preferred_element_type=f32)
        return carry

    lax.fori_loop(0, tiles[step], mix, 0)

    if last:
        for head, (g, rows) in enumerate(heads):
            whole = jnp.sum(total[g, rows, :], axis=1, keepdims=True)
            outs[0][:, head * LANES : (head + 1) * LANES] = (mixed[g, rows, :] / whole).astype(bf16)
    else:
        outs[0][0] = mixed[...]
        outs[1][0] = peak[...]
        outs[2][0] = total[...]


def attend(first, last, order, sel_column, queries, fresh, state, contexts):
    picked, features = queries.shape
    each, page_len, width = contexts[0].shape
    pages = each * len(contexts) + (TILE_PAGES if first else 0)
    steps = picked // QUERY_BLOCK
    rows = QUERY_GROUP * QUERY_BLOCK
    wide = pl.BlockSpec((QUERY_BLOCK, features), lambda b, *_: (b, 0))
    state_shape = (KEY_VALUE_HEADS, rows, LANES)
    state_specs = [pl.BlockSpec((1, *state_shape), lambda b, *_: (b, 0, 0, 0))] * 3
    state_shapes = [jax.ShapeDtypeStruct((steps, *state_shape), jnp.float32)] * 3
    share = 0.6
    return pl.pallas_call(
        functools.partial(attend_kernel, first, last, len(contexts)),
        grid_spec=pltpu.PrefetchScalarGridSpec(
            num_scalar_prefetch=2,
            grid=(steps,),
            in_specs=[
                pl.BlockSpec((1, pages * page_len), lambda b, *_: (0, 0)),
                pl.BlockSpec((QUERY_BLOCK, 1), lambda b, *_: (b, 0)),
                wide,
                *([pl.BlockSpec(fresh.shape, lambda b, *_: (0, 0))] if first else state_specs),
                *[pl.BlockSpec(memory_space=pltpu.HBM)] * len(contexts),
            ],
            out_specs=[wide] if last else state_specs,
            scratch_shapes=[
                pltpu.VMEM((pages, page_len, width), jnp.bfloat16),
                pltpu.VMEM(state_shape, jnp.bfloat16),
                pltpu.VMEM((KEY_VALUE_HEADS, rows, pages * page_len), jnp.float32),
                pltpu.VMEM((KEY_VALUE_HEADS, rows, TILE_PAGES * page_len), jnp.bfloat16),
                pltpu.VMEM(state_shape, jnp.float32),
                pltpu.VMEM(state_shape, jnp.float32),
                pltpu.VMEM(state_shape, jnp.float32),
                pltpu.VMEM(state_shape, jnp.float32),
                pltpu.SemaphoreType.DMA,
            ],
        ),
        out_shape=[jax.ShapeDtypeStruct((picked, features), jnp.bfloat16)] if last else state_shapes,
        compiler_params=pltpu.CompilerParams(
            dimension_semantics=("arbitrary",), vmem_limit_bytes=VMEM_LIMIT
        ),
        cost_estimate=pl.CostEstimate(
            flops=int(share * 8 * picked * features * pages * page_len),
            bytes_accessed=2 * pages * page_len * width + 6 * picked * features,
            transcendentals=int(share * picked * features // LANES * pages * page_len),
        ),
    )(*order, sel_column, queries, *([fresh] if first else state), *contexts)


def page_order(slots, positions, own, hold, capacity, groups, page_len):
    pages = slots.shape[0]
    number = jnp.arange(pages)
    before = number[None, :] < number[:, None]
    owners = slots // hold
    ranks = jnp.sum(((owners[None, :] == owners[:, None]) & before).astype(jnp.int32), axis=1)
    distance = owners ^ own
    last_page = positions.reshape(-1, QUERY_BLOCK)[:, -1] // page_len
    orders = []
    for at, group in enumerate(groups):
        if group is None:
            arrival = owners * capacity + ranks
            count = pages
        else:
            arrival = jnp.full((pages,), -1, jnp.int32)
            for i, d in enumerate(group):
                arrival = jnp.where(distance == d, i * capacity + ranks, arrival)
            count = len(group) * capacity
        member = arrival >= 0
        place = jnp.sum((member[None, :] & before).astype(jnp.int32), axis=1)
        index = jnp.arange(count)[:, None]
        places = jnp.sum(jnp.where(arrival[None, :] == index, place[None, :], 0), axis=1)
        page = jnp.sum(
            jnp.where(member[None, :] & (place[None, :] == index), number[None, :], 0), axis=1
        )
        seen = jnp.sum((page[None, :] <= last_page[:, None]).astype(jnp.int32), axis=1)
        tiles = (seen + TILE_PAGES - 1) // TILE_PAGES + (at == 0)
        rows = (page[:, None] * page_len + jnp.arange(page_len)[None, :]).reshape(-1)
        replaced = jnp.any(rows[:, None] == positions[None, :], axis=1)
        rows = jnp.where(replaced, FAR_POSITION, rows)
        if at == 0:
            room = TILE_PAGES * page_len - positions.shape[0]
            rows = jnp.concatenate([positions, jnp.full((room,), FAR_POSITION, jnp.int32), rows])
        orders.append((places, tiles, rows.reshape(1, -1)))
    return orders


def per_device(store, page_table, sel_pos, fresh_kv, queries):
    holders = lax.axis_size("store")
    hold, page_len, width = store.shape
    pages = page_table.shape[1]
    picked = sel_pos.shape[1]
    capacity = max(1, pages // holders)
    hbm = pl.BlockSpec(memory_space=pltpu.HBM)
    vmem = pl.BlockSpec(memory_space=pltpu.VMEM)
    dma = pltpu.SemaphoreType.DMA
    params = pltpu.CompilerParams(vmem_limit_bytes=VMEM_LIMIT)
    own = lax.axis_index("store")
    own_word = own.reshape(1).astype(jnp.int32)
    fresh = fresh_kv[0]
    wide = pltpu.VMEM((8, -(-picked // LANES) * LANES), jnp.int32)
    if holders == 16:
        first = (8, 12)
        groups = [(0, 8, 12, 4, 5, 1), (9, 6, 13, 7, 10, 2, 14, 3), (11, 15)]
        others = [d for group in groups for d in group if d not in first]
    else:
        first = ()
        groups = [None]
        others = None

    def swap(x, d):
        return lax.ppermute(x, "store", [(h, h ^ d) for h in range(holders)])

    def exchange(x):
        return lax.all_to_all(x, "store", split_axis=0, concat_axis=0, tiled=True)

    index, *lists = pl.pallas_call(
        functools.partial(index_kernel, hold, page_len, first),
        grid_spec=pltpu.PrefetchScalarGridSpec(
            num_scalar_prefetch=1,
            grid=(1,),
            in_specs=[vmem, vmem],
            out_specs=[vmem] * (1 + len(first)),
            scratch_shapes=[wide],
        ),
        out_shape=[
            jax.ShapeDtypeStruct((holders, 2, LANES), jnp.int32),
            *[jax.ShapeDtypeStruct((1, 2, LANES), jnp.int32)] * len(first),
        ],
        compiler_params=params,
    )(own_word, page_table, sel_pos)
    arrived = {}
    if first:
        lists = [swap(x, d) for x, d in zip(lists, first)]
        parts = pl.pallas_call(
            functools.partial(first_gather_kernel, len(first)),
            grid_spec=pltpu.PrefetchScalarGridSpec(
                num_scalar_prefetch=len(first),
                grid=(1,),
                in_specs=[hbm],
                out_specs=[hbm] * len(first),
                scratch_shapes=[
                    pltpu.VMEM((len(first), capacity, page_len, width), store.dtype),
                    dma,
                    dma,
                ],
            ),
            out_shape=[jax.ShapeDtypeStruct((capacity, page_len, width), store.dtype)] * len(first),
            compiler_params=params,
        )(*lists, store)
        parts, index, table, positions = lax.optimization_barrier(
            (parts, index, page_table, sel_pos)
        )
        arrived = {d: swap(part, d) for d, part in zip(first, parts)}
    else:
        table, positions = page_table, sel_pos
    index_in = exchange(index)

    packed = pl.pallas_call(
        functools.partial(rows_kernel, hold, page_len),
        out_shape=jax.ShapeDtypeStruct((holders, ROW_SLOTS, width), store.dtype),
        scratch_shapes=[wide],
        compiler_params=params,
    )(table, positions, fresh)

    each = jax.ShapeDtypeStruct((capacity, page_len, width), store.dtype)
    whole = jax.ShapeDtypeStruct((holders, capacity, page_len, width), store.dtype)
    parts = pl.pallas_call(
        functools.partial(gather_kernel, capacity, others),
        grid_spec=pltpu.PrefetchScalarGridSpec(
            num_scalar_prefetch=2,
            grid=(1,),
            in_specs=[hbm],
            out_specs=[hbm] * (len(others) if others else 1),
            scratch_shapes=[pltpu.VMEM(store.shape, store.dtype), dma, dma],
        ),
        out_shape=[each] * len(others) if others else [whole],
        compiler_params=params,
    )(own_word, index_in, store)
    parts, packed, table, positions = lax.optimization_barrier((parts, packed, table, positions))
    if others:
        for d, part in zip(others, parts):
            arrived[d] = swap(part, d) if d else part
        contexts = [[arrived[d] for d in group] for group in groups]
    else:
        contexts = [[exchange(parts[0]).reshape(pages, page_len, width)]]
    rows_in = exchange(packed)

    store_out = pl.pallas_call(
        write_back_kernel,
        grid_spec=pltpu.PrefetchScalarGridSpec(
            num_scalar_prefetch=1,
            grid=(1,),
            in_specs=[vmem, hbm, hbm],
            out_specs=hbm,
            scratch_shapes=[
                pltpu.VMEM(store.shape, store.dtype),
                pltpu.VMEM((holders, ROW_SLOTS, width), store.dtype),
                pltpu.VMEM((holders, capacity, page_len, width), store.dtype),
                dma,
                dma,
                dma,
            ],
        ),
        out_shape=jax.ShapeDtypeStruct(store.shape, store.dtype),
        compiler_params=params,
        cost_estimate=pl.CostEstimate(flops=0, bytes_accessed=4 * store.size, transcendentals=0),
    )(index_in, index_in, store, rows_in)

    orders = page_order(table[0], positions[0], own, hold, capacity, groups, page_len)
    sel_column = positions.reshape(picked, 1)
    store_out, sel_column = lax.optimization_barrier((store_out, sel_column))
    state = ()
    for at, (arrays, order) in enumerate(zip(contexts, orders)):
        last = at == len(groups) - 1
        state = attend(at == 0, last, order, sel_column, queries[0], fresh, state, arrays)
    return (state[0][None], store_out)


def solution(mesh):
    return jax.shard_map(
        per_device,
        mesh=mesh,
        in_specs=(
            P(("groups", "store"), None, None),
            P(("groups", "store"), None),
            P(("groups", "store"), None),
            P(("groups", "store"), None, None),
            P(("groups", "store"), None, None),
        ),
        out_specs=(P(("groups", "store"), None, None), P(("groups", "store"), None, None)),
        check_vma=False,
    )
```

```python
import functools

import jax
import jax.numpy as jnp
from jax import lax
from jax.experimental import pallas as pl
from jax.experimental.pallas import tpu as pltpu
from jax.sharding import PartitionSpec as P

HEAD_WIDTH = 128
KEY_VALUE_HEADS = 4
QUERY_GROUP = 12
SELP = 2
LANES = 128
ROW_SLOTS = 16
VMEM_LIMIT = 60 * 1024 * 1024
QUERY_BLOCK = 32
TILE_PAGES = 32
LATE_TILE_PAGES = 16
FRESH_PAGES = 16
HIDDEN = -1e30
FAR_POSITION = 1 << 24


def nt_dot(a, b):
    return lax.dot_general(a, b, (((1,), (1,)), ((), ())), preferred_element_type=jnp.float32)


def one_hot(condition):
    return jnp.where(condition, 1.0, 0.0)


def pair_places(hold, page_len, table_ref, sel_ref, wide):
    pages = table_ref.shape[1]
    picked = sel_ref.shape[1]
    f32 = jnp.float32
    slots = jnp.broadcast_to(table_ref[...], (pages, pages))
    owners = slots // hold
    local_row = (slots - owners * hold).astype(f32)[0:1]
    owner_row = owners.astype(f32)
    owner_col = owner_row.T
    sub = lax.broadcasted_iota(jnp.int32, (pages, pages), 0)
    lane = lax.broadcasted_iota(jnp.int32, (pages, pages), 1)
    earlier = one_hot((owner_row == owner_col) & (lane < sub))
    rank_col = jnp.sum(earlier, axis=1, keepdims=True)

    wide[...] = jnp.full(wide.shape, -1, jnp.int32)
    wide[0:1, 0:picked] = sel_ref[...]
    position = wide[...]
    page = lax.shift_right_arithmetic(position, page_len.bit_length() - 1)
    offset = (position & (page_len - 1)).astype(f32)[0:1]
    lane_wide = lax.broadcasted_iota(jnp.int32, wide.shape, 1)
    second = one_hot((page == pltpu.roll(page, 1, axis=1)) & (lane_wide > 0))[0:1]
    valid = lane_wide[0:1] < picked
    sub_wide = lax.broadcasted_iota(jnp.int32, (pages, wide.shape[1]), 0)
    in_page = one_hot(sub_wide == page[0:1])
    owner = jnp.sum(in_page * owner_col[:, 0:1], axis=0, keepdims=True)
    rank = jnp.sum(in_page * rank_col, axis=0, keepdims=True)
    return owner_row[0:1], local_row, rank_col, owner, rank, second, offset, valid


def index_kernel(hold, page_len, first, own, table_ref, sel_ref, out_ref, *rest):
    first_refs, wide = rest[:-1], rest[-1]
    holders = out_ref.shape[0]
    pages = table_ref.shape[1]
    f32 = jnp.float32
    bf16 = jnp.bfloat16
    owner_row, local_row, rank_col, owner, rank, second, offset, valid = pair_places(
        hold, page_len, table_ref, sel_ref, wide
    )
    holder = lax.broadcasted_iota(jnp.int32, (holders, pages), 0).astype(f32)
    owned = jnp.where(holder == owner_row, local_row, 0.0)
    lane = lax.broadcasted_iota(jnp.int32, (pages, LANES), 1).astype(f32)
    numbers = jnp.dot(
        owned.astype(bf16), one_hot(lane == rank_col).astype(bf16), preferred_element_type=f32
    )
    holder_wide = lax.broadcasted_iota(jnp.int32, (holders, wide.shape[1]), 0).astype(f32)
    marked = jnp.where((holder_wide == owner) & valid, rank * page_len + offset + 1.0, 0.0)
    place_lane = lax.broadcasted_iota(jnp.int32, (LANES, wide.shape[1]), 0).astype(f32)
    at_place = one_hot(place_lane == SELP * rank + second)
    targets = nt_dot(marked.astype(bf16), at_place.astype(bf16))
    for h in range(holders):
        out_ref[h, 0:1, :] = numbers[h : h + 1, :].astype(jnp.int32)
        out_ref[h, 1:2, :] = targets[h : h + 1, :].astype(jnp.int32)
    for d, ref in zip(first, first_refs):
        ref[0] = out_ref[own[0] ^ d]


def rows_kernel(hold, page_len, table_ref, sel_ref, fresh_ref, packed, wide):
    holders = packed.shape[0]
    picked = sel_ref.shape[1]
    f32 = jnp.float32
    _, _, _, owner, rank, second, _, valid = pair_places(hold, page_len, table_ref, sel_ref, wide)
    spot = jnp.where(valid, owner * ROW_SLOTS + SELP * rank + second, -1.0)[:, 0:picked]
    step = min(holders, 16)
    for start in range(0, holders, step):
        spot_id = lax.broadcasted_iota(jnp.int32, (step * ROW_SLOTS, picked), 0).astype(f32)
        choose = one_hot(spot_id + float(start * ROW_SLOTS) == spot).astype(jnp.bfloat16)
        rows = jnp.dot(choose, fresh_ref[...], preferred_element_type=f32).astype(jnp.bfloat16)
        packed[start : start + step] = rows.reshape(step, ROW_SLOTS, fresh_ref.shape[1])


def first_gather_kernel(count, *refs):
    lists, store_hbm, sends = refs[:count], refs[count], refs[count + 1 : 2 * count + 1]
    held, load_sem, send_sem = refs[2 * count + 1 :]
    capacity = held.shape[1]
    for i, numbers in enumerate(lists):
        for k in range(capacity):
            pltpu.make_async_copy(store_hbm.at[numbers[0, 0, k]], held.at[i, k], load_sem).start()
    pltpu.make_async_copy(held, held, load_sem).wait()
    for i, send in enumerate(sends):
        pltpu.make_async_copy(held.at[i], send, send_sem).start()
    pltpu.make_async_copy(held, held, send_sem).wait()


def gather_kernel(capacity, distances, own, index, store_hbm, *rest):
    sends, (store, load_sem, send_sem) = rest[:-3], rest[-3:]
    load = pltpu.make_async_copy(store_hbm, store, load_sem)
    load.start()
    load.wait()
    for i in range(len(distances) if distances else index.shape[0]):
        r = own[0] ^ distances[i] if distances else i
        send = sends[i] if distances else sends[0].at[i]
        for k in range(capacity):
            pltpu.make_async_copy(store.at[index[r, 0, k]], send.at[k], send_sem).start()
    for send in sends:
        pltpu.make_async_copy(send, send, send_sem).wait()


def write_back_kernel(index, targets_ref, store_hbm, rows_hbm, store_out, *scratch):
    store, rows, blended, load_sem, rows_sem, out_sem = scratch
    holders, capacity, page_len, width = blended.shape
    rows_here = capacity * page_len
    f32 = jnp.float32
    load = pltpu.make_async_copy(store_hbm, store, load_sem)
    load_rows = pltpu.make_async_copy(rows_hbm, rows, rows_sem)
    load.start()
    load_rows.start()
    load_rows.wait()
    load.wait()
    row_id = lax.broadcasted_iota(jnp.int32, (rows_here, ROW_SLOTS), 0)

    def one_request(r, carry):
        hit = one_hot(row_id == targets_ref[r][1:2, 0:ROW_SLOTS] - 1)
        keep = 1.0 - jnp.sum(hit, axis=1, keepdims=True)
        keep = jnp.broadcast_to(keep, (rows_here, LANES)).astype(jnp.bfloat16)
        hit = hit.astype(jnp.bfloat16)
        for c in range(width // LANES):
            lanes = slice(c * LANES, (c + 1) * LANES)
            fresh = jnp.dot(hit, rows[r, :, lanes], preferred_element_type=f32).astype(jnp.bfloat16)
            for k in range(capacity):
                part = slice(k * page_len, (k + 1) * page_len)
                blended[r, k, :, lanes] = store[index[r, 0, k], :, lanes] * keep[part] + fresh[part]
        for k in range(capacity):
            pltpu.make_async_copy(blended.at[r, k], store_out.at[index[r, 0, k]], out_sem).start()
        return carry

    lax.fori_loop(0, holders, one_request, 0)
    pltpu.make_async_copy(store_out, store_out, out_sem).wait()


def attend_kernel(first, last, tile_pages, sources, place, tiles, *rest):
    sel_ref, position, query_ref, *rest = rest
    if first:
        fresh_ref, *rest = rest
    state_in = () if first else rest[:2]
    rest = rest if first else rest[2:]
    contexts, rest = rest[:sources], rest[sources:]
    outs, rest = (rest[:1], rest[1:]) if last else (rest[:2], rest[2:])
    kv, values, query, scores, raised, mixed, stats, sem = rest
    pages, page_len, width = kv.shape
    each = contexts[0].shape[0]
    ahead = FRESH_PAGES if first else 0
    direct = last and not first
    block = query_ref.shape[0]
    tile = tile_pages * page_len
    lanes = QUERY_GROUP * block
    scale = 1.4426950408889634 / HEAD_WIDTH**0.5
    f32 = jnp.float32
    bf16 = jnp.bfloat16
    step = pl.program_id(0)
    eye = one_hot(
        lax.broadcasted_iota(jnp.int32, (LANES, LANES), 0)
        == lax.broadcasted_iota(jnp.int32, (LANES, LANES), 1)
    ).astype(bf16)

    @pl.when(step == 0)
    def _():
        for i, context in enumerate(contexts):
            if direct:
                kv[i * each : (i + 1) * each] = context[...]
            else:
                for k in range(each):
                    to = kv.at[ahead + place[i * each + k]]
                    pltpu.make_async_copy(context.at[k], to, sem).start()
        if first:
            count = fresh_ref.shape[0] // page_len
            kv[0:count] = fresh_ref[...].reshape(count, page_len, width)
            kv[count:ahead] = jnp.zeros((ahead - count, page_len, width), bf16)
        if not direct:
            used = kv.at[ahead:]
            pltpu.make_async_copy(used, used, sem).wait()

        def turn(t, carry):
            here = pl.ds(t * tile_pages, tile_pages)
            for g in range(KEY_VALUE_HEADS):
                at = (KEY_VALUE_HEADS + g) * LANES
                value = kv[here, :, at : at + LANES].reshape(tile, LANES)
                values[t, g] = nt_dot(eye, value).astype(bf16)
            return carry

        lax.fori_loop(0, pages // tile_pages, turn, 0)

    for g in range(KEY_VALUE_HEADS):
        for i in range(QUERY_GROUP):
            head = g * QUERY_GROUP + i
            query[g, i * block : (i + 1) * block, :] = query_ref[:, head * LANES : (head + 1) * LANES]
    if first:
        mixed[...] = jnp.zeros(mixed.shape, f32)
        stats[0:KEY_VALUE_HEADS, :] = jnp.full((KEY_VALUE_HEADS, lanes), HIDDEN, f32)
        stats[KEY_VALUE_HEADS:, :] = jnp.zeros((KEY_VALUE_HEADS, lanes), f32)
    else:
        mixed[...] = state_in[0][0]
        stats[...] = state_in[1][0]

    sel = sel_ref[0]

    def one_tile(t, carry):
        here = pl.ds(t * tile_pages, tile_pages)
        bias = jnp.where(
            position[pl.ds(pl.multiple_of(t * tile, tile), tile), :] <= sel, 0.0, HIDDEN
        ).astype(f32)

        parts = [slice(n * LANES, (n + 1) * LANES) for n in range(lanes // LANES)]
        chains = [(g, part) for g in range(KEY_VALUE_HEADS) for part in parts]
        for g in range(KEY_VALUE_HEADS):
            key = kv[here, :, g * LANES : (g + 1) * LANES].reshape(tile, LANES)
            product = nt_dot(key, query[g])
            for part in parts:
                scores[g, :, part] = product[:, part] + bias
        peaks, shrinks = [], []
        for g, part in chains:
            old = stats[g : g + 1, part]
            new = jnp.maximum(old, jnp.max(scores[g, :, part], axis=0, keepdims=True))
            stats[g : g + 1, part] = new
            peaks.append(new)
            shrinks.append(jnp.exp2((old - new) * scale))
        for (g, part), new, shrink in zip(chains, peaks, shrinks):
            at = KEY_VALUE_HEADS + g
            p = jnp.exp2((scores[g, :, part] - new) * scale)
            stats[at : at + 1, part] = stats[at : at + 1, part] * shrink + jnp.sum(
                p, axis=0, keepdims=True
            )
            raised[g, :, part] = p.astype(bf16)
        for g in range(KEY_VALUE_HEADS):
            shrink = jnp.concatenate(shrinks[g * len(parts) : (g + 1) * len(parts)], axis=1)
            mixed[g] = mixed[g] * shrink + jnp.dot(
                values[t, g], raised[g], preferred_element_type=f32
            )
        return carry

    lax.fori_loop(0, tiles[step], one_tile, 0)

    if last:
        done = []
        for g in range(KEY_VALUE_HEADS):
            at = KEY_VALUE_HEADS + g
            part = (mixed[g] * (1.0 / stats[at : at + 1, :])).astype(bf16)
            done += [part[:, n * LANES : (n + 1) * LANES] for n in range(lanes // LANES)]
        turned = nt_dot(eye, jnp.concatenate(done, axis=0)).astype(bf16)
        for n in range(len(done)):
            for i in range(LANES // block):
                head = n * (LANES // block) + i
                outs[0][:, head * LANES : (head + 1) * LANES] = turned[
                    i * block : (i + 1) * block, n * LANES : (n + 1) * LANES
                ]
    else:
        outs[0][0] = mixed[...]
        outs[1][0] = stats[...]


def attend(first, last, tile_pages, order, sel_lanes, queries, fresh, state, contexts):
    place, tiles, position = order
    picked, features = queries.shape
    each, page_len, width = contexts[0].shape
    pages = each * len(contexts) + (FRESH_PAGES if first else 0)
    steps = picked // QUERY_BLOCK
    lanes = QUERY_GROUP * QUERY_BLOCK
    wide = pl.BlockSpec((QUERY_BLOCK, features), lambda b, *_: (b, 0))
    state_specs = [
        pl.BlockSpec((1, KEY_VALUE_HEADS, LANES, lanes), lambda b, *_: (b, 0, 0, 0)),
        pl.BlockSpec((1, 2 * KEY_VALUE_HEADS, lanes), lambda b, *_: (b, 0, 0)),
    ]
    state_shapes = [
        jax.ShapeDtypeStruct((steps, KEY_VALUE_HEADS, LANES, lanes), jnp.float32),
        jax.ShapeDtypeStruct((steps, 2 * KEY_VALUE_HEADS, lanes), jnp.float32),
    ]
    share = 0.6
    return pl.pallas_call(
        functools.partial(attend_kernel, first, last, tile_pages, len(contexts)),
        grid_spec=pltpu.PrefetchScalarGridSpec(
            num_scalar_prefetch=2,
            grid=(steps,),
            in_specs=[
                pl.BlockSpec((1, 1, LANES), lambda b, *_: (b, 0, 0)),
                pl.BlockSpec(position.shape, lambda b, *_: (0, 0)),
                wide,
                *([pl.BlockSpec(fresh.shape, lambda b, *_: (0, 0))] if first else state_specs),
                *[
                    pl.BlockSpec(x.shape, lambda b, *_: (0, 0, 0))
                    if last and not first
                    else pl.BlockSpec(memory_space=pltpu.HBM)
                    for x in contexts
                ],
            ],
            out_specs=[wide] if last else state_specs,
            scratch_shapes=[
                pltpu.VMEM((pages, page_len, width), jnp.bfloat16),
                pltpu.VMEM(
                    (pages // tile_pages, KEY_VALUE_HEADS, LANES, tile_pages * page_len), jnp.bfloat16
                ),
                pltpu.VMEM((KEY_VALUE_HEADS, lanes, LANES), jnp.bfloat16),
                pltpu.VMEM((KEY_VALUE_HEADS, tile_pages * page_len, lanes), jnp.float32),
                pltpu.VMEM((KEY_VALUE_HEADS, tile_pages * page_len, lanes), jnp.bfloat16),
                pltpu.VMEM((KEY_VALUE_HEADS, LANES, lanes), jnp.float32),
                pltpu.VMEM((2 * KEY_VALUE_HEADS, lanes), jnp.float32),
                pltpu.SemaphoreType.DMA,
            ],
        ),
        out_shape=[jax.ShapeDtypeStruct((picked, features), jnp.bfloat16)] if last else state_shapes,
        compiler_params=pltpu.CompilerParams(
            dimension_semantics=("arbitrary",), vmem_limit_bytes=VMEM_LIMIT
        ),
        cost_estimate=pl.CostEstimate(
            flops=int(share * 8 * picked * features * pages * page_len),
            bytes_accessed=2 * pages * page_len * width + 6 * picked * features,
            transcendentals=int(share * picked * features // LANES * pages * page_len),
        ),
    )(place, tiles, sel_lanes, position, queries, *([fresh] if first else state), *contexts)


def page_order(slots, positions, own, hold, capacity, groups, tiles, page_len):
    pages = slots.shape[0]
    number = jnp.arange(pages)
    before = number[None, :] < number[:, None]
    owners = slots // hold
    ranks = jnp.sum(((owners[None, :] == owners[:, None]) & before).astype(jnp.int32), axis=1)
    distance = owners ^ own
    last_page = positions.reshape(-1, QUERY_BLOCK)[:, -1] // page_len
    orders = []
    for at, (group, tile_pages) in enumerate(zip(groups, tiles)):
        if group is None:
            arrival = owners * capacity + ranks
            count = pages
        else:
            arrival = jnp.full((pages,), -1, jnp.int32)
            for i, d in enumerate(group):
                arrival = jnp.where(distance == d, i * capacity + ranks, arrival)
            count = len(group) * capacity
        member = arrival >= 0
        place = jnp.sum((member[None, :] & before).astype(jnp.int32), axis=1)
        if at == len(groups) - 1 and at > 0:
            place = arrival
        index = jnp.arange(count)[:, None]
        places = jnp.sum(jnp.where(arrival[None, :] == index, place[None, :], 0), axis=1)
        page = jnp.sum(
            jnp.where(member[None, :] & (place[None, :] == index), number[None, :], 0), axis=1
        )
        seen = jnp.sum((page[None, :] <= last_page[:, None]).astype(jnp.int32), axis=1)
        seen = seen + (FRESH_PAGES if at == 0 else 0)
        rows = (page[:, None] * page_len + jnp.arange(page_len)[None, :]).reshape(-1, 1)
        replaced = jnp.any(rows == positions[None, :], axis=1, keepdims=True)
        rows = jnp.where(replaced, FAR_POSITION, rows)
        if at == 0:
            room = FRESH_PAGES * page_len - positions.shape[0]
            room = jnp.full((room, 1), FAR_POSITION, jnp.int32)
            rows = jnp.concatenate([positions[:, None], room, rows])
        rows = jnp.broadcast_to(rows, (rows.shape[0], LANES))
        orders.append((places, (seen + tile_pages - 1) // tile_pages, rows))
    return orders


def per_device(store, page_table, sel_pos, fresh_kv, queries):
    holders = lax.axis_size("store")
    hold, page_len, width = store.shape
    pages = page_table.shape[1]
    picked = sel_pos.shape[1]
    capacity = max(1, pages // holders)
    hbm = pl.BlockSpec(memory_space=pltpu.HBM)
    vmem = pl.BlockSpec(memory_space=pltpu.VMEM)
    dma = pltpu.SemaphoreType.DMA
    params = pltpu.CompilerParams(vmem_limit_bytes=VMEM_LIMIT)
    own = lax.axis_index("store")
    own_word = own.reshape(1).astype(jnp.int32)
    fresh = fresh_kv[0]
    wide = pltpu.VMEM((8, -(-picked // LANES) * LANES), jnp.int32)
    if holders == 16:
        first = (8, 12)
        groups = [(0, 8, 12, 4, 5, 1), (9, 6, 13, 7, 10, 2, 14, 3), (11, 15)]
        others = [d for group in groups for d in group if d not in first]
    else:
        first = ()
        groups = [None]
        others = None

    def swap(x, d):
        return lax.ppermute(x, "store", [(h, h ^ d) for h in range(holders)])

    def exchange(x):
        return lax.all_to_all(x, "store", split_axis=0, concat_axis=0, tiled=True)

    index, *lists = pl.pallas_call(
        functools.partial(index_kernel, hold, page_len, first),
        grid_spec=pltpu.PrefetchScalarGridSpec(
            num_scalar_prefetch=1,
            grid=(1,),
            in_specs=[vmem, vmem],
            out_specs=[vmem] * (1 + len(first)),
            scratch_shapes=[wide],
        ),
        out_shape=[
            jax.ShapeDtypeStruct((holders, 2, LANES), jnp.int32),
            *[jax.ShapeDtypeStruct((1, 2, LANES), jnp.int32)] * len(first),
        ],
        compiler_params=params,
    )(own_word, page_table, sel_pos)
    arrived = {}
    if first:
        lists = [swap(x, d) for x, d in zip(lists, first)]
        parts = pl.pallas_call(
            functools.partial(first_gather_kernel, len(first)),
            grid_spec=pltpu.PrefetchScalarGridSpec(
                num_scalar_prefetch=len(first),
                grid=(1,),
                in_specs=[hbm],
                out_specs=[hbm] * len(first),
                scratch_shapes=[
                    pltpu.VMEM((len(first), capacity, page_len, width), store.dtype),
                    dma,
                    dma,
                ],
            ),
            out_shape=[jax.ShapeDtypeStruct((capacity, page_len, width), store.dtype)] * len(first),
            compiler_params=params,
        )(*lists, store)
        parts, index, table, positions = lax.optimization_barrier(
            (parts, index, page_table, sel_pos)
        )
        arrived = {d: swap(part, d) for d, part in zip(first, parts)}
    else:
        table, positions = page_table, sel_pos
    index_in = exchange(index)

    packed = pl.pallas_call(
        functools.partial(rows_kernel, hold, page_len),
        out_shape=jax.ShapeDtypeStruct((holders, ROW_SLOTS, width), store.dtype),
        scratch_shapes=[wide],
        compiler_params=params,
    )(table, positions, fresh)

    each = jax.ShapeDtypeStruct((capacity, page_len, width), store.dtype)
    whole = jax.ShapeDtypeStruct((holders, capacity, page_len, width), store.dtype)
    parts = pl.pallas_call(
        functools.partial(gather_kernel, capacity, others),
        grid_spec=pltpu.PrefetchScalarGridSpec(
            num_scalar_prefetch=2,
            grid=(1,),
            in_specs=[hbm],
            out_specs=[hbm] * (len(others) if others else 1),
            scratch_shapes=[pltpu.VMEM(store.shape, store.dtype), dma, dma],
        ),
        out_shape=[each] * len(others) if others else [whole],
        compiler_params=params,
    )(own_word, index_in, store)
    parts, packed, table, positions = lax.optimization_barrier((parts, packed, table, positions))
    if others:
        parts = dict(zip(others, parts))
        held = others[-4:]
        for d in others[:-4]:
            arrived[d] = swap(parts[d], d) if d else parts[d]
    else:
        arrived[None] = exchange(parts[0]).reshape(pages, page_len, width)
    rows_in = exchange(packed)

    store_out = pl.pallas_call(
        write_back_kernel,
        grid_spec=pltpu.PrefetchScalarGridSpec(
            num_scalar_prefetch=1,
            grid=(1,),
            in_specs=[vmem, hbm, hbm],
            out_specs=hbm,
            scratch_shapes=[
                pltpu.VMEM(store.shape, store.dtype),
                pltpu.VMEM((holders, ROW_SLOTS, width), store.dtype),
                pltpu.VMEM((holders, capacity, page_len, width), store.dtype),
                dma,
                dma,
                dma,
            ],
        ),
        out_shape=jax.ShapeDtypeStruct(store.shape, store.dtype),
        compiler_params=params,
        cost_estimate=pl.CostEstimate(flops=0, bytes_accessed=4 * store.size, transcendentals=0),
    )(index_in, index_in, store, rows_in)

    tiles = [LATE_TILE_PAGES if at == len(groups) - 1 else TILE_PAGES for at in range(len(groups))]
    orders = page_order(table[0], positions[0], own, hold, capacity, groups, tiles, page_len)
    sel_lanes = jnp.tile(positions.reshape(-1, 1, QUERY_BLOCK), (1, 1, LANES // QUERY_BLOCK))
    store_out, sel_lanes = lax.optimization_barrier((store_out, sel_lanes))
    state = ()
    for at, (group, order) in enumerate(zip(groups, orders)):
        state = attend(
            at == 0,
            at == len(groups) - 1,
            tiles[at],
            order,
            sel_lanes,
            queries[0],
            fresh,
            state,
            [arrived[d] for d in group or [None]],
        )
        if at == 0 and others:
            state, late = lax.optimization_barrier((state, [parts[d] for d in held]))
            for d, part in zip(held, late):
                arrived[d] = swap(part, d)
    return (state[0][None], store_out)


def solution(mesh):
    return jax.shard_map(
        per_device,
        mesh=mesh,
        in_specs=(
            P(("groups", "store"), None, None),
            P(("groups", "store"), None),
            P(("groups", "store"), None),
            P(("groups", "store"), None, None),
            P(("groups", "store"), None, None),
        ),
        out_specs=(P(("groups", "store"), None, None), P(("groups", "store"), None, None)),
        check_vma=False,
    )
```

```python
import functools

import jax
import jax.numpy as jnp
from jax import lax
from jax.experimental import pallas as pl
from jax.experimental.pallas import tpu as pltpu
from jax.sharding import PartitionSpec as P

HEAD_WIDTH = 128
KEY_VALUE_HEADS = 4
QUERY_GROUP = 12
SELP = 2
LANES = 128
ROW_SLOTS = 16
VMEM_LIMIT = 60 * 1024 * 1024
QUERY_BLOCK = 32
TILE_PAGES = 16
HIDDEN = -1e30
FAR_POSITION = 1 << 24


def nt_dot(a, b):
    return lax.dot_general(a, b, (((1,), (1,)), ((), ())), preferred_element_type=jnp.float32)


def one_hot(condition):
    return jnp.where(condition, 1.0, 0.0)


def pair_places(hold, page_len, table_ref, sel_ref, wide):
    pages = table_ref.shape[1]
    picked = sel_ref.shape[1]
    f32 = jnp.float32
    slots = jnp.broadcast_to(table_ref[...], (pages, pages))
    owners = slots // hold
    local_row = (slots - owners * hold).astype(f32)[0:1]
    owner_row = owners.astype(f32)
    owner_col = owner_row.T
    sub = lax.broadcasted_iota(jnp.int32, (pages, pages), 0)
    lane = lax.broadcasted_iota(jnp.int32, (pages, pages), 1)
    earlier = one_hot((owner_row == owner_col) & (lane < sub))
    rank_col = jnp.sum(earlier, axis=1, keepdims=True)

    wide[...] = jnp.full(wide.shape, -1, jnp.int32)
    wide[0:1, 0:picked] = sel_ref[...]
    position = wide[...]
    page = lax.shift_right_arithmetic(position, page_len.bit_length() - 1)
    offset = (position & (page_len - 1)).astype(f32)[0:1]
    lane_wide = lax.broadcasted_iota(jnp.int32, wide.shape, 1)
    second = one_hot((page == pltpu.roll(page, 1, axis=1)) & (lane_wide > 0))[0:1]
    valid = lane_wide[0:1] < picked
    sub_wide = lax.broadcasted_iota(jnp.int32, (pages, wide.shape[1]), 0)
    in_page = one_hot(sub_wide == page[0:1])
    owner = jnp.sum(in_page * owner_col[:, 0:1], axis=0, keepdims=True)
    rank = jnp.sum(in_page * rank_col, axis=0, keepdims=True)
    return owner_row[0:1], local_row, rank_col, owner, rank, second, offset, valid


def index_kernel(hold, page_len, first, own, table_ref, sel_ref, out_ref, *rest):
    first_refs, wide = rest[:-1], rest[-1]
    holders = out_ref.shape[0]
    pages = table_ref.shape[1]
    f32 = jnp.float32
    bf16 = jnp.bfloat16
    owner_row, local_row, rank_col, owner, rank, second, offset, valid = pair_places(
        hold, page_len, table_ref, sel_ref, wide
    )
    holder = lax.broadcasted_iota(jnp.int32, (holders, pages), 0).astype(f32)
    owned = jnp.where(holder == owner_row, local_row, 0.0)
    lane = lax.broadcasted_iota(jnp.int32, (pages, LANES), 1).astype(f32)
    numbers = jnp.dot(
        owned.astype(bf16), one_hot(lane == rank_col).astype(bf16), preferred_element_type=f32
    )
    holder_wide = lax.broadcasted_iota(jnp.int32, (holders, wide.shape[1]), 0).astype(f32)
    marked = jnp.where((holder_wide == owner) & valid, rank * page_len + offset + 1.0, 0.0)
    place_lane = lax.broadcasted_iota(jnp.int32, (LANES, wide.shape[1]), 0).astype(f32)
    at_place = one_hot(place_lane == SELP * rank + second)
    targets = nt_dot(marked.astype(bf16), at_place.astype(bf16))
    for h in range(holders):
        out_ref[h, 0:1, :] = numbers[h : h + 1, :].astype(jnp.int32)
        out_ref[h, 1:2, :] = targets[h : h + 1, :].astype(jnp.int32)
    for d, ref in zip(first, first_refs):
        ref[0] = out_ref[own[0] ^ d]


def rows_kernel(hold, page_len, table_ref, sel_ref, fresh_ref, packed, wide):
    holders = packed.shape[0]
    picked = sel_ref.shape[1]
    f32 = jnp.float32
    _, _, _, owner, rank, second, _, valid = pair_places(hold, page_len, table_ref, sel_ref, wide)
    spot = jnp.where(valid, owner * ROW_SLOTS + SELP * rank + second, -1.0)[:, 0:picked]
    step = min(holders, 16)
    for start in range(0, holders, step):
        spot_id = lax.broadcasted_iota(jnp.int32, (step * ROW_SLOTS, picked), 0).astype(f32)
        choose = one_hot(spot_id + float(start * ROW_SLOTS) == spot).astype(jnp.bfloat16)
        rows = jnp.dot(choose, fresh_ref[...], preferred_element_type=f32).astype(jnp.bfloat16)
        packed[start : start + step] = rows.reshape(step, ROW_SLOTS, fresh_ref.shape[1])


def first_gather_kernel(count, *refs):
    lists, store_hbm, sends = refs[:count], refs[count], refs[count + 1 : 2 * count + 1]
    held, load_sem, send_sem = refs[2 * count + 1 :]
    capacity = held.shape[1]
    for i, numbers in enumerate(lists):
        for k in range(capacity):
            pltpu.make_async_copy(store_hbm.at[numbers[0, 0, k]], held.at[i, k], load_sem).start()
    pltpu.make_async_copy(held, held, load_sem).wait()
    for i, send in enumerate(sends):
        pltpu.make_async_copy(held.at[i], send, send_sem).start()
    pltpu.make_async_copy(held, held, send_sem).wait()


def gather_kernel(capacity, distances, own, index, store_hbm, *rest):
    sends, (store, load_sem, send_sem) = rest[:-3], rest[-3:]
    load = pltpu.make_async_copy(store_hbm, store, load_sem)
    load.start()
    load.wait()
    for i in range(len(distances) if distances else index.shape[0]):
        r = own[0] ^ distances[i] if distances else i
        send = sends[i] if distances else sends[0].at[i]
        for k in range(capacity):
            pltpu.make_async_copy(store.at[index[r, 0, k]], send.at[k], send_sem).start()
    for send in sends:
        pltpu.make_async_copy(send, send, send_sem).wait()


def write_back_kernel(index, targets_ref, store_hbm, rows_hbm, store_out, *scratch):
    store, rows, blended, load_sem, rows_sem, out_sem = scratch
    holders, capacity, page_len, width = blended.shape
    rows_here = capacity * page_len
    f32 = jnp.float32
    load = pltpu.make_async_copy(store_hbm, store, load_sem)
    load_rows = pltpu.make_async_copy(rows_hbm, rows, rows_sem)
    load.start()
    load_rows.start()
    load_rows.wait()
    load.wait()
    row_id = lax.broadcasted_iota(jnp.int32, (rows_here, ROW_SLOTS), 0)

    def one_request(r, carry):
        hit = one_hot(row_id == targets_ref[r][1:2, 0:ROW_SLOTS] - 1)
        keep = 1.0 - jnp.sum(hit, axis=1, keepdims=True)
        keep = jnp.broadcast_to(keep, (rows_here, LANES)).astype(jnp.bfloat16)
        hit = hit.astype(jnp.bfloat16)
        for c in range(width // LANES):
            lanes = slice(c * LANES, (c + 1) * LANES)
            fresh = jnp.dot(hit, rows[r, :, lanes], preferred_element_type=f32).astype(jnp.bfloat16)
            for k in range(capacity):
                part = slice(k * page_len, (k + 1) * page_len)
                blended[r, k, :, lanes] = store[index[r, 0, k], :, lanes] * keep[part] + fresh[part]
        for k in range(capacity):
            pltpu.make_async_copy(blended.at[r, k], store_out.at[index[r, 0, k]], out_sem).start()
        return carry

    lax.fori_loop(0, holders, one_request, 0)
    pltpu.make_async_copy(store_out, store_out, out_sem).wait()


def attend_kernel(first, last, sources, place, tiles, *rest):
    sel_ref, position, query_ref, *rest = rest
    if first:
        fresh_ref, *rest = rest
    state_in = () if first else rest[:2]
    rest = rest if first else rest[2:]
    contexts, rest = rest[:sources], rest[sources:]
    outs, rest = (rest[:1], rest[1:]) if last else (rest[:2], rest[2:])
    kv, values, query, scores, raised, mixed, stats, sem = rest
    pages, page_len, width = kv.shape
    each = contexts[0].shape[0]
    direct = last and not first
    block = query_ref.shape[0]
    tile = TILE_PAGES * page_len
    lanes = QUERY_GROUP * block
    scale = 1.4426950408889634 / HEAD_WIDTH**0.5
    f32 = jnp.float32
    bf16 = jnp.bfloat16
    step = pl.program_id(0)
    eye = one_hot(
        lax.broadcasted_iota(jnp.int32, (LANES, LANES), 0)
        == lax.broadcasted_iota(jnp.int32, (LANES, LANES), 1)
    ).astype(bf16)

    @pl.when(step == 0)
    def _():
        for i, context in enumerate(contexts):
            if direct:
                kv[i * each : (i + 1) * each] = context[...]
            else:
                for k in range(each):
                    to = kv.at[place[i * each + k]]
                    pltpu.make_async_copy(context.at[k], to, sem).start()
        if first:
            count = fresh_ref.shape[0] // page_len
            for p in range(count):
                page = fresh_ref[p * page_len : (p + 1) * page_len, :]
                kv[place[sources * each + p]] = page
            used = sources * each + count
            if pages > used:
                kv[used:] = jnp.zeros((pages - used, page_len, width), bf16)
        if not direct:
            arrived = kv.at[0 : sources * each]
            pltpu.make_async_copy(arrived, arrived, sem).wait()

        def turn(t, carry):
            here = pl.ds(t * TILE_PAGES, TILE_PAGES)
            for g in range(KEY_VALUE_HEADS):
                at = (KEY_VALUE_HEADS + g) * LANES
                value = kv[here, :, at : at + LANES].reshape(tile, LANES)
                values[t, g] = nt_dot(eye, value).astype(bf16)
            return carry

        lax.fori_loop(0, pages // TILE_PAGES, turn, 0)

    for g in range(KEY_VALUE_HEADS):
        for i in range(QUERY_GROUP):
            head = g * QUERY_GROUP + i
            query[g, i * block : (i + 1) * block, :] = query_ref[:, head * LANES : (head + 1) * LANES]
    if first:
        mixed[...] = jnp.zeros(mixed.shape, f32)
        stats[0:KEY_VALUE_HEADS, :] = jnp.full((KEY_VALUE_HEADS, lanes), HIDDEN, f32)
        stats[KEY_VALUE_HEADS:, :] = jnp.zeros((KEY_VALUE_HEADS, lanes), f32)
    else:
        mixed[...] = state_in[0][0]
        stats[...] = state_in[1][0]

    sel = sel_ref[0]

    def one_tile(t, carry):
        here = pl.ds(t * TILE_PAGES, TILE_PAGES)
        bias = jnp.where(
            position[pl.ds(pl.multiple_of(t * tile, tile), tile), :] <= sel, 0.0, HIDDEN
        ).astype(f32)

        parts = [slice(n * LANES, (n + 1) * LANES) for n in range(lanes // LANES)]
        chains = [(g, part) for g in range(KEY_VALUE_HEADS) for part in parts]
        for g in range(KEY_VALUE_HEADS):
            key = kv[here, :, g * LANES : (g + 1) * LANES].reshape(tile, LANES)
            product = nt_dot(key, query[g])
            for part in parts:
                scores[g, :, part] = product[:, part] + bias
        peaks, shrinks = [], []
        for g, part in chains:
            old = stats[g : g + 1, part]
            new = jnp.maximum(old, jnp.max(scores[g, :, part], axis=0, keepdims=True))
            stats[g : g + 1, part] = new
            peaks.append(new)
            shrinks.append(jnp.exp2((old - new) * scale))
        for (g, part), new, shrink in zip(chains, peaks, shrinks):
            at = KEY_VALUE_HEADS + g
            p = jnp.exp2((scores[g, :, part] - new) * scale)
            stats[at : at + 1, part] = stats[at : at + 1, part] * shrink + jnp.sum(
                p, axis=0, keepdims=True
            )
            raised[g, :, part] = p.astype(bf16)
        for g in range(KEY_VALUE_HEADS):
            shrink = jnp.concatenate(shrinks[g * len(parts) : (g + 1) * len(parts)], axis=1)
            mixed[g] = mixed[g] * shrink + jnp.dot(
                values[t, g], raised[g], preferred_element_type=f32
            )
        return carry

    lax.fori_loop(0, tiles[step], one_tile, 0)

    if last:
        done = []
        for g in range(KEY_VALUE_HEADS):
            at = KEY_VALUE_HEADS + g
            part = (mixed[g] * (1.0 / stats[at : at + 1, :])).astype(bf16)
            done += [part[:, n * LANES : (n + 1) * LANES] for n in range(lanes // LANES)]
        turned = nt_dot(eye, jnp.concatenate(done, axis=0)).astype(bf16)
        for n in range(len(done)):
            for i in range(LANES // block):
                head = n * (LANES // block) + i
                outs[0][:, head * LANES : (head + 1) * LANES] = turned[
                    i * block : (i + 1) * block, n * LANES : (n + 1) * LANES
                ]
    else:
        outs[0][0] = mixed[...]
        outs[1][0] = stats[...]


def attend(first, last, order, sel_lanes, queries, fresh, state, contexts):
    place, tiles, position = order
    picked, features = queries.shape
    each, page_len, width = contexts[0].shape
    pages = position.shape[0] // page_len
    steps = picked // QUERY_BLOCK
    lanes = QUERY_GROUP * QUERY_BLOCK
    wide = pl.BlockSpec((QUERY_BLOCK, features), lambda b, *_: (b, 0))
    state_specs = [
        pl.BlockSpec((1, KEY_VALUE_HEADS, LANES, lanes), lambda b, *_: (b, 0, 0, 0)),
        pl.BlockSpec((1, 2 * KEY_VALUE_HEADS, lanes), lambda b, *_: (b, 0, 0)),
    ]
    state_shapes = [
        jax.ShapeDtypeStruct((steps, KEY_VALUE_HEADS, LANES, lanes), jnp.float32),
        jax.ShapeDtypeStruct((steps, 2 * KEY_VALUE_HEADS, lanes), jnp.float32),
    ]
    share = 0.6
    return pl.pallas_call(
        functools.partial(attend_kernel, first, last, len(contexts)),
        grid_spec=pltpu.PrefetchScalarGridSpec(
            num_scalar_prefetch=2,
            grid=(steps,),
            in_specs=[
                pl.BlockSpec((1, 1, LANES), lambda b, *_: (b, 0, 0)),
                pl.BlockSpec(position.shape, lambda b, *_: (0, 0)),
                wide,
                *([pl.BlockSpec(fresh.shape, lambda b, *_: (0, 0))] if first else state_specs),
                *[
                    pl.BlockSpec(x.shape, lambda b, *_: (0, 0, 0))
                    if last and not first
                    else pl.BlockSpec(memory_space=pltpu.HBM)
                    for x in contexts
                ],
            ],
            out_specs=[wide] if last else state_specs,
            scratch_shapes=[
                pltpu.VMEM((pages, page_len, width), jnp.bfloat16),
                pltpu.VMEM(
                    (pages // TILE_PAGES, KEY_VALUE_HEADS, LANES, TILE_PAGES * page_len), jnp.bfloat16
                ),
                pltpu.VMEM((KEY_VALUE_HEADS, lanes, LANES), jnp.bfloat16),
                pltpu.VMEM((KEY_VALUE_HEADS, TILE_PAGES * page_len, lanes), jnp.float32),
                pltpu.VMEM((KEY_VALUE_HEADS, TILE_PAGES * page_len, lanes), jnp.bfloat16),
                pltpu.VMEM((KEY_VALUE_HEADS, LANES, lanes), jnp.float32),
                pltpu.VMEM((2 * KEY_VALUE_HEADS, lanes), jnp.float32),
                pltpu.SemaphoreType.DMA,
            ],
        ),
        out_shape=[jax.ShapeDtypeStruct((picked, features), jnp.bfloat16)] if last else state_shapes,
        compiler_params=pltpu.CompilerParams(
            dimension_semantics=("arbitrary",), vmem_limit_bytes=VMEM_LIMIT
        ),
        cost_estimate=pl.CostEstimate(
            flops=int(share * 8 * picked * features * pages * page_len),
            bytes_accessed=2 * pages * page_len * width + 6 * picked * features,
            transcendentals=int(share * picked * features // LANES * pages * page_len),
        ),
    )(place, tiles, sel_lanes, position, queries, *([fresh] if first else state), *contexts)


def page_order(slots, positions, own, hold, capacity, groups, page_len):
    pages = slots.shape[0]
    number = jnp.arange(pages)
    before = number[None, :] < number[:, None]
    owners = slots // hold
    ranks = jnp.sum(((owners[None, :] == owners[:, None]) & before).astype(jnp.int32), axis=1)
    distance = owners ^ own
    last_position = positions.reshape(-1, QUERY_BLOCK)[:, -1:]
    starts = number * page_len
    replaced = jnp.any(
        (starts[:, None] + jnp.arange(page_len)[None, :])[:, :, None] == positions, axis=2
    )
    fresh = positions.reshape(-1, page_len)
    orders = []
    for at, group in enumerate(groups):
        if group is None:
            arrival = owners * capacity + ranks
            count = pages
        else:
            arrival = jnp.full((pages,), -1, jnp.int32)
            for i, d in enumerate(group):
                arrival = jnp.where(distance == d, i * capacity + ranks, arrival)
            count = len(group) * capacity
        member = arrival >= 0
        place = jnp.sum((member[None, :] & before).astype(jnp.int32), axis=1)
        seen = jnp.sum((member & (starts <= last_position)).astype(jnp.int32), axis=1)
        total = count
        if at == 0:
            place = place + jnp.sum((fresh[None, :, 0] < starts[:, None]).astype(jnp.int32), axis=1)
            ahead = jnp.sum((member & (starts <= fresh[:, 0:1])).astype(jnp.int32), axis=1)
            fresh_place = jnp.arange(fresh.shape[0]) + ahead
            seen = seen + jnp.sum((fresh[None, :, 0] <= last_position).astype(jnp.int32), axis=1)
            total = count + fresh.shape[0]
        elif at == len(groups) - 1:
            place = arrival
        places = jnp.where(arrival == jnp.arange(count)[:, None], place, 0)
        places = jnp.sum(places, axis=1)
        index = jnp.arange(-(-total // TILE_PAGES) * TILE_PAGES)[:, None]
        here = member & (place == index)
        inside = jnp.arange(page_len)
        rows = starts[:, None] + inside
        rows = jnp.where(replaced, FAR_POSITION, rows)
        rows = jnp.sum(jnp.where(here[:, :, None], rows, 0), axis=1)
        filled = jnp.any(here, axis=1, keepdims=True)
        if at == 0:
            there = fresh_place == index
            rows = rows + jnp.sum(jnp.where(there[:, :, None], fresh, 0), axis=1)
            filled = filled | jnp.any(there, axis=1, keepdims=True)
            places = jnp.concatenate([places, fresh_place])
        rows = jnp.where(filled, rows, FAR_POSITION).reshape(-1, 1)
        rows = jnp.broadcast_to(rows, (rows.shape[0], LANES))
        orders.append((places, (seen + TILE_PAGES - 1) // TILE_PAGES, rows))
    return orders


def per_device(store, page_table, sel_pos, fresh_kv, queries):
    holders = lax.axis_size("store")
    hold, page_len, width = store.shape
    pages = page_table.shape[1]
    picked = sel_pos.shape[1]
    capacity = max(1, pages // holders)
    hbm = pl.BlockSpec(memory_space=pltpu.HBM)
    vmem = pl.BlockSpec(memory_space=pltpu.VMEM)
    dma = pltpu.SemaphoreType.DMA
    params = pltpu.CompilerParams(vmem_limit_bytes=VMEM_LIMIT)
    own = lax.axis_index("store")
    own_word = own.reshape(1).astype(jnp.int32)
    fresh = fresh_kv[0]
    wide = pltpu.VMEM((8, -(-picked // LANES) * LANES), jnp.int32)
    if holders == 16:
        first = (8, 12)
        groups = [(0, 8, 12, 4), (5, 1, 9, 6, 13, 7, 10, 2, 14, 3), (11, 15)]
        others = [d for group in groups for d in group if d not in first]
    else:
        first = ()
        groups = [None]
        others = None

    def swap(x, d):
        return lax.ppermute(x, "store", [(h, h ^ d) for h in range(holders)])

    def exchange(x):
        return lax.all_to_all(x, "store", split_axis=0, concat_axis=0, tiled=True)

    index, *lists = pl.pallas_call(
        functools.partial(index_kernel, hold, page_len, first),
        grid_spec=pltpu.PrefetchScalarGridSpec(
            num_scalar_prefetch=1,
            grid=(1,),
            in_specs=[vmem, vmem],
            out_specs=[vmem] * (1 + len(first)),
            scratch_shapes=[wide],
        ),
        out_shape=[
            jax.ShapeDtypeStruct((holders, 2, LANES), jnp.int32),
            *[jax.ShapeDtypeStruct((1, 2, LANES), jnp.int32)] * len(first),
        ],
        compiler_params=params,
    )(own_word, page_table, sel_pos)
    arrived = {}
    if first:
        lists = [swap(x, d) for x, d in zip(lists, first)]
        parts = pl.pallas_call(
            functools.partial(first_gather_kernel, len(first)),
            grid_spec=pltpu.PrefetchScalarGridSpec(
                num_scalar_prefetch=len(first),
                grid=(1,),
                in_specs=[hbm],
                out_specs=[hbm] * len(first),
                scratch_shapes=[
                    pltpu.VMEM((len(first), capacity, page_len, width), store.dtype),
                    dma,
                    dma,
                ],
            ),
            out_shape=[jax.ShapeDtypeStruct((capacity, page_len, width), store.dtype)] * len(first),
            compiler_params=params,
        )(*lists, store)
        parts, index, table, positions = lax.optimization_barrier(
            (parts, index, page_table, sel_pos)
        )
        arrived = {d: swap(part, d) for d, part in zip(first, parts)}
    else:
        table, positions = page_table, sel_pos
    index_in = exchange(index)

    packed = pl.pallas_call(
        functools.partial(rows_kernel, hold, page_len),
        out_shape=jax.ShapeDtypeStruct((holders, ROW_SLOTS, width), store.dtype),
        scratch_shapes=[wide],
        compiler_params=params,
    )(table, positions, fresh)

    each = jax.ShapeDtypeStruct((capacity, page_len, width), store.dtype)
    whole = jax.ShapeDtypeStruct((holders, capacity, page_len, width), store.dtype)
    parts = pl.pallas_call(
        functools.partial(gather_kernel, capacity, others),
        grid_spec=pltpu.PrefetchScalarGridSpec(
            num_scalar_prefetch=2,
            grid=(1,),
            in_specs=[hbm],
            out_specs=[hbm] * (len(others) if others else 1),
            scratch_shapes=[pltpu.VMEM(store.shape, store.dtype), dma, dma],
        ),
        out_shape=[each] * len(others) if others else [whole],
        compiler_params=params,
    )(own_word, index_in, store)
    parts, packed, table, positions = lax.optimization_barrier((parts, packed, table, positions))
    if others:
        parts = dict(zip(others, parts))
        for d in others:
            arrived[d] = swap(parts[d], d) if d else parts[d]
    else:
        arrived[None] = exchange(parts[0]).reshape(pages, page_len, width)
    rows_in = exchange(packed)

    store_out = pl.pallas_call(
        write_back_kernel,
        grid_spec=pltpu.PrefetchScalarGridSpec(
            num_scalar_prefetch=1,
            grid=(1,),
            in_specs=[vmem, hbm, hbm],
            out_specs=hbm,
            scratch_shapes=[
                pltpu.VMEM(store.shape, store.dtype),
                pltpu.VMEM((holders, ROW_SLOTS, width), store.dtype),
                pltpu.VMEM((holders, capacity, page_len, width), store.dtype),
                dma,
                dma,
                dma,
            ],
        ),
        out_shape=jax.ShapeDtypeStruct(store.shape, store.dtype),
        compiler_params=params,
        cost_estimate=pl.CostEstimate(flops=0, bytes_accessed=4 * store.size, transcendentals=0),
    )(index_in, index_in, store, rows_in)

    orders = page_order(table[0], positions[0], own, hold, capacity, groups, page_len)
    sel_lanes = jnp.tile(positions.reshape(-1, 1, QUERY_BLOCK), (1, 1, LANES // QUERY_BLOCK))
    store_out, sel_lanes = lax.optimization_barrier((store_out, sel_lanes))
    state = ()
    for at, (group, order) in enumerate(zip(groups, orders)):
        state = attend(
            at == 0,
            at == len(groups) - 1,
            order,
            sel_lanes,
            queries[0],
            fresh,
            state,
            [arrived[d] for d in group or [None]],
        )
    return (state[0][None], store_out)


def solution(mesh):
    return jax.shard_map(
        per_device,
        mesh=mesh,
        in_specs=(
            P(("groups", "store"), None, None),
            P(("groups", "store"), None),
            P(("groups", "store"), None),
            P(("groups", "store"), None, None),
            P(("groups", "store"), None, None),
        ),
        out_specs=(P(("groups", "store"), None, None), P(("groups", "store"), None, None)),
        check_vma=False,
    )
```

```python
import functools

import jax
import jax.numpy as jnp
from jax import lax
from jax.experimental import pallas as pl
from jax.experimental.pallas import tpu as pltpu
from jax.sharding import PartitionSpec as P

HEAD_WIDTH = 128
KEY_VALUE_HEADS = 4
QUERY_GROUP = 12
SELP = 2
LANES = 128
ROW_SLOTS = 16
VMEM_LIMIT = 60 * 1024 * 1024
QUERY_BLOCK = 32
TILE_PAGES = 16
HIDDEN = -1e30
FAR_POSITION = 1 << 24


def nt_dot(a, b):
    return lax.dot_general(a, b, (((1,), (1,)), ((), ())), preferred_element_type=jnp.float32)


def one_hot(condition):
    return jnp.where(condition, 1.0, 0.0)


def pair_places(hold, page_len, table_ref, sel_ref, wide):
    pages = table_ref.shape[1]
    picked = sel_ref.shape[1]
    f32 = jnp.float32
    slots = jnp.broadcast_to(table_ref[...], (pages, pages))
    owners = slots // hold
    local_row = (slots - owners * hold).astype(f32)[0:1]
    owner_row = owners.astype(f32)
    owner_col = owner_row.T
    sub = lax.broadcasted_iota(jnp.int32, (pages, pages), 0)
    lane = lax.broadcasted_iota(jnp.int32, (pages, pages), 1)
    earlier = one_hot((owner_row == owner_col) & (lane < sub))
    rank_col = jnp.sum(earlier, axis=1, keepdims=True)

    wide[...] = jnp.full(wide.shape, -1, jnp.int32)
    wide[0:1, 0:picked] = sel_ref[...]
    position = wide[...]
    page = lax.shift_right_arithmetic(position, page_len.bit_length() - 1)
    offset = (position & (page_len - 1)).astype(f32)[0:1]
    lane_wide = lax.broadcasted_iota(jnp.int32, wide.shape, 1)
    second = one_hot((page == pltpu.roll(page, 1, axis=1)) & (lane_wide > 0))[0:1]
    valid = lane_wide[0:1] < picked
    sub_wide = lax.broadcasted_iota(jnp.int32, (pages, wide.shape[1]), 0)
    in_page = one_hot(sub_wide == page[0:1])
    owner = jnp.sum(in_page * owner_col[:, 0:1], axis=0, keepdims=True)
    rank = jnp.sum(in_page * rank_col, axis=0, keepdims=True)
    return owner_row[0:1], local_row, rank_col, owner, rank, second, offset, valid


def index_kernel(hold, page_len, first, own, table_ref, sel_ref, out_ref, *rest):
    first_refs, wide = rest[:-1], rest[-1]
    holders = out_ref.shape[0]
    pages = table_ref.shape[1]
    f32 = jnp.float32
    bf16 = jnp.bfloat16
    owner_row, local_row, rank_col, owner, rank, second, offset, valid = pair_places(
        hold, page_len, table_ref, sel_ref, wide
    )
    holder = lax.broadcasted_iota(jnp.int32, (holders, pages), 0).astype(f32)
    owned = jnp.where(holder == owner_row, local_row, 0.0)
    lane = lax.broadcasted_iota(jnp.int32, (pages, LANES), 1).astype(f32)
    numbers = jnp.dot(
        owned.astype(bf16), one_hot(lane == rank_col).astype(bf16), preferred_element_type=f32
    )
    holder_wide = lax.broadcasted_iota(jnp.int32, (holders, wide.shape[1]), 0).astype(f32)
    marked = jnp.where((holder_wide == owner) & valid, rank * page_len + offset + 1.0, 0.0)
    place_lane = lax.broadcasted_iota(jnp.int32, (LANES, wide.shape[1]), 0).astype(f32)
    at_place = one_hot(place_lane == SELP * rank + second)
    targets = nt_dot(marked.astype(bf16), at_place.astype(bf16))
    for h in range(holders):
        out_ref[h, 0:1, :] = numbers[h : h + 1, :].astype(jnp.int32)
        out_ref[h, 1:2, :] = targets[h : h + 1, :].astype(jnp.int32)
    for d, ref in zip(first, first_refs):
        ref[0] = out_ref[own[0] ^ d]


def rows_kernel(hold, page_len, table_ref, sel_ref, fresh_ref, packed, wide):
    holders = packed.shape[0]
    picked = sel_ref.shape[1]
    f32 = jnp.float32
    _, _, _, owner, rank, second, _, valid = pair_places(hold, page_len, table_ref, sel_ref, wide)
    spot = jnp.where(valid, owner * ROW_SLOTS + SELP * rank + second, -1.0)[:, 0:picked]
    step = min(holders, 16)
    for start in range(0, holders, step):
        spot_id = lax.broadcasted_iota(jnp.int32, (step * ROW_SLOTS, picked), 0).astype(f32)
        choose = one_hot(spot_id + float(start * ROW_SLOTS) == spot).astype(jnp.bfloat16)
        rows = jnp.dot(choose, fresh_ref[...], preferred_element_type=f32).astype(jnp.bfloat16)
        packed[start : start + step] = rows.reshape(step, ROW_SLOTS, fresh_ref.shape[1])


def first_gather_kernel(count, *refs):
    lists, store_hbm, sends = refs[:count], refs[count], refs[count + 1 : 2 * count + 1]
    held, load_sem, send_sem = refs[2 * count + 1 :]
    capacity = held.shape[1]
    for i, numbers in enumerate(lists):
        for k in range(capacity):
            pltpu.make_async_copy(store_hbm.at[numbers[0, 0, k]], held.at[i, k], load_sem).start()
    pltpu.make_async_copy(held, held, load_sem).wait()
    for i, send in enumerate(sends):
        pltpu.make_async_copy(held.at[i], send, send_sem).start()
    pltpu.make_async_copy(held, held, send_sem).wait()


def gather_kernel(capacity, distances, own, index, store_hbm, *rest):
    sends, (store, load_sem, send_sem) = rest[:-3], rest[-3:]
    load = pltpu.make_async_copy(store_hbm, store, load_sem)
    load.start()
    load.wait()
    for i in range(len(distances) if distances else index.shape[0]):
        r = own[0] ^ distances[i] if distances else i
        send = sends[i] if distances else sends[0].at[i]
        for k in range(capacity):
            pltpu.make_async_copy(store.at[index[r, 0, k]], send.at[k], send_sem).start()
    for send in sends:
        pltpu.make_async_copy(send, send, send_sem).wait()


def write_back_kernel(index, targets_ref, store_hbm, rows_hbm, store_out, *scratch):
    store, rows, blended, load_sem, rows_sem, out_sem = scratch
    holders, capacity, page_len, width = blended.shape
    rows_here = capacity * page_len
    f32 = jnp.float32
    load = pltpu.make_async_copy(store_hbm, store, load_sem)
    load_rows = pltpu.make_async_copy(rows_hbm, rows, rows_sem)
    load.start()
    load_rows.start()
    load_rows.wait()
    load.wait()
    row_id = lax.broadcasted_iota(jnp.int32, (rows_here, ROW_SLOTS), 0)

    def one_request(r, carry):
        hit = one_hot(row_id == targets_ref[r][1:2, 0:ROW_SLOTS] - 1)
        keep = 1.0 - jnp.sum(hit, axis=1, keepdims=True)
        keep = jnp.broadcast_to(keep, (rows_here, LANES)).astype(jnp.bfloat16)
        hit = hit.astype(jnp.bfloat16)
        for c in range(width // LANES):
            lanes = slice(c * LANES, (c + 1) * LANES)
            fresh = jnp.dot(hit, rows[r, :, lanes], preferred_element_type=f32).astype(jnp.bfloat16)
            for k in range(capacity):
                part = slice(k * page_len, (k + 1) * page_len)
                blended[r, k, :, lanes] = store[index[r, 0, k], :, lanes] * keep[part] + fresh[part]
        for k in range(capacity):
            pltpu.make_async_copy(blended.at[r, k], store_out.at[index[r, 0, k]], out_sem).start()
        return carry

    lax.fori_loop(0, holders, one_request, 0)
    pltpu.make_async_copy(store_out, store_out, out_sem).wait()


def attend_kernel(first, last, sources, place, tiles, *rest):
    sel_ref, position, query_ref, *rest = rest
    if first:
        fresh_ref, *rest = rest
    state_in = () if first else rest[:2]
    rest = rest if first else rest[2:]
    contexts, rest = rest[:sources], rest[sources:]
    outs, rest = (rest[:1], rest[1:]) if last else (rest[:2], rest[2:])
    kv, values, query, scores, raised, mixed, stats, sem = rest
    pages, page_len, width = kv.shape
    each = contexts[0].shape[0]
    direct = last and not first
    block = query_ref.shape[0]
    tile = TILE_PAGES * page_len
    lanes = QUERY_GROUP * block
    scale = 1.4426950408889634 / HEAD_WIDTH**0.5
    f32 = jnp.float32
    bf16 = jnp.bfloat16
    step = pl.program_id(0)
    eye = one_hot(
        lax.broadcasted_iota(jnp.int32, (LANES, LANES), 0)
        == lax.broadcasted_iota(jnp.int32, (LANES, LANES), 1)
    ).astype(bf16)

    @pl.when(step == 0)
    def _():
        for i, context in enumerate(contexts):
            if direct:
                kv[i * each : (i + 1) * each] = context[...]
            else:
                for k in range(each):
                    to = kv.at[place[i * each + k]]
                    pltpu.make_async_copy(context.at[k], to, sem).start()
        if first:
            count = fresh_ref.shape[0] // page_len
            for p in range(count):
                page = fresh_ref[p * page_len : (p + 1) * page_len, :]
                kv[place[sources * each + p]] = page
            used = sources * each + count
            if pages > used:
                kv[used:] = jnp.zeros((pages - used, page_len, width), bf16)
        if not direct:
            arrived = kv.at[0 : sources * each]
            pltpu.make_async_copy(arrived, arrived, sem).wait()

        def turn(t, carry):
            here = pl.ds(t * TILE_PAGES, TILE_PAGES)
            for g in range(KEY_VALUE_HEADS):
                at = (KEY_VALUE_HEADS + g) * LANES
                value = kv[here, :, at : at + LANES].reshape(tile, LANES)
                values[t, g] = nt_dot(eye, value).astype(bf16)
            return carry

        lax.fori_loop(0, pages // TILE_PAGES, turn, 0)

    for g in range(KEY_VALUE_HEADS):
        for i in range(QUERY_GROUP):
            head = g * QUERY_GROUP + i
            query[g, i * block : (i + 1) * block, :] = query_ref[:, head * LANES : (head + 1) * LANES]
    if first:
        mixed[...] = jnp.zeros(mixed.shape, f32)
        stats[0:KEY_VALUE_HEADS, :] = jnp.full((KEY_VALUE_HEADS, lanes), HIDDEN, f32)
        stats[KEY_VALUE_HEADS:, :] = jnp.zeros((KEY_VALUE_HEADS, lanes), f32)
    else:
        mixed[...] = state_in[0][0]
        stats[...] = state_in[1][0]

    sel = sel_ref[0]

    def one_tile(t, carry):
        here = pl.ds(t * TILE_PAGES, TILE_PAGES)
        bias = jnp.where(
            position[pl.ds(pl.multiple_of(t * tile, tile), tile), :] <= sel, 0.0, HIDDEN
        ).astype(f32)

        parts = [slice(n * LANES, (n + 1) * LANES) for n in range(lanes // LANES)]
        chains = [(g, part) for g in range(KEY_VALUE_HEADS) for part in parts]
        for g in range(KEY_VALUE_HEADS):
            key = kv[here, :, g * LANES : (g + 1) * LANES].reshape(tile, LANES)
            product = nt_dot(key, query[g])
            for part in parts:
                scores[g, :, part] = product[:, part] + bias
        peaks, shrinks = [], []
        for g, part in chains:
            old = stats[g : g + 1, part]
            new = jnp.maximum(old, jnp.max(scores[g, :, part], axis=0, keepdims=True))
            stats[g : g + 1, part] = new
            peaks.append(new)
            shrinks.append(jnp.exp2((old - new) * scale))
        for (g, part), new, shrink in zip(chains, peaks, shrinks):
            at = KEY_VALUE_HEADS + g
            p = jnp.exp2((scores[g, :, part] - new) * scale)
            stats[at : at + 1, part] = stats[at : at + 1, part] * shrink + jnp.sum(
                p, axis=0, keepdims=True
            )
            raised[g, :, part] = p.astype(bf16)
        for g in range(KEY_VALUE_HEADS):
            shrink = jnp.concatenate(shrinks[g * len(parts) : (g + 1) * len(parts)], axis=1)
            mixed[g] = mixed[g] * shrink + jnp.dot(
                values[t, g], raised[g], preferred_element_type=f32
            )
        return carry

    lax.fori_loop(0, tiles[step], one_tile, 0)

    if last:
        done = []
        for g in range(KEY_VALUE_HEADS):
            at = KEY_VALUE_HEADS + g
            part = (mixed[g] * (1.0 / stats[at : at + 1, :])).astype(bf16)
            done += [part[:, n * LANES : (n + 1) * LANES] for n in range(lanes // LANES)]
        turned = nt_dot(eye, jnp.concatenate(done, axis=0)).astype(bf16)
        for n in range(len(done)):
            for i in range(LANES // block):
                head = n * (LANES // block) + i
                outs[0][:, head * LANES : (head + 1) * LANES] = turned[
                    i * block : (i + 1) * block, n * LANES : (n + 1) * LANES
                ]
    else:
        outs[0][0] = mixed[...]
        outs[1][0] = stats[...]


def attend(first, last, order, sel_lanes, queries, fresh, state, contexts):
    place, tiles, position = order
    picked, features = queries.shape
    each, page_len, width = contexts[0].shape
    pages = position.shape[0] // page_len
    steps = picked // QUERY_BLOCK
    lanes = QUERY_GROUP * QUERY_BLOCK
    wide = pl.BlockSpec((QUERY_BLOCK, features), lambda b, *_: (b, 0))
    state_specs = [
        pl.BlockSpec((1, KEY_VALUE_HEADS, LANES, lanes), lambda b, *_: (b, 0, 0, 0)),
        pl.BlockSpec((1, 2 * KEY_VALUE_HEADS, lanes), lambda b, *_: (b, 0, 0)),
    ]
    state_shapes = [
        jax.ShapeDtypeStruct((steps, KEY_VALUE_HEADS, LANES, lanes), jnp.float32),
        jax.ShapeDtypeStruct((steps, 2 * KEY_VALUE_HEADS, lanes), jnp.float32),
    ]
    share = 0.6
    return pl.pallas_call(
        functools.partial(attend_kernel, first, last, len(contexts)),
        grid_spec=pltpu.PrefetchScalarGridSpec(
            num_scalar_prefetch=2,
            grid=(steps,),
            in_specs=[
                pl.BlockSpec((1, 1, LANES), lambda b, *_: (b, 0, 0)),
                pl.BlockSpec(position.shape, lambda b, *_: (0, 0)),
                wide,
                *([pl.BlockSpec(fresh.shape, lambda b, *_: (0, 0))] if first else state_specs),
                *[
                    pl.BlockSpec(x.shape, lambda b, *_: (0, 0, 0))
                    if last and not first
                    else pl.BlockSpec(memory_space=pltpu.HBM)
                    for x in contexts
                ],
            ],
            out_specs=[wide] if last else state_specs,
            scratch_shapes=[
                pltpu.VMEM((pages, page_len, width), jnp.bfloat16),
                pltpu.VMEM(
                    (pages // TILE_PAGES, KEY_VALUE_HEADS, LANES, TILE_PAGES * page_len), jnp.bfloat16
                ),
                pltpu.VMEM((KEY_VALUE_HEADS, lanes, LANES), jnp.bfloat16),
                pltpu.VMEM((KEY_VALUE_HEADS, TILE_PAGES * page_len, lanes), jnp.float32),
                pltpu.VMEM((KEY_VALUE_HEADS, TILE_PAGES * page_len, lanes), jnp.bfloat16),
                pltpu.VMEM((KEY_VALUE_HEADS, LANES, lanes), jnp.float32),
                pltpu.VMEM((2 * KEY_VALUE_HEADS, lanes), jnp.float32),
                pltpu.SemaphoreType.DMA,
            ],
        ),
        out_shape=[jax.ShapeDtypeStruct((picked, features), jnp.bfloat16)] if last else state_shapes,
        compiler_params=pltpu.CompilerParams(
            dimension_semantics=("arbitrary",), vmem_limit_bytes=VMEM_LIMIT
        ),
        cost_estimate=pl.CostEstimate(
            flops=int(share * 8 * picked * features * pages * page_len),
            bytes_accessed=2 * pages * page_len * width + 6 * picked * features,
            transcendentals=int(share * picked * features // LANES * pages * page_len),
        ),
    )(place, tiles, sel_lanes, position, queries, *([fresh] if first else state), *contexts)


def page_order(slots, positions, own, hold, capacity, groups, page_len):
    pages = slots.shape[0]
    number = jnp.arange(pages)
    before = number[None, :] < number[:, None]
    owners = slots // hold
    ranks = jnp.sum(((owners[None, :] == owners[:, None]) & before).astype(jnp.int32), axis=1)
    distance = owners ^ own
    last_position = positions.reshape(-1, QUERY_BLOCK)[:, -1:]
    starts = number * page_len
    replaced = jnp.any(
        (starts[:, None] + jnp.arange(page_len)[None, :])[:, :, None] == positions, axis=2
    )
    fresh = positions.reshape(-1, page_len)
    orders = []
    for at, group in enumerate(groups):
        if group is None:
            arrival = owners * capacity + ranks
            count = pages
        else:
            arrival = jnp.full((pages,), -1, jnp.int32)
            for i, d in enumerate(group):
                arrival = jnp.where(distance == d, i * capacity + ranks, arrival)
            count = len(group) * capacity
        member = arrival >= 0
        place = jnp.sum((member[None, :] & before).astype(jnp.int32), axis=1)
        seen = jnp.sum((member & (starts <= last_position)).astype(jnp.int32), axis=1)
        total = count
        if at == 0:
            place = place + jnp.sum((fresh[None, :, 0] < starts[:, None]).astype(jnp.int32), axis=1)
            ahead = jnp.sum((member & (starts <= fresh[:, 0:1])).astype(jnp.int32), axis=1)
            fresh_place = jnp.arange(fresh.shape[0]) + ahead
            seen = seen + jnp.sum((fresh[None, :, 0] <= last_position).astype(jnp.int32), axis=1)
            total = count + fresh.shape[0]
        elif at == len(groups) - 1:
            place = arrival
        places = jnp.where(arrival == jnp.arange(count)[:, None], place, 0)
        places = jnp.sum(places, axis=1)
        index = jnp.arange(-(-total // TILE_PAGES) * TILE_PAGES)[:, None]
        here = member & (place == index)
        inside = jnp.arange(page_len)
        rows = starts[:, None] + inside
        rows = jnp.where(replaced, FAR_POSITION, rows)
        rows = jnp.sum(jnp.where(here[:, :, None], rows, 0), axis=1)
        filled = jnp.any(here, axis=1, keepdims=True)
        if at == 0:
            there = fresh_place == index
            rows = rows + jnp.sum(jnp.where(there[:, :, None], fresh, 0), axis=1)
            filled = filled | jnp.any(there, axis=1, keepdims=True)
            places = jnp.concatenate([places, fresh_place])
        rows = jnp.where(filled, rows, FAR_POSITION).reshape(-1, 1)
        rows = jnp.broadcast_to(rows, (rows.shape[0], LANES))
        orders.append((places, (seen + TILE_PAGES - 1) // TILE_PAGES, rows))
    return orders


def per_device(store, page_table, sel_pos, fresh_kv, queries):
    holders = lax.axis_size("store")
    hold, page_len, width = store.shape
    pages = page_table.shape[1]
    picked = sel_pos.shape[1]
    capacity = max(1, pages // holders)
    hbm = pl.BlockSpec(memory_space=pltpu.HBM)
    vmem = pl.BlockSpec(memory_space=pltpu.VMEM)
    dma = pltpu.SemaphoreType.DMA
    params = pltpu.CompilerParams(vmem_limit_bytes=VMEM_LIMIT)
    own = lax.axis_index("store")
    own_word = own.reshape(1).astype(jnp.int32)
    fresh = fresh_kv[0]
    wide = pltpu.VMEM((8, -(-picked // LANES) * LANES), jnp.int32)
    if holders == 16:
        first = (8, 12)
        groups = [(0, 8, 12, 4), (7, 10, 2, 14, 3, 5, 1, 9, 6, 13), (11, 15)]
        others = [d for group in groups for d in group if d not in first]
    else:
        first = ()
        groups = [None]
        others = None

    def swap(x, d):
        return lax.ppermute(x, "store", [(h, h ^ d) for h in range(holders)])

    def exchange(x):
        return lax.all_to_all(x, "store", split_axis=0, concat_axis=0, tiled=True)

    index, *lists = pl.pallas_call(
        functools.partial(index_kernel, hold, page_len, first),
        grid_spec=pltpu.PrefetchScalarGridSpec(
            num_scalar_prefetch=1,
            grid=(1,),
            in_specs=[vmem, vmem],
            out_specs=[vmem] * (1 + len(first)),
            scratch_shapes=[wide],
        ),
        out_shape=[
            jax.ShapeDtypeStruct((holders, 2, LANES), jnp.int32),
            *[jax.ShapeDtypeStruct((1, 2, LANES), jnp.int32)] * len(first),
        ],
        compiler_params=params,
    )(own_word, page_table, sel_pos)
    arrived = {}
    if first:
        lists = [swap(x, d) for x, d in zip(lists, first)]
        parts = pl.pallas_call(
            functools.partial(first_gather_kernel, len(first)),
            grid_spec=pltpu.PrefetchScalarGridSpec(
                num_scalar_prefetch=len(first),
                grid=(1,),
                in_specs=[hbm],
                out_specs=[hbm] * len(first),
                scratch_shapes=[
                    pltpu.VMEM((len(first), capacity, page_len, width), store.dtype),
                    dma,
                    dma,
                ],
            ),
            out_shape=[jax.ShapeDtypeStruct((capacity, page_len, width), store.dtype)] * len(first),
            compiler_params=params,
        )(*lists, store)
        parts, index, table, positions = lax.optimization_barrier(
            (parts, index, page_table, sel_pos)
        )
        arrived = {d: swap(part, d) for d, part in zip(first, parts)}
    else:
        table, positions = page_table, sel_pos
    index_in = exchange(index)

    packed = pl.pallas_call(
        functools.partial(rows_kernel, hold, page_len),
        out_shape=jax.ShapeDtypeStruct((holders, ROW_SLOTS, width), store.dtype),
        scratch_shapes=[wide],
        compiler_params=params,
    )(table, positions, fresh)

    each = jax.ShapeDtypeStruct((capacity, page_len, width), store.dtype)
    whole = jax.ShapeDtypeStruct((holders, capacity, page_len, width), store.dtype)
    parts = pl.pallas_call(
        functools.partial(gather_kernel, capacity, others),
        grid_spec=pltpu.PrefetchScalarGridSpec(
            num_scalar_prefetch=2,
            grid=(1,),
            in_specs=[hbm],
            out_specs=[hbm] * (len(others) if others else 1),
            scratch_shapes=[pltpu.VMEM(store.shape, store.dtype), dma, dma],
        ),
        out_shape=[each] * len(others) if others else [whole],
        compiler_params=params,
    )(own_word, index_in, store)
    parts, packed, table, positions = lax.optimization_barrier((parts, packed, table, positions))
    if others:
        parts = dict(zip(others, parts))
        for d in others:
            arrived[d] = swap(parts[d], d) if d else parts[d]
    else:
        arrived[None] = exchange(parts[0]).reshape(pages, page_len, width)
    rows_in = exchange(packed)

    store_out = pl.pallas_call(
        write_back_kernel,
        grid_spec=pltpu.PrefetchScalarGridSpec(
            num_scalar_prefetch=1,
            grid=(1,),
            in_specs=[vmem, hbm, hbm],
            out_specs=hbm,
            scratch_shapes=[
                pltpu.VMEM(store.shape, store.dtype),
                pltpu.VMEM((holders, ROW_SLOTS, width), store.dtype),
                pltpu.VMEM((holders, capacity, page_len, width), store.dtype),
                dma,
                dma,
                dma,
            ],
        ),
        out_shape=jax.ShapeDtypeStruct(store.shape, store.dtype),
        compiler_params=params,
        cost_estimate=pl.CostEstimate(flops=0, bytes_accessed=4 * store.size, transcendentals=0),
    )(index_in, index_in, store, rows_in)

    orders = page_order(table[0], positions[0], own, hold, capacity, groups, page_len)
    sel_lanes = jnp.tile(positions.reshape(-1, 1, QUERY_BLOCK), (1, 1, LANES // QUERY_BLOCK))
    store_out, sel_lanes = lax.optimization_barrier((store_out, sel_lanes))
    state = ()
    for at, (group, order) in enumerate(zip(groups, orders)):
        state = attend(
            at == 0,
            at == len(groups) - 1,
            order,
            sel_lanes,
            queries[0],
            fresh,
            state,
            [arrived[d] for d in group or [None]],
        )
    return (state[0][None], store_out)


def solution(mesh):
    return jax.shard_map(
        per_device,
        mesh=mesh,
        in_specs=(
            P(("groups", "store"), None, None),
            P(("groups", "store"), None),
            P(("groups", "store"), None),
            P(("groups", "store"), None, None),
            P(("groups", "store"), None, None),
        ),
        out_specs=(P(("groups", "store"), None, None), P(("groups", "store"), None, None)),
        check_vma=False,
    )
```

```python
import functools

import jax
import jax.numpy as jnp
from jax import lax
from jax.experimental import pallas as pl
from jax.experimental.pallas import tpu as pltpu
from jax.sharding import PartitionSpec as P

HEAD_WIDTH = 128
KEY_VALUE_HEADS = 4
QUERY_GROUP = 12
SELP = 2
LANES = 128
ROW_SLOTS = 16
VMEM_LIMIT = 60 * 1024 * 1024
QUERY_BLOCK = 32
TILE_PAGES = 16
HIDDEN = -1e30
FAR_POSITION = 1 << 24


def nt_dot(a, b):
    return lax.dot_general(a, b, (((1,), (1,)), ((), ())), preferred_element_type=jnp.float32)


def one_hot(condition):
    return jnp.where(condition, 1.0, 0.0)


def pair_places(hold, page_len, table_ref, sel_ref, wide):
    pages = table_ref.shape[1]
    picked = sel_ref.shape[1]
    f32 = jnp.float32
    slots = jnp.broadcast_to(table_ref[...], (pages, pages))
    owners = slots // hold
    local_row = (slots - owners * hold).astype(f32)[0:1]
    owner_row = owners.astype(f32)
    owner_col = owner_row.T
    sub = lax.broadcasted_iota(jnp.int32, (pages, pages), 0)
    lane = lax.broadcasted_iota(jnp.int32, (pages, pages), 1)
    earlier = one_hot((owner_row == owner_col) & (lane < sub))
    rank_col = jnp.sum(earlier, axis=1, keepdims=True)

    wide[...] = jnp.full(wide.shape, -1, jnp.int32)
    wide[0:1, 0:picked] = sel_ref[...]
    position = wide[...]
    page = lax.shift_right_arithmetic(position, page_len.bit_length() - 1)
    offset = (position & (page_len - 1)).astype(f32)[0:1]
    lane_wide = lax.broadcasted_iota(jnp.int32, wide.shape, 1)
    second = one_hot((page == pltpu.roll(page, 1, axis=1)) & (lane_wide > 0))[0:1]
    valid = lane_wide[0:1] < picked
    sub_wide = lax.broadcasted_iota(jnp.int32, (pages, wide.shape[1]), 0)
    in_page = one_hot(sub_wide == page[0:1])
    owner = jnp.sum(in_page * owner_col[:, 0:1], axis=0, keepdims=True)
    rank = jnp.sum(in_page * rank_col, axis=0, keepdims=True)
    return owner_row[0:1], local_row, rank_col, owner, rank, second, offset, valid


def index_kernel(hold, page_len, first, own, table_ref, sel_ref, out_ref, *rest):
    first_refs, wide = rest[:-1], rest[-1]
    holders = out_ref.shape[0]
    pages = table_ref.shape[1]
    f32 = jnp.float32
    bf16 = jnp.bfloat16
    owner_row, local_row, rank_col, owner, rank, second, offset, valid = pair_places(
        hold, page_len, table_ref, sel_ref, wide
    )
    holder = lax.broadcasted_iota(jnp.int32, (holders, pages), 0).astype(f32)
    owned = jnp.where(holder == owner_row, local_row, 0.0)
    lane = lax.broadcasted_iota(jnp.int32, (pages, LANES), 1).astype(f32)
    numbers = jnp.dot(
        owned.astype(bf16), one_hot(lane == rank_col).astype(bf16), preferred_element_type=f32
    )
    holder_wide = lax.broadcasted_iota(jnp.int32, (holders, wide.shape[1]), 0).astype(f32)
    marked = jnp.where((holder_wide == owner) & valid, rank * page_len + offset + 1.0, 0.0)
    place_lane = lax.broadcasted_iota(jnp.int32, (LANES, wide.shape[1]), 0).astype(f32)
    at_place = one_hot(place_lane == SELP * rank + second)
    targets = nt_dot(marked.astype(bf16), at_place.astype(bf16))
    for h in range(holders):
        out_ref[h, 0:1, :] = numbers[h : h + 1, :].astype(jnp.int32)
        out_ref[h, 1:2, :] = targets[h : h + 1, :].astype(jnp.int32)
    for d, ref in zip(first, first_refs):
        ref[0] = out_ref[own[0] ^ d]


def rows_kernel(hold, page_len, table_ref, sel_ref, fresh_ref, packed, wide):
    holders = packed.shape[0]
    picked = sel_ref.shape[1]
    f32 = jnp.float32
    _, _, _, owner, rank, second, _, valid = pair_places(hold, page_len, table_ref, sel_ref, wide)
    spot = jnp.where(valid, owner * ROW_SLOTS + SELP * rank + second, -1.0)[:, 0:picked]
    step = min(holders, 16)
    for start in range(0, holders, step):
        spot_id = lax.broadcasted_iota(jnp.int32, (step * ROW_SLOTS, picked), 0).astype(f32)
        choose = one_hot(spot_id + float(start * ROW_SLOTS) == spot).astype(jnp.bfloat16)
        rows = jnp.dot(choose, fresh_ref[...], preferred_element_type=f32).astype(jnp.bfloat16)
        packed[start : start + step] = rows.reshape(step, ROW_SLOTS, fresh_ref.shape[1])


def first_gather_kernel(count, *refs):
    lists, store_hbm, sends = refs[:count], refs[count], refs[count + 1 : 2 * count + 1]
    held, load_sem, send_sem = refs[2 * count + 1 :]
    capacity = held.shape[1]
    for i, numbers in enumerate(lists):
        for k in range(capacity):
            pltpu.make_async_copy(store_hbm.at[numbers[0, 0, k]], held.at[i, k], load_sem).start()
    pltpu.make_async_copy(held, held, load_sem).wait()
    for i, send in enumerate(sends):
        pltpu.make_async_copy(held.at[i], send, send_sem).start()
    pltpu.make_async_copy(held, held, send_sem).wait()


def gather_kernel(capacity, distances, own, index, store_hbm, *rest):
    sends, (store, load_sem, send_sem) = rest[:-3], rest[-3:]
    load = pltpu.make_async_copy(store_hbm, store, load_sem)
    load.start()
    load.wait()
    for i in range(len(distances) if distances else index.shape[0]):
        r = own[0] ^ distances[i] if distances else i
        send = sends[i] if distances else sends[0].at[i]
        for k in range(capacity):
            pltpu.make_async_copy(store.at[index[r, 0, k]], send.at[k], send_sem).start()
    for send in sends:
        pltpu.make_async_copy(send, send, send_sem).wait()


def write_back_kernel(index, targets_ref, store_hbm, rows_hbm, store_out, *scratch):
    store, rows, blended, load_sem, rows_sem, out_sem = scratch
    holders, capacity, page_len, width = blended.shape
    rows_here = capacity * page_len
    f32 = jnp.float32
    load = pltpu.make_async_copy(store_hbm, store, load_sem)
    load_rows = pltpu.make_async_copy(rows_hbm, rows, rows_sem)
    load.start()
    load_rows.start()
    load_rows.wait()
    load.wait()
    row_id = lax.broadcasted_iota(jnp.int32, (rows_here, ROW_SLOTS), 0)

    def one_request(r, carry):
        hit = one_hot(row_id == targets_ref[r][1:2, 0:ROW_SLOTS] - 1)
        keep = 1.0 - jnp.sum(hit, axis=1, keepdims=True)
        keep = jnp.broadcast_to(keep, (rows_here, LANES)).astype(jnp.bfloat16)
        hit = hit.astype(jnp.bfloat16)
        for c in range(width // LANES):
            lanes = slice(c * LANES, (c + 1) * LANES)
            fresh = jnp.dot(hit, rows[r, :, lanes], preferred_element_type=f32).astype(jnp.bfloat16)
            for k in range(capacity):
                part = slice(k * page_len, (k + 1) * page_len)
                blended[r, k, :, lanes] = store[index[r, 0, k], :, lanes] * keep[part] + fresh[part]
        for k in range(capacity):
            pltpu.make_async_copy(blended.at[r, k], store_out.at[index[r, 0, k]], out_sem).start()
        return carry

    lax.fori_loop(0, holders, one_request, 0)
    pltpu.make_async_copy(store_out, store_out, out_sem).wait()


def attend_kernel(first, last, sources, place, tiles, *rest):
    sel_ref, position, query_ref, *rest = rest
    if first:
        fresh_ref, *rest = rest
    state_in = () if first else rest[:2]
    rest = rest if first else rest[2:]
    contexts, rest = rest[:sources], rest[sources:]
    outs, rest = (rest[:1], rest[1:]) if last else (rest[:2], rest[2:])
    kv, values, query, scores, raised, mixed, stats, sem = rest
    pages, page_len, width = kv.shape
    each = contexts[0].shape[0]
    direct = last and not first
    block = query_ref.shape[0]
    tile = TILE_PAGES * page_len
    lanes = QUERY_GROUP * block
    scale = 1.4426950408889634 / HEAD_WIDTH**0.5
    f32 = jnp.float32
    bf16 = jnp.bfloat16
    step = pl.program_id(0)
    eye = one_hot(
        lax.broadcasted_iota(jnp.int32, (LANES, LANES), 0)
        == lax.broadcasted_iota(jnp.int32, (LANES, LANES), 1)
    ).astype(bf16)

    @pl.when(step == 0)
    def _():
        for i, context in enumerate(contexts):
            if direct:
                kv[i * each : (i + 1) * each] = context[...]
            else:
                for k in range(each):
                    to = kv.at[place[i * each + k]]
                    pltpu.make_async_copy(context.at[k], to, sem).start()
        if first:
            count = fresh_ref.shape[0] // page_len
            for p in range(count):
                page = fresh_ref[p * page_len : (p + 1) * page_len, :]
                kv[place[sources * each + p]] = page
            used = sources * each + count
            if pages > used:
                kv[used:] = jnp.zeros((pages - used, page_len, width), bf16)
        if not direct:
            arrived = kv.at[0 : sources * each]
            pltpu.make_async_copy(arrived, arrived, sem).wait()

        def turn(t, carry):
            here = pl.ds(t * TILE_PAGES, TILE_PAGES)
            for g in range(KEY_VALUE_HEADS):
                at = (KEY_VALUE_HEADS + g) * LANES
                value = kv[here, :, at : at + LANES].reshape(tile, LANES)
                values[t, g] = nt_dot(eye, value).astype(bf16)
            return carry

        lax.fori_loop(0, pages // TILE_PAGES, turn, 0)

    for g in range(KEY_VALUE_HEADS):
        for i in range(QUERY_GROUP):
            head = g * QUERY_GROUP + i
            query[g, i * block : (i + 1) * block, :] = query_ref[:, head * LANES : (head + 1) * LANES]
    if first:
        mixed[...] = jnp.zeros(mixed.shape, f32)
        stats[0:KEY_VALUE_HEADS, :] = jnp.full((KEY_VALUE_HEADS, lanes), HIDDEN, f32)
        stats[KEY_VALUE_HEADS:, :] = jnp.zeros((KEY_VALUE_HEADS, lanes), f32)
    else:
        mixed[...] = state_in[0][0]
        stats[...] = state_in[1][0]

    sel = sel_ref[0]

    def one_tile(t, carry):
        here = pl.ds(t * TILE_PAGES, TILE_PAGES)
        bias = jnp.where(
            position[pl.ds(pl.multiple_of(t * tile, tile), tile), :] <= sel, 0.0, HIDDEN
        ).astype(f32)

        parts = [slice(n * LANES, (n + 1) * LANES) for n in range(lanes // LANES)]
        chains = [(g, part) for g in range(KEY_VALUE_HEADS) for part in parts]
        for g in range(KEY_VALUE_HEADS):
            key = kv[here, :, g * LANES : (g + 1) * LANES].reshape(tile, LANES)
            product = nt_dot(key, query[g])
            for part in parts:
                scores[g, :, part] = product[:, part] + bias
        peaks, shrinks = [], []
        for g, part in chains:
            old = stats[g : g + 1, part]
            new = jnp.maximum(old, jnp.max(scores[g, :, part], axis=0, keepdims=True))
            stats[g : g + 1, part] = new
            peaks.append(new)
            shrinks.append(jnp.exp2((old - new) * scale))
        for (g, part), new, shrink in zip(chains, peaks, shrinks):
            at = KEY_VALUE_HEADS + g
            p = jnp.exp2((scores[g, :, part] - new) * scale)
            stats[at : at + 1, part] = stats[at : at + 1, part] * shrink + jnp.sum(
                p, axis=0, keepdims=True
            )
            raised[g, :, part] = p.astype(bf16)
        for g in range(KEY_VALUE_HEADS):
            shrink = jnp.concatenate(shrinks[g * len(parts) : (g + 1) * len(parts)], axis=1)
            mixed[g] = mixed[g] * shrink + jnp.dot(
                values[t, g], raised[g], preferred_element_type=f32
            )
        return carry

    lax.fori_loop(0, tiles[step], one_tile, 0)

    if last:
        done = []
        for g in range(KEY_VALUE_HEADS):
            at = KEY_VALUE_HEADS + g
            part = (mixed[g] * (1.0 / stats[at : at + 1, :])).astype(bf16)
            done += [part[:, n * LANES : (n + 1) * LANES] for n in range(lanes // LANES)]
        turned = nt_dot(eye, jnp.concatenate(done, axis=0)).astype(bf16)
        for n in range(len(done)):
            for i in range(LANES // block):
                head = n * (LANES // block) + i
                outs[0][:, head * LANES : (head + 1) * LANES] = turned[
                    i * block : (i + 1) * block, n * LANES : (n + 1) * LANES
                ]
    else:
        outs[0][0] = mixed[...]
        outs[1][0] = stats[...]


def attend(first, last, order, sel_lanes, queries, fresh, state, contexts):
    place, tiles, position = order
    picked, features = queries.shape
    each, page_len, width = contexts[0].shape
    pages = position.shape[0] // page_len
    steps = picked // QUERY_BLOCK
    lanes = QUERY_GROUP * QUERY_BLOCK
    wide = pl.BlockSpec((QUERY_BLOCK, features), lambda b, *_: (b, 0))
    state_specs = [
        pl.BlockSpec((1, KEY_VALUE_HEADS, LANES, lanes), lambda b, *_: (b, 0, 0, 0)),
        pl.BlockSpec((1, 2 * KEY_VALUE_HEADS, lanes), lambda b, *_: (b, 0, 0)),
    ]
    state_shapes = [
        jax.ShapeDtypeStruct((steps, KEY_VALUE_HEADS, LANES, lanes), jnp.float32),
        jax.ShapeDtypeStruct((steps, 2 * KEY_VALUE_HEADS, lanes), jnp.float32),
    ]
    share = 0.6
    return pl.pallas_call(
        functools.partial(attend_kernel, first, last, len(contexts)),
        grid_spec=pltpu.PrefetchScalarGridSpec(
            num_scalar_prefetch=2,
            grid=(steps,),
            in_specs=[
                pl.BlockSpec((1, 1, LANES), lambda b, *_: (b, 0, 0)),
                pl.BlockSpec(position.shape, lambda b, *_: (0, 0)),
                wide,
                *([pl.BlockSpec(fresh.shape, lambda b, *_: (0, 0))] if first else state_specs),
                *[
                    pl.BlockSpec(x.shape, lambda b, *_: (0, 0, 0))
                    if last and not first
                    else pl.BlockSpec(memory_space=pltpu.HBM)
                    for x in contexts
                ],
            ],
            out_specs=[wide] if last else state_specs,
            scratch_shapes=[
                pltpu.VMEM((pages, page_len, width), jnp.bfloat16),
                pltpu.VMEM(
                    (pages // TILE_PAGES, KEY_VALUE_HEADS, LANES, TILE_PAGES * page_len), jnp.bfloat16
                ),
                pltpu.VMEM((KEY_VALUE_HEADS, lanes, LANES), jnp.bfloat16),
                pltpu.VMEM((KEY_VALUE_HEADS, TILE_PAGES * page_len, lanes), jnp.float32),
                pltpu.VMEM((KEY_VALUE_HEADS, TILE_PAGES * page_len, lanes), jnp.bfloat16),
                pltpu.VMEM((KEY_VALUE_HEADS, LANES, lanes), jnp.float32),
                pltpu.VMEM((2 * KEY_VALUE_HEADS, lanes), jnp.float32),
                pltpu.SemaphoreType.DMA,
            ],
        ),
        out_shape=[jax.ShapeDtypeStruct((picked, features), jnp.bfloat16)] if last else state_shapes,
        compiler_params=pltpu.CompilerParams(
            dimension_semantics=("arbitrary",), vmem_limit_bytes=VMEM_LIMIT
        ),
        cost_estimate=pl.CostEstimate(
            flops=int(share * 8 * picked * features * pages * page_len),
            bytes_accessed=2 * pages * page_len * width + 6 * picked * features,
            transcendentals=int(share * picked * features // LANES * pages * page_len),
        ),
    )(place, tiles, sel_lanes, position, queries, *([fresh] if first else state), *contexts)


def page_order(slots, positions, own, hold, capacity, groups, page_len):
    pages = slots.shape[0]
    number = jnp.arange(pages)
    before = number[None, :] < number[:, None]
    owners = slots // hold
    ranks = jnp.sum(((owners[None, :] == owners[:, None]) & before).astype(jnp.int32), axis=1)
    distance = owners ^ own
    last_position = positions.reshape(-1, QUERY_BLOCK)[:, -1:]
    starts = number * page_len
    replaced = jnp.any(
        (starts[:, None] + jnp.arange(page_len)[None, :])[:, :, None] == positions, axis=2
    )
    fresh = positions.reshape(-1, page_len)
    orders = []
    for at, group in enumerate(groups):
        if group is None:
            arrival = owners * capacity + ranks
            count = pages
        else:
            arrival = jnp.full((pages,), -1, jnp.int32)
            for i, d in enumerate(group):
                arrival = jnp.where(distance == d, i * capacity + ranks, arrival)
            count = len(group) * capacity
        member = arrival >= 0
        place = jnp.sum((member[None, :] & before).astype(jnp.int32), axis=1)
        seen = jnp.sum((member & (starts <= last_position)).astype(jnp.int32), axis=1)
        total = count
        if at == 0:
            place = place + jnp.sum((fresh[None, :, 0] < starts[:, None]).astype(jnp.int32), axis=1)
            ahead = jnp.sum((member & (starts <= fresh[:, 0:1])).astype(jnp.int32), axis=1)
            fresh_place = jnp.arange(fresh.shape[0]) + ahead
            seen = seen + jnp.sum((fresh[None, :, 0] <= last_position).astype(jnp.int32), axis=1)
            total = count + fresh.shape[0]
        elif at == len(groups) - 1:
            place = arrival
        places = jnp.where(arrival == jnp.arange(count)[:, None], place, 0)
        places = jnp.sum(places, axis=1)
        index = jnp.arange(-(-total // TILE_PAGES) * TILE_PAGES)[:, None]
        here = member & (place == index)
        inside = jnp.arange(page_len)
        rows = starts[:, None] + inside
        rows = jnp.where(replaced, FAR_POSITION, rows)
        rows = jnp.sum(jnp.where(here[:, :, None], rows, 0), axis=1)
        filled = jnp.any(here, axis=1, keepdims=True)
        if at == 0:
            there = fresh_place == index
            rows = rows + jnp.sum(jnp.where(there[:, :, None], fresh, 0), axis=1)
            filled = filled | jnp.any(there, axis=1, keepdims=True)
            places = jnp.concatenate([places, fresh_place])
        rows = jnp.where(filled, rows, FAR_POSITION).reshape(-1, 1)
        rows = jnp.broadcast_to(rows, (rows.shape[0], LANES))
        orders.append((places, (seen + TILE_PAGES - 1) // TILE_PAGES, rows))
    return orders


def per_device(store, page_table, sel_pos, fresh_kv, queries):
    holders = lax.axis_size("store")
    hold, page_len, width = store.shape
    pages = page_table.shape[1]
    picked = sel_pos.shape[1]
    capacity = max(1, pages // holders)
    hbm = pl.BlockSpec(memory_space=pltpu.HBM)
    vmem = pl.BlockSpec(memory_space=pltpu.VMEM)
    dma = pltpu.SemaphoreType.DMA
    params = pltpu.CompilerParams(vmem_limit_bytes=VMEM_LIMIT)
    own = lax.axis_index("store")
    own_word = own.reshape(1).astype(jnp.int32)
    fresh = fresh_kv[0]
    wide = pltpu.VMEM((8, -(-picked // LANES) * LANES), jnp.int32)
    if holders == 16:
        first = (8, 12)
        groups = [(0, 8, 12, 4, 5, 1), (9, 6, 13, 7, 10, 2, 14, 3), (11, 15)]
        others = [d for group in groups for d in group if d not in first]
    else:
        first = ()
        groups = [None]
        others = None

    def swap(x, d):
        return lax.ppermute(x, "store", [(h, h ^ d) for h in range(holders)])

    def exchange(x):
        return lax.all_to_all(x, "store", split_axis=0, concat_axis=0, tiled=True)

    index, *lists = pl.pallas_call(
        functools.partial(index_kernel, hold, page_len, first),
        grid_spec=pltpu.PrefetchScalarGridSpec(
            num_scalar_prefetch=1,
            grid=(1,),
            in_specs=[vmem, vmem],
            out_specs=[vmem] * (1 + len(first)),
            scratch_shapes=[wide],
        ),
        out_shape=[
            jax.ShapeDtypeStruct((holders, 2, LANES), jnp.int32),
            *[jax.ShapeDtypeStruct((1, 2, LANES), jnp.int32)] * len(first),
        ],
        compiler_params=params,
    )(own_word, page_table, sel_pos)
    arrived = {}
    if first:
        lists = [swap(x, d) for x, d in zip(lists, first)]
        parts = pl.pallas_call(
            functools.partial(first_gather_kernel, len(first)),
            grid_spec=pltpu.PrefetchScalarGridSpec(
                num_scalar_prefetch=len(first),
                grid=(1,),
                in_specs=[hbm],
                out_specs=[hbm] * len(first),
                scratch_shapes=[
                    pltpu.VMEM((len(first), capacity, page_len, width), store.dtype),
                    dma,
                    dma,
                ],
            ),
            out_shape=[jax.ShapeDtypeStruct((capacity, page_len, width), store.dtype)] * len(first),
            compiler_params=params,
        )(*lists, store)
        parts, index, table, positions = lax.optimization_barrier(
            (parts, index, page_table, sel_pos)
        )
        arrived = {d: swap(part, d) for d, part in zip(first, parts)}
    else:
        table, positions = page_table, sel_pos
    index_in = exchange(index)

    packed = pl.pallas_call(
        functools.partial(rows_kernel, hold, page_len),
        out_shape=jax.ShapeDtypeStruct((holders, ROW_SLOTS, width), store.dtype),
        scratch_shapes=[wide],
        compiler_params=params,
    )(table, positions, fresh)

    each = jax.ShapeDtypeStruct((capacity, page_len, width), store.dtype)
    whole = jax.ShapeDtypeStruct((holders, capacity, page_len, width), store.dtype)
    parts = pl.pallas_call(
        functools.partial(gather_kernel, capacity, others),
        grid_spec=pltpu.PrefetchScalarGridSpec(
            num_scalar_prefetch=2,
            grid=(1,),
            in_specs=[hbm],
            out_specs=[hbm] * (len(others) if others else 1),
            scratch_shapes=[pltpu.VMEM(store.shape, store.dtype), dma, dma],
        ),
        out_shape=[each] * len(others) if others else [whole],
        compiler_params=params,
    )(own_word, index_in, store)
    parts, packed, table, positions = lax.optimization_barrier((parts, packed, table, positions))
    if others:
        parts = dict(zip(others, parts))
        for d in others:
            arrived[d] = swap(parts[d], d) if d else parts[d]
    else:
        arrived[None] = exchange(parts[0]).reshape(pages, page_len, width)
    rows_in = exchange(packed)

    store_out = pl.pallas_call(
        write_back_kernel,
        grid_spec=pltpu.PrefetchScalarGridSpec(
            num_scalar_prefetch=1,
            grid=(1,),
            in_specs=[vmem, hbm, hbm],
            out_specs=hbm,
            scratch_shapes=[
                pltpu.VMEM(store.shape, store.dtype),
                pltpu.VMEM((holders, ROW_SLOTS, width), store.dtype),
                pltpu.VMEM((holders, capacity, page_len, width), store.dtype),
                dma,
                dma,
                dma,
            ],
        ),
        out_shape=jax.ShapeDtypeStruct(store.shape, store.dtype),
        compiler_params=params,
        cost_estimate=pl.CostEstimate(flops=0, bytes_accessed=4 * store.size, transcendentals=0),
    )(index_in, index_in, store, rows_in)

    orders = page_order(table[0], positions[0], own, hold, capacity, groups, page_len)
    sel_lanes = jnp.tile(positions.reshape(-1, 1, QUERY_BLOCK), (1, 1, LANES // QUERY_BLOCK))
    store_out, sel_lanes, orders = lax.optimization_barrier((store_out, sel_lanes, orders))
    state = ()
    for at, (group, order) in enumerate(zip(groups, orders)):
        state = attend(
            at == 0,
            at == len(groups) - 1,
            order,
            sel_lanes,
            queries[0],
            fresh,
            state,
            [arrived[d] for d in group or [None]],
        )
    return (state[0][None], store_out)


def solution(mesh):
    return jax.shard_map(
        per_device,
        mesh=mesh,
        in_specs=(
            P(("groups", "store"), None, None),
            P(("groups", "store"), None),
            P(("groups", "store"), None),
            P(("groups", "store"), None, None),
            P(("groups", "store"), None, None),
        ),
        out_specs=(P(("groups", "store"), None, None), P(("groups", "store"), None, None)),
        check_vma=False,
    )
```

```python
import functools

import jax
import jax.numpy as jnp
from jax import lax
from jax.experimental import pallas as pl
from jax.experimental.pallas import tpu as pltpu
from jax.sharding import PartitionSpec as P

HEAD_WIDTH = 128
KEY_VALUE_HEADS = 4
QUERY_GROUP = 12
SELP = 2
LANES = 128
ROW_SLOTS = 16
VMEM_LIMIT = 60 * 1024 * 1024
QUERY_BLOCK = 32
TILE_PAGES = 16
HIDDEN = -1e30
FAR_POSITION = 1 << 24


def nt_dot(a, b):
    return lax.dot_general(a, b, (((1,), (1,)), ((), ())), preferred_element_type=jnp.float32)


def one_hot(condition):
    return jnp.where(condition, 1.0, 0.0)


def pair_places(hold, page_len, table_ref, sel_ref, wide):
    pages = table_ref.shape[1]
    picked = sel_ref.shape[1]
    f32 = jnp.float32
    slots = jnp.broadcast_to(table_ref[...], (pages, pages))
    owners = slots // hold
    local_row = (slots - owners * hold).astype(f32)[0:1]
    owner_row = owners.astype(f32)
    owner_col = owner_row.T
    sub = lax.broadcasted_iota(jnp.int32, (pages, pages), 0)
    lane = lax.broadcasted_iota(jnp.int32, (pages, pages), 1)
    earlier = one_hot((owner_row == owner_col) & (lane < sub))
    rank_col = jnp.sum(earlier, axis=1, keepdims=True)

    wide[...] = jnp.full(wide.shape, -1, jnp.int32)
    wide[0:1, 0:picked] = sel_ref[...]
    position = wide[...]
    page = lax.shift_right_arithmetic(position, page_len.bit_length() - 1)
    offset = (position & (page_len - 1)).astype(f32)[0:1]
    lane_wide = lax.broadcasted_iota(jnp.int32, wide.shape, 1)
    second = one_hot((page == pltpu.roll(page, 1, axis=1)) & (lane_wide > 0))[0:1]
    valid = lane_wide[0:1] < picked
    sub_wide = lax.broadcasted_iota(jnp.int32, (pages, wide.shape[1]), 0)
    in_page = one_hot(sub_wide == page[0:1])
    owner = jnp.sum(in_page * owner_col[:, 0:1], axis=0, keepdims=True)
    rank = jnp.sum(in_page * rank_col, axis=0, keepdims=True)
    return owner_row[0:1], local_row, rank_col, owner, rank, second, offset, valid


def index_kernel(hold, page_len, first, own, table_ref, sel_ref, out_ref, *rest):
    first_refs, wide = rest[:-1], rest[-1]
    holders = out_ref.shape[0]
    pages = table_ref.shape[1]
    f32 = jnp.float32
    bf16 = jnp.bfloat16
    owner_row, local_row, rank_col, owner, rank, second, offset, valid = pair_places(
        hold, page_len, table_ref, sel_ref, wide
    )
    holder = lax.broadcasted_iota(jnp.int32, (holders, pages), 0).astype(f32)
    owned = jnp.where(holder == owner_row, local_row, 0.0)
    lane = lax.broadcasted_iota(jnp.int32, (pages, LANES), 1).astype(f32)
    numbers = jnp.dot(
        owned.astype(bf16), one_hot(lane == rank_col).astype(bf16), preferred_element_type=f32
    )
    holder_wide = lax.broadcasted_iota(jnp.int32, (holders, wide.shape[1]), 0).astype(f32)
    marked = jnp.where((holder_wide == owner) & valid, rank * page_len + offset + 1.0, 0.0)
    place_lane = lax.broadcasted_iota(jnp.int32, (LANES, wide.shape[1]), 0).astype(f32)
    at_place = one_hot(place_lane == SELP * rank + second)
    targets = nt_dot(marked.astype(bf16), at_place.astype(bf16))
    for h in range(holders):
        out_ref[h, 0:1, :] = numbers[h : h + 1, :].astype(jnp.int32)
        out_ref[h, 1:2, :] = targets[h : h + 1, :].astype(jnp.int32)
    for d, ref in zip(first, first_refs):
        ref[0] = out_ref[own[0] ^ d]


def rows_kernel(hold, page_len, table_ref, sel_ref, fresh_ref, packed, wide):
    holders = packed.shape[0]
    picked = sel_ref.shape[1]
    f32 = jnp.float32
    _, _, _, owner, rank, second, _, valid = pair_places(hold, page_len, table_ref, sel_ref, wide)
    spot = jnp.where(valid, owner * ROW_SLOTS + SELP * rank + second, -1.0)[:, 0:picked]
    step = min(holders, 16)
    for start in range(0, holders, step):
        spot_id = lax.broadcasted_iota(jnp.int32, (step * ROW_SLOTS, picked), 0).astype(f32)
        choose = one_hot(spot_id + float(start * ROW_SLOTS) == spot).astype(jnp.bfloat16)
        rows = jnp.dot(choose, fresh_ref[...], preferred_element_type=f32).astype(jnp.bfloat16)
        packed[start : start + step] = rows.reshape(step, ROW_SLOTS, fresh_ref.shape[1])


def first_gather_kernel(count, *refs):
    lists, store_hbm, sends = refs[:count], refs[count], refs[count + 1 : 2 * count + 1]
    held, load_sem, send_sem = refs[2 * count + 1 :]
    capacity = held.shape[1]
    for i, numbers in enumerate(lists):
        for k in range(capacity):
            pltpu.make_async_copy(store_hbm.at[numbers[0, 0, k]], held.at[i, k], load_sem).start()
    pltpu.make_async_copy(held, held, load_sem).wait()
    for i, send in enumerate(sends):
        pltpu.make_async_copy(held.at[i], send, send_sem).start()
    pltpu.make_async_copy(held, held, send_sem).wait()


def gather_kernel(capacity, distances, own, index, store_hbm, *rest):
    sends, (store, load_sem, send_sem) = rest[:-3], rest[-3:]
    load = pltpu.make_async_copy(store_hbm, store, load_sem)
    load.start()
    load.wait()
    for i in range(len(distances) if distances else index.shape[0]):
        r = own[0] ^ distances[i] if distances else i
        send = sends[i] if distances else sends[0].at[i]
        for k in range(capacity):
            pltpu.make_async_copy(store.at[index[r, 0, k]], send.at[k], send_sem).start()
    for send in sends:
        pltpu.make_async_copy(send, send, send_sem).wait()


def write_back_kernel(index, targets_ref, store_hbm, rows_hbm, store_out, *scratch):
    store, rows, blended, load_sem, rows_sem, out_sem = scratch
    holders, capacity, page_len, width = blended.shape
    rows_here = capacity * page_len
    f32 = jnp.float32
    load = pltpu.make_async_copy(store_hbm, store, load_sem)
    load_rows = pltpu.make_async_copy(rows_hbm, rows, rows_sem)
    load.start()
    load_rows.start()
    load_rows.wait()
    load.wait()
    row_id = lax.broadcasted_iota(jnp.int32, (rows_here, ROW_SLOTS), 0)

    def one_request(r, carry):
        hit = one_hot(row_id == targets_ref[r][1:2, 0:ROW_SLOTS] - 1)
        keep = 1.0 - jnp.sum(hit, axis=1, keepdims=True)
        keep = jnp.broadcast_to(keep, (rows_here, LANES)).astype(jnp.bfloat16)
        hit = hit.astype(jnp.bfloat16)
        for c in range(width // LANES):
            lanes = slice(c * LANES, (c + 1) * LANES)
            fresh = jnp.dot(hit, rows[r, :, lanes], preferred_element_type=f32).astype(jnp.bfloat16)
            for k in range(capacity):
                part = slice(k * page_len, (k + 1) * page_len)
                blended[r, k, :, lanes] = store[index[r, 0, k], :, lanes] * keep[part] + fresh[part]
        for k in range(capacity):
            pltpu.make_async_copy(blended.at[r, k], store_out.at[index[r, 0, k]], out_sem).start()
        return carry

    lax.fori_loop(0, holders, one_request, 0)
    pltpu.make_async_copy(store_out, store_out, out_sem).wait()


def attend_kernel(first, last, sources, place, tiles, *rest):
    sel_ref, position_ref, query_ref, *rest = rest
    if first:
        fresh_ref, *rest = rest
    state_in = () if first else rest[:2]
    rest = rest if first else rest[2:]
    contexts, rest = rest[:sources], rest[sources:]
    outs, rest = (rest[:1], rest[1:]) if last else (rest[:2], rest[2:])
    kv, values, position, query, scores, raised, mixed, stats, sem = rest
    pages, page_len, width = kv.shape
    each = contexts[0].shape[0]
    direct = last and not first
    block = query_ref.shape[0]
    tile = TILE_PAGES * page_len
    lanes = QUERY_GROUP * block
    scale = 1.4426950408889634 / HEAD_WIDTH**0.5
    f32 = jnp.float32
    bf16 = jnp.bfloat16
    step = pl.program_id(0)
    eye = one_hot(
        lax.broadcasted_iota(jnp.int32, (LANES, LANES), 0)
        == lax.broadcasted_iota(jnp.int32, (LANES, LANES), 1)
    ).astype(bf16)

    @pl.when(step == 0)
    def _():
        for i, context in enumerate(contexts):
            if direct:
                kv[i * each : (i + 1) * each] = context[...]
            else:
                for k in range(each):
                    to = kv.at[place[i * each + k]]
                    pltpu.make_async_copy(context.at[k], to, sem).start()
        if first:
            count = fresh_ref.shape[0] // page_len
            for p in range(count):
                page = fresh_ref[p * page_len : (p + 1) * page_len, :]
                kv[place[sources * each + p]] = page
            used = sources * each + count
            if pages > used:
                kv[used:] = jnp.zeros((pages - used, page_len, width), bf16)
        for c in range(position_ref.shape[1] // LANES):
            part = slice(c * LANES, (c + 1) * LANES)
            row = jnp.broadcast_to(position_ref[:, part], (LANES, LANES)).astype(f32)
            position[part, :] = row.T.astype(jnp.int32)
        if not direct:
            arrived = kv.at[0 : sources * each]
            pltpu.make_async_copy(arrived, arrived, sem).wait()

        def turn(t, carry):
            here = pl.ds(t * TILE_PAGES, TILE_PAGES)
            for g in range(KEY_VALUE_HEADS):
                at = (KEY_VALUE_HEADS + g) * LANES
                value = kv[here, :, at : at + LANES].reshape(tile, LANES)
                values[t, g] = nt_dot(eye, value).astype(bf16)
            return carry

        lax.fori_loop(0, pages // TILE_PAGES, turn, 0)

    for g in range(KEY_VALUE_HEADS):
        for i in range(QUERY_GROUP):
            head = g * QUERY_GROUP + i
            query[g, i * block : (i + 1) * block, :] = query_ref[:, head * LANES : (head + 1) * LANES]
    if first:
        mixed[...] = jnp.zeros(mixed.shape, f32)
        stats[0:KEY_VALUE_HEADS, :] = jnp.full((KEY_VALUE_HEADS, lanes), HIDDEN, f32)
        stats[KEY_VALUE_HEADS:, :] = jnp.zeros((KEY_VALUE_HEADS, lanes), f32)
    else:
        mixed[...] = state_in[0][0]
        stats[...] = state_in[1][0]

    sel = sel_ref[0]

    def one_tile(t, carry):
        here = pl.ds(t * TILE_PAGES, TILE_PAGES)
        bias = jnp.where(
            position[pl.ds(pl.multiple_of(t * tile, tile), tile), :] <= sel, 0.0, HIDDEN
        ).astype(f32)

        parts = [slice(n * LANES, (n + 1) * LANES) for n in range(lanes // LANES)]
        chains = [(g, part) for g in range(KEY_VALUE_HEADS) for part in parts]
        for g in range(KEY_VALUE_HEADS):
            key = kv[here, :, g * LANES : (g + 1) * LANES].reshape(tile, LANES)
            product = nt_dot(key, query[g])
            for part in parts:
                scores[g, :, part] = product[:, part] + bias
        peaks, shrinks = [], []
        for g, part in chains:
            old = stats[g : g + 1, part]
            new = jnp.maximum(old, jnp.max(scores[g, :, part], axis=0, keepdims=True))
            stats[g : g + 1, part] = new
            peaks.append(new)
            shrinks.append(jnp.exp2((old - new) * scale))
        for (g, part), new, shrink in zip(chains, peaks, shrinks):
            at = KEY_VALUE_HEADS + g
            p = jnp.exp2((scores[g, :, part] - new) * scale)
            stats[at : at + 1, part] = stats[at : at + 1, part] * shrink + jnp.sum(
                p, axis=0, keepdims=True
            )
            raised[g, :, part] = p.astype(bf16)
        for g in range(KEY_VALUE_HEADS):
            shrink = jnp.concatenate(shrinks[g * len(parts) : (g + 1) * len(parts)], axis=1)
            mixed[g] = mixed[g] * shrink + jnp.dot(
                values[t, g], raised[g], preferred_element_type=f32
            )
        return carry

    lax.fori_loop(0, tiles[step], one_tile, 0)

    if last:
        done = []
        for g in range(KEY_VALUE_HEADS):
            at = KEY_VALUE_HEADS + g
            part = (mixed[g] * (1.0 / stats[at : at + 1, :])).astype(bf16)
            done += [part[:, n * LANES : (n + 1) * LANES] for n in range(lanes // LANES)]
        turned = nt_dot(eye, jnp.concatenate(done, axis=0)).astype(bf16)
        for n in range(len(done)):
            for i in range(LANES // block):
                head = n * (LANES // block) + i
                outs[0][:, head * LANES : (head + 1) * LANES] = turned[
                    i * block : (i + 1) * block, n * LANES : (n + 1) * LANES
                ]
    else:
        outs[0][0] = mixed[...]
        outs[1][0] = stats[...]


def attend(first, last, order, sel_lanes, queries, fresh, state, contexts):
    place, tiles, position = order
    picked, features = queries.shape
    each, page_len, width = contexts[0].shape
    pages = position.shape[1] // page_len
    steps = picked // QUERY_BLOCK
    lanes = QUERY_GROUP * QUERY_BLOCK
    wide = pl.BlockSpec((QUERY_BLOCK, features), lambda b, *_: (b, 0))
    state_specs = [
        pl.BlockSpec((1, KEY_VALUE_HEADS, LANES, lanes), lambda b, *_: (b, 0, 0, 0)),
        pl.BlockSpec((1, 2 * KEY_VALUE_HEADS, lanes), lambda b, *_: (b, 0, 0)),
    ]
    state_shapes = [
        jax.ShapeDtypeStruct((steps, KEY_VALUE_HEADS, LANES, lanes), jnp.float32),
        jax.ShapeDtypeStruct((steps, 2 * KEY_VALUE_HEADS, lanes), jnp.float32),
    ]
    share = 0.6
    return pl.pallas_call(
        functools.partial(attend_kernel, first, last, len(contexts)),
        grid_spec=pltpu.PrefetchScalarGridSpec(
            num_scalar_prefetch=2,
            grid=(steps,),
            in_specs=[
                pl.BlockSpec((1, 1, LANES), lambda b, *_: (b, 0, 0)),
                pl.BlockSpec(position.shape, lambda b, *_: (0, 0)),
                wide,
                *([pl.BlockSpec(fresh.shape, lambda b, *_: (0, 0))] if first else state_specs),
                *[
                    pl.BlockSpec(x.shape, lambda b, *_: (0, 0, 0))
                    if last and not first
                    else pl.BlockSpec(memory_space=pltpu.HBM)
                    for x in contexts
                ],
            ],
            out_specs=[wide] if last else state_specs,
            scratch_shapes=[
                pltpu.VMEM((pages, page_len, width), jnp.bfloat16),
                pltpu.VMEM(
                    (pages // TILE_PAGES, KEY_VALUE_HEADS, LANES, TILE_PAGES * page_len), jnp.bfloat16
                ),
                pltpu.VMEM((pages * page_len, LANES), jnp.int32),
                pltpu.VMEM((KEY_VALUE_HEADS, lanes, LANES), jnp.bfloat16),
                pltpu.VMEM((KEY_VALUE_HEADS, TILE_PAGES * page_len, lanes), jnp.float32),
                pltpu.VMEM((KEY_VALUE_HEADS, TILE_PAGES * page_len, lanes), jnp.bfloat16),
                pltpu.VMEM((KEY_VALUE_HEADS, LANES, lanes), jnp.float32),
                pltpu.VMEM((2 * KEY_VALUE_HEADS, lanes), jnp.float32),
                pltpu.SemaphoreType.DMA,
            ],
        ),
        out_shape=[jax.ShapeDtypeStruct((picked, features), jnp.bfloat16)] if last else state_shapes,
        compiler_params=pltpu.CompilerParams(
            dimension_semantics=("arbitrary",), vmem_limit_bytes=VMEM_LIMIT
        ),
        cost_estimate=pl.CostEstimate(
            flops=int(share * 8 * picked * features * pages * page_len),
            bytes_accessed=2 * pages * page_len * width + 6 * picked * features,
            transcendentals=int(share * picked * features // LANES * pages * page_len),
        ),
    )(place, tiles, sel_lanes, position, queries, *([fresh] if first else state), *contexts)


def page_order(slots, positions, own, hold, capacity, groups, page_len):
    pages = slots.shape[0]
    number = jnp.arange(pages)
    before = number[None, :] < number[:, None]
    owners = slots // hold
    ranks = jnp.sum(((owners[None, :] == owners[:, None]) & before).astype(jnp.int32), axis=1)
    distance = owners ^ own
    last_position = positions.reshape(-1, QUERY_BLOCK)[:, -1:]
    starts = number * page_len
    replaced = jnp.any(
        (starts[:, None] + jnp.arange(page_len)[None, :])[:, :, None] == positions, axis=2
    )
    fresh = positions.reshape(-1, page_len)
    orders = []
    for at, group in enumerate(groups):
        if group is None:
            arrival = owners * capacity + ranks
            count = pages
        else:
            arrival = jnp.full((pages,), -1, jnp.int32)
            for i, d in enumerate(group):
                arrival = jnp.where(distance == d, i * capacity + ranks, arrival)
            count = len(group) * capacity
        member = arrival >= 0
        place = jnp.sum((member[None, :] & before).astype(jnp.int32), axis=1)
        seen = jnp.sum((member & (starts <= last_position)).astype(jnp.int32), axis=1)
        total = count
        if at == 0:
            place = place + jnp.sum((fresh[None, :, 0] < starts[:, None]).astype(jnp.int32), axis=1)
            ahead = jnp.sum((member & (starts <= fresh[:, 0:1])).astype(jnp.int32), axis=1)
            fresh_place = jnp.arange(fresh.shape[0]) + ahead
            seen = seen + jnp.sum((fresh[None, :, 0] <= last_position).astype(jnp.int32), axis=1)
            total = count + fresh.shape[0]
        elif at == len(groups) - 1:
            place = arrival
        places = jnp.where(arrival == jnp.arange(count)[:, None], place, 0)
        places = jnp.sum(places, axis=1)
        index = jnp.arange(-(-total // TILE_PAGES) * TILE_PAGES)[:, None]
        here = member & (place == index)
        inside = jnp.arange(page_len)
        rows = starts[:, None] + inside
        rows = jnp.where(replaced, FAR_POSITION, rows)
        rows = jnp.sum(jnp.where(here[:, :, None], rows, 0), axis=1)
        filled = jnp.any(here, axis=1, keepdims=True)
        if at == 0:
            there = fresh_place == index
            rows = rows + jnp.sum(jnp.where(there[:, :, None], fresh, 0), axis=1)
            filled = filled | jnp.any(there, axis=1, keepdims=True)
            places = jnp.concatenate([places, fresh_place])
        rows = jnp.where(filled, rows, FAR_POSITION).reshape(1, -1)
        orders.append((places, (seen + TILE_PAGES - 1) // TILE_PAGES, rows))
    return orders


def per_device(store, page_table, sel_pos, fresh_kv, queries):
    holders = lax.axis_size("store")
    hold, page_len, width = store.shape
    pages = page_table.shape[1]
    picked = sel_pos.shape[1]
    capacity = max(1, pages // holders)
    hbm = pl.BlockSpec(memory_space=pltpu.HBM)
    vmem = pl.BlockSpec(memory_space=pltpu.VMEM)
    dma = pltpu.SemaphoreType.DMA
    params = pltpu.CompilerParams(vmem_limit_bytes=VMEM_LIMIT)
    own = lax.axis_index("store")
    own_word = own.reshape(1).astype(jnp.int32)
    fresh = fresh_kv[0]
    wide = pltpu.VMEM((8, -(-picked // LANES) * LANES), jnp.int32)
    if holders == 16:
        first = (8, 12)
        groups = [(0, 8, 12, 4, 5, 1), (9, 6, 13, 7, 10, 2, 14, 3), (11, 15)]
        others = [d for group in groups for d in group if d not in first]
    else:
        first = ()
        groups = [None]
        others = None

    def swap(x, d):
        return lax.ppermute(x, "store", [(h, h ^ d) for h in range(holders)])

    def exchange(x):
        return lax.all_to_all(x, "store", split_axis=0, concat_axis=0, tiled=True)

    index, *lists = pl.pallas_call(
        functools.partial(index_kernel, hold, page_len, first),
        grid_spec=pltpu.PrefetchScalarGridSpec(
            num_scalar_prefetch=1,
            grid=(1,),
            in_specs=[vmem, vmem],
            out_specs=[vmem] * (1 + len(first)),
            scratch_shapes=[wide],
        ),
        out_shape=[
            jax.ShapeDtypeStruct((holders, 2, LANES), jnp.int32),
            *[jax.ShapeDtypeStruct((1, 2, LANES), jnp.int32)] * len(first),
        ],
        compiler_params=params,
    )(own_word, page_table, sel_pos)
    arrived = {}
    if first:
        lists = [swap(x, d) for x, d in zip(lists, first)]
        parts = pl.pallas_call(
            functools.partial(first_gather_kernel, len(first)),
            grid_spec=pltpu.PrefetchScalarGridSpec(
                num_scalar_prefetch=len(first),
                grid=(1,),
                in_specs=[hbm],
                out_specs=[hbm] * len(first),
                scratch_shapes=[
                    pltpu.VMEM((len(first), capacity, page_len, width), store.dtype),
                    dma,
                    dma,
                ],
            ),
            out_shape=[jax.ShapeDtypeStruct((capacity, page_len, width), store.dtype)] * len(first),
            compiler_params=params,
        )(*lists, store)
        parts, index, table, positions = lax.optimization_barrier(
            (parts, index, page_table, sel_pos)
        )
        arrived = {d: swap(part, d) for d, part in zip(first, parts)}
    else:
        table, positions = page_table, sel_pos
    index_in = exchange(index)

    packed = pl.pallas_call(
        functools.partial(rows_kernel, hold, page_len),
        out_shape=jax.ShapeDtypeStruct((holders, ROW_SLOTS, width), store.dtype),
        scratch_shapes=[wide],
        compiler_params=params,
    )(table, positions, fresh)

    each = jax.ShapeDtypeStruct((capacity, page_len, width), store.dtype)
    whole = jax.ShapeDtypeStruct((holders, capacity, page_len, width), store.dtype)
    parts = pl.pallas_call(
        functools.partial(gather_kernel, capacity, others),
        grid_spec=pltpu.PrefetchScalarGridSpec(
            num_scalar_prefetch=2,
            grid=(1,),
            in_specs=[hbm],
            out_specs=[hbm] * (len(others) if others else 1),
            scratch_shapes=[pltpu.VMEM(store.shape, store.dtype), dma, dma],
        ),
        out_shape=[each] * len(others) if others else [whole],
        compiler_params=params,
    )(own_word, index_in, store)
    parts, packed, table, positions = lax.optimization_barrier((parts, packed, table, positions))
    if others:
        parts = dict(zip(others, parts))
        for d in others:
            if d not in groups[2]:
                arrived[d] = swap(parts[d], d) if d else parts[d]
    else:
        arrived[None] = exchange(parts[0]).reshape(pages, page_len, width)
    rows_in = exchange(packed)

    store_out = pl.pallas_call(
        write_back_kernel,
        grid_spec=pltpu.PrefetchScalarGridSpec(
            num_scalar_prefetch=1,
            grid=(1,),
            in_specs=[vmem, hbm, hbm],
            out_specs=hbm,
            scratch_shapes=[
                pltpu.VMEM(store.shape, store.dtype),
                pltpu.VMEM((holders, ROW_SLOTS, width), store.dtype),
                pltpu.VMEM((holders, capacity, page_len, width), store.dtype),
                dma,
                dma,
                dma,
            ],
        ),
        out_shape=jax.ShapeDtypeStruct(store.shape, store.dtype),
        compiler_params=params,
        cost_estimate=pl.CostEstimate(flops=0, bytes_accessed=4 * store.size, transcendentals=0),
    )(index_in, index_in, store, rows_in)

    orders = page_order(table[0], positions[0], own, hold, capacity, groups, page_len)
    sel_lanes = jnp.tile(positions.reshape(-1, 1, QUERY_BLOCK), (1, 1, LANES // QUERY_BLOCK))
    store_out, sel_lanes = lax.optimization_barrier((store_out, sel_lanes))
    state = ()
    for at, (group, order) in enumerate(zip(groups, orders)):
        state = attend(
            at == 0,
            at == len(groups) - 1,
            order,
            sel_lanes,
            queries[0],
            fresh,
            state,
            [arrived[d] for d in group or [None]],
        )
        if at == 0 and others:
            middle = [arrived[d] for d in groups[1]]
            late, state, _ = lax.optimization_barrier(([parts[d] for d in groups[2]], state, middle))
            for d, part in zip(groups[2], late):
                arrived[d] = swap(part, d)
    return (state[0][None], store_out)


def solution(mesh):
    return jax.shard_map(
        per_device,
        mesh=mesh,
        in_specs=(
            P(("groups", "store"), None, None),
            P(("groups", "store"), None),
            P(("groups", "store"), None),
            P(("groups", "store"), None, None),
            P(("groups", "store"), None, None),
        ),
        out_specs=(P(("groups", "store"), None, None), P(("groups", "store"), None, None)),
        check_vma=False,
    )
```

```python
import functools

import jax
import jax.numpy as jnp
from jax import lax
from jax.experimental import pallas as pl
from jax.experimental.pallas import tpu as pltpu
from jax.sharding import PartitionSpec as P

HEAD_WIDTH = 128
KEY_VALUE_HEADS = 4
QUERY_GROUP = 12
SELP = 2
LANES = 128
ROW_SLOTS = 16
VMEM_LIMIT = 60 * 1024 * 1024
QUERY_BLOCK = 32
TILE_PAGES = 16
HIDDEN = -1e30
FAR_POSITION = 1 << 24


def nt_dot(a, b):
    return lax.dot_general(a, b, (((1,), (1,)), ((), ())), preferred_element_type=jnp.float32)


def one_hot(condition):
    return jnp.where(condition, 1.0, 0.0)


def pair_places(hold, page_len, table_ref, sel_ref, wide):
    pages = table_ref.shape[1]
    picked = sel_ref.shape[1]
    f32 = jnp.float32
    slots = jnp.broadcast_to(table_ref[...], (pages, pages))
    owners = slots // hold
    local_row = (slots - owners * hold).astype(f32)[0:1]
    owner_row = owners.astype(f32)
    owner_col = owner_row.T
    sub = lax.broadcasted_iota(jnp.int32, (pages, pages), 0)
    lane = lax.broadcasted_iota(jnp.int32, (pages, pages), 1)
    earlier = one_hot((owner_row == owner_col) & (lane < sub))
    rank_col = jnp.sum(earlier, axis=1, keepdims=True)

    wide[...] = jnp.full(wide.shape, -1, jnp.int32)
    wide[0:1, 0:picked] = sel_ref[...]
    position = wide[...]
    page = lax.shift_right_arithmetic(position, page_len.bit_length() - 1)
    offset = (position & (page_len - 1)).astype(f32)[0:1]
    lane_wide = lax.broadcasted_iota(jnp.int32, wide.shape, 1)
    second = one_hot((page == pltpu.roll(page, 1, axis=1)) & (lane_wide > 0))[0:1]
    valid = lane_wide[0:1] < picked
    sub_wide = lax.broadcasted_iota(jnp.int32, (pages, wide.shape[1]), 0)
    in_page = one_hot(sub_wide == page[0:1])
    owner = jnp.sum(in_page * owner_col[:, 0:1], axis=0, keepdims=True)
    rank = jnp.sum(in_page * rank_col, axis=0, keepdims=True)
    return owner_row[0:1], local_row, rank_col, owner, rank, second, offset, valid


def index_kernel(hold, page_len, first, own, table_ref, sel_ref, out_ref, *rest):
    first_refs, wide = rest[:-1], rest[-1]
    holders = out_ref.shape[0]
    pages = table_ref.shape[1]
    f32 = jnp.float32
    bf16 = jnp.bfloat16
    owner_row, local_row, rank_col, owner, rank, second, offset, valid = pair_places(
        hold, page_len, table_ref, sel_ref, wide
    )
    holder = lax.broadcasted_iota(jnp.int32, (holders, pages), 0).astype(f32)
    owned = jnp.where(holder == owner_row, local_row, 0.0)
    lane = lax.broadcasted_iota(jnp.int32, (pages, LANES), 1).astype(f32)
    numbers = jnp.dot(
        owned.astype(bf16), one_hot(lane == rank_col).astype(bf16), preferred_element_type=f32
    )
    holder_wide = lax.broadcasted_iota(jnp.int32, (holders, wide.shape[1]), 0).astype(f32)
    marked = jnp.where((holder_wide == owner) & valid, rank * page_len + offset + 1.0, 0.0)
    place_lane = lax.broadcasted_iota(jnp.int32, (LANES, wide.shape[1]), 0).astype(f32)
    at_place = one_hot(place_lane == SELP * rank + second)
    targets = nt_dot(marked.astype(bf16), at_place.astype(bf16))
    for h in range(holders):
        out_ref[h, 0:1, :] = numbers[h : h + 1, :].astype(jnp.int32)
        out_ref[h, 1:2, :] = targets[h : h + 1, :].astype(jnp.int32)
    for d, ref in zip(first, first_refs):
        ref[0] = out_ref[own[0] ^ d]


def rows_kernel(hold, page_len, table_ref, sel_ref, fresh_ref, packed, wide):
    holders = packed.shape[0]
    picked = sel_ref.shape[1]
    f32 = jnp.float32
    _, _, _, owner, rank, second, _, valid = pair_places(hold, page_len, table_ref, sel_ref, wide)
    spot = jnp.where(valid, owner * ROW_SLOTS + SELP * rank + second, -1.0)[:, 0:picked]
    step = min(holders, 16)
    for start in range(0, holders, step):
        spot_id = lax.broadcasted_iota(jnp.int32, (step * ROW_SLOTS, picked), 0).astype(f32)
        choose = one_hot(spot_id + float(start * ROW_SLOTS) == spot).astype(jnp.bfloat16)
        rows = jnp.dot(choose, fresh_ref[...], preferred_element_type=f32).astype(jnp.bfloat16)
        packed[start : start + step] = rows.reshape(step, ROW_SLOTS, fresh_ref.shape[1])


def first_gather_kernel(count, *refs):
    lists, store_hbm, sends = refs[:count], refs[count], refs[count + 1 : 2 * count + 1]
    held, load_sem, send_sem = refs[2 * count + 1 :]
    capacity = held.shape[1]
    for i, numbers in enumerate(lists):
        for k in range(capacity):
            pltpu.make_async_copy(store_hbm.at[numbers[0, 0, k]], held.at[i, k], load_sem).start()
    pltpu.make_async_copy(held, held, load_sem).wait()
    for i, send in enumerate(sends):
        pltpu.make_async_copy(held.at[i], send, send_sem).start()
    pltpu.make_async_copy(held, held, send_sem).wait()


def gather_kernel(capacity, distances, own, index, store_hbm, *rest):
    sends, (store, load_sem, send_sem) = rest[:-3], rest[-3:]
    load = pltpu.make_async_copy(store_hbm, store, load_sem)
    load.start()
    load.wait()
    for i in range(len(distances) if distances else index.shape[0]):
        r = own[0] ^ distances[i] if distances else i
        send = sends[i] if distances else sends[0].at[i]
        for k in range(capacity):
            pltpu.make_async_copy(store.at[index[r, 0, k]], send.at[k], send_sem).start()
    for send in sends:
        pltpu.make_async_copy(send, send, send_sem).wait()


def write_back_kernel(index, targets_ref, store_hbm, rows_hbm, store_out, *scratch):
    store, rows, blended, load_sem, rows_sem, out_sem = scratch
    holders, capacity, page_len, width = blended.shape
    rows_here = capacity * page_len
    f32 = jnp.float32
    load = pltpu.make_async_copy(store_hbm, store, load_sem)
    load_rows = pltpu.make_async_copy(rows_hbm, rows, rows_sem)
    load.start()
    load_rows.start()
    load_rows.wait()
    load.wait()
    row_id = lax.broadcasted_iota(jnp.int32, (rows_here, ROW_SLOTS), 0)

    def one_request(r, carry):
        hit = one_hot(row_id == targets_ref[r][1:2, 0:ROW_SLOTS] - 1)
        keep = 1.0 - jnp.sum(hit, axis=1, keepdims=True)
        keep = jnp.broadcast_to(keep, (rows_here, LANES)).astype(jnp.bfloat16)
        hit = hit.astype(jnp.bfloat16)
        for c in range(width // LANES):
            lanes = slice(c * LANES, (c + 1) * LANES)
            fresh = jnp.dot(hit, rows[r, :, lanes], preferred_element_type=f32).astype(jnp.bfloat16)
            for k in range(capacity):
                part = slice(k * page_len, (k + 1) * page_len)
                blended[r, k, :, lanes] = store[index[r, 0, k], :, lanes] * keep[part] + fresh[part]
        for k in range(capacity):
            pltpu.make_async_copy(blended.at[r, k], store_out.at[index[r, 0, k]], out_sem).start()
        return carry

    lax.fori_loop(0, holders, one_request, 0)
    pltpu.make_async_copy(store_out, store_out, out_sem).wait()


def attend_kernel(first, last, sources, place, tiles, *rest):
    sel_ref, position_ref, query_ref, *rest = rest
    if first:
        fresh_ref, *rest = rest
    state_in = () if first else rest[:2]
    rest = rest if first else rest[2:]
    contexts, rest = rest[:sources], rest[sources:]
    outs, rest = (rest[:1], rest[1:]) if last else (rest[:2], rest[2:])
    kv, values, position, query, scores, raised, mixed, stats, sem = rest
    pages, page_len, width = kv.shape
    each = contexts[0].shape[0]
    direct = last and not first
    block = query_ref.shape[0]
    tile = TILE_PAGES * page_len
    lanes = QUERY_GROUP * block
    scale = 1.4426950408889634 / HEAD_WIDTH**0.5
    f32 = jnp.float32
    bf16 = jnp.bfloat16
    step = pl.program_id(0)
    eye = one_hot(
        lax.broadcasted_iota(jnp.int32, (LANES, LANES), 0)
        == lax.broadcasted_iota(jnp.int32, (LANES, LANES), 1)
    ).astype(bf16)

    @pl.when(step == 0)
    def _():
        for i, context in enumerate(contexts):
            if direct:
                kv[i * each : (i + 1) * each] = context[...]
            else:
                for k in range(each):
                    to = kv.at[place[i * each + k]]
                    pltpu.make_async_copy(context.at[k], to, sem).start()
        if first:
            count = fresh_ref.shape[0] // page_len
            for p in range(count):
                page = fresh_ref[p * page_len : (p + 1) * page_len, :]
                kv[place[sources * each + p]] = page
            used = sources * each + count
            if pages > used:
                kv[used:] = jnp.zeros((pages - used, page_len, width), bf16)
        for c in range(position_ref.shape[1] // LANES):
            part = slice(c * LANES, (c + 1) * LANES)
            row = jnp.broadcast_to(position_ref[:, part], (LANES, LANES)).astype(f32)
            position[part, :] = row.T.astype(jnp.int32)
        if not direct:
            arrived = kv.at[0 : sources * each]
            pltpu.make_async_copy(arrived, arrived, sem).wait()

        def turn(t, carry):
            here = pl.ds(t * TILE_PAGES, TILE_PAGES)
            for g in range(KEY_VALUE_HEADS):
                at = (KEY_VALUE_HEADS + g) * LANES
                value = kv[here, :, at : at + LANES].reshape(tile, LANES)
                values[t, g] = nt_dot(eye, value).astype(bf16)
            return carry

        lax.fori_loop(0, pages // TILE_PAGES, turn, 0)

    for g in range(KEY_VALUE_HEADS):
        for i in range(QUERY_GROUP):
            head = g * QUERY_GROUP + i
            query[g, i * block : (i + 1) * block, :] = query_ref[:, head * LANES : (head + 1) * LANES]
    if first:
        mixed[...] = jnp.zeros(mixed.shape, f32)
        stats[0:KEY_VALUE_HEADS, :] = jnp.full((KEY_VALUE_HEADS, lanes), HIDDEN, f32)
        stats[KEY_VALUE_HEADS:, :] = jnp.zeros((KEY_VALUE_HEADS, lanes), f32)
    else:
        mixed[...] = state_in[0][0]
        stats[...] = state_in[1][0]

    sel = sel_ref[0]

    def one_tile(t, carry):
        here = pl.ds(t * TILE_PAGES, TILE_PAGES)
        bias = jnp.where(
            position[pl.ds(pl.multiple_of(t * tile, tile), tile), :] <= sel, 0.0, HIDDEN
        ).astype(f32)

        parts = [slice(n * LANES, (n + 1) * LANES) for n in range(lanes // LANES)]
        chains = [(g, part) for g in range(KEY_VALUE_HEADS) for part in parts]
        for g in range(KEY_VALUE_HEADS):
            key = kv[here, :, g * LANES : (g + 1) * LANES].reshape(tile, LANES)
            product = nt_dot(key, query[g])
            for part in parts:
                scores[g, :, part] = product[:, part] + bias
        peaks, shrinks = [], []
        for g, part in chains:
            old = stats[g : g + 1, part]
            new = jnp.maximum(old, jnp.max(scores[g, :, part], axis=0, keepdims=True))
            stats[g : g + 1, part] = new
            peaks.append(new)
            shrinks.append(jnp.exp2((old - new) * scale))
        for (g, part), new, shrink in zip(chains, peaks, shrinks):
            at = KEY_VALUE_HEADS + g
            p = jnp.exp2((scores[g, :, part] - new) * scale)
            stats[at : at + 1, part] = stats[at : at + 1, part] * shrink + jnp.sum(
                p, axis=0, keepdims=True
            )
            raised[g, :, part] = p.astype(bf16)
        for g in range(KEY_VALUE_HEADS):
            shrink = jnp.concatenate(shrinks[g * len(parts) : (g + 1) * len(parts)], axis=1)
            mixed[g] = mixed[g] * shrink + jnp.dot(
                values[t, g], raised[g], preferred_element_type=f32
            )
        return carry

    lax.fori_loop(0, tiles[step], one_tile, 0)

    if last:
        done = []
        for g in range(KEY_VALUE_HEADS):
            at = KEY_VALUE_HEADS + g
            part = (mixed[g] * (1.0 / stats[at : at + 1, :])).astype(bf16)
            done += [part[:, n * LANES : (n + 1) * LANES] for n in range(lanes // LANES)]
        turned = nt_dot(eye, jnp.concatenate(done, axis=0)).astype(bf16)
        for n in range(len(done)):
            for i in range(LANES // block):
                head = n * (LANES // block) + i
                outs[0][:, head * LANES : (head + 1) * LANES] = turned[
                    i * block : (i + 1) * block, n * LANES : (n + 1) * LANES
                ]
    else:
        outs[0][0] = mixed[...]
        outs[1][0] = stats[...]


def attend(first, last, order, sel_lanes, queries, fresh, state, contexts):
    place, tiles, position = order
    picked, features = queries.shape
    each, page_len, width = contexts[0].shape
    pages = position.shape[1] // page_len
    steps = picked // QUERY_BLOCK
    lanes = QUERY_GROUP * QUERY_BLOCK
    wide = pl.BlockSpec((QUERY_BLOCK, features), lambda b, *_: (b, 0))
    state_specs = [
        pl.BlockSpec((1, KEY_VALUE_HEADS, LANES, lanes), lambda b, *_: (b, 0, 0, 0)),
        pl.BlockSpec((1, 2 * KEY_VALUE_HEADS, lanes), lambda b, *_: (b, 0, 0)),
    ]
    state_shapes = [
        jax.ShapeDtypeStruct((steps, KEY_VALUE_HEADS, LANES, lanes), jnp.float32),
        jax.ShapeDtypeStruct((steps, 2 * KEY_VALUE_HEADS, lanes), jnp.float32),
    ]
    share = 0.6
    return pl.pallas_call(
        functools.partial(attend_kernel, first, last, len(contexts)),
        grid_spec=pltpu.PrefetchScalarGridSpec(
            num_scalar_prefetch=2,
            grid=(steps,),
            in_specs=[
                pl.BlockSpec((1, 1, LANES), lambda b, *_: (b, 0, 0)),
                pl.BlockSpec(position.shape, lambda b, *_: (0, 0)),
                wide,
                *([pl.BlockSpec(fresh.shape, lambda b, *_: (0, 0))] if first else state_specs),
                *[
                    pl.BlockSpec(x.shape, lambda b, *_: (0, 0, 0))
                    if last and not first
                    else pl.BlockSpec(memory_space=pltpu.HBM)
                    for x in contexts
                ],
            ],
            out_specs=[wide] if last else state_specs,
            scratch_shapes=[
                pltpu.VMEM((pages, page_len, width), jnp.bfloat16),
                pltpu.VMEM(
                    (pages // TILE_PAGES, KEY_VALUE_HEADS, LANES, TILE_PAGES * page_len), jnp.bfloat16
                ),
                pltpu.VMEM((pages * page_len, LANES), jnp.int32),
                pltpu.VMEM((KEY_VALUE_HEADS, lanes, LANES), jnp.bfloat16),
                pltpu.VMEM((KEY_VALUE_HEADS, TILE_PAGES * page_len, lanes), jnp.float32),
                pltpu.VMEM((KEY_VALUE_HEADS, TILE_PAGES * page_len, lanes), jnp.bfloat16),
                pltpu.VMEM((KEY_VALUE_HEADS, LANES, lanes), jnp.float32),
                pltpu.VMEM((2 * KEY_VALUE_HEADS, lanes), jnp.float32),
                pltpu.SemaphoreType.DMA,
            ],
        ),
        out_shape=[jax.ShapeDtypeStruct((picked, features), jnp.bfloat16)] if last else state_shapes,
        compiler_params=pltpu.CompilerParams(
            dimension_semantics=("arbitrary",), vmem_limit_bytes=VMEM_LIMIT
        ),
        cost_estimate=pl.CostEstimate(
            flops=int(share * 8 * picked * features * pages * page_len),
            bytes_accessed=2 * pages * page_len * width + 6 * picked * features,
            transcendentals=int(share * picked * features // LANES * pages * page_len),
        ),
    )(place, tiles, sel_lanes, position, queries, *([fresh] if first else state), *contexts)


def page_order(slots, positions, own, hold, capacity, groups, page_len):
    pages = slots.shape[0]
    number = jnp.arange(pages)
    before = number[None, :] < number[:, None]
    owners = slots // hold
    ranks = jnp.sum(((owners[None, :] == owners[:, None]) & before).astype(jnp.int32), axis=1)
    distance = owners ^ own
    last_position = positions.reshape(-1, QUERY_BLOCK)[:, -1:]
    starts = number * page_len
    replaced = jnp.any(
        (starts[:, None] + jnp.arange(page_len)[None, :])[:, :, None] == positions, axis=2
    )
    fresh = positions.reshape(-1, page_len)
    orders = []
    for at, group in enumerate(groups):
        if group is None:
            arrival = owners * capacity + ranks
            count = pages
        else:
            arrival = jnp.full((pages,), -1, jnp.int32)
            for i, d in enumerate(group):
                arrival = jnp.where(distance == d, i * capacity + ranks, arrival)
            count = len(group) * capacity
        member = arrival >= 0
        place = jnp.sum((member[None, :] & before).astype(jnp.int32), axis=1)
        seen = jnp.sum((member & (starts <= last_position)).astype(jnp.int32), axis=1)
        total = count
        if at == 0:
            place = place + jnp.sum((fresh[None, :, 0] < starts[:, None]).astype(jnp.int32), axis=1)
            ahead = jnp.sum((member & (starts <= fresh[:, 0:1])).astype(jnp.int32), axis=1)
            fresh_place = jnp.arange(fresh.shape[0]) + ahead
            seen = seen + jnp.sum((fresh[None, :, 0] <= last_position).astype(jnp.int32), axis=1)
            total = count + fresh.shape[0]
        elif at == len(groups) - 1:
            place = arrival
        places = jnp.where(arrival == jnp.arange(count)[:, None], place, 0)
        places = jnp.sum(places, axis=1)
        index = jnp.arange(-(-total // TILE_PAGES) * TILE_PAGES)[:, None]
        here = member & (place == index)
        inside = jnp.arange(page_len)
        rows = starts[:, None] + inside
        rows = jnp.where(replaced, FAR_POSITION, rows)
        rows = jnp.sum(jnp.where(here[:, :, None], rows, 0), axis=1)
        filled = jnp.any(here, axis=1, keepdims=True)
        if at == 0:
            there = fresh_place == index
            rows = rows + jnp.sum(jnp.where(there[:, :, None], fresh, 0), axis=1)
            filled = filled | jnp.any(there, axis=1, keepdims=True)
            places = jnp.concatenate([places, fresh_place])
        rows = jnp.where(filled, rows, FAR_POSITION).reshape(1, -1)
        orders.append((places, (seen + TILE_PAGES - 1) // TILE_PAGES, rows))
    return orders


def per_device(store, page_table, sel_pos, fresh_kv, queries):
    holders = lax.axis_size("store")
    hold, page_len, width = store.shape
    pages = page_table.shape[1]
    picked = sel_pos.shape[1]
    capacity = max(1, pages // holders)
    hbm = pl.BlockSpec(memory_space=pltpu.HBM)
    vmem = pl.BlockSpec(memory_space=pltpu.VMEM)
    dma = pltpu.SemaphoreType.DMA
    params = pltpu.CompilerParams(vmem_limit_bytes=VMEM_LIMIT)
    own = lax.axis_index("store")
    own_word = own.reshape(1).astype(jnp.int32)
    fresh = fresh_kv[0]
    wide = pltpu.VMEM((8, -(-picked // LANES) * LANES), jnp.int32)
    if holders == 16:
        first = (8, 12)
        groups = [(0, 8, 12, 4, 5, 1), (9, 6, 13, 7, 10, 2, 14, 3), (11, 15)]
        others = [d for group in groups for d in group if d not in first]
    else:
        first = ()
        groups = [None]
        others = None

    def swap(x, d):
        return lax.ppermute(x, "store", [(h, h ^ d) for h in range(holders)])

    def exchange(x):
        return lax.all_to_all(x, "store", split_axis=0, concat_axis=0, tiled=True)

    index, *lists = pl.pallas_call(
        functools.partial(index_kernel, hold, page_len, first),
        grid_spec=pltpu.PrefetchScalarGridSpec(
            num_scalar_prefetch=1,
            grid=(1,),
            in_specs=[vmem, vmem],
            out_specs=[vmem] * (1 + len(first)),
            scratch_shapes=[wide],
        ),
        out_shape=[
            jax.ShapeDtypeStruct((holders, 2, LANES), jnp.int32),
            *[jax.ShapeDtypeStruct((1, 2, LANES), jnp.int32)] * len(first),
        ],
        compiler_params=params,
    )(own_word, page_table, sel_pos)
    arrived = {}
    if first:
        lists = [swap(x, d) for x, d in zip(lists, first)]
        parts = pl.pallas_call(
            functools.partial(first_gather_kernel, len(first)),
            grid_spec=pltpu.PrefetchScalarGridSpec(
                num_scalar_prefetch=len(first),
                grid=(1,),
                in_specs=[hbm],
                out_specs=[hbm] * len(first),
                scratch_shapes=[
                    pltpu.VMEM((len(first), capacity, page_len, width), store.dtype),
                    dma,
                    dma,
                ],
            ),
            out_shape=[jax.ShapeDtypeStruct((capacity, page_len, width), store.dtype)] * len(first),
            compiler_params=params,
        )(*lists, store)
        parts, index, table, positions = lax.optimization_barrier(
            (parts, index, page_table, sel_pos)
        )
        arrived = {d: swap(part, d) for d, part in zip(first, parts)}
    else:
        table, positions = page_table, sel_pos
    index_in = exchange(index)

    packed = pl.pallas_call(
        functools.partial(rows_kernel, hold, page_len),
        out_shape=jax.ShapeDtypeStruct((holders, ROW_SLOTS, width), store.dtype),
        scratch_shapes=[wide],
        compiler_params=params,
    )(table, positions, fresh)

    each = jax.ShapeDtypeStruct((capacity, page_len, width), store.dtype)
    whole = jax.ShapeDtypeStruct((holders, capacity, page_len, width), store.dtype)
    parts = pl.pallas_call(
        functools.partial(gather_kernel, capacity, others),
        grid_spec=pltpu.PrefetchScalarGridSpec(
            num_scalar_prefetch=2,
            grid=(1,),
            in_specs=[hbm],
            out_specs=[hbm] * (len(others) if others else 1),
            scratch_shapes=[pltpu.VMEM(store.shape, store.dtype), dma, dma],
        ),
        out_shape=[each] * len(others) if others else [whole],
        compiler_params=params,
    )(own_word, index_in, store)
    parts, packed, table, positions = lax.optimization_barrier((parts, packed, table, positions))
    if others:
        parts = dict(zip(others, parts))
        for d in others:
            if d not in groups[2]:
                arrived[d] = swap(parts[d], d) if d else parts[d]
    else:
        arrived[None] = exchange(parts[0]).reshape(pages, page_len, width)
    rows_in = exchange(packed)

    if others:
        table, positions, _ = lax.optimization_barrier((table, positions, arrived[8]))
    orders = page_order(table[0], positions[0], own, hold, capacity, groups, page_len)
    sel_lanes = jnp.tile(positions.reshape(-1, 1, QUERY_BLOCK), (1, 1, LANES // QUERY_BLOCK))
    write_back = pl.pallas_call(
        write_back_kernel,
        grid_spec=pltpu.PrefetchScalarGridSpec(
            num_scalar_prefetch=1,
            grid=(1,),
            in_specs=[vmem, hbm, hbm],
            out_specs=hbm,
            scratch_shapes=[
                pltpu.VMEM(store.shape, store.dtype),
                pltpu.VMEM((holders, ROW_SLOTS, width), store.dtype),
                pltpu.VMEM((holders, capacity, page_len, width), store.dtype),
                dma,
                dma,
                dma,
            ],
        ),
        out_shape=jax.ShapeDtypeStruct(store.shape, store.dtype),
        compiler_params=params,
        cost_estimate=pl.CostEstimate(flops=0, bytes_accessed=4 * store.size, transcendentals=0),
    )
    state = ()
    for at, (group, order) in enumerate(zip(groups, orders)):
        state = attend(
            at == 0,
            at == len(groups) - 1,
            order,
            sel_lanes,
            queries[0],
            fresh,
            state,
            [arrived[d] for d in group or [None]],
        )
        if at == 0:
            rows_in, state = lax.optimization_barrier((rows_in, state))
            store_out = write_back(index_in, index_in, store, rows_in)
            if others:
                middle = [arrived[d] for d in groups[1]]
                late = [parts[d] for d in groups[2]]
                late, state, store_out, _ = lax.optimization_barrier((late, state, store_out, middle))
                for d, part in zip(groups[2], late):
                    arrived[d] = swap(part, d)
    return (state[0][None], store_out)


def solution(mesh):
    return jax.shard_map(
        per_device,
        mesh=mesh,
        in_specs=(
            P(("groups", "store"), None, None),
            P(("groups", "store"), None),
            P(("groups", "store"), None),
            P(("groups", "store"), None, None),
            P(("groups", "store"), None, None),
        ),
        out_specs=(P(("groups", "store"), None, None), P(("groups", "store"), None, None)),
        check_vma=False,
    )
```

```python
import functools

import jax
import jax.numpy as jnp
from jax import lax
from jax.experimental import pallas as pl
from jax.experimental.pallas import tpu as pltpu
from jax.sharding import PartitionSpec as P

HEAD_WIDTH = 128
KEY_VALUE_HEADS = 4
QUERY_GROUP = 12
SELP = 2
LANES = 128
ROW_SLOTS = 16
VMEM_LIMIT = 60 * 1024 * 1024
QUERY_BLOCK = 32
TILE_PAGES = 32
LATE_TILE_PAGES = 16
FRESH_PAGES = 16
HIDDEN = -1e30
FAR_POSITION = 1 << 24


def nt_dot(a, b):
    return lax.dot_general(a, b, (((1,), (1,)), ((), ())), preferred_element_type=jnp.float32)


def one_hot(condition):
    return jnp.where(condition, 1.0, 0.0)


def pair_places(hold, page_len, table_ref, sel_ref, wide):
    pages = table_ref.shape[1]
    picked = sel_ref.shape[1]
    f32 = jnp.float32
    slots = jnp.broadcast_to(table_ref[...], (pages, pages))
    owners = slots // hold
    local_row = (slots - owners * hold).astype(f32)[0:1]
    owner_row = owners.astype(f32)
    owner_col = owner_row.T
    sub = lax.broadcasted_iota(jnp.int32, (pages, pages), 0)
    lane = lax.broadcasted_iota(jnp.int32, (pages, pages), 1)
    earlier = one_hot((owner_row == owner_col) & (lane < sub))
    rank_col = jnp.sum(earlier, axis=1, keepdims=True)

    wide[...] = jnp.full(wide.shape, -1, jnp.int32)
    wide[0:1, 0:picked] = sel_ref[...]
    position = wide[...]
    page = lax.shift_right_arithmetic(position, page_len.bit_length() - 1)
    offset = (position & (page_len - 1)).astype(f32)[0:1]
    lane_wide = lax.broadcasted_iota(jnp.int32, wide.shape, 1)
    second = one_hot((page == pltpu.roll(page, 1, axis=1)) & (lane_wide > 0))[0:1]
    valid = lane_wide[0:1] < picked
    sub_wide = lax.broadcasted_iota(jnp.int32, (pages, wide.shape[1]), 0)
    in_page = one_hot(sub_wide == page[0:1])
    owner = jnp.sum(in_page * owner_col[:, 0:1], axis=0, keepdims=True)
    rank = jnp.sum(in_page * rank_col, axis=0, keepdims=True)
    return owner_row[0:1], local_row, rank_col, owner, rank, second, offset, valid


def index_kernel(hold, page_len, first, own, table_ref, sel_ref, out_ref, *rest):
    first_refs, wide = rest[:-1], rest[-1]
    holders = out_ref.shape[0]
    pages = table_ref.shape[1]
    f32 = jnp.float32
    bf16 = jnp.bfloat16
    owner_row, local_row, rank_col, owner, rank, second, offset, valid = pair_places(
        hold, page_len, table_ref, sel_ref, wide
    )
    holder = lax.broadcasted_iota(jnp.int32, (holders, pages), 0).astype(f32)
    owned = jnp.where(holder == owner_row, local_row, 0.0)
    lane = lax.broadcasted_iota(jnp.int32, (pages, LANES), 1).astype(f32)
    numbers = jnp.dot(
        owned.astype(bf16), one_hot(lane == rank_col).astype(bf16), preferred_element_type=f32
    )
    holder_wide = lax.broadcasted_iota(jnp.int32, (holders, wide.shape[1]), 0).astype(f32)
    marked = jnp.where((holder_wide == owner) & valid, rank * page_len + offset + 1.0, 0.0)
    place_lane = lax.broadcasted_iota(jnp.int32, (LANES, wide.shape[1]), 0).astype(f32)
    at_place = one_hot(place_lane == SELP * rank + second)
    targets = nt_dot(marked.astype(bf16), at_place.astype(bf16))
    for h in range(holders):
        out_ref[h, 0:1, :] = numbers[h : h + 1, :].astype(jnp.int32)
        out_ref[h, 1:2, :] = targets[h : h + 1, :].astype(jnp.int32)
    for d, ref in zip(first, first_refs):
        ref[0] = out_ref[own[0] ^ d]


def rows_kernel(hold, page_len, table_ref, sel_ref, fresh_ref, packed, wide):
    holders = packed.shape[0]
    picked = sel_ref.shape[1]
    f32 = jnp.float32
    _, _, _, owner, rank, second, _, valid = pair_places(hold, page_len, table_ref, sel_ref, wide)
    spot = jnp.where(valid, owner * ROW_SLOTS + SELP * rank + second, -1.0)[:, 0:picked]
    step = min(holders, 16)
    for start in range(0, holders, step):
        spot_id = lax.broadcasted_iota(jnp.int32, (step * ROW_SLOTS, picked), 0).astype(f32)
        choose = one_hot(spot_id + float(start * ROW_SLOTS) == spot).astype(jnp.bfloat16)
        rows = jnp.dot(choose, fresh_ref[...], preferred_element_type=f32).astype(jnp.bfloat16)
        packed[start : start + step] = rows.reshape(step, ROW_SLOTS, fresh_ref.shape[1])


def first_gather_kernel(count, *refs):
    lists, store_hbm, sends = refs[:count], refs[count], refs[count + 1 : 2 * count + 1]
    held, load_sem, send_sem = refs[2 * count + 1 :]
    capacity = held.shape[1]
    for i, numbers in enumerate(lists):
        for k in range(capacity):
            pltpu.make_async_copy(store_hbm.at[numbers[0, 0, k]], held.at[i, k], load_sem).start()
    pltpu.make_async_copy(held, held, load_sem).wait()
    for i, send in enumerate(sends):
        pltpu.make_async_copy(held.at[i], send, send_sem).start()
    pltpu.make_async_copy(held, held, send_sem).wait()


def gather_kernel(capacity, distances, own, index, store_hbm, *rest):
    sends, (store, load_sem, send_sem) = rest[:-3], rest[-3:]
    load = pltpu.make_async_copy(store_hbm, store, load_sem)
    load.start()
    load.wait()
    for i in range(len(distances) if distances else index.shape[0]):
        r = own[0] ^ distances[i] if distances else i
        send = sends[i] if distances else sends[0].at[i]
        for k in range(capacity):
            pltpu.make_async_copy(store.at[index[r, 0, k]], send.at[k], send_sem).start()
    for send in sends:
        pltpu.make_async_copy(send, send, send_sem).wait()


def write_back_kernel(index, targets_ref, store_hbm, rows_hbm, store_out, *scratch):
    store, rows, blended, load_sem, rows_sem, out_sem = scratch
    holders, capacity, page_len, width = blended.shape
    rows_here = capacity * page_len
    f32 = jnp.float32
    load = pltpu.make_async_copy(store_hbm, store, load_sem)
    load_rows = pltpu.make_async_copy(rows_hbm, rows, rows_sem)
    load.start()
    load_rows.start()
    load_rows.wait()
    load.wait()
    row_id = lax.broadcasted_iota(jnp.int32, (rows_here, ROW_SLOTS), 0)

    def one_request(r, carry):
        hit = one_hot(row_id == targets_ref[r][1:2, 0:ROW_SLOTS] - 1)
        keep = 1.0 - jnp.sum(hit, axis=1, keepdims=True)
        keep = jnp.broadcast_to(keep, (rows_here, LANES)).astype(jnp.bfloat16)
        hit = hit.astype(jnp.bfloat16)
        for c in range(width // LANES):
            lanes = slice(c * LANES, (c + 1) * LANES)
            fresh = jnp.dot(hit, rows[r, :, lanes], preferred_element_type=f32).astype(jnp.bfloat16)
            for k in range(capacity):
                part = slice(k * page_len, (k + 1) * page_len)
                blended[r, k, :, lanes] = store[index[r, 0, k], :, lanes] * keep[part] + fresh[part]
        for k in range(capacity):
            pltpu.make_async_copy(blended.at[r, k], store_out.at[index[r, 0, k]], out_sem).start()
        return carry

    lax.fori_loop(0, holders, one_request, 0)
    pltpu.make_async_copy(store_out, store_out, out_sem).wait()


def attend_kernel(first, last, tile_pages, sources, place, page_number, tiles, *rest):
    sel_ref, positions_ref, query_ref, *rest = rest
    if first:
        fresh_ref, fresh_positions, *rest = rest
    state_in = () if first else rest[:2]
    rest = rest if first else rest[2:]
    contexts, rest = rest[:sources], rest[sources:]
    outs, rest = (rest[:1], rest[1:]) if last else (rest[:2], rest[2:])
    kv, values, position, query, scores, raised, mixed, stats, sem = rest
    pages, page_len, width = kv.shape
    each = contexts[0].shape[0]
    ahead = FRESH_PAGES if first else 0
    direct = last and not first
    block = query_ref.shape[0]
    tile = tile_pages * page_len
    lanes = QUERY_GROUP * block
    scale = 1.4426950408889634 / HEAD_WIDTH**0.5
    f32 = jnp.float32
    bf16 = jnp.bfloat16
    step = pl.program_id(0)
    eye = one_hot(
        lax.broadcasted_iota(jnp.int32, (LANES, LANES), 0)
        == lax.broadcasted_iota(jnp.int32, (LANES, LANES), 1)
    ).astype(bf16)

    @pl.when(step == 0)
    def _():
        for i, context in enumerate(contexts):
            if direct:
                kv[i * each : (i + 1) * each] = context[...]
            else:
                for k in range(each):
                    to = kv.at[ahead + place[i * each + k]]
                    pltpu.make_async_copy(context.at[k], to, sem).start()
        if first:
            picked = fresh_ref.shape[0]
            count = picked // page_len
            kv[0:count] = fresh_ref[...].reshape(count, page_len, width)
            kv[count:ahead] = jnp.zeros((ahead - count, page_len, width), bf16)
            position[0:picked, :] = fresh_positions[...]
            start = ahead * page_len
            position[picked:start, :] = jnp.full((start - picked, LANES), FAR_POSITION, jnp.int32)
        positions = positions_ref[...]
        row = lax.broadcasted_iota(jnp.int32, (page_len, positions.shape[1]), 0)
        ones = jnp.ones((positions.shape[1], LANES), bf16)
        row_lanes = lax.broadcasted_iota(jnp.int32, (page_len, LANES), 0)

        def place_rows(t, carry):
            starts = [page_number[t * FRESH_PAGES + k] * page_len for k in range(FRESH_PAGES)]
            hit = jnp.concatenate([one_hot(row + start == positions) for start in starts], axis=0)
            hidden = jnp.dot(hit.astype(bf16), ones, preferred_element_type=f32)
            plain = jnp.concatenate([row_lanes + start for start in starts], axis=0)
            some = FRESH_PAGES * page_len
            here = pl.ds(pl.multiple_of(ahead * page_len + t * some, some), some)
            position[here, :] = jnp.where(hidden > 0.0, FAR_POSITION, plain)
            return carry

        lax.fori_loop(0, (pages - ahead) // FRESH_PAGES, place_rows, 0)
        if not direct:
            used = kv.at[ahead:]
            pltpu.make_async_copy(used, used, sem).wait()

        def turn(t, carry):
            here = pl.ds(t * tile_pages, tile_pages)
            for g in range(KEY_VALUE_HEADS):
                at = (KEY_VALUE_HEADS + g) * LANES
                value = kv[here, :, at : at + LANES].reshape(tile, LANES)
                values[t, g] = nt_dot(eye, value).astype(bf16)
            return carry

        lax.fori_loop(0, pages // tile_pages, turn, 0)

    for g in range(KEY_VALUE_HEADS):
        for i in range(QUERY_GROUP):
            head = g * QUERY_GROUP + i
            query[g, i * block : (i + 1) * block, :] = query_ref[:, head * LANES : (head + 1) * LANES]
    if first:
        mixed[...] = jnp.zeros(mixed.shape, f32)
        stats[0:KEY_VALUE_HEADS, :] = jnp.full((KEY_VALUE_HEADS, lanes), HIDDEN, f32)
        stats[KEY_VALUE_HEADS:, :] = jnp.zeros((KEY_VALUE_HEADS, lanes), f32)
    else:
        mixed[...] = state_in[0][0]
        stats[...] = state_in[1][0]

    sel = sel_ref[0]

    def one_tile(t, carry):
        here = pl.ds(t * tile_pages, tile_pages)
        bias = jnp.where(
            position[pl.ds(pl.multiple_of(t * tile, tile), tile), :] <= sel, 0.0, HIDDEN
        ).astype(f32)

        parts = [slice(n * LANES, (n + 1) * LANES) for n in range(lanes // LANES)]
        chains = [(g, part) for g in range(KEY_VALUE_HEADS) for part in parts]
        for g in range(KEY_VALUE_HEADS):
            key = kv[here, :, g * LANES : (g + 1) * LANES].reshape(tile, LANES)
            product = nt_dot(key, query[g])
            for part in parts:
                scores[g, :, part] = product[:, part] + bias
        peaks, shrinks = [], []
        for g, part in chains:
            old = stats[g : g + 1, part]
            new = jnp.maximum(old, jnp.max(scores[g, :, part], axis=0, keepdims=True))
            stats[g : g + 1, part] = new
            peaks.append(new)
            shrinks.append(jnp.exp2((old - new) * scale))
        for (g, part), new, shrink in zip(chains, peaks, shrinks):
            at = KEY_VALUE_HEADS + g
            p = jnp.exp2((scores[g, :, part] - new) * scale)
            stats[at : at + 1, part] = stats[at : at + 1, part] * shrink + jnp.sum(
                p, axis=0, keepdims=True
            )
            raised[g, :, part] = p.astype(bf16)
        for g in range(KEY_VALUE_HEADS):
            shrink = jnp.concatenate(shrinks[g * len(parts) : (g + 1) * len(parts)], axis=1)
            mixed[g] = mixed[g] * shrink + jnp.dot(
                values[t, g], raised[g], preferred_element_type=f32
            )
        return carry

    lax.fori_loop(0, tiles[step], one_tile, 0)

    if last:
        done = []
        for g in range(KEY_VALUE_HEADS):
            at = KEY_VALUE_HEADS + g
            part = (mixed[g] * (1.0 / stats[at : at + 1, :])).astype(bf16)
            done += [part[:, n * LANES : (n + 1) * LANES] for n in range(lanes // LANES)]
        turned = nt_dot(eye, jnp.concatenate(done, axis=0)).astype(bf16)
        for n in range(len(done)):
            for i in range(LANES // block):
                head = n * (LANES // block) + i
                outs[0][:, head * LANES : (head + 1) * LANES] = turned[
                    i * block : (i + 1) * block, n * LANES : (n + 1) * LANES
                ]
    else:
        outs[0][0] = mixed[...]
        outs[1][0] = stats[...]


def attend(first, last, tile_pages, order, sel_lanes, positions, queries, fresh, state, contexts):
    picked, features = queries.shape
    each, page_len, width = contexts[0].shape
    pages = each * len(contexts) + (FRESH_PAGES if first else 0)
    steps = picked // QUERY_BLOCK
    lanes = QUERY_GROUP * QUERY_BLOCK
    wide = pl.BlockSpec((QUERY_BLOCK, features), lambda b, *_: (b, 0))
    state_specs = [
        pl.BlockSpec((1, KEY_VALUE_HEADS, LANES, lanes), lambda b, *_: (b, 0, 0, 0)),
        pl.BlockSpec((1, 2 * KEY_VALUE_HEADS, lanes), lambda b, *_: (b, 0, 0)),
    ]
    state_shapes = [
        jax.ShapeDtypeStruct((steps, KEY_VALUE_HEADS, LANES, lanes), jnp.float32),
        jax.ShapeDtypeStruct((steps, 2 * KEY_VALUE_HEADS, lanes), jnp.float32),
    ]
    share = 0.6
    return pl.pallas_call(
        functools.partial(attend_kernel, first, last, tile_pages, len(contexts)),
        grid_spec=pltpu.PrefetchScalarGridSpec(
            num_scalar_prefetch=3,
            grid=(steps,),
            in_specs=[
                pl.BlockSpec((1, 1, LANES), lambda b, *_: (b, 0, 0)),
                pl.BlockSpec(positions.shape, lambda b, *_: (0, 0)),
                wide,
                *[pl.BlockSpec(x.shape, lambda b, *_: (0, 0)) for x in fresh if first],
                *([] if first else state_specs),
                *[
                    pl.BlockSpec(x.shape, lambda b, *_: (0, 0, 0))
                    if last and not first
                    else pl.BlockSpec(memory_space=pltpu.HBM)
                    for x in contexts
                ],
            ],
            out_specs=[wide] if last else state_specs,
            scratch_shapes=[
                pltpu.VMEM((pages, page_len, width), jnp.bfloat16),
                pltpu.VMEM(
                    (pages // tile_pages, KEY_VALUE_HEADS, LANES, tile_pages * page_len), jnp.bfloat16
                ),
                pltpu.VMEM((pages * page_len, LANES), jnp.int32),
                pltpu.VMEM((KEY_VALUE_HEADS, lanes, LANES), jnp.bfloat16),
                pltpu.VMEM((KEY_VALUE_HEADS, tile_pages * page_len, lanes), jnp.float32),
                pltpu.VMEM((KEY_VALUE_HEADS, tile_pages * page_len, lanes), jnp.bfloat16),
                pltpu.VMEM((KEY_VALUE_HEADS, LANES, lanes), jnp.float32),
                pltpu.VMEM((2 * KEY_VALUE_HEADS, lanes), jnp.float32),
                pltpu.SemaphoreType.DMA,
            ],
        ),
        out_shape=[jax.ShapeDtypeStruct((picked, features), jnp.bfloat16)] if last else state_shapes,
        compiler_params=pltpu.CompilerParams(
            dimension_semantics=("arbitrary",), vmem_limit_bytes=VMEM_LIMIT
        ),
        cost_estimate=pl.CostEstimate(
            flops=int(share * 8 * picked * features * pages * page_len),
            bytes_accessed=2 * pages * page_len * width + 6 * picked * features,
            transcendentals=int(share * picked * features // LANES * pages * page_len),
        ),
    )(*order, sel_lanes, positions, queries, *[x for x in fresh if first], *state, *contexts)


def page_order(slots, positions, own, hold, capacity, groups, tiles, page_len):
    pages = slots.shape[0]
    number = jnp.arange(pages)
    before = number[None, :] < number[:, None]
    owners = slots // hold
    ranks = jnp.sum(((owners[None, :] == owners[:, None]) & before).astype(jnp.int32), axis=1)
    distance = owners ^ own
    last_page = positions.reshape(-1, QUERY_BLOCK)[:, -1] // page_len
    orders = []
    for at, (group, tile_pages) in enumerate(zip(groups, tiles)):
        if group is None:
            arrival = owners * capacity + ranks
            count = pages
        else:
            arrival = jnp.full((pages,), -1, jnp.int32)
            for i, d in enumerate(group):
                arrival = jnp.where(distance == d, i * capacity + ranks, arrival)
            count = len(group) * capacity
        member = arrival >= 0
        place = jnp.sum((member[None, :] & before).astype(jnp.int32), axis=1)
        if at == len(groups) - 1 and at > 0:
            place = arrival
        index = jnp.arange(count)[:, None]
        places = jnp.sum(jnp.where(arrival[None, :] == index, place[None, :], 0), axis=1)
        page = jnp.sum(
            jnp.where(member[None, :] & (place[None, :] == index), number[None, :], 0), axis=1
        )
        seen = jnp.sum((page[None, :] <= last_page[:, None]).astype(jnp.int32), axis=1)
        seen = seen + (FRESH_PAGES if at == 0 else 0)
        orders.append((places, page, (seen + tile_pages - 1) // tile_pages))
    return orders


def per_device(store, page_table, sel_pos, fresh_kv, queries):
    holders = lax.axis_size("store")
    hold, page_len, width = store.shape
    pages = page_table.shape[1]
    picked = sel_pos.shape[1]
    capacity = max(1, pages // holders)
    hbm = pl.BlockSpec(memory_space=pltpu.HBM)
    vmem = pl.BlockSpec(memory_space=pltpu.VMEM)
    dma = pltpu.SemaphoreType.DMA
    params = pltpu.CompilerParams(vmem_limit_bytes=VMEM_LIMIT)
    own = lax.axis_index("store")
    own_word = own.reshape(1).astype(jnp.int32)
    fresh = fresh_kv[0]
    wide = pltpu.VMEM((8, -(-picked // LANES) * LANES), jnp.int32)
    if holders == 16:
        first = (8, 12)
        groups = [(0, 8, 12, 4, 5, 1), (9, 6, 13, 7, 10, 2, 14, 3), (11, 15)]
        others = [d for group in groups for d in group if d not in first]
    else:
        first = ()
        groups = [None]
        others = None

    def swap(x, d):
        return lax.ppermute(x, "store", [(h, h ^ d) for h in range(holders)])

    def exchange(x):
        return lax.all_to_all(x, "store", split_axis=0, concat_axis=0, tiled=True)

    index, *lists = pl.pallas_call(
        functools.partial(index_kernel, hold, page_len, first),
        grid_spec=pltpu.PrefetchScalarGridSpec(
            num_scalar_prefetch=1,
            grid=(1,),
            in_specs=[vmem, vmem],
            out_specs=[vmem] * (1 + len(first)),
            scratch_shapes=[wide],
        ),
        out_shape=[
            jax.ShapeDtypeStruct((holders, 2, LANES), jnp.int32),
            *[jax.ShapeDtypeStruct((1, 2, LANES), jnp.int32)] * len(first),
        ],
        compiler_params=params,
    )(own_word, page_table, sel_pos)
    arrived = {}
    if first:
        lists = [swap(x, d) for x, d in zip(lists, first)]
        parts = pl.pallas_call(
            functools.partial(first_gather_kernel, len(first)),
            grid_spec=pltpu.PrefetchScalarGridSpec(
                num_scalar_prefetch=len(first),
                grid=(1,),
                in_specs=[hbm],
                out_specs=[hbm] * len(first),
                scratch_shapes=[
                    pltpu.VMEM((len(first), capacity, page_len, width), store.dtype),
                    dma,
                    dma,
                ],
            ),
            out_shape=[jax.ShapeDtypeStruct((capacity, page_len, width), store.dtype)] * len(first),
            compiler_params=params,
        )(*lists, store)
        parts, index, table, positions = lax.optimization_barrier(
            (parts, index, page_table, sel_pos)
        )
        arrived = {d: swap(part, d) for d, part in zip(first, parts)}
    else:
        table, positions = page_table, sel_pos
    index_in = exchange(index)

    packed = pl.pallas_call(
        functools.partial(rows_kernel, hold, page_len),
        out_shape=jax.ShapeDtypeStruct((holders, ROW_SLOTS, width), store.dtype),
        scratch_shapes=[wide],
        compiler_params=params,
    )(table, positions, fresh)

    each = jax.ShapeDtypeStruct((capacity, page_len, width), store.dtype)
    whole = jax.ShapeDtypeStruct((holders, capacity, page_len, width), store.dtype)
    parts = pl.pallas_call(
        functools.partial(gather_kernel, capacity, others),
        grid_spec=pltpu.PrefetchScalarGridSpec(
            num_scalar_prefetch=2,
            grid=(1,),
            in_specs=[hbm],
            out_specs=[hbm] * (len(others) if others else 1),
            scratch_shapes=[pltpu.VMEM(store.shape, store.dtype), dma, dma],
        ),
        out_shape=[each] * len(others) if others else [whole],
        compiler_params=params,
    )(own_word, index_in, store)
    parts, packed, table, positions = lax.optimization_barrier((parts, packed, table, positions))
    if others:
        parts = dict(zip(others, parts))
        for d in others:
            if d not in groups[2]:
                arrived[d] = swap(parts[d], d) if d else parts[d]
    else:
        arrived[None] = [exchange(parts[0]).reshape(pages, page_len, width)]
    rows_in = exchange(packed)

    tiles = [LATE_TILE_PAGES if at == len(groups) - 1 else TILE_PAGES for at in range(len(groups))]
    orders = page_order(table[0], positions[0], own, hold, capacity, groups, tiles, page_len)
    sel_lanes = jnp.tile(positions.reshape(-1, 1, QUERY_BLOCK), (1, 1, LANES // QUERY_BLOCK))
    sel_rows = jnp.broadcast_to(positions.reshape(picked, 1), (picked, LANES))
    write_back = pl.pallas_call(
        write_back_kernel,
        grid_spec=pltpu.PrefetchScalarGridSpec(
            num_scalar_prefetch=1,
            grid=(1,),
            in_specs=[vmem, hbm, hbm],
            out_specs=hbm,
            scratch_shapes=[
                pltpu.VMEM(store.shape, store.dtype),
                pltpu.VMEM((holders, ROW_SLOTS, width), store.dtype),
                pltpu.VMEM((holders, capacity, page_len, width), store.dtype),
                dma,
                dma,
                dma,
            ],
        ),
        out_shape=jax.ShapeDtypeStruct(store.shape, store.dtype),
        compiler_params=params,
        cost_estimate=pl.CostEstimate(flops=0, bytes_accessed=4 * store.size, transcendentals=0),
    )
    state = ()
    for at, (group, order) in enumerate(zip(groups, orders)):
        state = attend(
            at == 0,
            at == len(groups) - 1,
            tiles[at],
            order,
            sel_lanes,
            positions,
            queries[0],
            (fresh, sel_rows),
            state,
            [arrived[d] for d in group] if group else arrived[None],
        )
        if at == 0:
            rows_in, state = lax.optimization_barrier((rows_in, state))
            store_out = write_back(index_in, index_in, store, rows_in)
            if others:
                middle = [arrived[d] for d in groups[1]]
                late = [parts[d] for d in groups[2]]
                late, state, store_out, _ = lax.optimization_barrier((late, state, store_out, middle))
                for d, part in zip(groups[2], late):
                    arrived[d] = swap(part, d)
    return (state[0][None], store_out)


def solution(mesh):
    return jax.shard_map(
        per_device,
        mesh=mesh,
        in_specs=(
            P(("groups", "store"), None, None),
            P(("groups", "store"), None),
            P(("groups", "store"), None),
            P(("groups", "store"), None, None),
            P(("groups", "store"), None, None),
        ),
        out_specs=(P(("groups", "store"), None, None), P(("groups", "store"), None, None)),
        check_vma=False,
    )
```

```python
import functools

import jax
import jax.numpy as jnp
from jax import lax
from jax.experimental import pallas as pl
from jax.experimental.pallas import tpu as pltpu
from jax.sharding import PartitionSpec as P

HEAD_WIDTH = 128
KEY_VALUE_HEADS = 4
QUERY_GROUP = 12
SELP = 2
LANES = 128
ROW_SLOTS = 16
VMEM_LIMIT = 60 * 1024 * 1024
QUERY_BLOCK = 32
TILE_PAGES = 32
LATE_TILE_PAGES = 16
FRESH_PAGES = 16
HIDDEN = -1e30
FAR_POSITION = 1 << 24


def nt_dot(a, b):
    return lax.dot_general(a, b, (((1,), (1,)), ((), ())), preferred_element_type=jnp.float32)


def one_hot(condition):
    return jnp.where(condition, 1.0, 0.0)


def pair_places(hold, page_len, table_ref, sel_ref, wide):
    pages = table_ref.shape[1]
    picked = sel_ref.shape[1]
    f32 = jnp.float32
    slots = jnp.broadcast_to(table_ref[...], (pages, pages))
    owners = slots // hold
    local_row = (slots - owners * hold).astype(f32)[0:1]
    owner_row = owners.astype(f32)
    owner_col = owner_row.T
    sub = lax.broadcasted_iota(jnp.int32, (pages, pages), 0)
    lane = lax.broadcasted_iota(jnp.int32, (pages, pages), 1)
    earlier = one_hot((owner_row == owner_col) & (lane < sub))
    rank_col = jnp.sum(earlier, axis=1, keepdims=True)

    wide[...] = jnp.full(wide.shape, -1, jnp.int32)
    wide[0:1, 0:picked] = sel_ref[...]
    position = wide[...]
    page = lax.shift_right_arithmetic(position, page_len.bit_length() - 1)
    offset = (position & (page_len - 1)).astype(f32)[0:1]
    lane_wide = lax.broadcasted_iota(jnp.int32, wide.shape, 1)
    second = one_hot((page == pltpu.roll(page, 1, axis=1)) & (lane_wide > 0))[0:1]
    valid = lane_wide[0:1] < picked
    sub_wide = lax.broadcasted_iota(jnp.int32, (pages, wide.shape[1]), 0)
    in_page = one_hot(sub_wide == page[0:1])
    owner = jnp.sum(in_page * owner_col[:, 0:1], axis=0, keepdims=True)
    rank = jnp.sum(in_page * rank_col, axis=0, keepdims=True)
    return owner_row[0:1], local_row, rank_col, owner, rank, second, offset, valid


def index_kernel(hold, page_len, first, own, table_ref, sel_ref, out_ref, *rest):
    first_refs, wide = rest[:-1], rest[-1]
    holders = out_ref.shape[0]
    pages = table_ref.shape[1]
    f32 = jnp.float32
    bf16 = jnp.bfloat16
    owner_row, local_row, rank_col, owner, rank, second, offset, valid = pair_places(
        hold, page_len, table_ref, sel_ref, wide
    )
    holder = lax.broadcasted_iota(jnp.int32, (holders, pages), 0).astype(f32)
    owned = jnp.where(holder == owner_row, local_row, 0.0)
    lane = lax.broadcasted_iota(jnp.int32, (pages, LANES), 1).astype(f32)
    numbers = jnp.dot(
        owned.astype(bf16), one_hot(lane == rank_col).astype(bf16), preferred_element_type=f32
    )
    holder_wide = lax.broadcasted_iota(jnp.int32, (holders, wide.shape[1]), 0).astype(f32)
    marked = jnp.where((holder_wide == owner) & valid, rank * page_len + offset + 1.0, 0.0)
    place_lane = lax.broadcasted_iota(jnp.int32, (LANES, wide.shape[1]), 0).astype(f32)
    at_place = one_hot(place_lane == SELP * rank + second)
    targets = nt_dot(marked.astype(bf16), at_place.astype(bf16))
    for h in range(holders):
        out_ref[h, 0:1, :] = numbers[h : h + 1, :].astype(jnp.int32)
        out_ref[h, 1:2, :] = targets[h : h + 1, :].astype(jnp.int32)
    for d, ref in zip(first, first_refs):
        ref[0] = out_ref[own[0] ^ d]


def rows_kernel(hold, page_len, table_ref, sel_ref, fresh_ref, packed, wide):
    holders = packed.shape[0]
    picked = sel_ref.shape[1]
    f32 = jnp.float32
    _, _, _, owner, rank, second, _, valid = pair_places(hold, page_len, table_ref, sel_ref, wide)
    spot = jnp.where(valid, owner * ROW_SLOTS + SELP * rank + second, -1.0)[:, 0:picked]
    step = min(holders, 16)
    for start in range(0, holders, step):
        spot_id = lax.broadcasted_iota(jnp.int32, (step * ROW_SLOTS, picked), 0).astype(f32)
        choose = one_hot(spot_id + float(start * ROW_SLOTS) == spot).astype(jnp.bfloat16)
        rows = jnp.dot(choose, fresh_ref[...], preferred_element_type=f32).astype(jnp.bfloat16)
        packed[start : start + step] = rows.reshape(step, ROW_SLOTS, fresh_ref.shape[1])


def first_gather_kernel(count, *refs):
    lists, store_hbm, sends = refs[:count], refs[count], refs[count + 1 : 2 * count + 1]
    held, load_sem, send_sem = refs[2 * count + 1 :]
    capacity = held.shape[1]
    for i, numbers in enumerate(lists):
        for k in range(capacity):
            pltpu.make_async_copy(store_hbm.at[numbers[0, 0, k]], held.at[i, k], load_sem).start()
    pltpu.make_async_copy(held, held, load_sem).wait()
    for i, send in enumerate(sends):
        pltpu.make_async_copy(held.at[i], send, send_sem).start()
    pltpu.make_async_copy(held, held, send_sem).wait()


def gather_kernel(capacity, distances, own, index, store_hbm, *rest):
    sends, (store, load_sem, send_sem) = rest[:-3], rest[-3:]
    load = pltpu.make_async_copy(store_hbm, store, load_sem)
    load.start()
    load.wait()
    for i in range(len(distances) if distances else index.shape[0]):
        r = own[0] ^ distances[i] if distances else i
        send = sends[i] if distances else sends[0].at[i]
        for k in range(capacity):
            pltpu.make_async_copy(store.at[index[r, 0, k]], send.at[k], send_sem).start()
    for send in sends:
        pltpu.make_async_copy(send, send, send_sem).wait()


def write_back_kernel(index, targets_ref, store_hbm, rows_hbm, store_out, *scratch):
    store, rows, blended, load_sem, rows_sem, out_sem = scratch
    holders, capacity, page_len, width = blended.shape
    rows_here = capacity * page_len
    f32 = jnp.float32
    load = pltpu.make_async_copy(store_hbm, store, load_sem)
    load_rows = pltpu.make_async_copy(rows_hbm, rows, rows_sem)
    load.start()
    load_rows.start()
    load_rows.wait()
    load.wait()
    row_id = lax.broadcasted_iota(jnp.int32, (rows_here, ROW_SLOTS), 0)

    def one_request(r, carry):
        hit = one_hot(row_id == targets_ref[r][1:2, 0:ROW_SLOTS] - 1)
        keep = 1.0 - jnp.sum(hit, axis=1, keepdims=True)
        keep = jnp.broadcast_to(keep, (rows_here, LANES)).astype(jnp.bfloat16)
        hit = hit.astype(jnp.bfloat16)
        for c in range(width // LANES):
            lanes = slice(c * LANES, (c + 1) * LANES)
            fresh = jnp.dot(hit, rows[r, :, lanes], preferred_element_type=f32).astype(jnp.bfloat16)
            for k in range(capacity):
                part = slice(k * page_len, (k + 1) * page_len)
                blended[r, k, :, lanes] = store[index[r, 0, k], :, lanes] * keep[part] + fresh[part]
        for k in range(capacity):
            pltpu.make_async_copy(blended.at[r, k], store_out.at[index[r, 0, k]], out_sem).start()
        return carry

    lax.fori_loop(0, holders, one_request, 0)
    pltpu.make_async_copy(store_out, store_out, out_sem).wait()


def attend_kernel(first, last, tile_pages, sources, place, page_number, tiles, *rest):
    sel_ref, positions_ref, query_ref, *rest = rest
    if first:
        fresh_ref, fresh_positions, *rest = rest
    state_in = () if first else rest[:2]
    rest = rest if first else rest[2:]
    contexts, rest = rest[:sources], rest[sources:]
    outs, rest = (rest[:1], rest[1:]) if last else (rest[:2], rest[2:])
    kv, values, position, query, scores, raised, mixed, stats, sem = rest
    pages, page_len, width = kv.shape
    each = contexts[0].shape[0]
    ahead = FRESH_PAGES if first else 0
    direct = last and not first
    block = query_ref.shape[0]
    tile = tile_pages * page_len
    lanes = QUERY_GROUP * block
    scale = 1.4426950408889634 / HEAD_WIDTH**0.5
    f32 = jnp.float32
    bf16 = jnp.bfloat16
    step = pl.program_id(0)
    eye = one_hot(
        lax.broadcasted_iota(jnp.int32, (LANES, LANES), 0)
        == lax.broadcasted_iota(jnp.int32, (LANES, LANES), 1)
    ).astype(bf16)

    @pl.when(step == 0)
    def _():
        for i, context in enumerate(contexts):
            if direct:
                kv[i * each : (i + 1) * each] = context[...]
            else:
                for k in range(each):
                    to = kv.at[ahead + place[i * each + k]]
                    pltpu.make_async_copy(context.at[k], to, sem).start()
        if first:
            picked = fresh_ref.shape[0]
            count = picked // page_len
            kv[0:count] = fresh_ref[...].reshape(count, page_len, width)
            kv[count:ahead] = jnp.zeros((ahead - count, page_len, width), bf16)
            position[0:picked, :] = fresh_positions[...]
            start = ahead * page_len
            position[picked:start, :] = jnp.full((start - picked, LANES), FAR_POSITION, jnp.int32)
        positions = positions_ref[...]
        row = lax.broadcasted_iota(jnp.int32, (page_len, positions.shape[1]), 0)
        ones = jnp.ones((positions.shape[1], LANES), bf16)
        row_lanes = lax.broadcasted_iota(jnp.int32, (page_len, LANES), 0)

        def place_rows(t, carry):
            starts = [page_number[t * FRESH_PAGES + k] * page_len for k in range(FRESH_PAGES)]
            hit = jnp.concatenate([one_hot(row + start == positions) for start in starts], axis=0)
            hidden = jnp.dot(hit.astype(bf16), ones, preferred_element_type=f32)
            plain = jnp.concatenate([row_lanes + start for start in starts], axis=0)
            some = FRESH_PAGES * page_len
            here = pl.ds(pl.multiple_of(ahead * page_len + t * some, some), some)
            position[here, :] = jnp.where(hidden > 0.0, FAR_POSITION, plain)
            return carry

        lax.fori_loop(0, (pages - ahead) // FRESH_PAGES, place_rows, 0)
        if not direct:
            used = kv.at[ahead:]
            pltpu.make_async_copy(used, used, sem).wait()

        def turn(t, carry):
            here = pl.ds(t * tile_pages, tile_pages)
            for g in range(KEY_VALUE_HEADS):
                at = (KEY_VALUE_HEADS + g) * LANES
                value = kv[here, :, at : at + LANES].reshape(tile, LANES)
                values[t, g] = nt_dot(eye, value).astype(bf16)
            return carry

        lax.fori_loop(0, pages // tile_pages, turn, 0)

    for g in range(KEY_VALUE_HEADS):
        for i in range(QUERY_GROUP):
            head = g * QUERY_GROUP + i
            query[g, i * block : (i + 1) * block, :] = query_ref[:, head * LANES : (head + 1) * LANES]
    if first:
        mixed[...] = jnp.zeros(mixed.shape, f32)
        stats[0:KEY_VALUE_HEADS, :] = jnp.full((KEY_VALUE_HEADS, lanes), HIDDEN, f32)
        stats[KEY_VALUE_HEADS:, :] = jnp.zeros((KEY_VALUE_HEADS, lanes), f32)
    else:
        mixed[...] = state_in[0][0]
        stats[...] = state_in[1][0]

    sel = sel_ref[0]

    def one_tile(t, carry):
        here = pl.ds(t * tile_pages, tile_pages)
        bias = jnp.where(
            position[pl.ds(pl.multiple_of(t * tile, tile), tile), :] <= sel, 0.0, HIDDEN
        ).astype(f32)

        parts = [slice(n * LANES, (n + 1) * LANES) for n in range(lanes // LANES)]
        chains = [(g, part) for g in range(KEY_VALUE_HEADS) for part in parts]
        for g in range(KEY_VALUE_HEADS):
            key = kv[here, :, g * LANES : (g + 1) * LANES].reshape(tile, LANES)
            product = nt_dot(key, query[g])
            for part in parts:
                scores[g, :, part] = product[:, part] + bias
        peaks, shrinks = [], []
        for g, part in chains:
            old = stats[g : g + 1, part]
            new = jnp.maximum(old, jnp.max(scores[g, :, part], axis=0, keepdims=True))
            stats[g : g + 1, part] = new
            peaks.append(new)
            shrinks.append(jnp.exp2((old - new) * scale))
        for (g, part), new, shrink in zip(chains, peaks, shrinks):
            at = KEY_VALUE_HEADS + g
            p = jnp.exp2((scores[g, :, part] - new) * scale)
            stats[at : at + 1, part] = stats[at : at + 1, part] * shrink + jnp.sum(
                p, axis=0, keepdims=True
            )
            raised[g, :, part] = p.astype(bf16)
        for g in range(KEY_VALUE_HEADS):
            shrink = jnp.concatenate(shrinks[g * len(parts) : (g + 1) * len(parts)], axis=1)
            mixed[g] = mixed[g] * shrink + jnp.dot(
                values[t, g], raised[g], preferred_element_type=f32
            )
        return carry

    lax.fori_loop(0, tiles[step], one_tile, 0)

    if last:
        done = []
        for g in range(KEY_VALUE_HEADS):
            at = KEY_VALUE_HEADS + g
            part = (mixed[g] * (1.0 / stats[at : at + 1, :])).astype(bf16)
            done += [part[:, n * LANES : (n + 1) * LANES] for n in range(lanes // LANES)]
        turned = nt_dot(eye, jnp.concatenate(done, axis=0)).astype(bf16)
        for n in range(len(done)):
            for i in range(LANES // block):
                head = n * (LANES // block) + i
                outs[0][:, head * LANES : (head + 1) * LANES] = turned[
                    i * block : (i + 1) * block, n * LANES : (n + 1) * LANES
                ]
    else:
        outs[0][0] = mixed[...]
        outs[1][0] = stats[...]


def attend(first, last, tile_pages, order, sel_lanes, positions, queries, fresh, state, contexts):
    picked, features = queries.shape
    each, page_len, width = contexts[0].shape
    pages = each * len(contexts) + (FRESH_PAGES if first else 0)
    steps = picked // QUERY_BLOCK
    lanes = QUERY_GROUP * QUERY_BLOCK
    wide = pl.BlockSpec((QUERY_BLOCK, features), lambda b, *_: (b, 0))
    state_specs = [
        pl.BlockSpec((1, KEY_VALUE_HEADS, LANES, lanes), lambda b, *_: (b, 0, 0, 0)),
        pl.BlockSpec((1, 2 * KEY_VALUE_HEADS, lanes), lambda b, *_: (b, 0, 0)),
    ]
    state_shapes = [
        jax.ShapeDtypeStruct((steps, KEY_VALUE_HEADS, LANES, lanes), jnp.float32),
        jax.ShapeDtypeStruct((steps, 2 * KEY_VALUE_HEADS, lanes), jnp.float32),
    ]
    share = 0.6
    return pl.pallas_call(
        functools.partial(attend_kernel, first, last, tile_pages, len(contexts)),
        grid_spec=pltpu.PrefetchScalarGridSpec(
            num_scalar_prefetch=3,
            grid=(steps,),
            in_specs=[
                pl.BlockSpec((1, 1, LANES), lambda b, *_: (b, 0, 0)),
                pl.BlockSpec(positions.shape, lambda b, *_: (0, 0)),
                wide,
                *[pl.BlockSpec(x.shape, lambda b, *_: (0, 0)) for x in fresh if first],
                *([] if first else state_specs),
                *[
                    pl.BlockSpec(x.shape, lambda b, *_: (0, 0, 0))
                    if last and not first
                    else pl.BlockSpec(memory_space=pltpu.HBM)
                    for x in contexts
                ],
            ],
            out_specs=[wide] if last else state_specs,
            scratch_shapes=[
                pltpu.VMEM((pages, page_len, width), jnp.bfloat16),
                pltpu.VMEM(
                    (pages // tile_pages, KEY_VALUE_HEADS, LANES, tile_pages * page_len), jnp.bfloat16
                ),
                pltpu.VMEM((pages * page_len, LANES), jnp.int32),
                pltpu.VMEM((KEY_VALUE_HEADS, lanes, LANES), jnp.bfloat16),
                pltpu.VMEM((KEY_VALUE_HEADS, tile_pages * page_len, lanes), jnp.float32),
                pltpu.VMEM((KEY_VALUE_HEADS, tile_pages * page_len, lanes), jnp.bfloat16),
                pltpu.VMEM((KEY_VALUE_HEADS, LANES, lanes), jnp.float32),
                pltpu.VMEM((2 * KEY_VALUE_HEADS, lanes), jnp.float32),
                pltpu.SemaphoreType.DMA,
            ],
        ),
        out_shape=[jax.ShapeDtypeStruct((picked, features), jnp.bfloat16)] if last else state_shapes,
        compiler_params=pltpu.CompilerParams(
            dimension_semantics=("arbitrary",), vmem_limit_bytes=VMEM_LIMIT
        ),
        cost_estimate=pl.CostEstimate(
            flops=int(share * 8 * picked * features * pages * page_len),
            bytes_accessed=2 * pages * page_len * width + 6 * picked * features,
            transcendentals=int(share * picked * features // LANES * pages * page_len),
        ),
    )(*order, sel_lanes, positions, queries, *[x for x in fresh if first], *state, *contexts)


def page_order(slots, positions, own, hold, capacity, groups, tiles, page_len):
    pages = slots.shape[0]
    number = jnp.arange(pages)
    before = number[None, :] < number[:, None]
    owners = slots // hold
    ranks = jnp.sum(((owners[None, :] == owners[:, None]) & before).astype(jnp.int32), axis=1)
    distance = owners ^ own
    last_page = positions.reshape(-1, QUERY_BLOCK)[:, -1] // page_len
    orders = []
    for at, (group, tile_pages) in enumerate(zip(groups, tiles)):
        if group is None:
            arrival = owners * capacity + ranks
            count = pages
        else:
            arrival = jnp.full((pages,), -1, jnp.int32)
            for i, d in enumerate(group):
                arrival = jnp.where(distance == d, i * capacity + ranks, arrival)
            count = len(group) * capacity
        member = arrival >= 0
        place = jnp.sum((member[None, :] & before).astype(jnp.int32), axis=1)
        if at == len(groups) - 1 and at > 0:
            place = arrival
        index = jnp.arange(count)[:, None]
        places = jnp.sum(jnp.where(arrival[None, :] == index, place[None, :], 0), axis=1)
        page = jnp.sum(
            jnp.where(member[None, :] & (place[None, :] == index), number[None, :], 0), axis=1
        )
        seen = jnp.sum((page[None, :] <= last_page[:, None]).astype(jnp.int32), axis=1)
        seen = seen + (FRESH_PAGES if at == 0 else 0)
        orders.append((places, page, (seen + tile_pages - 1) // tile_pages))
    return orders


def per_device(store, page_table, sel_pos, fresh_kv, queries):
    holders = lax.axis_size("store")
    hold, page_len, width = store.shape
    pages = page_table.shape[1]
    picked = sel_pos.shape[1]
    capacity = max(1, pages // holders)
    hbm = pl.BlockSpec(memory_space=pltpu.HBM)
    vmem = pl.BlockSpec(memory_space=pltpu.VMEM)
    dma = pltpu.SemaphoreType.DMA
    params = pltpu.CompilerParams(vmem_limit_bytes=VMEM_LIMIT)
    own = lax.axis_index("store")
    own_word = own.reshape(1).astype(jnp.int32)
    fresh = fresh_kv[0]
    wide = pltpu.VMEM((8, -(-picked // LANES) * LANES), jnp.int32)
    if holders == 16:
        first = (8, 12)
        groups = [(0, 8, 12, 4, 5, 1), (9, 6, 13, 7, 10, 2, 14, 3), (11, 15)]
        others = [d for group in groups for d in group if d not in first]
    else:
        first = ()
        groups = [None]
        others = None

    def swap(x, d):
        return lax.ppermute(x, "store", [(h, h ^ d) for h in range(holders)])

    def exchange(x):
        return lax.all_to_all(x, "store", split_axis=0, concat_axis=0, tiled=True)

    index, *lists = pl.pallas_call(
        functools.partial(index_kernel, hold, page_len, first),
        grid_spec=pltpu.PrefetchScalarGridSpec(
            num_scalar_prefetch=1,
            grid=(1,),
            in_specs=[vmem, vmem],
            out_specs=[vmem] * (1 + len(first)),
            scratch_shapes=[wide],
        ),
        out_shape=[
            jax.ShapeDtypeStruct((holders, 2, LANES), jnp.int32),
            *[jax.ShapeDtypeStruct((1, 2, LANES), jnp.int32)] * len(first),
        ],
        compiler_params=params,
    )(own_word, page_table, sel_pos)
    arrived = {}
    if first:
        lists = [swap(x, d) for x, d in zip(lists, first)]
        parts = pl.pallas_call(
            functools.partial(first_gather_kernel, len(first)),
            grid_spec=pltpu.PrefetchScalarGridSpec(
                num_scalar_prefetch=len(first),
                grid=(1,),
                in_specs=[hbm],
                out_specs=[hbm] * len(first),
                scratch_shapes=[
                    pltpu.VMEM((len(first), capacity, page_len, width), store.dtype),
                    dma,
                    dma,
                ],
            ),
            out_shape=[jax.ShapeDtypeStruct((capacity, page_len, width), store.dtype)] * len(first),
            compiler_params=params,
        )(*lists, store)
        parts, index, table, positions = lax.optimization_barrier(
            (parts, index, page_table, sel_pos)
        )
        arrived = {d: swap(part, d) for d, part in zip(first, parts)}
    else:
        table, positions = page_table, sel_pos
    index_in = exchange(index)

    packed = pl.pallas_call(
        functools.partial(rows_kernel, hold, page_len),
        out_shape=jax.ShapeDtypeStruct((holders, ROW_SLOTS, width), store.dtype),
        scratch_shapes=[wide],
        compiler_params=params,
    )(table, positions, fresh)

    each = jax.ShapeDtypeStruct((capacity, page_len, width), store.dtype)
    whole = jax.ShapeDtypeStruct((holders, capacity, page_len, width), store.dtype)
    parts = pl.pallas_call(
        functools.partial(gather_kernel, capacity, others),
        grid_spec=pltpu.PrefetchScalarGridSpec(
            num_scalar_prefetch=2,
            grid=(1,),
            in_specs=[hbm],
            out_specs=[hbm] * (len(others) if others else 1),
            scratch_shapes=[pltpu.VMEM(store.shape, store.dtype), dma, dma],
        ),
        out_shape=[each] * len(others) if others else [whole],
        compiler_params=params,
    )(own_word, index_in, store)
    parts, packed, table, positions = lax.optimization_barrier((parts, packed, table, positions))
    if others:
        for d, part in zip(others, parts):
            arrived[d] = swap(part, d) if d else part
        contexts = [[arrived[d] for d in group] for group in groups]
    else:
        contexts = [[exchange(parts[0]).reshape(pages, page_len, width)]]
    rows_in = exchange(packed)

    store_out = pl.pallas_call(
        write_back_kernel,
        grid_spec=pltpu.PrefetchScalarGridSpec(
            num_scalar_prefetch=1,
            grid=(1,),
            in_specs=[vmem, hbm, hbm],
            out_specs=hbm,
            scratch_shapes=[
                pltpu.VMEM(store.shape, store.dtype),
                pltpu.VMEM((holders, ROW_SLOTS, width), store.dtype),
                pltpu.VMEM((holders, capacity, page_len, width), store.dtype),
                dma,
                dma,
                dma,
            ],
        ),
        out_shape=jax.ShapeDtypeStruct(store.shape, store.dtype),
        compiler_params=params,
        cost_estimate=pl.CostEstimate(flops=0, bytes_accessed=4 * store.size, transcendentals=0),
    )(index_in, index_in, store, rows_in)

    tiles = [LATE_TILE_PAGES if at == len(groups) - 1 else TILE_PAGES for at in range(len(groups))]
    orders = page_order(table[0], positions[0], own, hold, capacity, groups, tiles, page_len)
    sel_lanes = jnp.tile(positions.reshape(-1, 1, QUERY_BLOCK), (1, 1, LANES // QUERY_BLOCK))
    sel_rows = jnp.broadcast_to(positions.reshape(picked, 1), (picked, LANES))
    store_out, sel_lanes = lax.optimization_barrier((store_out, sel_lanes))
    state = ()
    for at, (arrays, order) in enumerate(zip(contexts, orders)):
        state = attend(
            at == 0,
            at == len(groups) - 1,
            tiles[at],
            order,
            sel_lanes,
            positions,
            queries[0],
            (fresh, sel_rows),
            state,
            arrays,
        )
    return (state[0][None], store_out)


def solution(mesh):
    return jax.shard_map(
        per_device,
        mesh=mesh,
        in_specs=(
            P(("groups", "store"), None, None),
            P(("groups", "store"), None),
            P(("groups", "store"), None),
            P(("groups", "store"), None, None),
            P(("groups", "store"), None, None),
        ),
        out_specs=(P(("groups", "store"), None, None), P(("groups", "store"), None, None)),
        check_vma=False,
    )
```

```python
import functools

import jax
import jax.numpy as jnp
from jax import lax
from jax.experimental import pallas as pl
from jax.experimental.pallas import tpu as pltpu
from jax.sharding import PartitionSpec as P

HEAD_WIDTH = 128
KEY_VALUE_HEADS = 4
QUERY_GROUP = 12
SELP = 2
LANES = 128
ROW_SLOTS = 16
VMEM_LIMIT = 60 * 1024 * 1024
QUERY_BLOCK = 32
TILE_PAGES = 32
LATE_TILE_PAGES = 16
FRESH_PAGES = 16
HIDDEN = -1e30
FAR_POSITION = 1 << 24


def nt_dot(a, b):
    return lax.dot_general(a, b, (((1,), (1,)), ((), ())), preferred_element_type=jnp.float32)


def one_hot(condition):
    return jnp.where(condition, 1.0, 0.0)


def pair_places(hold, page_len, table_ref, sel_ref, wide):
    pages = table_ref.shape[1]
    picked = sel_ref.shape[1]
    f32 = jnp.float32
    slots = jnp.broadcast_to(table_ref[...], (pages, pages))
    owners = slots // hold
    local_row = (slots - owners * hold).astype(f32)[0:1]
    owner_row = owners.astype(f32)
    owner_col = owner_row.T
    sub = lax.broadcasted_iota(jnp.int32, (pages, pages), 0)
    lane = lax.broadcasted_iota(jnp.int32, (pages, pages), 1)
    earlier = one_hot((owner_row == owner_col) & (lane < sub))
    rank_col = jnp.sum(earlier, axis=1, keepdims=True)

    wide[...] = jnp.full(wide.shape, -1, jnp.int32)
    wide[0:1, 0:picked] = sel_ref[...]
    position = wide[...]
    page = lax.shift_right_arithmetic(position, page_len.bit_length() - 1)
    offset = (position & (page_len - 1)).astype(f32)[0:1]
    lane_wide = lax.broadcasted_iota(jnp.int32, wide.shape, 1)
    second = one_hot((page == pltpu.roll(page, 1, axis=1)) & (lane_wide > 0))[0:1]
    valid = lane_wide[0:1] < picked
    sub_wide = lax.broadcasted_iota(jnp.int32, (pages, wide.shape[1]), 0)
    in_page = one_hot(sub_wide == page[0:1])
    owner = jnp.sum(in_page * owner_col[:, 0:1], axis=0, keepdims=True)
    rank = jnp.sum(in_page * rank_col, axis=0, keepdims=True)
    return owner_row[0:1], local_row, rank_col, owner, rank, second, offset, valid


def index_kernel(hold, page_len, first, own, table_ref, sel_ref, out_ref, *rest):
    first_refs, wide = rest[:-1], rest[-1]
    holders = out_ref.shape[0]
    pages = table_ref.shape[1]
    f32 = jnp.float32
    bf16 = jnp.bfloat16
    owner_row, local_row, rank_col, owner, rank, second, offset, valid = pair_places(
        hold, page_len, table_ref, sel_ref, wide
    )
    holder = lax.broadcasted_iota(jnp.int32, (holders, pages), 0).astype(f32)
    owned = jnp.where(holder == owner_row, local_row, 0.0)
    lane = lax.broadcasted_iota(jnp.int32, (pages, LANES), 1).astype(f32)
    numbers = jnp.dot(
        owned.astype(bf16), one_hot(lane == rank_col).astype(bf16), preferred_element_type=f32
    )
    holder_wide = lax.broadcasted_iota(jnp.int32, (holders, wide.shape[1]), 0).astype(f32)
    marked = jnp.where((holder_wide == owner) & valid, rank * page_len + offset + 1.0, 0.0)
    place_lane = lax.broadcasted_iota(jnp.int32, (LANES, wide.shape[1]), 0).astype(f32)
    at_place = one_hot(place_lane == SELP * rank + second)
    targets = nt_dot(marked.astype(bf16), at_place.astype(bf16))
    for h in range(holders):
        out_ref[h, 0:1, :] = numbers[h : h + 1, :].astype(jnp.int32)
        out_ref[h, 1:2, :] = targets[h : h + 1, :].astype(jnp.int32)
    for d, ref in zip(first, first_refs):
        ref[0] = out_ref[own[0] ^ d]


def rows_kernel(hold, page_len, table_ref, sel_ref, fresh_ref, packed, wide):
    holders = packed.shape[0]
    picked = sel_ref.shape[1]
    f32 = jnp.float32
    _, _, _, owner, rank, second, _, valid = pair_places(hold, page_len, table_ref, sel_ref, wide)
    spot = jnp.where(valid, owner * ROW_SLOTS + SELP * rank + second, -1.0)[:, 0:picked]
    step = min(holders, 16)
    for start in range(0, holders, step):
        spot_id = lax.broadcasted_iota(jnp.int32, (step * ROW_SLOTS, picked), 0).astype(f32)
        choose = one_hot(spot_id + float(start * ROW_SLOTS) == spot).astype(jnp.bfloat16)
        rows = jnp.dot(choose, fresh_ref[...], preferred_element_type=f32).astype(jnp.bfloat16)
        packed[start : start + step] = rows.reshape(step, ROW_SLOTS, fresh_ref.shape[1])


def first_gather_kernel(count, *refs):
    lists, store_hbm, sends = refs[:count], refs[count], refs[count + 1 : 2 * count + 1]
    held, load_sem, send_sem = refs[2 * count + 1 :]
    capacity = held.shape[1]
    for i, numbers in enumerate(lists):
        for k in range(capacity):
            pltpu.make_async_copy(store_hbm.at[numbers[0, 0, k]], held.at[i, k], load_sem).start()
    pltpu.make_async_copy(held, held, load_sem).wait()
    for i, send in enumerate(sends):
        pltpu.make_async_copy(held.at[i], send, send_sem).start()
    pltpu.make_async_copy(held, held, send_sem).wait()


def gather_kernel(capacity, distances, own, index, store_hbm, *rest):
    sends, (store, load_sem, send_sem) = rest[:-3], rest[-3:]
    load = pltpu.make_async_copy(store_hbm, store, load_sem)
    load.start()
    load.wait()
    for i in range(len(distances) if distances else index.shape[0]):
        r = own[0] ^ distances[i] if distances else i
        send = sends[i] if distances else sends[0].at[i]
        for k in range(capacity):
            pltpu.make_async_copy(store.at[index[r, 0, k]], send.at[k], send_sem).start()
    for send in sends:
        pltpu.make_async_copy(send, send, send_sem).wait()


def write_back_kernel(index, targets_ref, store_hbm, rows_hbm, store_out, *scratch):
    store, rows, blended, load_sem, rows_sem, out_sem = scratch
    holders, capacity, page_len, width = blended.shape
    rows_here = capacity * page_len
    f32 = jnp.float32
    load = pltpu.make_async_copy(store_hbm, store, load_sem)
    load_rows = pltpu.make_async_copy(rows_hbm, rows, rows_sem)
    load.start()
    load_rows.start()
    load_rows.wait()
    load.wait()
    row_id = lax.broadcasted_iota(jnp.int32, (rows_here, ROW_SLOTS), 0)

    def one_request(r, carry):
        hit = one_hot(row_id == targets_ref[r][1:2, 0:ROW_SLOTS] - 1)
        keep = 1.0 - jnp.sum(hit, axis=1, keepdims=True)
        keep = jnp.broadcast_to(keep, (rows_here, LANES)).astype(jnp.bfloat16)
        hit = hit.astype(jnp.bfloat16)
        for c in range(width // LANES):
            lanes = slice(c * LANES, (c + 1) * LANES)
            fresh = jnp.dot(hit, rows[r, :, lanes], preferred_element_type=f32).astype(jnp.bfloat16)
            for k in range(capacity):
                part = slice(k * page_len, (k + 1) * page_len)
                blended[r, k, :, lanes] = store[index[r, 0, k], :, lanes] * keep[part] + fresh[part]
        for k in range(capacity):
            pltpu.make_async_copy(blended.at[r, k], store_out.at[index[r, 0, k]], out_sem).start()
        return carry

    lax.fori_loop(0, holders, one_request, 0)
    pltpu.make_async_copy(store_out, store_out, out_sem).wait()


def attend_kernel(first, last, tile_pages, sources, place, page_number, tiles, *rest):
    sel_ref, positions_ref, query_ref, *rest = rest
    if first:
        fresh_ref, fresh_positions, *rest = rest
    state_in = () if first else rest[:2]
    rest = rest if first else rest[2:]
    contexts, rest = rest[:sources], rest[sources:]
    outs, rest = (rest[:1], rest[1:]) if last else (rest[:2], rest[2:])
    kv, values, position, query, scores, raised, mixed, stats, sem = rest
    pages, page_len, width = kv.shape
    each = contexts[0].shape[0]
    ahead = FRESH_PAGES if first else 0
    direct = last and not first
    block = query_ref.shape[0]
    tile = tile_pages * page_len
    lanes = QUERY_GROUP * block
    scale = 1.4426950408889634 / HEAD_WIDTH**0.5
    f32 = jnp.float32
    bf16 = jnp.bfloat16
    step = pl.program_id(0)
    eye = one_hot(
        lax.broadcasted_iota(jnp.int32, (LANES, LANES), 0)
        == lax.broadcasted_iota(jnp.int32, (LANES, LANES), 1)
    ).astype(bf16)

    @pl.when(step == 0)
    def _():
        for i, context in enumerate(contexts):
            if direct:
                kv[i * each : (i + 1) * each] = context[...]
            else:
                for k in range(each):
                    to = kv.at[ahead + place[i * each + k]]
                    pltpu.make_async_copy(context.at[k], to, sem).start()
        if first:
            picked = fresh_ref.shape[0]
            count = picked // page_len
            kv[0:count] = fresh_ref[...].reshape(count, page_len, width)
            kv[count:ahead] = jnp.zeros((ahead - count, page_len, width), bf16)
            position[0:picked, :] = fresh_positions[...]
            start = ahead * page_len
            position[picked:start, :] = jnp.full((start - picked, LANES), FAR_POSITION, jnp.int32)
        positions = positions_ref[...]
        row = lax.broadcasted_iota(jnp.int32, (page_len, positions.shape[1]), 0)
        ones = jnp.ones((positions.shape[1], LANES), bf16)
        row_lanes = lax.broadcasted_iota(jnp.int32, (page_len, LANES), 0)

        def place_rows(t, carry):
            starts = [page_number[t * FRESH_PAGES + k] * page_len for k in range(FRESH_PAGES)]
            hit = jnp.concatenate([one_hot(row + start == positions) for start in starts], axis=0)
            hidden = jnp.dot(hit.astype(bf16), ones, preferred_element_type=f32)
            plain = jnp.concatenate([row_lanes + start for start in starts], axis=0)
            some = FRESH_PAGES * page_len
            here = pl.ds(pl.multiple_of(ahead * page_len + t * some, some), some)
            position[here, :] = jnp.where(hidden > 0.0, FAR_POSITION, plain)
            return carry

        lax.fori_loop(0, (pages - ahead) // FRESH_PAGES, place_rows, 0)
        if not direct:
            used = kv.at[ahead:]
            pltpu.make_async_copy(used, used, sem).wait()

        def turn(t, carry):
            here = pl.ds(t * tile_pages, tile_pages)
            for g in range(KEY_VALUE_HEADS):
                at = (KEY_VALUE_HEADS + g) * LANES
                value = kv[here, :, at : at + LANES].reshape(tile, LANES)
                values[t, g] = nt_dot(eye, value).astype(bf16)
            return carry

        lax.fori_loop(0, pages // tile_pages, turn, 0)

    for g in range(KEY_VALUE_HEADS):
        for i in range(QUERY_GROUP):
            head = g * QUERY_GROUP + i
            query[g, i * block : (i + 1) * block, :] = query_ref[:, head * LANES : (head + 1) * LANES]
    if first:
        mixed[...] = jnp.zeros(mixed.shape, f32)
        stats[0:KEY_VALUE_HEADS, :] = jnp.full((KEY_VALUE_HEADS, lanes), HIDDEN, f32)
        stats[KEY_VALUE_HEADS:, :] = jnp.zeros((KEY_VALUE_HEADS, lanes), f32)
    else:
        mixed[...] = state_in[0][0]
        stats[...] = state_in[1][0]

    sel = sel_ref[0]

    def one_tile(t, carry):
        here = pl.ds(t * tile_pages, tile_pages)
        bias = jnp.where(
            position[pl.ds(pl.multiple_of(t * tile, tile), tile), :] <= sel, 0.0, HIDDEN
        ).astype(f32)

        parts = [slice(n * LANES, (n + 1) * LANES) for n in range(lanes // LANES)]
        chains = [(g, part) for g in range(KEY_VALUE_HEADS) for part in parts]
        for g in range(KEY_VALUE_HEADS):
            key = kv[here, :, g * LANES : (g + 1) * LANES].reshape(tile, LANES)
            product = nt_dot(key, query[g])
            for part in parts:
                scores[g, :, part] = product[:, part] + bias
        peaks, shrinks = [], []
        for g, part in chains:
            old = stats[g : g + 1, part]
            new = jnp.maximum(old, jnp.max(scores[g, :, part], axis=0, keepdims=True))
            stats[g : g + 1, part] = new
            peaks.append(new)
            shrinks.append(jnp.exp2((old - new) * scale))
        for (g, part), new, shrink in zip(chains, peaks, shrinks):
            at = KEY_VALUE_HEADS + g
            p = jnp.exp2((scores[g, :, part] - new) * scale)
            stats[at : at + 1, part] = stats[at : at + 1, part] * shrink + jnp.sum(
                p, axis=0, keepdims=True
            )
            raised[g, :, part] = p.astype(bf16)
        for g in range(KEY_VALUE_HEADS):
            shrink = jnp.concatenate(shrinks[g * len(parts) : (g + 1) * len(parts)], axis=1)
            mixed[g] = mixed[g] * shrink + jnp.dot(
                values[t, g], raised[g], preferred_element_type=f32
            )
        return carry

    lax.fori_loop(0, tiles[step], one_tile, 0)

    if last:
        done = []
        for g in range(KEY_VALUE_HEADS):
            at = KEY_VALUE_HEADS + g
            part = (mixed[g] * (1.0 / stats[at : at + 1, :])).astype(bf16)
            done += [part[:, n * LANES : (n + 1) * LANES] for n in range(lanes // LANES)]
        turned = nt_dot(eye, jnp.concatenate(done, axis=0)).astype(bf16)
        for n in range(len(done)):
            for i in range(LANES // block):
                head = n * (LANES // block) + i
                outs[0][:, head * LANES : (head + 1) * LANES] = turned[
                    i * block : (i + 1) * block, n * LANES : (n + 1) * LANES
                ]
    else:
        outs[0][0] = mixed[...]
        outs[1][0] = stats[...]


def attend(first, last, tile_pages, order, sel_lanes, positions, queries, fresh, state, contexts):
    picked, features = queries.shape
    each, page_len, width = contexts[0].shape
    pages = each * len(contexts) + (FRESH_PAGES if first else 0)
    steps = picked // QUERY_BLOCK
    lanes = QUERY_GROUP * QUERY_BLOCK
    wide = pl.BlockSpec((QUERY_BLOCK, features), lambda b, *_: (b, 0))
    state_specs = [
        pl.BlockSpec((1, KEY_VALUE_HEADS, LANES, lanes), lambda b, *_: (b, 0, 0, 0)),
        pl.BlockSpec((1, 2 * KEY_VALUE_HEADS, lanes), lambda b, *_: (b, 0, 0)),
    ]
    state_shapes = [
        jax.ShapeDtypeStruct((steps, KEY_VALUE_HEADS, LANES, lanes), jnp.float32),
        jax.ShapeDtypeStruct((steps, 2 * KEY_VALUE_HEADS, lanes), jnp.float32),
    ]
    share = 0.6
    return pl.pallas_call(
        functools.partial(attend_kernel, first, last, tile_pages, len(contexts)),
        grid_spec=pltpu.PrefetchScalarGridSpec(
            num_scalar_prefetch=3,
            grid=(steps,),
            in_specs=[
                pl.BlockSpec((1, 1, LANES), lambda b, *_: (b, 0, 0)),
                pl.BlockSpec(positions.shape, lambda b, *_: (0, 0)),
                wide,
                *[pl.BlockSpec(x.shape, lambda b, *_: (0, 0)) for x in fresh if first],
                *([] if first else state_specs),
                *[
                    pl.BlockSpec(x.shape, lambda b, *_: (0, 0, 0))
                    if last and not first
                    else pl.BlockSpec(memory_space=pltpu.HBM)
                    for x in contexts
                ],
            ],
            out_specs=[wide] if last else state_specs,
            scratch_shapes=[
                pltpu.VMEM((pages, page_len, width), jnp.bfloat16),
                pltpu.VMEM(
                    (pages // tile_pages, KEY_VALUE_HEADS, LANES, tile_pages * page_len), jnp.bfloat16
                ),
                pltpu.VMEM((pages * page_len, LANES), jnp.int32),
                pltpu.VMEM((KEY_VALUE_HEADS, lanes, LANES), jnp.bfloat16),
                pltpu.VMEM((KEY_VALUE_HEADS, tile_pages * page_len, lanes), jnp.float32),
                pltpu.VMEM((KEY_VALUE_HEADS, tile_pages * page_len, lanes), jnp.bfloat16),
                pltpu.VMEM((KEY_VALUE_HEADS, LANES, lanes), jnp.float32),
                pltpu.VMEM((2 * KEY_VALUE_HEADS, lanes), jnp.float32),
                pltpu.SemaphoreType.DMA,
            ],
        ),
        out_shape=[jax.ShapeDtypeStruct((picked, features), jnp.bfloat16)] if last else state_shapes,
        compiler_params=pltpu.CompilerParams(
            dimension_semantics=("arbitrary",), vmem_limit_bytes=VMEM_LIMIT
        ),
        cost_estimate=pl.CostEstimate(
            flops=int(share * 8 * picked * features * pages * page_len),
            bytes_accessed=2 * pages * page_len * width + 6 * picked * features,
            transcendentals=int(share * picked * features // LANES * pages * page_len),
        ),
    )(*order, sel_lanes, positions, queries, *[x for x in fresh if first], *state, *contexts)


def page_order(slots, positions, own, hold, capacity, groups, tiles, page_len):
    pages = slots.shape[0]
    number = jnp.arange(pages)
    before = number[None, :] < number[:, None]
    owners = slots // hold
    ranks = jnp.sum(((owners[None, :] == owners[:, None]) & before).astype(jnp.int32), axis=1)
    distance = owners ^ own
    last_page = positions.reshape(-1, QUERY_BLOCK)[:, -1] // page_len
    orders = []
    for at, (group, tile_pages) in enumerate(zip(groups, tiles)):
        if group is None:
            arrival = owners * capacity + ranks
            count = pages
        else:
            arrival = jnp.full((pages,), -1, jnp.int32)
            for i, d in enumerate(group):
                arrival = jnp.where(distance == d, i * capacity + ranks, arrival)
            count = len(group) * capacity
        member = arrival >= 0
        place = jnp.sum((member[None, :] & before).astype(jnp.int32), axis=1)
        if at == len(groups) - 1 and at > 0:
            place = arrival
        index = jnp.arange(count)[:, None]
        places = jnp.sum(jnp.where(arrival[None, :] == index, place[None, :], 0), axis=1)
        page = jnp.sum(
            jnp.where(member[None, :] & (place[None, :] == index), number[None, :], 0), axis=1
        )
        seen = jnp.sum((page[None, :] <= last_page[:, None]).astype(jnp.int32), axis=1)
        seen = seen + (FRESH_PAGES if at == 0 else 0)
        orders.append((places, page, (seen + tile_pages - 1) // tile_pages))
    return orders


def per_device(store, page_table, sel_pos, fresh_kv, queries):
    holders = lax.axis_size("store")
    hold, page_len, width = store.shape
    pages = page_table.shape[1]
    picked = sel_pos.shape[1]
    capacity = max(1, pages // holders)
    hbm = pl.BlockSpec(memory_space=pltpu.HBM)
    vmem = pl.BlockSpec(memory_space=pltpu.VMEM)
    dma = pltpu.SemaphoreType.DMA
    params = pltpu.CompilerParams(vmem_limit_bytes=VMEM_LIMIT)
    own = lax.axis_index("store")
    own_word = own.reshape(1).astype(jnp.int32)
    fresh = fresh_kv[0]
    wide = pltpu.VMEM((8, -(-picked // LANES) * LANES), jnp.int32)
    if holders == 16:
        first = (8, 12)
        groups = [(0, 8, 12, 4, 2, 1), (9, 5, 13, 6, 10, 7, 14, 3), (11, 15)]
        others = [d for group in groups for d in group if d not in first]
    else:
        first = ()
        groups = [None]
        others = None

    def swap(x, d):
        return lax.ppermute(x, "store", [(h, h ^ d) for h in range(holders)])

    def exchange(x):
        return lax.all_to_all(x, "store", split_axis=0, concat_axis=0, tiled=True)

    index, *lists = pl.pallas_call(
        functools.partial(index_kernel, hold, page_len, first),
        grid_spec=pltpu.PrefetchScalarGridSpec(
            num_scalar_prefetch=1,
            grid=(1,),
            in_specs=[vmem, vmem],
            out_specs=[vmem] * (1 + len(first)),
            scratch_shapes=[wide],
        ),
        out_shape=[
            jax.ShapeDtypeStruct((holders, 2, LANES), jnp.int32),
            *[jax.ShapeDtypeStruct((1, 2, LANES), jnp.int32)] * len(first),
        ],
        compiler_params=params,
    )(own_word, page_table, sel_pos)
    arrived = {}
    if first:
        lists = [swap(x, d) for x, d in zip(lists, first)]
        parts = pl.pallas_call(
            functools.partial(first_gather_kernel, len(first)),
            grid_spec=pltpu.PrefetchScalarGridSpec(
                num_scalar_prefetch=len(first),
                grid=(1,),
                in_specs=[hbm],
                out_specs=[hbm] * len(first),
                scratch_shapes=[
                    pltpu.VMEM((len(first), capacity, page_len, width), store.dtype),
                    dma,
                    dma,
                ],
            ),
            out_shape=[jax.ShapeDtypeStruct((capacity, page_len, width), store.dtype)] * len(first),
            compiler_params=params,
        )(*lists, store)
        parts, index, table, positions = lax.optimization_barrier(
            (parts, index, page_table, sel_pos)
        )
        arrived = {d: swap(part, d) for d, part in zip(first, parts)}
    else:
        table, positions = page_table, sel_pos
    index_in = exchange(index)

    packed = pl.pallas_call(
        functools.partial(rows_kernel, hold, page_len),
        out_shape=jax.ShapeDtypeStruct((holders, ROW_SLOTS, width), store.dtype),
        scratch_shapes=[wide],
        compiler_params=params,
    )(table, positions, fresh)

    each = jax.ShapeDtypeStruct((capacity, page_len, width), store.dtype)
    whole = jax.ShapeDtypeStruct((holders, capacity, page_len, width), store.dtype)
    parts = pl.pallas_call(
        functools.partial(gather_kernel, capacity, others),
        grid_spec=pltpu.PrefetchScalarGridSpec(
            num_scalar_prefetch=2,
            grid=(1,),
            in_specs=[hbm],
            out_specs=[hbm] * (len(others) if others else 1),
            scratch_shapes=[pltpu.VMEM(store.shape, store.dtype), dma, dma],
        ),
        out_shape=[each] * len(others) if others else [whole],
        compiler_params=params,
    )(own_word, index_in, store)
    parts, packed, table, positions = lax.optimization_barrier((parts, packed, table, positions))
    if others:
        for d, part in zip(others, parts):
            arrived[d] = swap(part, d) if d else part
        contexts = [[arrived[d] for d in group] for group in groups]
    else:
        contexts = [[exchange(parts[0]).reshape(pages, page_len, width)]]
    rows_in = exchange(packed)

    store_out = pl.pallas_call(
        write_back_kernel,
        grid_spec=pltpu.PrefetchScalarGridSpec(
            num_scalar_prefetch=1,
            grid=(1,),
            in_specs=[vmem, hbm, hbm],
            out_specs=hbm,
            scratch_shapes=[
                pltpu.VMEM(store.shape, store.dtype),
                pltpu.VMEM((holders, ROW_SLOTS, width), store.dtype),
                pltpu.VMEM((holders, capacity, page_len, width), store.dtype),
                dma,
                dma,
                dma,
            ],
        ),
        out_shape=jax.ShapeDtypeStruct(store.shape, store.dtype),
        compiler_params=params,
        cost_estimate=pl.CostEstimate(flops=0, bytes_accessed=4 * store.size, transcendentals=0),
    )(index_in, index_in, store, rows_in)

    tiles = [LATE_TILE_PAGES if at == len(groups) - 1 else TILE_PAGES for at in range(len(groups))]
    orders = page_order(table[0], positions[0], own, hold, capacity, groups, tiles, page_len)
    sel_lanes = jnp.tile(positions.reshape(-1, 1, QUERY_BLOCK), (1, 1, LANES // QUERY_BLOCK))
    sel_rows = jnp.broadcast_to(positions.reshape(picked, 1), (picked, LANES))
    store_out, sel_lanes = lax.optimization_barrier((store_out, sel_lanes))
    state = ()
    for at, (arrays, order) in enumerate(zip(contexts, orders)):
        state = attend(
            at == 0,
            at == len(groups) - 1,
            tiles[at],
            order,
            sel_lanes,
            positions,
            queries[0],
            (fresh, sel_rows),
            state,
            arrays,
        )
    return (state[0][None], store_out)


def solution(mesh):
    return jax.shard_map(
        per_device,
        mesh=mesh,
        in_specs=(
            P(("groups", "store"), None, None),
            P(("groups", "store"), None),
            P(("groups", "store"), None),
            P(("groups", "store"), None, None),
            P(("groups", "store"), None, None),
        ),
        out_specs=(P(("groups", "store"), None, None), P(("groups", "store"), None, None)),
        check_vma=False,
    )
```

```python
import functools

import jax
import jax.numpy as jnp
from jax import lax
from jax.experimental import pallas as pl
from jax.experimental.pallas import tpu as pltpu
from jax.sharding import PartitionSpec as P

HEAD_WIDTH = 128
KEY_VALUE_HEADS = 4
QUERY_GROUP = 12
SELP = 2
LANES = 128
ROW_SLOTS = 16
VMEM_LIMIT = 60 * 1024 * 1024
QUERY_BLOCK = 32
TILE_PAGES = 32
LATE_TILE_PAGES = 16
FRESH_PAGES = 16
HIDDEN = -1e30
FAR_POSITION = 1 << 24


def nt_dot(a, b):
    return lax.dot_general(a, b, (((1,), (1,)), ((), ())), preferred_element_type=jnp.float32)


def one_hot(condition):
    return jnp.where(condition, 1.0, 0.0)


def pair_places(hold, page_len, table_ref, sel_ref, wide):
    pages = table_ref.shape[1]
    picked = sel_ref.shape[1]
    f32 = jnp.float32
    slots = jnp.broadcast_to(table_ref[...], (pages, pages))
    owners = slots // hold
    local_row = (slots - owners * hold).astype(f32)[0:1]
    owner_row = owners.astype(f32)
    owner_col = owner_row.T
    sub = lax.broadcasted_iota(jnp.int32, (pages, pages), 0)
    lane = lax.broadcasted_iota(jnp.int32, (pages, pages), 1)
    earlier = one_hot((owner_row == owner_col) & (lane < sub))
    rank_col = jnp.sum(earlier, axis=1, keepdims=True)

    wide[...] = jnp.full(wide.shape, -1, jnp.int32)
    wide[0:1, 0:picked] = sel_ref[...]
    position = wide[...]
    page = lax.shift_right_arithmetic(position, page_len.bit_length() - 1)
    offset = (position & (page_len - 1)).astype(f32)[0:1]
    lane_wide = lax.broadcasted_iota(jnp.int32, wide.shape, 1)
    second = one_hot((page == pltpu.roll(page, 1, axis=1)) & (lane_wide > 0))[0:1]
    valid = lane_wide[0:1] < picked
    sub_wide = lax.broadcasted_iota(jnp.int32, (pages, wide.shape[1]), 0)
    in_page = one_hot(sub_wide == page[0:1])
    owner = jnp.sum(in_page * owner_col[:, 0:1], axis=0, keepdims=True)
    rank = jnp.sum(in_page * rank_col, axis=0, keepdims=True)
    return owner_row[0:1], local_row, rank_col, owner, rank, second, offset, valid


def index_kernel(hold, page_len, first, own, table_ref, sel_ref, out_ref, *rest):
    first_refs, wide = rest[:-1], rest[-1]
    holders = out_ref.shape[0]
    pages = table_ref.shape[1]
    f32 = jnp.float32
    bf16 = jnp.bfloat16
    owner_row, local_row, rank_col, owner, rank, second, offset, valid = pair_places(
        hold, page_len, table_ref, sel_ref, wide
    )
    holder = lax.broadcasted_iota(jnp.int32, (holders, pages), 0).astype(f32)
    owned = jnp.where(holder == owner_row, local_row, 0.0)
    lane = lax.broadcasted_iota(jnp.int32, (pages, LANES), 1).astype(f32)
    numbers = jnp.dot(
        owned.astype(bf16), one_hot(lane == rank_col).astype(bf16), preferred_element_type=f32
    )
    holder_wide = lax.broadcasted_iota(jnp.int32, (holders, wide.shape[1]), 0).astype(f32)
    marked = jnp.where((holder_wide == owner) & valid, rank * page_len + offset + 1.0, 0.0)
    place_lane = lax.broadcasted_iota(jnp.int32, (LANES, wide.shape[1]), 0).astype(f32)
    at_place = one_hot(place_lane == SELP * rank + second)
    targets = nt_dot(marked.astype(bf16), at_place.astype(bf16))
    for h in range(holders):
        out_ref[h, 0:1, :] = numbers[h : h + 1, :].astype(jnp.int32)
        out_ref[h, 1:2, :] = targets[h : h + 1, :].astype(jnp.int32)
    for d, ref in zip(first, first_refs):
        ref[0] = out_ref[own[0] ^ d]


def rows_kernel(hold, page_len, table_ref, sel_ref, fresh_ref, packed, wide):
    holders = packed.shape[0]
    picked = sel_ref.shape[1]
    f32 = jnp.float32
    _, _, _, owner, rank, second, _, valid = pair_places(hold, page_len, table_ref, sel_ref, wide)
    spot = jnp.where(valid, owner * ROW_SLOTS + SELP * rank + second, -1.0)[:, 0:picked]
    step = min(holders, 16)
    for start in range(0, holders, step):
        spot_id = lax.broadcasted_iota(jnp.int32, (step * ROW_SLOTS, picked), 0).astype(f32)
        choose = one_hot(spot_id + float(start * ROW_SLOTS) == spot).astype(jnp.bfloat16)
        rows = jnp.dot(choose, fresh_ref[...], preferred_element_type=f32).astype(jnp.bfloat16)
        packed[start : start + step] = rows.reshape(step, ROW_SLOTS, fresh_ref.shape[1])


def first_gather_kernel(count, *refs):
    lists, store_hbm, sends = refs[:count], refs[count], refs[count + 1 : 2 * count + 1]
    held, load_sem, send_sem = refs[2 * count + 1 :]
    capacity = held.shape[1]
    for i, numbers in enumerate(lists):
        for k in range(capacity):
            pltpu.make_async_copy(store_hbm.at[numbers[0, 0, k]], held.at[i, k], load_sem).start()
    pltpu.make_async_copy(held, held, load_sem).wait()
    for i, send in enumerate(sends):
        pltpu.make_async_copy(held.at[i], send, send_sem).start()
    pltpu.make_async_copy(held, held, send_sem).wait()


def gather_kernel(capacity, distances, own, index, store_hbm, *rest):
    sends, (store, load_sem, send_sem) = rest[:-3], rest[-3:]
    load = pltpu.make_async_copy(store_hbm, store, load_sem)
    load.start()
    load.wait()
    for i in range(len(distances) if distances else index.shape[0]):
        r = own[0] ^ distances[i] if distances else i
        send = sends[i] if distances else sends[0].at[i]
        for k in range(capacity):
            pltpu.make_async_copy(store.at[index[r, 0, k]], send.at[k], send_sem).start()
    for send in sends:
        pltpu.make_async_copy(send, send, send_sem).wait()


def write_back_kernel(index, targets_ref, store_hbm, rows_hbm, store_out, *scratch):
    store, rows, blended, load_sem, rows_sem, out_sem = scratch
    holders, capacity, page_len, width = blended.shape
    rows_here = capacity * page_len
    f32 = jnp.float32
    load = pltpu.make_async_copy(store_hbm, store, load_sem)
    load_rows = pltpu.make_async_copy(rows_hbm, rows, rows_sem)
    load.start()
    load_rows.start()
    load_rows.wait()
    load.wait()
    row_id = lax.broadcasted_iota(jnp.int32, (rows_here, ROW_SLOTS), 0)

    def one_request(r, carry):
        hit = one_hot(row_id == targets_ref[r][1:2, 0:ROW_SLOTS] - 1)
        keep = 1.0 - jnp.sum(hit, axis=1, keepdims=True)
        keep = jnp.broadcast_to(keep, (rows_here, LANES)).astype(jnp.bfloat16)
        hit = hit.astype(jnp.bfloat16)
        for c in range(width // LANES):
            lanes = slice(c * LANES, (c + 1) * LANES)
            fresh = jnp.dot(hit, rows[r, :, lanes], preferred_element_type=f32).astype(jnp.bfloat16)
            for k in range(capacity):
                part = slice(k * page_len, (k + 1) * page_len)
                blended[r, k, :, lanes] = store[index[r, 0, k], :, lanes] * keep[part] + fresh[part]
        for k in range(capacity):
            pltpu.make_async_copy(blended.at[r, k], store_out.at[index[r, 0, k]], out_sem).start()
        return carry

    lax.fori_loop(0, holders, one_request, 0)
    pltpu.make_async_copy(store_out, store_out, out_sem).wait()


def attend_kernel(first, last, tile_pages, sources, place, page_number, tiles, *rest):
    sel_ref, positions_ref, query_ref, *rest = rest
    if first:
        fresh_ref, fresh_positions, *rest = rest
    state_in = () if first else rest[:2]
    rest = rest if first else rest[2:]
    contexts, rest = rest[:sources], rest[sources:]
    outs, rest = (rest[:1], rest[1:]) if last else (rest[:2], rest[2:])
    kv, values, position, query, scores, raised, mixed, stats, sem = rest
    pages, page_len, width = kv.shape
    each = contexts[0].shape[0]
    ahead = FRESH_PAGES if first else 0
    direct = last and not first
    block = query_ref.shape[0]
    tile = tile_pages * page_len
    lanes = QUERY_GROUP * block
    scale = 1.4426950408889634 / HEAD_WIDTH**0.5
    f32 = jnp.float32
    bf16 = jnp.bfloat16
    step = pl.program_id(0)
    eye = one_hot(
        lax.broadcasted_iota(jnp.int32, (LANES, LANES), 0)
        == lax.broadcasted_iota(jnp.int32, (LANES, LANES), 1)
    ).astype(bf16)

    @pl.when(step == 0)
    def _():
        for i, context in enumerate(contexts):
            if direct:
                kv[i * each : (i + 1) * each] = context[...]
            else:
                for k in range(each):
                    to = kv.at[ahead + place[i * each + k]]
                    pltpu.make_async_copy(context.at[k], to, sem).start()
        if first:
            picked = fresh_ref.shape[0]
            count = picked // page_len
            kv[0:count] = fresh_ref[...].reshape(count, page_len, width)
            kv[count:ahead] = jnp.zeros((ahead - count, page_len, width), bf16)
            position[0:picked, :] = fresh_positions[...]
            start = ahead * page_len
            position[picked:start, :] = jnp.full((start - picked, LANES), FAR_POSITION, jnp.int32)
        positions = positions_ref[...]
        row = lax.broadcasted_iota(jnp.int32, (page_len, positions.shape[1]), 0)
        ones = jnp.ones((positions.shape[1], LANES), bf16)
        row_lanes = lax.broadcasted_iota(jnp.int32, (page_len, LANES), 0)

        def place_rows(t, carry):
            starts = [page_number[t * FRESH_PAGES + k] * page_len for k in range(FRESH_PAGES)]
            hit = jnp.concatenate([one_hot(row + start == positions) for start in starts], axis=0)
            hidden = jnp.dot(hit.astype(bf16), ones, preferred_element_type=f32)
            plain = jnp.concatenate([row_lanes + start for start in starts], axis=0)
            some = FRESH_PAGES * page_len
            here = pl.ds(pl.multiple_of(ahead * page_len + t * some, some), some)
            position[here, :] = jnp.where(hidden > 0.0, FAR_POSITION, plain)
            return carry

        lax.fori_loop(0, (pages - ahead) // FRESH_PAGES, place_rows, 0)
        if not direct:
            used = kv.at[ahead:]
            pltpu.make_async_copy(used, used, sem).wait()

        def turn(t, carry):
            here = pl.ds(t * tile_pages, tile_pages)
            for g in range(KEY_VALUE_HEADS):
                at = (KEY_VALUE_HEADS + g) * LANES
                value = kv[here, :, at : at + LANES].reshape(tile, LANES)
                values[t, g] = nt_dot(eye, value).astype(bf16)
            return carry

        lax.fori_loop(0, pages // tile_pages, turn, 0)

    for g in range(KEY_VALUE_HEADS):
        for i in range(QUERY_GROUP):
            head = g * QUERY_GROUP + i
            query[g, i * block : (i + 1) * block, :] = query_ref[:, head * LANES : (head + 1) * LANES]
    if first:
        mixed[...] = jnp.zeros(mixed.shape, f32)
        stats[0:KEY_VALUE_HEADS, :] = jnp.full((KEY_VALUE_HEADS, lanes), HIDDEN, f32)
        stats[KEY_VALUE_HEADS:, :] = jnp.zeros((KEY_VALUE_HEADS, lanes), f32)
    else:
        mixed[...] = state_in[0][0]
        stats[...] = state_in[1][0]

    sel = sel_ref[0]

    def one_tile(t, carry):
        here = pl.ds(t * tile_pages, tile_pages)
        bias = jnp.where(
            position[pl.ds(pl.multiple_of(t * tile, tile), tile), :] <= sel, 0.0, HIDDEN
        ).astype(f32)

        parts = [slice(n * LANES, (n + 1) * LANES) for n in range(lanes // LANES)]
        chains = [(g, part) for g in range(KEY_VALUE_HEADS) for part in parts]
        for g in range(KEY_VALUE_HEADS):
            key = kv[here, :, g * LANES : (g + 1) * LANES].reshape(tile, LANES)
            product = nt_dot(key, query[g])
            for part in parts:
                scores[g, :, part] = product[:, part] + bias
        peaks, shrinks = [], []
        for g, part in chains:
            old = stats[g : g + 1, part]
            new = jnp.maximum(old, jnp.max(scores[g, :, part], axis=0, keepdims=True))
            stats[g : g + 1, part] = new
            peaks.append(new)
            shrinks.append(jnp.exp2((old - new) * scale))
        for (g, part), new, shrink in zip(chains, peaks, shrinks):
            at = KEY_VALUE_HEADS + g
            p = jnp.exp2((scores[g, :, part] - new) * scale)
            stats[at : at + 1, part] = stats[at : at + 1, part] * shrink + jnp.sum(
                p, axis=0, keepdims=True
            )
            raised[g, :, part] = p.astype(bf16)
        for g in range(KEY_VALUE_HEADS):
            shrink = jnp.concatenate(shrinks[g * len(parts) : (g + 1) * len(parts)], axis=1)
            mixed[g] = mixed[g] * shrink + jnp.dot(
                values[t, g], raised[g], preferred_element_type=f32
            )
        return carry

    lax.fori_loop(0, tiles[step], one_tile, 0)

    if last:
        done = []
        for g in range(KEY_VALUE_HEADS):
            at = KEY_VALUE_HEADS + g
            part = (mixed[g] * (1.0 / stats[at : at + 1, :])).astype(bf16)
            done += [part[:, n * LANES : (n + 1) * LANES] for n in range(lanes // LANES)]
        turned = nt_dot(eye, jnp.concatenate(done, axis=0)).astype(bf16)
        for n in range(len(done)):
            for i in range(LANES // block):
                head = n * (LANES // block) + i
                outs[0][:, head * LANES : (head + 1) * LANES] = turned[
                    i * block : (i + 1) * block, n * LANES : (n + 1) * LANES
                ]
    else:
        outs[0][0] = mixed[...]
        outs[1][0] = stats[...]


def attend(first, last, tile_pages, order, sel_lanes, positions, queries, fresh, state, contexts):
    picked, features = queries.shape
    each, page_len, width = contexts[0].shape
    pages = each * len(contexts) + (FRESH_PAGES if first else 0)
    steps = picked // QUERY_BLOCK
    lanes = QUERY_GROUP * QUERY_BLOCK
    wide = pl.BlockSpec((QUERY_BLOCK, features), lambda b, *_: (b, 0))
    state_specs = [
        pl.BlockSpec((1, KEY_VALUE_HEADS, LANES, lanes), lambda b, *_: (b, 0, 0, 0)),
        pl.BlockSpec((1, 2 * KEY_VALUE_HEADS, lanes), lambda b, *_: (b, 0, 0)),
    ]
    state_shapes = [
        jax.ShapeDtypeStruct((steps, KEY_VALUE_HEADS, LANES, lanes), jnp.float32),
        jax.ShapeDtypeStruct((steps, 2 * KEY_VALUE_HEADS, lanes), jnp.float32),
    ]
    share = 0.6
    return pl.pallas_call(
        functools.partial(attend_kernel, first, last, tile_pages, len(contexts)),
        grid_spec=pltpu.PrefetchScalarGridSpec(
            num_scalar_prefetch=3,
            grid=(steps,),
            in_specs=[
                pl.BlockSpec((1, 1, LANES), lambda b, *_: (b, 0, 0)),
                pl.BlockSpec(positions.shape, lambda b, *_: (0, 0)),
                wide,
                *[pl.BlockSpec(x.shape, lambda b, *_: (0, 0)) for x in fresh if first],
                *([] if first else state_specs),
                *[
                    pl.BlockSpec(x.shape, lambda b, *_: (0, 0, 0))
                    if last and not first
                    else pl.BlockSpec(memory_space=pltpu.HBM)
                    for x in contexts
                ],
            ],
            out_specs=[wide] if last else state_specs,
            scratch_shapes=[
                pltpu.VMEM((pages, page_len, width), jnp.bfloat16),
                pltpu.VMEM(
                    (pages // tile_pages, KEY_VALUE_HEADS, LANES, tile_pages * page_len), jnp.bfloat16
                ),
                pltpu.VMEM((pages * page_len, LANES), jnp.int32),
                pltpu.VMEM((KEY_VALUE_HEADS, lanes, LANES), jnp.bfloat16),
                pltpu.VMEM((KEY_VALUE_HEADS, tile_pages * page_len, lanes), jnp.float32),
                pltpu.VMEM((KEY_VALUE_HEADS, tile_pages * page_len, lanes), jnp.bfloat16),
                pltpu.VMEM((KEY_VALUE_HEADS, LANES, lanes), jnp.float32),
                pltpu.VMEM((2 * KEY_VALUE_HEADS, lanes), jnp.float32),
                pltpu.SemaphoreType.DMA,
            ],
        ),
        out_shape=[jax.ShapeDtypeStruct((picked, features), jnp.bfloat16)] if last else state_shapes,
        compiler_params=pltpu.CompilerParams(
            dimension_semantics=("arbitrary",), vmem_limit_bytes=VMEM_LIMIT
        ),
        cost_estimate=pl.CostEstimate(
            flops=int(share * 8 * picked * features * pages * page_len),
            bytes_accessed=2 * pages * page_len * width + 6 * picked * features,
            transcendentals=int(share * picked * features // LANES * pages * page_len),
        ),
    )(*order, sel_lanes, positions, queries, *[x for x in fresh if first], *state, *contexts)


def page_order(slots, positions, own, hold, capacity, groups, tiles, page_len):
    pages = slots.shape[0]
    number = jnp.arange(pages)
    before = number[None, :] < number[:, None]
    owners = slots // hold
    ranks = jnp.sum(((owners[None, :] == owners[:, None]) & before).astype(jnp.int32), axis=1)
    distance = owners ^ own
    last_page = positions.reshape(-1, QUERY_BLOCK)[:, -1] // page_len
    orders = []
    for at, (group, tile_pages) in enumerate(zip(groups, tiles)):
        if group is None:
            arrival = owners * capacity + ranks
            count = pages
        else:
            arrival = jnp.full((pages,), -1, jnp.int32)
            for i, d in enumerate(group):
                arrival = jnp.where(distance == d, i * capacity + ranks, arrival)
            count = len(group) * capacity
        member = arrival >= 0
        place = jnp.sum((member[None, :] & before).astype(jnp.int32), axis=1)
        if at == len(groups) - 1 and at > 0:
            place = arrival
        index = jnp.arange(count)[:, None]
        places = jnp.sum(jnp.where(arrival[None, :] == index, place[None, :], 0), axis=1)
        page = jnp.sum(
            jnp.where(member[None, :] & (place[None, :] == index), number[None, :], 0), axis=1
        )
        seen = jnp.sum((page[None, :] <= last_page[:, None]).astype(jnp.int32), axis=1)
        seen = seen + (FRESH_PAGES if at == 0 else 0)
        orders.append((places, page, (seen + tile_pages - 1) // tile_pages))
    return orders


def per_device(store, page_table, sel_pos, fresh_kv, queries):
    holders = lax.axis_size("store")
    hold, page_len, width = store.shape
    pages = page_table.shape[1]
    picked = sel_pos.shape[1]
    capacity = max(1, pages // holders)
    hbm = pl.BlockSpec(memory_space=pltpu.HBM)
    vmem = pl.BlockSpec(memory_space=pltpu.VMEM)
    dma = pltpu.SemaphoreType.DMA
    params = pltpu.CompilerParams(vmem_limit_bytes=VMEM_LIMIT)
    own = lax.axis_index("store")
    own_word = own.reshape(1).astype(jnp.int32)
    fresh = fresh_kv[0]
    wide = pltpu.VMEM((8, -(-picked // LANES) * LANES), jnp.int32)
    if holders == 16:
        first = (8, 12)
        groups = [(0, 8, 12, 4, 2, 1), (9, 3, 13, 5, 10, 6, 14, 7), (11, 15)]
        others = [d for group in groups for d in group if d not in first]
    else:
        first = ()
        groups = [None]
        others = None

    def swap(x, d):
        return lax.ppermute(x, "store", [(h, h ^ d) for h in range(holders)])

    def exchange(x):
        return lax.all_to_all(x, "store", split_axis=0, concat_axis=0, tiled=True)

    index, *lists = pl.pallas_call(
        functools.partial(index_kernel, hold, page_len, first),
        grid_spec=pltpu.PrefetchScalarGridSpec(
            num_scalar_prefetch=1,
            grid=(1,),
            in_specs=[vmem, vmem],
            out_specs=[vmem] * (1 + len(first)),
            scratch_shapes=[wide],
        ),
        out_shape=[
            jax.ShapeDtypeStruct((holders, 2, LANES), jnp.int32),
            *[jax.ShapeDtypeStruct((1, 2, LANES), jnp.int32)] * len(first),
        ],
        compiler_params=params,
    )(own_word, page_table, sel_pos)
    arrived = {}
    if first:
        lists = [swap(x, d) for x, d in zip(lists, first)]
        parts = pl.pallas_call(
            functools.partial(first_gather_kernel, len(first)),
            grid_spec=pltpu.PrefetchScalarGridSpec(
                num_scalar_prefetch=len(first),
                grid=(1,),
                in_specs=[hbm],
                out_specs=[hbm] * len(first),
                scratch_shapes=[
                    pltpu.VMEM((len(first), capacity, page_len, width), store.dtype),
                    dma,
                    dma,
                ],
            ),
            out_shape=[jax.ShapeDtypeStruct((capacity, page_len, width), store.dtype)] * len(first),
            compiler_params=params,
        )(*lists, store)
        parts, index, table, positions = lax.optimization_barrier(
            (parts, index, page_table, sel_pos)
        )
        arrived = {d: swap(part, d) for d, part in zip(first, parts)}
    else:
        table, positions = page_table, sel_pos
    index_in = exchange(index)

    packed = pl.pallas_call(
        functools.partial(rows_kernel, hold, page_len),
        out_shape=jax.ShapeDtypeStruct((holders, ROW_SLOTS, width), store.dtype),
        scratch_shapes=[wide],
        compiler_params=params,
    )(table, positions, fresh)

    each = jax.ShapeDtypeStruct((capacity, page_len, width), store.dtype)
    whole = jax.ShapeDtypeStruct((holders, capacity, page_len, width), store.dtype)
    parts = pl.pallas_call(
        functools.partial(gather_kernel, capacity, others),
        grid_spec=pltpu.PrefetchScalarGridSpec(
            num_scalar_prefetch=2,
            grid=(1,),
            in_specs=[hbm],
            out_specs=[hbm] * (len(others) if others else 1),
            scratch_shapes=[pltpu.VMEM(store.shape, store.dtype), dma, dma],
        ),
        out_shape=[each] * len(others) if others else [whole],
        compiler_params=params,
    )(own_word, index_in, store)
    parts, packed, table, positions = lax.optimization_barrier((parts, packed, table, positions))
    if others:
        for d, part in zip(others, parts):
            arrived[d] = swap(part, d) if d else part
        contexts = [[arrived[d] for d in group] for group in groups]
    else:
        contexts = [[exchange(parts[0]).reshape(pages, page_len, width)]]
    rows_in = exchange(packed)

    store_out = pl.pallas_call(
        write_back_kernel,
        grid_spec=pltpu.PrefetchScalarGridSpec(
            num_scalar_prefetch=1,
            grid=(1,),
            in_specs=[vmem, hbm, hbm],
            out_specs=hbm,
            scratch_shapes=[
                pltpu.VMEM(store.shape, store.dtype),
                pltpu.VMEM((holders, ROW_SLOTS, width), store.dtype),
                pltpu.VMEM((holders, capacity, page_len, width), store.dtype),
                dma,
                dma,
                dma,
            ],
        ),
        out_shape=jax.ShapeDtypeStruct(store.shape, store.dtype),
        compiler_params=params,
        cost_estimate=pl.CostEstimate(flops=0, bytes_accessed=4 * store.size, transcendentals=0),
    )(index_in, index_in, store, rows_in)

    tiles = [LATE_TILE_PAGES if at == len(groups) - 1 else TILE_PAGES for at in range(len(groups))]
    orders = page_order(table[0], positions[0], own, hold, capacity, groups, tiles, page_len)
    sel_lanes = jnp.tile(positions.reshape(-1, 1, QUERY_BLOCK), (1, 1, LANES // QUERY_BLOCK))
    sel_rows = jnp.broadcast_to(positions.reshape(picked, 1), (picked, LANES))
    store_out, sel_lanes = lax.optimization_barrier((store_out, sel_lanes))
    state = ()
    for at, (arrays, order) in enumerate(zip(contexts, orders)):
        state = attend(
            at == 0,
            at == len(groups) - 1,
            tiles[at],
            order,
            sel_lanes,
            positions,
            queries[0],
            (fresh, sel_rows),
            state,
            arrays,
        )
    return (state[0][None], store_out)


def solution(mesh):
    return jax.shard_map(
        per_device,
        mesh=mesh,
        in_specs=(
            P(("groups", "store"), None, None),
            P(("groups", "store"), None),
            P(("groups", "store"), None),
            P(("groups", "store"), None, None),
            P(("groups", "store"), None, None),
        ),
        out_specs=(P(("groups", "store"), None, None), P(("groups", "store"), None, None)),
        check_vma=False,
    )
```
